32 devices in a mesh: dp: 4 (over y, x), ctx: 8 (over z, core).
Axes of the slice: x: 2, y: 2, z: 4, core: 2. Of those that a mesh axis runs over, the one named last changes fastest.
Arguments:
- queries: bfloat16 [2048, 1024], P('ctx'), may hold values from -12 to 12
- keys: bfloat16 [2048, 128], P('ctx'), may hold values from -5 to 5
- values: bfloat16 [2048, 128], P('ctx'), may hold values from -5 to 5
- out_grad: bfloat16 [2048, 1024], P('ctx'), may hold values from -5 to 5
- segment_ids: int32 [2048], replicated, may hold values from 0 to 3, never falling along the last dimension, each value on 1 to 1792 neighbouring positions
Outputs:
- attn_out: bfloat16 [2048, 1024], P('ctx', 'dp')
- grad_q: bfloat16 [2048, 1024], P('ctx', 'dp')
- grad_k: bfloat16 [2048, 128], P(('dp', 'ctx'))
- grad_v: bfloat16 [2048, 128], P(('dp', 'ctx'))
The draws below stay inside these ranges and needn't reach their ends.
Inputs may be any that keep to these rules, and one draw needn't show every extreme that they name: `segment_ids`: document numbers never fall along the tokens; each document is a run of positions, the longest exactly 1792.
All inputs are finite; a program needn't handle non-finite values.
Results may differ from the reference program's by a relative error of at most 0.04.
Values may be sent and summed in bfloat16 or wider, within the bound.
No kernel may reach another device: no remote copies, remote signals or barrier semaphores. Data moves between devices by JAX's collectives and lax.ppermute only.
A program may use at most 64 MiB of HBM per device.

```python
import math
import jax
import jax.numpy as jnp
import numpy as np
from jax import lax

HEAD = 128
GROUP_HEADS = 8
DOCS = 4
SEQ_TOKENS = 2048


def draw_queries(key, part):
    key = jax.random.fold_in(key, 11)
    drawn = jnp.clip(2.5 * jax.random.normal(key, (SEQ_TOKENS, GROUP_HEADS * HEAD), jnp.float32), -12.0, 12.0)
    return drawn.astype(jnp.bfloat16)


def draw_keys(key, part):
    key = jax.random.fold_in(key, 23)
    drawn = jnp.clip(jax.random.normal(key, (SEQ_TOKENS, HEAD), jnp.float32), -5.0, 5.0)
    return drawn.astype(jnp.bfloat16)


def shard_levels(stream_key, extent, pieces, smallest, largest):
    def one(dim, parts):
        draws = jax.random.uniform(jax.random.fold_in(jax.random.fold_in(stream_key, 6), dim), (parts,), jnp.float32, smallest / len(pieces), largest / len(pieces))
        return jnp.repeat(jnp.exp(draws), extent[dim] // parts).reshape((-1,) + (1,) * (len(extent) - dim - 1))

    level = one(*pieces[0])
    for cut in pieces[1:]:
        level = level * one(*cut)
    return level


def length_profile(amount, total, most, skew):
    portions = [(1 << 20) // math.isqrt(standing ** skew) + 1 for standing in range(2, amount + 1)]
    surplus, counts = total - most - (amount - 1), [1] * (amount - 1)
    while surplus > 0:
        movable = [i for i in range(amount - 1) if counts[i] < most]
        mass, left = sum([portions[i] for i in movable]), surplus
        for i in movable:
            extra = min(most - counts[i], max(1, left * portions[i] // mass), surplus)
            counts[i] = counts[i] + extra
            surplus = surplus - extra
    return np.array([most] + counts)


def ragged_sizes(rng, number_of, total, reach, skew):
    if number_of == 2:
        one = jax.random.randint(rng, (), max(1, total - reach), min(reach, total - 1) + 1)
        return jnp.stack([one, total - one])
    sizes = jnp.asarray(length_profile(number_of, total, reach, skew), jnp.int32)
    pairs = (number_of - 1) // 2
    giver, receiver = sizes[1:1 + 2 * pairs:2], sizes[2:2 + 2 * pairs:2]
    slack = jnp.minimum(giver - 1, reach - receiver)
    shifted = jax.random.randint(jax.random.fold_in(rng, 1), (pairs,), 0, 1 << 20) % (slack + 1)
    sizes = sizes.at[1:1 + 2 * pairs:2].set(giver - shifted).at[2:2 + 2 * pairs:2].set(receiver + shifted)
    return sizes[jax.random.permutation(jax.random.fold_in(rng, 2), number_of)]


def gaussian(own_key, dims, spread, reach, pieces=(), kind=jnp.bfloat16):
    values = jax.random.normal(own_key, dims, jnp.float32) * spread
    if len(pieces) > 0:
        values = shard_levels(own_key, dims, pieces, -0.22, 0.18) * values
    return jnp.clip(values, min=-reach, max=reach).astype(kind)


def setup_inputs(seed: int = 0) -> dict:
    streams_of = jax.random.split(jax.random.key(seed), 6)
    queries = draw_queries(jax.random.fold_in(streams_of[5], 71), 0)
    keys = draw_keys(jax.random.fold_in(streams_of[5], 71), 0)
    values = gaussian(streams_of[2], (SEQ_TOKENS, HEAD), 1.0, 5.0, ((0, 8),))
    out_grad = gaussian(streams_of[3], (SEQ_TOKENS, GROUP_HEADS * HEAD), 1.0, 5.0, ((0, 8),))
    segment_ids = jnp.searchsorted(jnp.cumsum(ragged_sizes(streams_of[4], DOCS, SEQ_TOKENS, 7 * SEQ_TOKENS // 8, 2)), jnp.arange(SEQ_TOKENS), side="right").astype(jnp.int32)
    return dict(queries=queries, keys=keys, values=values, out_grad=out_grad, segment_ids=segment_ids)


def to_half(value):
    return lax.optimization_barrier(value.astype(jnp.bfloat16)).astype(jnp.float32)


def reference(queries, keys, values, out_grad, segment_ids):
    seq = keys.shape[0]
    width = keys.shape[1]
    heads = queries.shape[1] // width
    scale = width ** -0.5
    block = math.gcd(256, seq)
    key_pos = jnp.arange(seq, dtype=jnp.int32)
    key_f = keys.astype(jnp.float32)
    val_f = values.astype(jnp.float32)

    def one_block(carry, index):
        grad_keys, grad_vals = carry
        start = (index * block).astype(jnp.int32)
        query_b = lax.dynamic_slice_in_dim(queries, start, block, 0).astype(jnp.float32)
        query_h = query_b.reshape(block, heads, width).transpose(1, 0, 2)
        grad_b = lax.dynamic_slice_in_dim(out_grad, start, block, 0).astype(jnp.float32)
        grad_h = grad_b.reshape(block, heads, width).transpose(1, 0, 2)
        query_pos = start + jnp.arange(block, dtype=jnp.int32)
        seg_q = lax.dynamic_slice_in_dim(segment_ids, start, block, 0)
        allowed = (seg_q[:, None] == segment_ids[None, :]) & (key_pos[None, :] <= query_pos[:, None])
        scores = jnp.einsum('hqd,kd->hqk', query_h, key_f) * scale
        scores = jnp.where(allowed[None], scores, -jnp.inf)
        rowmax = jnp.max(scores, axis=-1)
        expd = jnp.exp(scores - rowmax[..., None])
        total = jnp.sum(expd, axis=-1)
        weights = to_half(expd)
        output = jnp.einsum('hqk,kd->hqd', weights, val_f) / total[..., None]
        output_bf = output.astype(jnp.bfloat16)
        delta = jnp.sum(grad_h * output_bf.astype(jnp.float32), axis=-1)
        lse = rowmax + jnp.log(total)
        probs = jnp.exp(scores - lse[..., None])
        probs_bf = to_half(probs)
        grad_vals = grad_vals + jnp.einsum('hqk,hqd->kd', probs_bf, grad_h)
        dprobs = jnp.einsum('hqd,kd->hqk', grad_h, val_f)
        dscores = to_half(probs * (dprobs - delta[..., None]))
        grad_query = jnp.einsum('hqk,kd->hqd', dscores, key_f) * scale
        grad_keys = grad_keys + jnp.einsum('hqk,hqd->kd', dscores, query_h) * scale
        out_rows = output_bf.transpose(1, 0, 2).reshape(block, heads * width)
        gq_rows = grad_query.astype(jnp.bfloat16).transpose(1, 0, 2).reshape(block, heads * width)
        return (grad_keys, grad_vals), (out_rows, gq_rows)

    zeros = jnp.zeros((seq, width), jnp.float32)
    (grad_keys, grad_vals), (out_rows, gq_rows) = lax.scan(
        one_block, (zeros, zeros), jnp.arange(seq // block, dtype=jnp.int32))
    attn_out = out_rows.reshape(seq, heads * width)
    grad_q = gq_rows.reshape(seq, heads * width)
    return attn_out, grad_q, grad_keys.astype(jnp.bfloat16), grad_vals.astype(jnp.bfloat16)
```

```python
import functools
import math

import jax
import jax.numpy as jnp
from jax import lax
from jax.experimental import pallas as pl
from jax.experimental.pallas import tpu as pltpu
from jax.sharding import PartitionSpec as P

NEG = -1e30
LOG2E = 1.4426950408889634
DOC_NUMBERS = 4
VMEM_LIMIT = 40 * 1024 * 1024
NT = (((1,), (1,)), ((), ()))


def mask_bias(seg_ref, dp_index, ctx_index, rows, sub, keys_held):
    seg = seg_ref[...]
    lines = rows // 128
    seg_own = seg_ref[pl.ds(ctx_index * lines, lines), :]
    start = jnp.zeros((lines, 128), jnp.int32)
    for number in range(1, DOC_NUMBERS):
        before = jnp.sum((seg < number).astype(jnp.float32), axis=(0, 1), keepdims=True)
        start = jnp.where(seg_own == number, before.astype(jnp.int32), start)
    start = jnp.concatenate([start[k : k + 1] for k in range(lines)], axis=1)
    query_pos = ctx_index * rows + lax.broadcasted_iota(jnp.int32, (1, rows), 1)
    held = lax.broadcasted_iota(jnp.int32, (keys_held, rows), 0)
    key_pos = (held // sub) * rows + dp_index * sub + held % sub
    allowed = (key_pos >= start) & (key_pos <= query_pos)
    return jnp.where(allowed, 0.0, NEG)


def head_columns(head, width):
    return pl.ds(pl.multiple_of(head * width, width), width)


def forward_kernel(idx_ref, seg_ref, q_ref, g_ref, kv_ref, stats_ref, *refs, dims):
    heads, rows, width, sub, held, dp_count = dims
    outs, bias_ref, vt_ref = refs[:dp_count], refs[dp_count], refs[dp_count + 1]
    dp_index, ctx_index = idx_ref[0], idx_ref[1]
    pair = heads // dp_count
    unit = width**-0.5 * LOG2E
    bias_ref[...] = mask_bias(seg_ref, dp_index, ctx_index, rows, sub, held)
    vt_ref[...] = kv_ref[:, width:].astype(jnp.float32).T.astype(jnp.bfloat16)
    for slot in range(dp_count):
        for part in range(pair):
            head = (dp_index ^ slot) * pair + part
            cols = head_columns(head, width)
            raw = lax.dot_general(
                kv_ref[:, :width], q_ref[:, cols], NT, preferred_element_type=jnp.float32
            )
            scores = raw * unit + bias_ref[...]
            top = jnp.max(scores, axis=0, keepdims=True)
            expd = jnp.exp2(scores - top)
            total = jnp.sum(expd, axis=0, keepdims=True)
            accum = jnp.dot(
                vt_ref[...], expd.astype(jnp.bfloat16), preferred_element_type=jnp.float32
            )
            grad_t = g_ref[:, cols].astype(jnp.float32).T
            delta = jnp.sum(accum * grad_t, axis=0, keepdims=True)
            outs[slot][part * width : (part + 1) * width, :] = accum.astype(jnp.bfloat16)
            stats_ref[pl.ds(head, 1), :] = top
            stats_ref[pl.ds(heads + head, 1), :] = total
            stats_ref[pl.ds(2 * heads + head, 1), :] = delta


def merged_stats(stats, heads):
    tops = [s[:heads] for s in stats]
    top = functools.reduce(jnp.maximum, tops)
    shares = [jnp.exp2(t - top) for t in tops]
    total = sum(f * s[heads : 2 * heads] for f, s in zip(shares, stats))
    delta = sum(f * s[2 * heads :] for f, s in zip(shares, stats)) / total
    return top, shares, total, delta


def backward_kernel(idx_ref, seg_ref, q_ref, g_ref, kv_ref, *refs, dims, ctx_count):
    heads, rows, width, sub, held, dp_count = dims
    stats = refs[:dp_count]
    dq_outs = refs[dp_count : 2 * dp_count]
    kv_outs = refs[2 * dp_count : 2 * dp_count + ctx_count]
    bias_ref, kt_ref, lse_ref, delta_ref, acc_ref = refs[2 * dp_count + ctx_count :]
    dp_index, ctx_index = idx_ref[0], idx_ref[1]
    pair = heads // dp_count
    scale = width**-0.5
    unit = scale * LOG2E
    top, _, total, delta = merged_stats([s[...] for s in stats], heads)
    lse_ref[...] = top + jnp.log2(total)
    delta_ref[...] = delta
    bias_ref[...] = mask_bias(seg_ref, dp_index, ctx_index, rows, sub, held)
    kt_ref[...] = kv_ref[:, :width].astype(jnp.float32).T.astype(jnp.bfloat16)
    for slot in range(dp_count):
        for part in range(pair):
            head = (dp_index ^ slot) * pair + part
            cols = head_columns(head, width)
            query, grad = q_ref[:, cols], g_ref[:, cols]
            raw = lax.dot_general(
                kv_ref[:, :width], query, NT, preferred_element_type=jnp.float32
            )
            probs = jnp.exp2(raw * unit + bias_ref[...] - lse_ref[pl.ds(head, 1), :])
            dprobs = lax.dot_general(
                kv_ref[:, width:], grad, NT, preferred_element_type=jnp.float32
            )
            dscores = (probs * (dprobs - delta_ref[pl.ds(head, 1), :])).astype(jnp.bfloat16)
            dv = jnp.dot(probs.astype(jnp.bfloat16), grad, preferred_element_type=jnp.float32)
            dk = jnp.dot(dscores, query, preferred_element_type=jnp.float32)
            if slot == 0 and part == 0:
                acc_ref[:, :width] = dk
                acc_ref[:, width:] = dv
            else:
                acc_ref[:, :width] += dk
                acc_ref[:, width:] += dv
            dq = jnp.dot(kt_ref[...], dscores, preferred_element_type=jnp.float32)
            dq_outs[slot][part * width : (part + 1) * width, :] = (dq * scale).astype(jnp.bfloat16)
    for shift in range(ctx_count):
        block = lax.rem(ctx_index - shift + ctx_count, ctx_count)
        mine = pl.ds(pl.multiple_of(block * sub, sub), sub)
        kv_outs[shift][:, :width] = (acc_ref[mine, :width] * scale).astype(jnp.bfloat16)
        kv_outs[shift][:, width:] = acc_ref[mine, width:].astype(jnp.bfloat16)


def finish_kernel(idx_ref, *refs, dims, ctx_count):
    heads, rows, width, sub, held, dp_count = dims
    n = dp_count
    stats, outs, dqs = refs[:n], refs[n : 2 * n], refs[2 * n : 3 * n]
    terms = refs[3 * n : 3 * n + ctx_count]
    attn_ref, gq_ref, gk_ref, gv_ref = refs[3 * n + ctx_count :]
    pair = heads // n
    mine = [s[...] for s in stats]
    top, shares, total, _ = merged_stats(mine, heads)
    own = idx_ref[0] * pair
    row = lax.broadcasted_iota(jnp.int32, (heads, 1), 0)
    for part in range(pair):
        here = slice(part * width, (part + 1) * width)

        def pick(array):
            return jnp.sum(jnp.where(row == own + part, array, 0.0), axis=0, keepdims=True)

        joined = sum(o[here, :].astype(jnp.float32) * pick(f) for o, f in zip(outs, shares))
        attn_ref[:, here] = (joined / pick(total)).T.astype(jnp.bfloat16)
        query = sum(t[here, :].astype(jnp.float32) for t in dqs)
        gq_ref[:, here] = query.T.astype(jnp.bfloat16)
    both = sum(t[...].astype(jnp.float32) for t in terms)
    gk_ref[...] = both[:, :width].astype(jnp.bfloat16)
    gv_ref[...] = both[:, width:].astype(jnp.bfloat16)


def on_device(queries, keys, values, out_grad, segment_ids):
    rows = queries.shape[0]
    width = keys.shape[1]
    heads = queries.shape[1] // width
    seq = segment_ids.shape[0]
    dp_index, ctx_index = lax.axis_index("dp"), lax.axis_index("ctx")
    dp_count, ctx_count = lax.axis_size("dp"), lax.axis_size("ctx")
    sub = rows // dp_count
    held = sub * ctx_count
    pair = heads // dp_count
    dims = (heads, rows, width, sub, held, dp_count)
    idx = jnp.stack([dp_index, ctx_index]).astype(jnp.int32)
    seg = segment_ids.reshape(seq // 128, 128)
    params = pltpu.CompilerParams(vmem_limit_bytes=VMEM_LIMIT)
    smem = pl.BlockSpec(memory_space=pltpu.SMEM)
    vmem = pl.BlockSpec(memory_space=pltpu.VMEM)
    bf16, f32 = jnp.bfloat16, jnp.float32
    shape = jax.ShapeDtypeStruct

    def cost(products, exps):
        return pl.CostEstimate(
            flops=products * 2 * heads * rows * held * width,
            bytes_accessed=8 * rows * heads * width,
            transcendentals=exps * heads * rows * held,
        )

    own_kv = jnp.concatenate(
        [lax.dynamic_slice_in_dim(a, dp_index * sub, sub, 0) for a in (keys, values)], axis=1
    )
    kv = lax.all_gather(own_kv, "ctx", axis=0, tiled=True)

    stats, *outs = pl.pallas_call(
        functools.partial(forward_kernel, dims=dims),
        out_shape=[shape((3 * heads, rows), f32)]
        + [shape((pair * width, rows), bf16)] * dp_count,
        in_specs=[smem] + [vmem] * 4,
        out_specs=[vmem] * (1 + dp_count),
        scratch_shapes=[pltpu.VMEM((held, rows), f32), pltpu.VMEM((width, held), bf16)],
        compiler_params=params,
        cost_estimate=cost(2, 1),
        name="attend",
    )(idx, seg, queries, out_grad, kv)

    def over_dp(array, slot):
        return lax.ppermute(array, "dp", [(d, d ^ slot) for d in range(dp_count)])

    all_stats = [stats] + [over_dp(stats, s) for s in range(1, dp_count)]
    all_outs = [outs[0]] + [over_dp(outs[s], s) for s in range(1, dp_count)]

    grads = pl.pallas_call(
        functools.partial(backward_kernel, dims=dims, ctx_count=ctx_count),
        out_shape=[shape((pair * width, rows), bf16)] * dp_count
        + [shape((sub, 2 * width), bf16)] * ctx_count,
        in_specs=[smem] + [vmem] * (4 + dp_count),
        out_specs=[vmem] * (dp_count + ctx_count),
        scratch_shapes=[
            pltpu.VMEM((held, rows), f32),
            pltpu.VMEM((width, held), bf16),
            pltpu.VMEM((heads, rows), f32),
            pltpu.VMEM((heads, rows), f32),
            pltpu.VMEM((held, 2 * width), f32),
        ],
        compiler_params=params,
        cost_estimate=cost(5, 1),
        name="differentiate",
    )(idx, seg, queries, out_grad, kv, *all_stats)
    dqs, terms = grads[:dp_count], grads[dp_count:]
    all_dqs = [dqs[0]] + [over_dp(dqs[s], s) for s in range(1, dp_count)]

    def to_owner(array, shift):
        moves = [
            (d * ctx_count + c, dp_count * (c - shift) + d)
            for d in range(dp_count)
            for c in range(shift, ctx_count)
        ]
        return lax.ppermute(array, ("dp", "ctx"), moves)

    all_terms = [to_owner(t, k) for k, t in enumerate(terms)]

    return pl.pallas_call(
        functools.partial(finish_kernel, dims=dims, ctx_count=ctx_count),
        out_shape=[shape((rows, pair * width), bf16)] * 2 + [shape((sub, width), bf16)] * 2,
        in_specs=[smem] + [vmem] * (3 * dp_count + ctx_count),
        out_specs=[vmem] * 4,
        compiler_params=params,
        name="finish",
    )(idx, *all_stats, *all_outs, *all_dqs, *all_terms)


def solution(mesh):
    return jax.shard_map(
        on_device,
        mesh=mesh,
        in_specs=(P("ctx", None), P("ctx", None), P("ctx", None), P("ctx", None), P()),
        out_specs=(P("ctx", "dp"), P("ctx", "dp"), P(("dp", "ctx"), None), P(("dp", "ctx"), None)),
        check_vma=False,
    )
```

```python
import functools

import jax
import jax.numpy as jnp
from jax import lax
from jax.experimental import pallas as pl
from jax.experimental.pallas import tpu as pltpu
from jax.sharding import PartitionSpec as P

NEG = -1e30
LOG2E = 1.4426950408889634
DOC_NUMBERS = 4
VMEM_LIMIT = 40 * 1024 * 1024
NT = (((1,), (1,)), ((), ()))


def mask_bias(seg_ref, dp_index, ctx_index, rows, sub, keys_held):
    seg = seg_ref[...]
    lines = rows // 128
    seg_own = seg_ref[pl.ds(ctx_index * lines, lines), :]
    start = jnp.zeros((lines, 128), jnp.int32)
    for number in range(1, DOC_NUMBERS):
        before = jnp.sum((seg < number).astype(jnp.float32), axis=(0, 1), keepdims=True)
        start = jnp.where(seg_own == number, before.astype(jnp.int32), start)
    start = jnp.concatenate([start[k : k + 1] for k in range(lines)], axis=1)
    query_pos = ctx_index * rows + lax.broadcasted_iota(jnp.int32, (1, rows), 1)
    held = lax.broadcasted_iota(jnp.int32, (keys_held, rows), 0)
    key_pos = (held // sub) * rows + dp_index * sub + held % sub
    allowed = (key_pos >= start) & (key_pos <= query_pos)
    return jnp.where(allowed, 0.0, NEG)


def forward_kernel(
    idx_ref, seg_ref, q_ref, g_ref, kv_ref, stats_ref, out_ref, bias_ref, vt_ref, *, dims
):
    heads, rows, width, sub, held, dp_count = dims
    dp_index, ctx_index = idx_ref[0], idx_ref[1]
    unit = width**-0.5 * LOG2E
    bias_ref[...] = mask_bias(seg_ref, dp_index, ctx_index, rows, sub, held)
    vt_ref[...] = kv_ref[:, width:].astype(jnp.float32).T.astype(jnp.bfloat16)
    for head in range(heads):
        cols = slice(head * width, (head + 1) * width)
        raw = lax.dot_general(
            kv_ref[:, :width], q_ref[:, cols], NT, preferred_element_type=jnp.float32
        )
        scores = raw * unit + bias_ref[...]
        top = jnp.max(scores, axis=0, keepdims=True)
        expd = jnp.exp2(scores - top)
        total = jnp.sum(expd, axis=0, keepdims=True)
        accum = jnp.dot(vt_ref[...], expd.astype(jnp.bfloat16), preferred_element_type=jnp.float32)
        delta = jnp.sum(accum * g_ref[:, cols].astype(jnp.float32).T, axis=0, keepdims=True)
        out_ref[cols, :] = accum.astype(jnp.bfloat16)
        for row, value in enumerate((top, total, delta)):
            for copy in range(dp_count):
                stats_ref[copy, row * heads + head : row * heads + head + 1, :] = value


def merged_stats(stats, heads):
    top = jnp.max(stats[:, :heads], axis=0)
    shares = jnp.exp2(stats[:, :heads] - top)
    total = jnp.sum(shares * stats[:, heads : 2 * heads], axis=0)
    delta = jnp.sum(shares * stats[:, 2 * heads :], axis=0) / total
    return top, shares, total, delta


def backward_kernel(
    idx_ref,
    seg_ref,
    q_ref,
    g_ref,
    kv_ref,
    stats_ref,
    dq_ref,
    terms_ref,
    bias_ref,
    kt_ref,
    lse_ref,
    delta_ref,
    acc_ref,
    *,
    dims,
):
    heads, rows, width, sub, held, dp_count = dims
    dp_index, ctx_index = idx_ref[0], idx_ref[1]
    scale = width**-0.5
    unit = scale * LOG2E
    top, _, total, delta = merged_stats(stats_ref[...], heads)
    lse_ref[...] = top + jnp.log2(total)
    delta_ref[...] = delta
    bias_ref[...] = mask_bias(seg_ref, dp_index, ctx_index, rows, sub, held)
    kt_ref[...] = kv_ref[:, :width].astype(jnp.float32).T.astype(jnp.bfloat16)
    for head in range(heads):
        cols = slice(head * width, (head + 1) * width)
        query, grad = q_ref[:, cols], g_ref[:, cols]
        raw = lax.dot_general(kv_ref[:, :width], query, NT, preferred_element_type=jnp.float32)
        probs = jnp.exp2(raw * unit + bias_ref[...] - lse_ref[head : head + 1, :])
        dprobs = lax.dot_general(kv_ref[:, width:], grad, NT, preferred_element_type=jnp.float32)
        dscores = (probs * (dprobs - delta_ref[head : head + 1, :])).astype(jnp.bfloat16)
        dv = jnp.dot(probs.astype(jnp.bfloat16), grad, preferred_element_type=jnp.float32)
        dk = jnp.dot(dscores, query, preferred_element_type=jnp.float32)
        if head == 0:
            acc_ref[:, :width] = dk
            acc_ref[:, width:] = dv
        else:
            acc_ref[:, :width] += dk
            acc_ref[:, width:] += dv
        dq = jnp.dot(kt_ref[...], dscores, preferred_element_type=jnp.float32)
        dq_ref[cols, :] = (dq * scale).astype(jnp.bfloat16)
    terms_ref[:, :width] = (acc_ref[:, :width] * scale).astype(jnp.bfloat16)
    terms_ref[:, width:] = acc_ref[:, width:].astype(jnp.bfloat16)


def sum_kernel(terms_ref, out_ref, *, count):
    size = out_ref.shape[0]
    total = sum(
        terms_ref[k * size : (k + 1) * size, :].astype(jnp.float32) for k in range(count)
    )
    out_ref[...] = total.astype(jnp.bfloat16)


def finish_kernel(
    idx_ref, stats_ref, outs_ref, dqs_ref, terms_ref, attn_ref, gq_ref, gk_ref, gv_ref, *, dims
):
    heads, rows, width, sub, held, dp_count = dims
    pair = heads // dp_count
    top, shares, total, _ = merged_stats(stats_ref[...], heads)
    own = idx_ref[0] * pair
    row = lax.broadcasted_iota(jnp.int32, (heads, 1), 0)
    for part in range(pair):
        here = slice(part * width, (part + 1) * width)

        def pick(array):
            return jnp.sum(jnp.where(row == own + part, array, 0.0), axis=0, keepdims=True)

        def block(ref, k):
            start = (k * pair + part) * width
            return ref[start : start + width, :].astype(jnp.float32)

        joined = sum(block(outs_ref, k) * pick(shares[k]) for k in range(dp_count))
        attn_ref[:, here] = (joined / pick(total)).T.astype(jnp.bfloat16)
        query = sum(block(dqs_ref, k) for k in range(dp_count))
        gq_ref[:, here] = query.T.astype(jnp.bfloat16)
    gk_ref[...] = terms_ref[:, :width]
    gv_ref[...] = terms_ref[:, width:]


def on_device(queries, keys, values, out_grad, segment_ids):
    rows = queries.shape[0]
    width = keys.shape[1]
    heads = queries.shape[1] // width
    seq = segment_ids.shape[0]
    dp_index, ctx_index = lax.axis_index("dp"), lax.axis_index("ctx")
    dp_count, ctx_count = lax.axis_size("dp"), lax.axis_size("ctx")
    sub = rows // dp_count
    held = sub * ctx_count
    pair = heads // dp_count
    dims = (heads, rows, width, sub, held, dp_count)
    idx = jnp.stack([dp_index, ctx_index]).astype(jnp.int32)
    seg = segment_ids.reshape(seq // 128, 128)
    params = pltpu.CompilerParams(vmem_limit_bytes=VMEM_LIMIT)
    smem = pl.BlockSpec(memory_space=pltpu.SMEM)
    vmem = pl.BlockSpec(memory_space=pltpu.VMEM)
    bf16, f32 = jnp.bfloat16, jnp.float32
    shape = jax.ShapeDtypeStruct

    def cost(products, exps):
        return pl.CostEstimate(
            flops=products * 2 * heads * rows * held * width,
            bytes_accessed=8 * rows * heads * width,
            transcendentals=exps * heads * rows * held,
        )

    def swap(array, axis):
        return lax.all_to_all(array, axis, 0, 0, tiled=True)

    own_kv = jnp.concatenate(
        [lax.dynamic_slice_in_dim(a, dp_index * sub, sub, 0) for a in (keys, values)], axis=1
    )
    kv = swap(jnp.tile(own_kv, (ctx_count, 1)), "ctx")

    stats, outs = pl.pallas_call(
        functools.partial(forward_kernel, dims=dims),
        out_shape=[
            shape((dp_count, 3 * heads, rows), f32),
            shape((heads * width, rows), bf16),
        ],
        in_specs=[smem] + [vmem] * 4,
        out_specs=[vmem] * 2,
        scratch_shapes=[pltpu.VMEM((held, rows), f32), pltpu.VMEM((width, held), bf16)],
        compiler_params=params,
        cost_estimate=cost(2, 1),
        name="attend",
    )(idx, seg, queries, out_grad, kv)
    stats = swap(stats, "dp")
    outs = swap(outs, "dp")

    dqs, terms = pl.pallas_call(
        functools.partial(backward_kernel, dims=dims),
        out_shape=[shape((heads * width, rows), bf16), shape((held, 2 * width), bf16)],
        in_specs=[smem] + [vmem] * 5,
        out_specs=[vmem] * 2,
        scratch_shapes=[
            pltpu.VMEM((held, rows), f32),
            pltpu.VMEM((width, held), bf16),
            pltpu.VMEM((heads, rows), f32),
            pltpu.VMEM((heads, rows), f32),
            pltpu.VMEM((held, 2 * width), f32),
        ],
        compiler_params=params,
        cost_estimate=cost(5, 1),
        name="differentiate",
    )(idx, seg, queries, out_grad, kv, stats)

    terms = swap(terms, "ctx")
    summed = pl.pallas_call(
        functools.partial(sum_kernel, count=ctx_count),
        out_shape=shape((sub, 2 * width), bf16),
        in_specs=[vmem],
        out_specs=vmem,
        compiler_params=params,
        name="sum_terms",
    )(terms)
    moves = [
        (d * ctx_count + c, dp_count * c + d) for d in range(dp_count) for c in range(ctx_count)
    ]
    grad_kv = lax.ppermute(summed, ("dp", "ctx"), moves)
    dqs = swap(dqs, "dp")

    return pl.pallas_call(
        functools.partial(finish_kernel, dims=dims),
        out_shape=[shape((rows, pair * width), bf16)] * 2 + [shape((sub, width), bf16)] * 2,
        in_specs=[smem] + [vmem] * 4,
        out_specs=[vmem] * 4,
        compiler_params=params,
        name="finish",
    )(idx, stats, outs, dqs, grad_kv)


def solution(mesh):
    return jax.shard_map(
        on_device,
        mesh=mesh,
        in_specs=(P("ctx", None), P("ctx", None), P("ctx", None), P("ctx", None), P()),
        out_specs=(P("ctx", "dp"), P("ctx", "dp"), P(("dp", "ctx"), None), P(("dp", "ctx"), None)),
        check_vma=False,
    )
```

```python
import functools

import jax
import jax.numpy as jnp
from jax import lax
from jax.experimental import pallas as pl
from jax.experimental.pallas import tpu as pltpu
from jax.sharding import PartitionSpec as P

NEG = -1e30
LOG2E = 1.4426950408889634
DOC_NUMBERS = 4
VMEM_LIMIT = 40 * 1024 * 1024
NT = (((1,), (1,)), ((), ()))


def mask_bias(seg_ref, dp_index, ctx_index, rows, sub, held):
    seg = seg_ref[...]
    lines = rows // 128
    seg_own = seg_ref[pl.ds(ctx_index * lines, lines), :]
    start = jnp.zeros((lines, 128), jnp.int32)
    for number in range(1, DOC_NUMBERS):
        before = jnp.sum((seg < number).astype(jnp.float32), axis=(0, 1), keepdims=True)
        start = jnp.where(seg_own == number, before.astype(jnp.int32), start)
    start = jnp.concatenate([start[k : k + 1] for k in range(lines)], axis=1)
    query_pos = ctx_index * rows + lax.broadcasted_iota(jnp.int32, (1, rows), 1)
    line = lax.broadcasted_iota(jnp.int32, (held, rows), 0)
    place = line // sub
    chips = held // sub // 2
    block = (ctx_index // 2 ^ (place % chips)) * 2 + (ctx_index % 2 ^ (place // chips))
    key_pos = block * rows + dp_index * sub + line % sub
    allowed = (key_pos >= start) & (key_pos <= query_pos)
    return jnp.where(allowed, 0.0, NEG)


def pack_kernel(*refs):
    out_ref = refs[-1]
    size = refs[0].shape[0]
    for k, ref in enumerate(refs[:-1]):
        out_ref[k * size : (k + 1) * size, :] = ref[...]


def head_columns(head, width):
    return pl.ds(pl.multiple_of(head * width, width), width)


def forward_kernel(
    idx_ref, seg_ref, q_ref, g_ref, near_ref, far_ref, stats_ref, kv_ref, bias_ref, *refs, dims
):
    heads, rows, width, sub, held, dp_count = dims
    outs, vt_ref = refs[:dp_count], refs[dp_count]
    dp_index, ctx_index = idx_ref[0], idx_ref[1]
    pair = heads // dp_count
    unit = width**-0.5 * LOG2E
    kv_ref[: held // 2, :] = near_ref[...]
    kv_ref[held // 2 :, :] = far_ref[...]
    bias_ref[...] = mask_bias(seg_ref, dp_index, ctx_index, rows, sub, held)
    vt_ref[...] = kv_ref[:, width:].astype(jnp.float32).T.astype(jnp.bfloat16)
    for slot in range(dp_count):
        for part in range(pair):
            head = (dp_index ^ slot) * pair + part
            cols = head_columns(head, width)
            raw = lax.dot_general(
                kv_ref[:, :width], q_ref[:, cols], NT, preferred_element_type=jnp.float32
            )
            scores = raw * unit + bias_ref[...]
            top = jnp.max(scores, axis=0, keepdims=True)
            expd = jnp.exp2(scores - top)
            total = jnp.sum(expd, axis=0, keepdims=True)
            accum = jnp.dot(
                vt_ref[...], expd.astype(jnp.bfloat16), preferred_element_type=jnp.float32
            )
            delta = jnp.sum(accum * g_ref[:, cols].astype(jnp.float32).T, axis=0, keepdims=True)
            outs[slot][part * width : (part + 1) * width, :] = accum.astype(jnp.bfloat16)
            stats_ref[pl.ds(head, 1), :] = top
            stats_ref[pl.ds(heads + head, 1), :] = total
            stats_ref[pl.ds(2 * heads + head, 1), :] = delta


def merged_stats(stats, heads):
    top = functools.reduce(jnp.maximum, [s[:heads] for s in stats])
    shares = [jnp.exp2(s[:heads] - top) for s in stats]
    total = sum(f * s[heads : 2 * heads] for f, s in zip(shares, stats))
    delta = sum(f * s[2 * heads :] for f, s in zip(shares, stats)) / total
    return top, shares, total, delta


def backward_kernel(idx_ref, q_ref, g_ref, kv_ref, bias_ref, *refs, dims):
    heads, rows, width, sub, held, dp_count = dims
    stats = refs[:dp_count]
    dq_outs = refs[dp_count : 2 * dp_count]
    keep_ref, send_ref, kt_ref, lse_ref, delta_ref, acc_ref = refs[2 * dp_count :]
    dp_index = idx_ref[0]
    pair = heads // dp_count
    scale = width**-0.5
    unit = scale * LOG2E
    top, _, total, delta = merged_stats([s[...] for s in stats], heads)
    lse_ref[...] = top + jnp.log2(total)
    delta_ref[...] = delta
    kt_ref[...] = kv_ref[:, :width].astype(jnp.float32).T.astype(jnp.bfloat16)
    for slot in range(dp_count):
        for part in range(pair):
            head = (dp_index ^ slot) * pair + part
            cols = head_columns(head, width)
            query, grad = q_ref[:, cols], g_ref[:, cols]
            raw = lax.dot_general(
                kv_ref[:, :width], query, NT, preferred_element_type=jnp.float32
            )
            probs = jnp.exp2(raw * unit + bias_ref[...] - lse_ref[pl.ds(head, 1), :])
            dprobs = lax.dot_general(
                kv_ref[:, width:], grad, NT, preferred_element_type=jnp.float32
            )
            dscores = (probs * (dprobs - delta_ref[pl.ds(head, 1), :])).astype(jnp.bfloat16)
            dv = jnp.dot(probs.astype(jnp.bfloat16), grad, preferred_element_type=jnp.float32)
            dk = jnp.dot(dscores, query, preferred_element_type=jnp.float32)
            if slot == 0 and part == 0:
                acc_ref[:, :width] = dk
                acc_ref[:, width:] = dv
            else:
                acc_ref[:, :width] += dk
                acc_ref[:, width:] += dv
            dq = jnp.dot(kt_ref[...], dscores, preferred_element_type=jnp.float32)
            dq_outs[slot][part * width : (part + 1) * width, :] = (dq * scale).astype(jnp.bfloat16)
    half = held // 2
    keep_ref[:, :width] = acc_ref[:half, :width] * scale
    keep_ref[:, width:] = acc_ref[:half, width:]
    send_ref[:, :width] = (acc_ref[half:, :width] * scale).astype(jnp.bfloat16)
    send_ref[:, width:] = acc_ref[half:, width:].astype(jnp.bfloat16)


def join_kernel(keep_ref, got_ref, *out_refs):
    size = out_refs[0].shape[0]
    for k, out_ref in enumerate(out_refs):
        here = slice(k * size, (k + 1) * size)
        out_ref[...] = (keep_ref[here, :] + got_ref[here, :].astype(jnp.float32)).astype(
            jnp.bfloat16
        )


def finish_kernel(idx_ref, *refs, dims, chips):
    heads, rows, width, sub, held, dp_count = dims
    n = dp_count
    stats, outs, dqs = refs[:n], refs[n : 2 * n], refs[2 * n : 3 * n]
    terms = refs[3 * n : 3 * n + chips]
    attn_ref, gq_ref, gk_ref, gv_ref = refs[3 * n + chips :]
    pair = heads // n
    top, shares, total, _ = merged_stats([s[...] for s in stats], heads)
    own = idx_ref[0] * pair
    row = lax.broadcasted_iota(jnp.int32, (heads, 1), 0)
    for part in range(pair):
        here = slice(part * width, (part + 1) * width)

        def pick(array):
            return jnp.sum(jnp.where(row == own + part, array, 0.0), axis=0, keepdims=True)

        joined = sum(o[here, :].astype(jnp.float32) * pick(f) for o, f in zip(outs, shares))
        attn_ref[:, here] = (joined / pick(total)).T.astype(jnp.bfloat16)
        query = sum(t[here, :].astype(jnp.float32) for t in dqs)
        gq_ref[:, here] = query.T.astype(jnp.bfloat16)
    both = sum(t[...].astype(jnp.float32) for t in terms)
    gk_ref[...] = both[:, :width].astype(jnp.bfloat16)
    gv_ref[...] = both[:, width:].astype(jnp.bfloat16)


def on_device(queries, keys, values, out_grad, segment_ids):
    rows = queries.shape[0]
    width = keys.shape[1]
    heads = queries.shape[1] // width
    seq = segment_ids.shape[0]
    dp_index, ctx_index = lax.axis_index("dp"), lax.axis_index("ctx")
    dp_count, ctx_count = lax.axis_size("dp"), lax.axis_size("ctx")
    sub = rows // dp_count
    held = sub * ctx_count
    pair = heads // dp_count
    dims = (heads, rows, width, sub, held, dp_count)
    idx = jnp.stack([dp_index, ctx_index]).astype(jnp.int32)
    seg = segment_ids.reshape(seq // 128, 128)
    params = pltpu.CompilerParams(vmem_limit_bytes=VMEM_LIMIT)
    smem = pl.BlockSpec(memory_space=pltpu.SMEM)
    vmem = pl.BlockSpec(memory_space=pltpu.VMEM)
    bf16, f32 = jnp.bfloat16, jnp.float32
    shape = jax.ShapeDtypeStruct

    def cost(products, exps):
        return pl.CostEstimate(
            flops=products * 2 * heads * rows * held * width,
            bytes_accessed=8 * rows * heads * width,
            transcendentals=exps * heads * rows * held,
        )

    chips = ctx_count // 2

    def over_dp(array, slot):
        return lax.ppermute(array, "dp", [(d, d ^ slot) for d in range(dp_count)])

    def over_ctx(array, flip):
        return lax.ppermute(array, "ctx", [(c, c ^ flip) for c in range(ctx_count)])

    own_kv = jnp.concatenate(
        [lax.dynamic_slice_in_dim(a, dp_index * sub, sub, 0) for a in (keys, values)], axis=1
    )
    near = pl.pallas_call(
        pack_kernel,
        out_shape=shape((held // 2, 2 * width), bf16),
        in_specs=[vmem] * chips,
        out_specs=vmem,
        compiler_params=params,
        name="pack",
    )(own_kv, *[over_ctx(own_kv, 2 * t) for t in range(1, chips)])
    far = over_ctx(near, 1)

    stats, kv, bias, *outs = pl.pallas_call(
        functools.partial(forward_kernel, dims=dims),
        out_shape=[
            shape((3 * heads, rows), f32),
            shape((held, 2 * width), bf16),
            shape((held, rows), f32),
        ]
        + [shape((pair * width, rows), bf16)] * dp_count,
        in_specs=[smem] + [vmem] * 5,
        out_specs=[vmem] * (3 + dp_count),
        scratch_shapes=[pltpu.VMEM((width, held), bf16)],
        compiler_params=params,
        cost_estimate=cost(2, 1),
        name="attend",
    )(idx, seg, queries, out_grad, near, far)
    all_stats = [stats] + [over_dp(stats, s) for s in range(1, dp_count)]
    all_outs = [outs[0]] + [over_dp(outs[s], s) for s in range(1, dp_count)]

    *dqs, keep, send = pl.pallas_call(
        functools.partial(backward_kernel, dims=dims),
        out_shape=[shape((pair * width, rows), bf16)] * dp_count
        + [shape((held // 2, 2 * width), f32), shape((held // 2, 2 * width), bf16)],
        in_specs=[smem] + [vmem] * (4 + dp_count),
        out_specs=[vmem] * (dp_count + 2),
        scratch_shapes=[
            pltpu.VMEM((width, held), bf16),
            pltpu.VMEM((heads, rows), f32),
            pltpu.VMEM((heads, rows), f32),
            pltpu.VMEM((held, 2 * width), f32),
        ],
        compiler_params=params,
        cost_estimate=cost(5, 1),
        name="differentiate",
    )(idx, queries, out_grad, kv, bias, *all_stats)
    got = over_ctx(send, 1)
    all_dqs = [dqs[0]] + [over_dp(dqs[s], s) for s in range(1, dp_count)]
    terms = pl.pallas_call(
        join_kernel,
        out_shape=[shape((sub, 2 * width), bf16)] * chips,
        in_specs=[vmem] * 2,
        out_specs=[vmem] * chips,
        compiler_params=params,
        name="join",
    )(keep, got)

    def to_owner(array, flip):
        moves = [
            (d * ctx_count + c, dp_count * (c ^ flip) + d)
            for d in range(dp_count)
            for c in range(ctx_count)
        ]
        return lax.ppermute(array, ("dp", "ctx"), moves)

    all_terms = [to_owner(t, 2 * k) for k, t in enumerate(terms)]

    return pl.pallas_call(
        functools.partial(finish_kernel, dims=dims, chips=chips),
        out_shape=[shape((rows, pair * width), bf16)] * 2 + [shape((sub, width), bf16)] * 2,
        in_specs=[smem] + [vmem] * (3 * dp_count + chips),
        out_specs=[vmem] * 4,
        compiler_params=params,
        name="finish",
    )(idx, *all_stats, *all_outs, *all_dqs, *all_terms)


def solution(mesh):
    return jax.shard_map(
        on_device,
        mesh=mesh,
        in_specs=(P("ctx", None), P("ctx", None), P("ctx", None), P("ctx", None), P()),
        out_specs=(P("ctx", "dp"), P("ctx", "dp"), P(("dp", "ctx"), None), P(("dp", "ctx"), None)),
        check_vma=False,
    )
```

```python
import functools
import math

import jax
import jax.numpy as jnp
from jax import lax
from jax.experimental import pallas as pl
from jax.experimental.pallas import tpu as pltpu
from jax.sharding import PartitionSpec as P

NEG = -1e30
LOG2E = 1.4426950408889634
DOC_NUMBERS = 4
VMEM_LIMIT = 40 * 1024 * 1024
NT = (((1,), (1,)), ((), ()))


def mask_bias(seg_ref, dp_index, ctx_index, rows, sub, held):
    seg = seg_ref[...]
    lines = rows // 128
    seg_own = seg_ref[pl.ds(ctx_index * lines, lines), :]
    start = jnp.zeros((lines, 128), jnp.int32)
    for number in range(1, DOC_NUMBERS):
        before = jnp.sum((seg < number).astype(jnp.float32), axis=(0, 1), keepdims=True)
        start = jnp.where(seg_own == number, before.astype(jnp.int32), start)
    start = jnp.concatenate([start[k : k + 1] for k in range(lines)], axis=1)
    query_pos = ctx_index * rows + lax.broadcasted_iota(jnp.int32, (1, rows), 1)
    line = lax.broadcasted_iota(jnp.int32, (held, rows), 0)
    place = line // sub
    chips = held // sub // 2
    block = (ctx_index // 2 ^ (place % chips)) * 2 + (ctx_index % 2 ^ (place // chips))
    key_pos = block * rows + dp_index * sub + line % sub
    allowed = (key_pos >= start) & (key_pos <= query_pos)
    return jnp.where(allowed, 0.0, NEG)


def pack_kernel(*refs):
    out_ref = refs[-1]
    size = refs[0].shape[0]
    for k, ref in enumerate(refs[:-1]):
        out_ref[k * size : (k + 1) * size, :] = ref[...]


def prep_kernel(
    idx_ref, seg_ref, q_hbm, g_hbm, near_ref, q_ref, g_ref, gt_ref, bias_ref, sems, *, dims
):
    heads, rows, width, sub, held, dp_count = dims
    copies = []
    for head in range(heads):
        cols = slice(head * width, (head + 1) * width)
        for k, (source, target) in enumerate(((g_hbm, g_ref), (q_hbm, q_ref))):
            copies.append(
                pltpu.make_async_copy(source.at[:, cols], target.at[:, cols], sems.at[k, head])
            )
            copies[-1].start()
    bias_ref[...] = mask_bias(seg_ref, idx_ref[0], idx_ref[1], rows, sub, held)
    for head in range(heads):
        cols = slice(head * width, (head + 1) * width)
        copies[2 * head].wait()
        gt_ref[cols, :] = g_ref[:, cols].astype(jnp.float32).T.astype(jnp.bfloat16)
    for head in range(heads):
        copies[2 * head + 1].wait()


def head_columns(head, width):
    return pl.ds(pl.multiple_of(head * width, width), width)


def forward_kernel(
    idx_ref, q_ref, gt_ref, bias_ref, near_ref, far_ref, stats_ref, kv_ref, *refs, dims
):
    heads, rows, width, sub, held, dp_count = dims
    outs, vt_ref = refs[:dp_count], refs[dp_count]
    dp_index = idx_ref[0]
    pair = heads // dp_count
    unit = width**-0.5 * LOG2E
    kv_ref[: held // 2, :] = near_ref[...]
    kv_ref[held // 2 :, :] = far_ref[...]
    vt_ref[...] = kv_ref[:, width:].astype(jnp.float32).T.astype(jnp.bfloat16)
    for slot in range(dp_count):
        for part in range(pair):
            head = (dp_index ^ slot) * pair + part
            cols = head_columns(head, width)
            raw = lax.dot_general(
                kv_ref[:, :width], q_ref[:, cols], NT, preferred_element_type=jnp.float32
            )
            scores = raw * unit + bias_ref[...]
            top = jnp.max(scores, axis=0, keepdims=True)
            expd = jnp.exp2(scores - top)
            total = jnp.sum(expd, axis=0, keepdims=True)
            accum = jnp.dot(
                vt_ref[...], expd.astype(jnp.bfloat16), preferred_element_type=jnp.float32
            )
            delta = jnp.sum(accum * gt_ref[cols, :].astype(jnp.float32), axis=0, keepdims=True)
            outs[slot][part * width : (part + 1) * width, :] = accum.astype(jnp.bfloat16)
            stats_ref[pl.ds(head, 1), :] = top
            stats_ref[pl.ds(heads + head, 1), :] = total
            stats_ref[pl.ds(2 * heads + head, 1), :] = delta


def merged_stats(stats, heads):
    top = functools.reduce(jnp.maximum, [s[:heads] for s in stats])
    shares = [jnp.exp2(s[:heads] - top) for s in stats]
    total = sum(f * s[heads : 2 * heads] for f, s in zip(shares, stats))
    delta = sum(f * s[2 * heads :] for f, s in zip(shares, stats)) / total
    return top, shares, total, delta


def backward_kernel(
    q_ref,
    g_ref,
    kv_ref,
    bias_ref,
    *refs,
    dims,
):
    heads, rows, width, sub, held, dp_count = dims
    stats = refs[:dp_count]
    ds_ref, keep_ref, send_ref, lse_ref, delta_ref, acc_ref = refs[dp_count:]
    scale = width**-0.5
    unit = scale * LOG2E
    top, _, total, delta = merged_stats([s[...] for s in stats], heads)
    lse_ref[...] = top + jnp.log2(total)
    delta_ref[...] = delta
    for head in range(heads):
        cols = slice(head * width, (head + 1) * width)
        query, grad = q_ref[:, cols], g_ref[:, cols]
        raw = lax.dot_general(kv_ref[:, :width], query, NT, preferred_element_type=jnp.float32)
        probs = jnp.exp2(raw * unit + bias_ref[...] - lse_ref[head : head + 1, :])
        dprobs = lax.dot_general(kv_ref[:, width:], grad, NT, preferred_element_type=jnp.float32)
        dscores = (probs * (dprobs - delta_ref[head : head + 1, :])).astype(jnp.bfloat16)
        ds_ref[head] = dscores
        dv = jnp.dot(probs.astype(jnp.bfloat16), grad, preferred_element_type=jnp.float32)
        dk = jnp.dot(dscores, query, preferred_element_type=jnp.float32)
        if head == 0:
            acc_ref[:, :width] = dk
            acc_ref[:, width:] = dv
        else:
            acc_ref[:, :width] += dk
            acc_ref[:, width:] += dv
    half = held // 2
    keep_ref[:, :width] = acc_ref[:half, :width] * scale
    keep_ref[:, width:] = acc_ref[:half, width:]
    send_ref[:, :width] = (acc_ref[half:, :width] * scale).astype(jnp.bfloat16)
    send_ref[:, width:] = acc_ref[half:, width:].astype(jnp.bfloat16)


def query_kernel(idx_ref, kv_ref, ds_ref, *refs, dims):
    heads, rows, width, sub, held, dp_count = dims
    outs, kt_ref = refs[:dp_count], refs[dp_count]
    pair = heads // dp_count
    scale = width**-0.5
    kt_ref[...] = kv_ref[:, :width].astype(jnp.float32).T.astype(jnp.bfloat16)
    for slot in range(dp_count):
        for part in range(pair):
            head = (idx_ref[0] ^ slot) * pair + part
            dq = jnp.dot(kt_ref[...], ds_ref[head], preferred_element_type=jnp.float32)
            outs[slot][part * width : (part + 1) * width, :] = (dq * scale).astype(jnp.bfloat16)


def join_kernel(keep_ref, got_ref, *refs, chips):
    passed = refs[: (len(refs) - chips) // 2]
    outs = refs[len(passed) : len(passed) + chips]
    size = outs[0].shape[0]
    for k, out_ref in enumerate(outs):
        here = slice(k * size, (k + 1) * size)
        total = keep_ref[here, :] + got_ref[here, :].astype(jnp.float32)
        out_ref[...] = total.astype(out_ref.dtype)
    for source, target in zip(passed, refs[len(passed) + chips :]):
        target[...] = source[...]


def sum_kernel(*refs):
    refs[-1][...] = sum(r[...].astype(jnp.float32) for r in refs[:-1]).astype(refs[-1].dtype)


def finish_out_kernel(idx_ref, *refs, dims):
    heads, rows, width, sub, held, dp_count = dims
    stats, outs, attn_ref = refs[:dp_count], refs[dp_count : 2 * dp_count], refs[-1]
    pair = heads // dp_count
    top, shares, total, _ = merged_stats([s[...] for s in stats], heads)
    own = idx_ref[0] * pair
    row = lax.broadcasted_iota(jnp.int32, (heads, 1), 0)
    for part in range(pair):
        here = slice(part * width, (part + 1) * width)

        def pick(array):
            return jnp.sum(jnp.where(row == own + part, array, 0.0), axis=0, keepdims=True)

        joined = sum(o[here, :].astype(jnp.float32) * pick(f) for o, f in zip(outs, shares))
        attn_ref[:, here] = (joined / pick(total)).T.astype(jnp.bfloat16)


def finish_query_kernel(*refs):
    refs[-1][...] = sum(r[...].astype(jnp.float32) for r in refs[:-1]).T.astype(jnp.bfloat16)


def split_kernel(both_ref, first_ref, second_ref):
    width = first_ref.shape[1]
    first_ref[...] = both_ref[:, :width]
    second_ref[...] = both_ref[:, width:]


def on_device(queries, keys, values, out_grad, segment_ids):
    rows = queries.shape[0]
    width = keys.shape[1]
    heads = queries.shape[1] // width
    seq = segment_ids.shape[0]
    dp_index, ctx_index = lax.axis_index("dp"), lax.axis_index("ctx")
    dp_count, ctx_count = lax.axis_size("dp"), lax.axis_size("ctx")
    sub = rows // dp_count
    held = sub * ctx_count
    pair = heads // dp_count
    dims = (heads, rows, width, sub, held, dp_count)
    idx = jnp.stack([dp_index, ctx_index]).astype(jnp.int32)
    seg = segment_ids.reshape(seq // 128, 128)
    params = pltpu.CompilerParams(vmem_limit_bytes=VMEM_LIMIT)
    smem = pl.BlockSpec(memory_space=pltpu.SMEM)
    vmem = pl.BlockSpec(memory_space=pltpu.VMEM)
    bf16, f32 = jnp.bfloat16, jnp.float32
    shape = jax.ShapeDtypeStruct

    def call(kernel, outs, ins, name, scratch=(), work=0, **static):
        specs = [a[1] if isinstance(a, tuple) else vmem for a in ins]
        arrays = [a[0] if isinstance(a, tuple) else a for a in ins]
        out_shape = [shape(*o) for o in outs]
        return pl.pallas_call(
            functools.partial(kernel, **static),
            out_shape=out_shape,
            in_specs=specs,
            out_specs=[vmem] * len(outs),
            scratch_shapes=list(scratch),
            compiler_params=params,
            cost_estimate=pl.CostEstimate(
                flops=work * 2 * heads * rows * held * width,
                bytes_accessed=sum(math.prod(o[0]) * 2 for o in outs),
                transcendentals=0,
            ),
            name=name,
        )(*arrays)

    chips = ctx_count // 2

    def over_dp(array, slot):
        return lax.ppermute(array, "dp", [(d, d ^ slot) for d in range(dp_count)])

    def over_ctx(array, flip):
        return lax.ppermute(array, "ctx", [(c, c ^ flip) for c in range(ctx_count)])

    own_kv = jnp.concatenate(
        [lax.dynamic_slice_in_dim(a, dp_index * sub, sub, 0) for a in (keys, values)], axis=1
    )
    (near,) = call(
        pack_kernel,
        [((held // 2, 2 * width), bf16)],
        [own_kv] + [over_ctx(own_kv, 2 * t) for t in range(1, chips)],
        "pack",
    )
    far = over_ctx(near, 1)
    hbm = pl.BlockSpec(memory_space=pltpu.HBM)
    query_v, grad_v, grad_t, bias = call(
        prep_kernel,
        [
            ((rows, heads * width), bf16),
            ((rows, heads * width), bf16),
            ((heads * width, rows), bf16),
            ((held, rows), f32),
        ],
        [(idx, smem), seg, (pltpu.with_memory_space_constraint(queries, pltpu.HBM), hbm), (pltpu.with_memory_space_constraint(out_grad, pltpu.HBM), hbm), (near, hbm)],
        "prepare",
        scratch=[pltpu.SemaphoreType.DMA((2, heads))],
        work=1,
        dims=dims,
    )
    stats, kv, *outs = call(
        forward_kernel,
        [((3 * heads, rows), f32), ((held, 2 * width), bf16)]
        + [((pair * width, rows), bf16)] * dp_count,
        [(idx, smem), query_v, grad_t, bias, near, far],
        "attend",
        scratch=[pltpu.VMEM((width, held), bf16)],
        work=2,
        dims=dims,
    )
    all_stats = [stats] + [over_dp(stats, s) for s in range(1, dp_count)]
    all_outs = [outs[0]] + [over_dp(outs[s], s) for s in range(1, dp_count)]

    dscores, keep, send = call(
        backward_kernel,
        [
            ((heads, held, rows), bf16),
            ((held // 2, 2 * width), f32),
            ((held // 2, 2 * width), bf16),
        ],
        [query_v, grad_v, kv, bias] + all_stats,
        "differentiate",
        scratch=[
            pltpu.VMEM((heads, rows), f32),
            pltpu.VMEM((heads, rows), f32),
            pltpu.VMEM((held, 2 * width), f32),
        ],
        work=4,
        dims=dims,
    )
    got = over_ctx(send, 1)
    dqs = call(
        query_kernel,
        [((pair * width, rows), bf16)] * dp_count,
        [(idx, smem), kv, dscores],
        "query_terms",
        scratch=[pltpu.VMEM((width, held), bf16)],
        work=1,
        dims=dims,
    )
    joined = call(
        join_kernel,
        [((sub, 2 * width), f32)]
        + [((sub, 2 * width), bf16)] * (chips - 1)
        + [((pair * width, rows), bf16)] * (dp_count - 2),
        [keep, got] + list(dqs[1:-1]),
        "join",
        chips=chips,
    )
    terms = [joined[0]] + [over_ctx(joined[t], 2 * t) for t in range(1, chips)]
    sends = [dqs[0]] + list(joined[chips:]) + [dqs[-1]]
    all_dqs = [dqs[0]] + [over_dp(sends[s], s) for s in range(1, dp_count)]
    (summed,) = call(sum_kernel, [((sub, 2 * width), bf16)], terms, "sum_terms")
    moves = [
        (d * ctx_count + c, dp_count * c + d) for d in range(dp_count) for c in range(ctx_count)
    ]
    grad_kv = lax.ppermute(summed, ("dp", "ctx"), moves)

    (attn_out,) = call(
        finish_out_kernel,
        [((rows, pair * width), bf16)],
        [(idx, smem)] + all_stats + all_outs,
        "finish_out",
        dims=dims,
    )
    (grad_q,) = call(finish_query_kernel, [((rows, pair * width), bf16)], all_dqs, "finish_query")
    grad_k, grad_values = call(split_kernel, [((sub, width), bf16)] * 2, [grad_kv], "split")
    return attn_out, grad_q, grad_k, grad_values


def solution(mesh):
    return jax.shard_map(
        on_device,
        mesh=mesh,
        in_specs=(P("ctx", None), P("ctx", None), P("ctx", None), P("ctx", None), P()),
        out_specs=(P("ctx", "dp"), P("ctx", "dp"), P(("dp", "ctx"), None), P(("dp", "ctx"), None)),
        check_vma=False,
    )
```

```python
import functools
import math

import jax
import jax.numpy as jnp
from jax import lax
from jax.experimental import pallas as pl
from jax.experimental.pallas import tpu as pltpu
from jax.sharding import PartitionSpec as P

NEG = -1e30
LOG2E = 1.4426950408889634
DOC_NUMBERS = 4
VMEM_LIMIT = 40 * 1024 * 1024
NT = (((1,), (1,)), ((), ()))


def mask_bias(seg_ref, dp_index, ctx_index, rows, sub, held):
    seg = seg_ref[...]
    lines = rows // 128
    seg_own = seg_ref[pl.ds(ctx_index * lines, lines), :]
    start = jnp.zeros((lines, 128), jnp.int32)
    for number in range(1, DOC_NUMBERS):
        before = jnp.sum((seg < number).astype(jnp.float32), axis=(0, 1), keepdims=True)
        start = jnp.where(seg_own == number, before.astype(jnp.int32), start)
    start = jnp.concatenate([start[k : k + 1] for k in range(lines)], axis=1)
    query_pos = ctx_index * rows + lax.broadcasted_iota(jnp.int32, (1, rows), 1)
    line = lax.broadcasted_iota(jnp.int32, (held, rows), 0)
    place = line // sub
    chips = held // sub // 2
    block = (ctx_index // 2 ^ (place % chips)) * 2 + (ctx_index % 2 ^ (place // chips))
    key_pos = block * rows + dp_index * sub + line % sub
    allowed = (key_pos >= start) & (key_pos <= query_pos)
    return jnp.where(allowed, 0.0, NEG)


def pack_kernel(token_ref, *refs):
    out_ref = refs[-1]
    size = refs[0].shape[0]
    for k, ref in enumerate(refs[:-1]):
        out_ref[k * size : (k + 1) * size, :] = ref[...]


def prep_kernel(
    idx_ref, seg_hbm, q_hbm, g_hbm, q_ref, g_ref, gt_ref, bias_ref, token_ref, seg_ref, sems, *, dims
):
    heads, rows, width, sub, held, dp_count = dims
    seg_copy = pltpu.make_async_copy(seg_hbm, seg_ref, sems.at[2, 0])
    seg_copy.start()
    copies = []
    for head in range(heads):
        cols = slice(head * width, (head + 1) * width)
        for k, (source, target) in enumerate(((g_hbm, g_ref), (q_hbm, q_ref))):
            copies.append(
                pltpu.make_async_copy(source.at[:, cols], target.at[:, cols], sems.at[k, head])
            )
            copies[-1].start()
    token_ref[...] = jnp.zeros_like(token_ref)
    seg_copy.wait()
    bias_ref[...] = mask_bias(seg_ref, idx_ref[0], idx_ref[1], rows, sub, held)
    for head in range(heads):
        cols = slice(head * width, (head + 1) * width)
        copies[2 * head].wait()
        gt_ref[cols, :] = g_ref[:, cols].astype(jnp.float32).T.astype(jnp.bfloat16)
    for head in range(heads):
        copies[2 * head + 1].wait()


def head_columns(head, width):
    return pl.ds(pl.multiple_of(head * width, width), width)


def forward_kernel(
    idx_ref, q_ref, gt_ref, bias_ref, near_ref, far_ref, stats_ref, kv_ref, *refs, dims
):
    heads, rows, width, sub, held, dp_count = dims
    outs, vt_ref = refs[:dp_count], refs[dp_count]
    dp_index = idx_ref[0]
    pair = heads // dp_count
    unit = width**-0.5 * LOG2E
    kv_ref[: held // 2, :] = near_ref[...]
    kv_ref[held // 2 :, :] = far_ref[...]
    vt_ref[...] = kv_ref[:, width:].astype(jnp.float32).T.astype(jnp.bfloat16)
    for slot in range(dp_count):
        for part in range(pair):
            head = (dp_index ^ slot) * pair + part
            cols = head_columns(head, width)
            raw = lax.dot_general(
                kv_ref[:, :width], q_ref[:, cols], NT, preferred_element_type=jnp.float32
            )
            scores = raw * unit + bias_ref[...]
            top = jnp.max(scores, axis=0, keepdims=True)
            expd = jnp.exp2(scores - top)
            total = jnp.sum(expd, axis=0, keepdims=True)
            accum = jnp.dot(
                vt_ref[...], expd.astype(jnp.bfloat16), preferred_element_type=jnp.float32
            )
            delta = jnp.sum(accum * gt_ref[cols, :].astype(jnp.float32), axis=0, keepdims=True)
            outs[slot][part * width : (part + 1) * width, :] = accum.astype(jnp.bfloat16)
            stats_ref[pl.ds(head, 1), :] = top
            stats_ref[pl.ds(heads + head, 1), :] = total
            stats_ref[pl.ds(2 * heads + head, 1), :] = delta


def merged_stats(stats, heads):
    top = functools.reduce(jnp.maximum, [s[:heads] for s in stats])
    shares = [jnp.exp2(s[:heads] - top) for s in stats]
    total = sum(f * s[heads : 2 * heads] for f, s in zip(shares, stats))
    delta = sum(f * s[2 * heads :] for f, s in zip(shares, stats)) / total
    return top, shares, total, delta


def summed_block(ctx_index, dp_count, ctx_count):
    return (ctx_index % dp_count) * (ctx_count // dp_count) + ctx_index // dp_count


def backward_kernel(idx_ref, q_ref, g_ref, kv_ref, bias_ref, *refs, dims):
    heads, rows, width, sub, held, dp_count = dims
    stats = refs[:dp_count]
    ds_ref, keep_ref, send_ref, lse_ref, delta_ref, acc_ref = refs[dp_count:]
    scale = width**-0.5
    unit = scale * LOG2E
    top, _, total, delta = merged_stats([s[...] for s in stats], heads)
    lse_ref[...] = top + jnp.log2(total)
    delta_ref[...] = delta
    for head in range(heads):
        cols = slice(head * width, (head + 1) * width)
        query, grad = q_ref[:, cols], g_ref[:, cols]
        raw = lax.dot_general(kv_ref[:, :width], query, NT, preferred_element_type=jnp.float32)
        probs = jnp.exp2(raw * unit + bias_ref[...] - lse_ref[head : head + 1, :])
        dprobs = lax.dot_general(kv_ref[:, width:], grad, NT, preferred_element_type=jnp.float32)
        dscores = (probs * (dprobs - delta_ref[head : head + 1, :])).astype(jnp.bfloat16)
        ds_ref[head] = dscores
        dv = jnp.dot(probs.astype(jnp.bfloat16), grad, preferred_element_type=jnp.float32)
        dk = jnp.dot(dscores, query, preferred_element_type=jnp.float32)
        if head == 0:
            acc_ref[:, :width] = dk
            acc_ref[:, width:] = dv
        else:
            acc_ref[:, :width] += dk
            acc_ref[:, width:] += dv
    ctx_count = held // sub
    ctx_index = idx_ref[1]
    chip, core = ctx_index // 2, ctx_index % 2
    for flip in range(ctx_count // 2):
        here = slice(flip * sub, (flip + 1) * sub)
        for ref, side in ((keep_ref, core), (send_ref, 1 - core)):
            block = summed_block((chip ^ flip) * 2 + side, dp_count, ctx_count)
            line = (block % 2 ^ core) * (held // 2) + (block // 2 ^ chip) * sub
            mine = pl.ds(pl.multiple_of(line, sub), sub)
            ref[here, :width] = (acc_ref[mine, :width] * scale).astype(ref.dtype)
            ref[here, width:] = acc_ref[mine, width:].astype(ref.dtype)


def query_kernel(idx_ref, kv_ref, ds_ref, *refs, dims):
    heads, rows, width, sub, held, dp_count = dims
    outs, kt_ref = refs[:dp_count], refs[dp_count]
    pair = heads // dp_count
    scale = width**-0.5
    kt_ref[...] = kv_ref[:, :width].astype(jnp.float32).T.astype(jnp.bfloat16)
    for slot in range(dp_count):
        for part in range(pair):
            head = (idx_ref[0] ^ slot) * pair + part
            dq = jnp.dot(kt_ref[...], ds_ref[head], preferred_element_type=jnp.float32)
            outs[slot][part * width : (part + 1) * width, :] = (dq * scale).astype(jnp.bfloat16)


def join_kernel(keep_ref, got_ref, *refs, chips):
    passed = refs[: (len(refs) - chips) // 2]
    outs = refs[len(passed) : len(passed) + chips]
    size = outs[0].shape[0]
    for k, out_ref in enumerate(outs):
        here = slice(k * size, (k + 1) * size)
        total = keep_ref[here, :] + got_ref[here, :].astype(jnp.float32)
        out_ref[...] = total.astype(out_ref.dtype)
    for source, target in zip(passed, refs[len(passed) + chips :]):
        target[...] = source[...]


def sum_kernel(*refs):
    refs[-1][...] = sum(r[...].astype(jnp.float32) for r in refs[:-1]).astype(refs[-1].dtype)


def finish_out_kernel(idx_ref, *refs, dims):
    heads, rows, width, sub, held, dp_count = dims
    stats, outs, attn_ref = refs[:dp_count], refs[dp_count : 2 * dp_count], refs[-1]
    pair = heads // dp_count
    top, shares, total, _ = merged_stats([s[...] for s in stats], heads)
    own = idx_ref[0] * pair
    row = lax.broadcasted_iota(jnp.int32, (heads, 1), 0)
    for part in range(pair):
        here = slice(part * width, (part + 1) * width)

        def pick(array):
            return jnp.sum(jnp.where(row == own + part, array, 0.0), axis=0, keepdims=True)

        joined = sum(o[here, :].astype(jnp.float32) * pick(f) for o, f in zip(outs, shares))
        attn_ref[:, here] = (joined / pick(total)).T.astype(jnp.bfloat16)


def finish_kernel(both_ref, *refs):
    *dqs, gq_ref, gk_ref, gv_ref = refs
    width = gk_ref.shape[1]
    gq_ref[...] = sum(r[...].astype(jnp.float32) for r in dqs).T.astype(jnp.bfloat16)
    gk_ref[...] = both_ref[:, :width]
    gv_ref[...] = both_ref[:, width:]


def on_device(queries, keys, values, out_grad, segment_ids):
    rows = queries.shape[0]
    width = keys.shape[1]
    heads = queries.shape[1] // width
    seq = segment_ids.shape[0]
    dp_index, ctx_index = lax.axis_index("dp"), lax.axis_index("ctx")
    dp_count, ctx_count = lax.axis_size("dp"), lax.axis_size("ctx")
    sub = rows // dp_count
    held = sub * ctx_count
    pair = heads // dp_count
    dims = (heads, rows, width, sub, held, dp_count)
    idx = jnp.stack([dp_index, ctx_index]).astype(jnp.int32)
    seg = segment_ids.reshape(seq // 128, 128)
    params = pltpu.CompilerParams(vmem_limit_bytes=VMEM_LIMIT)
    smem = pl.BlockSpec(memory_space=pltpu.SMEM)
    vmem = pl.BlockSpec(memory_space=pltpu.VMEM)
    bf16, f32 = jnp.bfloat16, jnp.float32
    shape = jax.ShapeDtypeStruct

    def call(kernel, outs, ins, name, scratch=(), work=0, **static):
        specs = [a[1] if isinstance(a, tuple) else vmem for a in ins]
        arrays = [a[0] if isinstance(a, tuple) else a for a in ins]
        out_shape = [shape(*o) for o in outs]
        return pl.pallas_call(
            functools.partial(kernel, **static),
            out_shape=out_shape,
            in_specs=specs,
            out_specs=[vmem] * len(outs),
            scratch_shapes=list(scratch),
            compiler_params=params,
            cost_estimate=pl.CostEstimate(
                flops=work * 2 * heads * rows * held * width,
                bytes_accessed=sum(math.prod(o[0]) * 2 for o in outs),
                transcendentals=0,
            ),
            name=name,
        )(*arrays)

    chips = ctx_count // 2

    def over_dp(array, slot):
        return lax.ppermute(array, "dp", [(d, d ^ slot) for d in range(dp_count)])

    def over_ctx(array, flip):
        return lax.ppermute(array, "ctx", [(c, c ^ flip) for c in range(ctx_count)])

    own_kv = jnp.concatenate(
        [lax.dynamic_slice_in_dim(a, dp_index * sub, sub, 0) for a in (keys, values)], axis=1
    )
    def in_hbm(array):
        return pltpu.with_memory_space_constraint(array, pltpu.HBM), pl.BlockSpec(
            memory_space=pltpu.HBM
        )

    query_v, grad_v, grad_t, bias, token = call(
        prep_kernel,
        [
            ((rows, heads * width), bf16),
            ((rows, heads * width), bf16),
            ((heads * width, rows), bf16),
            ((held, rows), f32),
            ((8, 128), f32),
        ],
        [(idx, smem), in_hbm(seg), in_hbm(queries), in_hbm(out_grad)],
        "prepare",
        scratch=[pltpu.VMEM(seg.shape, seg.dtype), pltpu.SemaphoreType.DMA((3, heads))],
        work=1,
        dims=dims,
    )
    (near,) = call(
        pack_kernel,
        [((held // 2, 2 * width), bf16)],
        [token, own_kv] + [over_ctx(own_kv, 2 * t) for t in range(1, chips)],
        "pack",
    )
    far = over_ctx(near, 1)
    stats, kv, *outs = call(
        forward_kernel,
        [((3 * heads, rows), f32), ((held, 2 * width), bf16)]
        + [((pair * width, rows), bf16)] * dp_count,
        [(idx, smem), query_v, grad_t, bias, near, far],
        "attend",
        scratch=[pltpu.VMEM((width, held), bf16)],
        work=2,
        dims=dims,
    )
    all_stats = [stats] + [over_dp(stats, s) for s in range(1, dp_count)]
    all_outs = [outs[0]] + [over_dp(outs[s], s) for s in range(1, dp_count)]

    dscores, keep, send = call(
        backward_kernel,
        [
            ((heads, held, rows), bf16),
            ((held // 2, 2 * width), f32),
            ((held // 2, 2 * width), bf16),
        ],
        [(idx, smem), query_v, grad_v, kv, bias] + all_stats,
        "differentiate",
        scratch=[
            pltpu.VMEM((heads, rows), f32),
            pltpu.VMEM((heads, rows), f32),
            pltpu.VMEM((held, 2 * width), f32),
        ],
        work=4,
        dims=dims,
    )
    got = over_ctx(send, 1)
    dqs = call(
        query_kernel,
        [((pair * width, rows), bf16)] * dp_count,
        [(idx, smem), kv, dscores],
        "query_terms",
        scratch=[pltpu.VMEM((width, held), bf16)],
        work=1,
        dims=dims,
    )
    joined = call(
        join_kernel,
        [((sub, 2 * width), f32)]
        + [((sub, 2 * width), bf16)] * (chips - 1)
        + [((pair * width, rows), bf16)] * (dp_count - 2),
        [keep, got] + list(dqs[1:-1]),
        "join",
        chips=chips,
    )
    terms = [joined[0]] + [over_ctx(joined[t], 2 * t) for t in range(1, chips)]
    sends = [dqs[0]] + list(joined[chips:]) + [dqs[-1]]
    all_dqs = [dqs[0]] + [over_dp(sends[s], s) for s in range(1, dp_count)]
    (summed,) = call(sum_kernel, [((sub, 2 * width), bf16)], terms, "sum_terms")
    moves = [
        (d * ctx_count + c, dp_count * summed_block(c, dp_count, ctx_count) + d)
        for d in range(dp_count)
        for c in range(ctx_count)
    ]
    grad_kv = lax.ppermute(summed, ("dp", "ctx"), moves)

    (attn_out,) = call(
        finish_out_kernel,
        [((rows, pair * width), bf16)],
        [(idx, smem)] + all_stats + all_outs,
        "finish_out",
        dims=dims,
    )
    grad_q, grad_k, grad_values = call(
        finish_kernel,
        [((rows, pair * width), bf16)] + [((sub, width), bf16)] * 2,
        [grad_kv] + all_dqs,
        "finish",
    )
    return attn_out, grad_q, grad_k, grad_values


def solution(mesh):
    return jax.shard_map(
        on_device,
        mesh=mesh,
        in_specs=(P("ctx", None), P("ctx", None), P("ctx", None), P("ctx", None), P()),
        out_specs=(P("ctx", "dp"), P("ctx", "dp"), P(("dp", "ctx"), None), P(("dp", "ctx"), None)),
        check_vma=False,
    )
```

```python
import functools
import math

import jax
import jax.numpy as jnp
from jax import lax
from jax.experimental import pallas as pl
from jax.experimental.pallas import tpu as pltpu
from jax.sharding import PartitionSpec as P

NEG = -1e30
LOG2E = 1.4426950408889634
DOC_NUMBERS = 4
KEY_GROUPS = 2
MIB = 1024 * 1024
NT = (((1,), (1,)), ((), ()))


def mask_bias(seg_ref, key_group, ctx_index, rows, sub, held):
    seg = seg_ref[...]
    lines = rows // 128
    seg_own = seg_ref[pl.ds(ctx_index * lines, lines), :]
    start = jnp.zeros((lines, 128), jnp.int32)
    for number in range(1, DOC_NUMBERS):
        before = jnp.sum((seg < number).astype(jnp.float32), axis=(0, 1), keepdims=True)
        start = jnp.where(seg_own == number, before.astype(jnp.int32), start)
    start = jnp.concatenate([start[k : k + 1] for k in range(lines)], axis=1)
    query_pos = ctx_index * rows + lax.broadcasted_iota(jnp.int32, (1, rows), 1)
    line = lax.broadcasted_iota(jnp.int32, (held, rows), 0)
    place = line // sub
    chips = held // sub // 2
    block = (ctx_index // 2 ^ (place % chips)) * 2 + (ctx_index % 2 ^ (place // chips))
    key_pos = block * rows + key_group * sub + line % sub
    allowed = (key_pos >= start) & (key_pos <= query_pos)
    return jnp.where(allowed, 0.0, NEG)


def pack_kernel(token_ref, *refs):
    out_ref = refs[-1]
    size = refs[0].shape[0]
    for k, ref in enumerate(refs[:-1]):
        out_ref[k * size : (k + 1) * size, :] = ref[...]


def prep_kernel(
    idx_ref, seg_hbm, q_hbm, g_hbm, q_ref, g_ref, gt_ref, bias_ref, token_ref, seg_ref, sems, *, dims
):
    heads, rows, width, sub, held, ctx_count = dims
    head_group, key_group = idx_ref[0] // KEY_GROUPS, idx_ref[0] % KEY_GROUPS
    seg_copy = pltpu.make_async_copy(seg_hbm, seg_ref, sems.at[2, 0])
    seg_copy.start()
    copies = []
    for head in range(heads):
        source = head_columns(head_group * heads + head, width)
        target = slice(head * width, (head + 1) * width)
        for k, (full, part) in enumerate(((g_hbm, g_ref), (q_hbm, q_ref))):
            copies.append(
                pltpu.make_async_copy(full.at[:, source], part.at[:, target], sems.at[k, head])
            )
            copies[-1].start()
    token_ref[...] = jnp.zeros_like(token_ref)
    seg_copy.wait()
    bias_ref[...] = mask_bias(seg_ref, key_group, idx_ref[1], rows, sub, held)
    for head in range(heads):
        cols = slice(head * width, (head + 1) * width)
        copies[2 * head].wait()
        gt_ref[cols, :] = g_ref[:, cols].astype(jnp.float32).T.astype(jnp.bfloat16)
    for head in range(heads):
        copies[2 * head + 1].wait()


def head_columns(head, width):
    return pl.ds(pl.multiple_of(head * width, width), width)


def forward_kernel(
    idx_ref, q_ref, gt_ref, bias_ref, near_ref, far_ref, stats_ref, kv_ref, scores_ref, *refs, dims
):
    heads, rows, width, sub, held, ctx_count = dims
    outs, vt_ref = refs[:KEY_GROUPS], refs[KEY_GROUPS]
    pair = heads // KEY_GROUPS
    unit = width**-0.5 * LOG2E
    kv_ref[: held // 2, :] = near_ref[...]
    kv_ref[held // 2 :, :] = far_ref[...]
    vt_ref[...] = kv_ref[:, width:].astype(jnp.float32).T.astype(jnp.bfloat16)
    for head in range(heads):
        cols = slice(head * width, (head + 1) * width)
        raw = lax.dot_general(
            kv_ref[:, :width], q_ref[:, cols], NT, preferred_element_type=jnp.float32
        )
        scores = raw * unit + bias_ref[...]
        scores_ref[head] = scores
        stats_ref[head : head + 1, :] = jnp.max(scores, axis=0, keepdims=True)
    for slot in range(KEY_GROUPS):
        for part in range(pair):
            head = (idx_ref[0] % KEY_GROUPS ^ slot) * pair + part
            expd = jnp.exp2(scores_ref[head] - stats_ref[pl.ds(head, 1), :])
            total = jnp.sum(expd, axis=0, keepdims=True)
            accum = jnp.dot(
                vt_ref[...], expd.astype(jnp.bfloat16), preferred_element_type=jnp.float32
            )
            grad_t = gt_ref[head_columns(head, width), :].astype(jnp.float32)
            delta = jnp.sum(accum * grad_t, axis=0, keepdims=True)
            outs[slot][part * width : (part + 1) * width, :] = accum.astype(jnp.bfloat16)
            stats_ref[pl.ds(heads + head, 1), :] = total
            stats_ref[pl.ds(2 * heads + head, 1), :] = delta


def merged_stats(stats, heads):
    top = functools.reduce(jnp.maximum, [s[:heads] for s in stats])
    shares = [jnp.exp2(s[:heads] - top) for s in stats]
    total = sum(f * s[heads : 2 * heads] for f, s in zip(shares, stats))
    delta = sum(f * s[2 * heads :] for f, s in zip(shares, stats)) / total
    return top, shares, total, delta


def summed_block(ctx_index, dp_count, ctx_count):
    low, head_groups = ctx_index % dp_count, dp_count // KEY_GROUPS
    turned = low % head_groups * KEY_GROUPS + low // head_groups
    return turned * (ctx_count // dp_count) + ctx_index // dp_count


def backward_kernel(idx_ref, q_ref, g_ref, kv_ref, scores_ref, *refs, dims, dp_count):
    heads, rows, width, sub, held, ctx_count = dims
    stats = refs[:KEY_GROUPS]
    ds_ref, keep_ref, send_ref, acc_ref = refs[KEY_GROUPS:]
    scale = width**-0.5
    top, _, total, delta = merged_stats([s[...] for s in stats], heads)
    lse = top + jnp.log2(total)
    for head in range(heads):
        cols = slice(head * width, (head + 1) * width)
        query, grad = q_ref[:, cols], g_ref[:, cols]
        probs = jnp.exp2(scores_ref[head] - lse[head : head + 1])
        dprobs = lax.dot_general(kv_ref[:, width:], grad, NT, preferred_element_type=jnp.float32)
        dscores = (probs * (dprobs - delta[head : head + 1])).astype(jnp.bfloat16)
        ds_ref[head] = dscores
        dv = jnp.dot(probs.astype(jnp.bfloat16), grad, preferred_element_type=jnp.float32)
        dk = jnp.dot(dscores, query, preferred_element_type=jnp.float32)
        if head == 0:
            acc_ref[:, :width] = dk
            acc_ref[:, width:] = dv
        else:
            acc_ref[:, :width] += dk
            acc_ref[:, width:] += dv
    ctx_index = idx_ref[1]
    chip, core = ctx_index // 2, ctx_index % 2
    for flip in range(ctx_count // 2):
        here = slice(flip * sub, (flip + 1) * sub)
        for ref, side in ((keep_ref, core), (send_ref, 1 - core)):
            block = summed_block((chip ^ flip) * 2 + side, dp_count, ctx_count)
            line = (block % 2 ^ core) * (held // 2) + (block // 2 ^ chip) * sub
            mine = pl.ds(pl.multiple_of(line, sub), sub)
            ref[here, :width] = (acc_ref[mine, :width] * scale).astype(ref.dtype)
            ref[here, width:] = acc_ref[mine, width:].astype(ref.dtype)


def query_kernel(idx_ref, kv_ref, ds_ref, *refs, dims):
    heads, rows, width, sub, held, ctx_count = dims
    outs, kt_ref = refs[:KEY_GROUPS], refs[KEY_GROUPS]
    pair = heads // KEY_GROUPS
    scale = width**-0.5
    kt_ref[...] = kv_ref[:, :width].astype(jnp.float32).T.astype(jnp.bfloat16)
    for slot in range(KEY_GROUPS):
        for part in range(pair):
            head = (idx_ref[0] % KEY_GROUPS ^ slot) * pair + part
            dq = jnp.dot(kt_ref[...], ds_ref[head], preferred_element_type=jnp.float32)
            outs[slot][part * width : (part + 1) * width, :] = (dq * scale).astype(jnp.bfloat16)


def join_kernel(keep_ref, got_ref, *outs):
    size = outs[0].shape[0]
    for k, out_ref in enumerate(outs):
        here = slice(k * size, (k + 1) * size)
        total = keep_ref[here, :] + got_ref[here, :].astype(jnp.float32)
        out_ref[...] = total.astype(out_ref.dtype)


def sum_kernel(idx_ref, *refs, terms):
    parts, outs = refs[:terms], refs[terms:]
    size = outs[0].shape[0]
    group = idx_ref[0] // KEY_GROUPS
    for k, out_ref in enumerate(outs):
        mine = pl.ds(pl.multiple_of((group ^ k) * size, size), size)
        total = sum(r[mine, :].astype(jnp.float32) for r in parts)
        out_ref[...] = total.astype(out_ref.dtype)


def finish_out_kernel(idx_ref, *refs, dims):
    heads, rows, width, sub, held, ctx_count = dims
    stats, outs, attn_ref = refs[:KEY_GROUPS], refs[KEY_GROUPS : 2 * KEY_GROUPS], refs[-1]
    pair = heads // KEY_GROUPS
    top, shares, total, _ = merged_stats([s[...] for s in stats], heads)
    own = idx_ref[0] % KEY_GROUPS * pair
    row = lax.broadcasted_iota(jnp.int32, (heads, 1), 0)
    for part in range(pair):
        here = slice(part * width, (part + 1) * width)

        def pick(array):
            return jnp.sum(jnp.where(row == own + part, array, 0.0), axis=0, keepdims=True)

        joined = sum(o[here, :].astype(jnp.float32) * pick(f) for o, f in zip(outs, shares))
        attn_ref[:, here] = (joined / pick(total)).T.astype(jnp.bfloat16)


def finish_kernel(*refs):
    *sources, gq_ref, gk_ref, gv_ref = refs
    dqs, terms = sources[:KEY_GROUPS], sources[KEY_GROUPS:]
    width = gk_ref.shape[1]
    gq_ref[...] = sum(r[...].astype(jnp.float32) for r in dqs).T.astype(jnp.bfloat16)
    both = sum(r[...].astype(jnp.float32) for r in terms)
    gk_ref[...] = both[:, :width].astype(jnp.bfloat16)
    gv_ref[...] = both[:, width:].astype(jnp.bfloat16)


def on_device(queries, keys, values, out_grad, segment_ids):
    rows = queries.shape[0]
    width = keys.shape[1]
    seq = segment_ids.shape[0]
    dp_index, ctx_index = lax.axis_index("dp"), lax.axis_index("ctx")
    dp_count, ctx_count = lax.axis_size("dp"), lax.axis_size("ctx")
    key_group = dp_index % KEY_GROUPS
    head_groups = dp_count // KEY_GROUPS
    heads = queries.shape[1] // width // head_groups
    pair = heads // KEY_GROUPS
    chips = ctx_count // 2
    sub = rows // KEY_GROUPS
    held = sub * ctx_count
    piece = rows // dp_count
    dims = (heads, rows, width, sub, held, ctx_count)
    idx = jnp.stack([dp_index, ctx_index]).astype(jnp.int32)
    seg = segment_ids.reshape(seq // 128, 128)
    params = pltpu.CompilerParams(
        vmem_limit_bytes=min(56 * MIB, 12 * MIB + 12 * 4 * held * rows)
    )
    smem = pl.BlockSpec(memory_space=pltpu.SMEM)
    vmem = pl.BlockSpec(memory_space=pltpu.VMEM)
    bf16, f32 = jnp.bfloat16, jnp.float32

    def call(kernel, outs, ins, name, scratch=(), work=0, **static):
        specs = [a[1] if isinstance(a, tuple) else vmem for a in ins]
        arrays = [a[0] if isinstance(a, tuple) else a for a in ins]
        return pl.pallas_call(
            functools.partial(kernel, **static),
            out_shape=[jax.ShapeDtypeStruct(*o) for o in outs],
            in_specs=specs,
            out_specs=[vmem] * len(outs),
            scratch_shapes=list(scratch),
            compiler_params=params,
            cost_estimate=pl.CostEstimate(
                flops=work * 2 * heads * rows * held * width,
                bytes_accessed=sum(math.prod(o[0]) * 2 for o in outs),
                transcendentals=0,
            ),
            name=name,
        )(*arrays)

    def in_hbm(array):
        return pltpu.with_memory_space_constraint(array, pltpu.HBM), pl.BlockSpec(
            memory_space=pltpu.HBM
        )

    def over_keys(array):
        return lax.ppermute(array, "dp", [(d, d ^ 1) for d in range(dp_count)])

    def over_ctx(array, flip):
        return lax.ppermute(array, "ctx", [(c, c ^ flip) for c in range(ctx_count)])

    def to_owner(array, flip):
        moves = []
        for d in range(dp_count):
            part = d % KEY_GROUPS * head_groups + (d // KEY_GROUPS ^ flip)
            for c in range(ctx_count):
                block = summed_block(c, dp_count, ctx_count)
                moves.append((d * ctx_count + c, dp_count * block + part))
        return lax.ppermute(array, ("dp", "ctx"), moves)

    own_kv = jnp.concatenate(
        [lax.dynamic_slice_in_dim(a, key_group * sub, sub, 0) for a in (keys, values)], axis=1
    )
    query_v, grad_v, grad_t, bias, token = call(
        prep_kernel,
        [
            ((rows, heads * width), bf16),
            ((rows, heads * width), bf16),
            ((heads * width, rows), bf16),
            ((held, rows), f32),
            ((8, 128), f32),
        ],
        [(idx, smem), in_hbm(seg), in_hbm(queries), in_hbm(out_grad)],
        "prepare",
        scratch=[pltpu.VMEM(seg.shape, seg.dtype), pltpu.SemaphoreType.DMA((3, heads))],
        work=1,
        dims=dims,
    )
    (near,) = call(
        pack_kernel,
        [((held // 2, 2 * width), bf16)],
        [token, own_kv] + [over_ctx(own_kv, 2 * t) for t in range(1, chips)],
        "pack",
    )
    far = over_ctx(near, 1)
    stats, kv, scores, *outs = call(
        forward_kernel,
        [
            ((3 * heads, rows), f32),
            ((held, 2 * width), bf16),
            ((heads, held, rows), f32),
        ]
        + [((pair * width, rows), bf16)] * KEY_GROUPS,
        [(idx, smem), query_v, grad_t, bias, near, far],
        "attend",
        scratch=[pltpu.VMEM((width, held), bf16)],
        work=2,
        dims=dims,
    )
    all_stats = [stats, over_keys(stats)]
    all_outs = [outs[0], over_keys(outs[1])]

    dscores, keep, send = call(
        backward_kernel,
        [
            ((heads, held, rows), bf16),
            ((held // 2, 2 * width), f32),
            ((held // 2, 2 * width), bf16),
        ],
        [(idx, smem), query_v, grad_v, kv, scores] + all_stats,
        "differentiate",
        scratch=[pltpu.VMEM((held, 2 * width), f32)],
        work=4,
        dims=dims,
        dp_count=dp_count,
    )
    got = over_ctx(send, 1)
    dqs = call(
        query_kernel,
        [((pair * width, rows), bf16)] * KEY_GROUPS,
        [(idx, smem), kv, dscores],
        "query_terms",
        scratch=[pltpu.VMEM((width, held), bf16)],
        work=1,
        dims=dims,
    )
    joined = call(
        join_kernel,
        [((sub, 2 * width), f32)] + [((sub, 2 * width), bf16)] * (chips - 1),
        [keep, got],
        "join",
    )
    terms = [joined[0]] + [over_ctx(joined[t], 2 * t) for t in range(1, chips)]
    all_dqs = [dqs[0], over_keys(dqs[1])]
    pieces = call(
        sum_kernel,
        [((piece, 2 * width), bf16)] * head_groups,
        [(idx, smem)] + terms,
        "sum_terms",
        terms=chips,
    )
    grad_kv = [to_owner(p, k) for k, p in enumerate(pieces)]

    (attn_out,) = call(
        finish_out_kernel,
        [((rows, pair * width), bf16)],
        [(idx, smem)] + all_stats + all_outs,
        "finish_out",
        dims=dims,
    )
    grad_q, grad_k, grad_values = call(
        finish_kernel,
        [((rows, pair * width), bf16)] + [((piece, width), bf16)] * 2,
        all_dqs + grad_kv,
        "finish",
    )
    return attn_out, grad_q, grad_k, grad_values


def solution(mesh):
    return jax.shard_map(
        on_device,
        mesh=mesh,
        in_specs=(P("ctx", None), P("ctx", None), P("ctx", None), P("ctx", None), P()),
        out_specs=(P("ctx", "dp"), P("ctx", "dp"), P(("dp", "ctx"), None), P(("dp", "ctx"), None)),
        check_vma=False,
    )
```

```python
import functools
import math

import jax
import jax.numpy as jnp
from jax import lax
from jax.experimental import pallas as pl
from jax.experimental.pallas import tpu as pltpu
from jax.sharding import PartitionSpec as P

NEG = -1e30
LOG2E = 1.4426950408889634
DOC_NUMBERS = 4
KEY_GROUPS = 2
MIB = 1024 * 1024


def place():
    dp_index, ctx_index = lax.axis_index("dp"), lax.axis_index("ctx")
    return dp_index // KEY_GROUPS, dp_index % KEY_GROUPS, ctx_index // 2, ctx_index % 2

NT = (((1,), (1,)), ((), ()))


def mask_bias(seg_ref, rows, sub, held):
    _, key_group, chip, core = place()
    ctx_index = chip * 2 + core
    seg = seg_ref[...]
    lines = rows // 128
    seg_own = seg_ref[pl.ds(ctx_index * lines, lines), :]
    start = jnp.zeros((lines, 128), jnp.int32)
    for number in range(1, DOC_NUMBERS):
        before = jnp.sum((seg < number).astype(jnp.float32), axis=(0, 1), keepdims=True)
        start = jnp.where(seg_own == number, before.astype(jnp.int32), start)
    start = jnp.concatenate([start[k : k + 1] for k in range(lines)], axis=1)
    query_pos = ctx_index * rows + lax.broadcasted_iota(jnp.int32, (1, rows), 1)
    line = lax.broadcasted_iota(jnp.int32, (held, rows), 0)
    spot = line // sub
    chips = held // sub // 2
    block = (chip ^ (spot % chips)) * 2 + (core ^ (spot // chips))
    key_pos = block * rows + key_group * sub + line % sub
    allowed = (key_pos >= start) & (key_pos <= query_pos)
    return jnp.where(allowed, 0.0, NEG)


def pack_kernel(token_ref, *refs):
    out_ref = refs[-1]
    size = refs[0].shape[0]
    for k, ref in enumerate(refs[:-1]):
        out_ref[k * size : (k + 1) * size, :] = ref[...]


def prep_kernel(
    seg_hbm, q_hbm, g_hbm, q_ref, g_ref, gt_ref, bias_ref, token_ref, seg_ref, sems, *, dims
):
    heads, rows, width, sub, held, ctx_count = dims
    head_group = place()[0]
    seg_copy = pltpu.make_async_copy(seg_hbm, seg_ref, sems.at[2, 0])
    seg_copy.start()
    copies = []
    for head in range(heads):
        source = head_columns(head_group * heads + head, width)
        target = slice(head * width, (head + 1) * width)
        for k, (full, part) in enumerate(((g_hbm, g_ref), (q_hbm, q_ref))):
            copies.append(
                pltpu.make_async_copy(full.at[:, source], part.at[:, target], sems.at[k, head])
            )
            copies[-1].start()
    token_ref[...] = jnp.zeros_like(token_ref)
    seg_copy.wait()
    bias_ref[...] = mask_bias(seg_ref, rows, sub, held)
    for head in range(heads):
        cols = slice(head * width, (head + 1) * width)
        copies[2 * head].wait()
        gt_ref[cols, :] = g_ref[:, cols].astype(jnp.float32).T.astype(jnp.bfloat16)
    for head in range(heads):
        copies[2 * head + 1].wait()


def head_columns(head, width):
    return pl.ds(pl.multiple_of(head * width, width), width)


def forward_kernel(
    q_ref, gt_ref, bias_ref, near_ref, far_ref, stats_ref, kv_ref, scores_ref, *refs, dims
):
    heads, rows, width, sub, held, ctx_count = dims
    outs, vt_ref = refs[:KEY_GROUPS], refs[KEY_GROUPS]
    pair = heads // KEY_GROUPS
    key_group = place()[1]
    unit = width**-0.5 * LOG2E
    kv_ref[: held // 2, :] = near_ref[...]
    kv_ref[held // 2 :, :] = far_ref[...]
    vt_ref[...] = kv_ref[:, width:].astype(jnp.float32).T.astype(jnp.bfloat16)
    for head in range(heads):
        cols = slice(head * width, (head + 1) * width)
        raw = lax.dot_general(
            kv_ref[:, :width], q_ref[:, cols], NT, preferred_element_type=jnp.float32
        )
        scores = raw * unit + bias_ref[...]
        scores_ref[head] = scores
        stats_ref[head : head + 1, :] = jnp.max(scores, axis=0, keepdims=True)
    for slot in range(KEY_GROUPS):
        for part in range(pair):
            head = (key_group ^ slot) * pair + part
            expd = jnp.exp2(scores_ref[head] - stats_ref[pl.ds(head, 1), :])
            total = jnp.sum(expd, axis=0, keepdims=True)
            accum = jnp.dot(
                vt_ref[...], expd.astype(jnp.bfloat16), preferred_element_type=jnp.float32
            )
            grad_t = gt_ref[head_columns(head, width), :].astype(jnp.float32)
            delta = jnp.sum(accum * grad_t, axis=0, keepdims=True)
            outs[slot][part * width : (part + 1) * width, :] = accum.astype(jnp.bfloat16)
            stats_ref[pl.ds(heads + head, 1), :] = total
            stats_ref[pl.ds(2 * heads + head, 1), :] = delta


def merged_stats(stats, heads):
    top = functools.reduce(jnp.maximum, [s[:heads] for s in stats])
    shares = [jnp.exp2(s[:heads] - top) for s in stats]
    total = sum(f * s[heads : 2 * heads] for f, s in zip(shares, stats))
    delta = sum(f * s[2 * heads :] for f, s in zip(shares, stats)) / total
    return top, shares, total, delta


def summed_block(head_group, chip, ctx_count):
    return head_group * (ctx_count // 2) + chip % 2 * (ctx_count // 4) + chip // 2


def backward_kernel(q_ref, g_ref, kv_ref, scores_ref, *refs, dims):
    heads, rows, width, sub, held, ctx_count = dims
    stats = refs[:KEY_GROUPS]
    ds_ref, keep_ref, send_ref, acc_ref = refs[KEY_GROUPS:]
    scale = width**-0.5
    top, _, total, delta = merged_stats([s[...] for s in stats], heads)
    lse = top + jnp.log2(total)
    for head in range(heads):
        cols = slice(head * width, (head + 1) * width)
        query, grad = q_ref[:, cols], g_ref[:, cols]
        probs = jnp.exp2(scores_ref[head] - lse[head : head + 1])
        dprobs = lax.dot_general(kv_ref[:, width:], grad, NT, preferred_element_type=jnp.float32)
        dscores = (probs * (dprobs - delta[head : head + 1])).astype(jnp.bfloat16)
        ds_ref[head] = dscores
        dv = jnp.dot(probs.astype(jnp.bfloat16), grad, preferred_element_type=jnp.float32)
        dk = jnp.dot(dscores, query, preferred_element_type=jnp.float32)
        if head == 0:
            acc_ref[:, :width] = dk
            acc_ref[:, width:] = dv
        else:
            acc_ref[:, :width] += dk
            acc_ref[:, width:] += dv
    head_group, _, chip, core = place()
    chips, piece = ctx_count // 2, sub // 2
    for spot in range(2 * chips):
        here = slice(spot * piece, (spot + 1) * piece)
        block = summed_block(head_group ^ (spot // chips), chip ^ (spot % chips), ctx_count)
        line = (block % 2 ^ core) * (held // 2) + (block // 2 ^ chip) * sub
        for ref, side in ((keep_ref, core), (send_ref, 1 - core)):
            mine = pl.ds(pl.multiple_of(line + side * piece, piece), piece)
            ref[here, :width] = (acc_ref[mine, :width] * scale).astype(ref.dtype)
            ref[here, width:] = acc_ref[mine, width:].astype(ref.dtype)


def query_kernel(kv_ref, ds_ref, after_ref, *refs, dims):
    heads, rows, width, sub, held, ctx_count = dims
    outs, kt_ref = refs[:KEY_GROUPS], refs[KEY_GROUPS]
    pair = heads // KEY_GROUPS
    key_group = place()[1]
    scale = width**-0.5
    kt_ref[...] = kv_ref[:, :width].astype(jnp.float32).T.astype(jnp.bfloat16)
    for slot in range(KEY_GROUPS):
        for part in range(pair):
            head = (key_group ^ slot) * pair + part
            dq = jnp.dot(kt_ref[...], ds_ref[head], preferred_element_type=jnp.float32)
            outs[slot][part * width : (part + 1) * width, :] = (dq * scale).astype(jnp.bfloat16)


def join_kernel(keep_ref, got_ref, *refs, after):
    start = 0
    for out_ref in refs[after:]:
        here = slice(start, start + out_ref.shape[0])
        total = keep_ref[here, :] + got_ref[here, :].astype(jnp.float32)
        out_ref[...] = total.astype(out_ref.dtype)
        start = start + out_ref.shape[0]


def finish_out_kernel(*refs, dims):
    heads, rows, width, sub, held, ctx_count = dims
    stats, outs = refs[:KEY_GROUPS], refs[KEY_GROUPS : 2 * KEY_GROUPS]
    attn_ref, token_ref = refs[2 * KEY_GROUPS :]
    token_ref[...] = jnp.zeros_like(token_ref)
    pair = heads // KEY_GROUPS
    top, shares, total, _ = merged_stats([s[...] for s in stats], heads)
    own = place()[1] * pair
    row = lax.broadcasted_iota(jnp.int32, (heads, 1), 0)
    for part in range(pair):
        here = slice(part * width, (part + 1) * width)

        def pick(array):
            return jnp.sum(jnp.where(row == own + part, array, 0.0), axis=0, keepdims=True)

        joined = sum(o[here, :].astype(jnp.float32) * pick(f) for o, f in zip(outs, shares))
        attn_ref[:, here] = (joined / pick(total)).T.astype(jnp.bfloat16)


def finish_kernel(*refs):
    *sources, gq_ref, gk_ref, gv_ref = refs
    dqs, terms = sources[:KEY_GROUPS], sources[KEY_GROUPS:]
    width = gk_ref.shape[1]
    gq_ref[...] = sum(r[...].astype(jnp.float32) for r in dqs).T.astype(jnp.bfloat16)
    both = sum(r[...].astype(jnp.float32) for r in terms)
    gk_ref[...] = both[:, :width].astype(jnp.bfloat16)
    gv_ref[...] = both[:, width:].astype(jnp.bfloat16)


def on_device(queries, keys, values, out_grad, segment_ids):
    rows = queries.shape[0]
    width = keys.shape[1]
    seq = segment_ids.shape[0]
    dp_count, ctx_count = lax.axis_size("dp"), lax.axis_size("ctx")
    key_group = place()[1]
    head_groups = dp_count // KEY_GROUPS
    heads = queries.shape[1] // width // head_groups
    pair = heads // KEY_GROUPS
    chips = ctx_count // 2
    sub = rows // KEY_GROUPS
    held = sub * ctx_count
    piece = rows // dp_count
    dims = (heads, rows, width, sub, held, ctx_count)
    seg = segment_ids.reshape(seq // 128, 128)
    params = pltpu.CompilerParams(
        vmem_limit_bytes=min(56 * MIB, 12 * MIB + 12 * 4 * held * rows)
    )
    vmem = pl.BlockSpec(memory_space=pltpu.VMEM)
    bf16, f32 = jnp.bfloat16, jnp.float32

    def call(kernel, outs, ins, name, scratch=(), work=0, **static):
        specs = [a[1] if isinstance(a, tuple) else vmem for a in ins]
        arrays = [a[0] if isinstance(a, tuple) else a for a in ins]
        return pl.pallas_call(
            functools.partial(kernel, **static),
            out_shape=[jax.ShapeDtypeStruct(*o) for o in outs],
            in_specs=specs,
            out_specs=[vmem] * len(outs),
            scratch_shapes=list(scratch),
            compiler_params=params,
            cost_estimate=pl.CostEstimate(
                flops=work * 2 * heads * rows * held * width,
                bytes_accessed=sum(math.prod(o[0]) * 2 for o in outs),
                transcendentals=0,
            ),
            name=name,
        )(*arrays)

    def in_hbm(array):
        return pltpu.with_memory_space_constraint(array, pltpu.HBM), pl.BlockSpec(
            memory_space=pltpu.HBM
        )

    def over_dp(array, flip):
        return lax.ppermute(array, "dp", [(d, d ^ flip) for d in range(dp_count)])

    def over_ctx(array, flip):
        return lax.ppermute(array, "ctx", [(c, c ^ flip) for c in range(ctx_count)])

    def to_owner(array, flip):
        moves = []
        for d in range(dp_count):
            g, k = divmod(d, KEY_GROUPS)
            for c in range(ctx_count):
                chip, core = divmod(c, 2)
                block = summed_block(g, chip ^ flip, ctx_count)
                moves.append((d * ctx_count + c, dp_count * block + 2 * k + core))
        return lax.ppermute(array, ("dp", "ctx"), moves)

    own_kv = jnp.concatenate(
        [lax.dynamic_slice_in_dim(a, key_group * sub, sub, 0) for a in (keys, values)], axis=1
    )
    query_v, grad_v, grad_t, bias, token = call(
        prep_kernel,
        [
            ((rows, heads * width), bf16),
            ((rows, heads * width), bf16),
            ((heads * width, rows), bf16),
            ((held, rows), f32),
            ((8, 128), f32),
        ],
        [in_hbm(seg), in_hbm(queries), in_hbm(out_grad)],
        "prepare",
        scratch=[pltpu.VMEM(seg.shape, seg.dtype), pltpu.SemaphoreType.DMA((3, heads))],
        work=1,
        dims=dims,
    )
    (near,) = call(
        pack_kernel,
        [((held // 2, 2 * width), bf16)],
        [token, own_kv] + [over_ctx(own_kv, 2 * t) for t in range(1, chips)],
        "pack",
    )
    far = over_ctx(near, 1)
    stats, kv, scores, *outs = call(
        forward_kernel,
        [
            ((3 * heads, rows), f32),
            ((held, 2 * width), bf16),
            ((heads, held, rows), f32),
        ]
        + [((pair * width, rows), bf16)] * KEY_GROUPS,
        [query_v, grad_t, bias, near, far],
        "attend",
        scratch=[pltpu.VMEM((width, held), bf16)],
        work=2,
        dims=dims,
    )
    all_stats = [stats, over_dp(stats, 1)]
    all_outs = [outs[0], over_dp(outs[1], 1)]

    dscores, keep, send = call(
        backward_kernel,
        [
            ((heads, held, rows), bf16),
            ((held // 2, 2 * width), f32),
            ((held // 2, 2 * width), bf16),
        ],
        [query_v, grad_v, kv, scores] + all_stats,
        "differentiate",
        scratch=[pltpu.VMEM((held, 2 * width), f32)],
        work=4,
        dims=dims,
    )
    got = over_ctx(send, 1)
    dqs = call(
        query_kernel,
        [((pair * width, rows), bf16)] * KEY_GROUPS,
        [kv, dscores, all_outs[1]],
        "query_terms",
        scratch=[pltpu.VMEM((width, held), bf16)],
        work=1,
        dims=dims,
    )
    all_dqs = [dqs[0], over_dp(dqs[1], 1)]
    attn_out, token = call(
        finish_out_kernel,
        [((rows, pair * width), bf16), ((8, 128), f32)],
        all_stats + all_outs,
        "finish_out",
        dims=dims,
    )
    quarter = held // 4
    keep, send = call(
        join_kernel,
        [((quarter, 2 * width), f32), ((quarter, 2 * width), bf16)],
        [keep, got],
        "join_cores",
        after=0,
    )
    pieces = call(
        join_kernel,
        [((piece, 2 * width), bf16)] * chips,
        [keep, over_dp(send, 2), token],
        "join_heads",
        after=1,
    )
    grad_kv = [to_owner(p, k) for k, p in enumerate(pieces)]

    grad_q, grad_k, grad_values = call(
        finish_kernel,
        [((rows, pair * width), bf16)] + [((piece, width), bf16)] * 2,
        all_dqs + grad_kv,
        "finish",
    )
    return attn_out, grad_q, grad_k, grad_values


def solution(mesh):
    return jax.shard_map(
        on_device,
        mesh=mesh,
        in_specs=(P("ctx", None), P("ctx", None), P("ctx", None), P("ctx", None), P()),
        out_specs=(P("ctx", "dp"), P("ctx", "dp"), P(("dp", "ctx"), None), P(("dp", "ctx"), None)),
        check_vma=False,
    )
```

```python
import functools
import math

import jax
import jax.numpy as jnp
from jax import lax
from jax.experimental import pallas as pl
from jax.experimental.pallas import tpu as pltpu
from jax.sharding import PartitionSpec as P

NEG = -1e30
LOG2E = 1.4426950408889634
DOC_NUMBERS = 4
KEY_GROUPS = 2
MIB = 1024 * 1024


def place():
    dp_index, ctx_index = lax.axis_index("dp"), lax.axis_index("ctx")
    return dp_index // KEY_GROUPS, dp_index % KEY_GROUPS, ctx_index // 2, ctx_index % 2

NT = (((1,), (1,)), ((), ()))


def home_chip(spot, key_group, chip, chips):
    level = chips // 4
    flip = spot // level * (2 * level) + spot % level
    home = chip ^ flip
    return home ^ ((home // level % 2) ^ key_group) * level


def mask_bias(seg_ref, rows, held):
    _, key_group, chip, core = place()
    seg = seg_ref[...]
    lines = rows // 128
    seg_own = seg_ref[pl.ds((chip * 2 + core) * lines, lines), :]
    start = jnp.zeros((lines, 128), jnp.int32)
    for number in range(1, DOC_NUMBERS):
        before = jnp.sum((seg < number).astype(jnp.float32), axis=(0, 1), keepdims=True)
        start = jnp.where(seg_own == number, before.astype(jnp.int32), start)
    start = jnp.concatenate([start[k : k + 1] for k in range(lines)], axis=1)
    query_pos = (chip * 2 + core) * rows + lax.broadcasted_iota(jnp.int32, (1, rows), 1)
    blocks = held // rows
    bias = []
    for block in range(blocks):
        spot, side = block % (blocks // 2), block // (blocks // 2)
        home = home_chip(spot, key_group, chip, blocks) * 2 + (core ^ side)
        key_pos = home * rows + lax.broadcasted_iota(jnp.int32, (rows, rows), 0)
        allowed = (key_pos >= start) & (key_pos <= query_pos)
        bias.append(jnp.where(allowed, 0.0, NEG))
    return bias


def load_kernel(k_hbm, v_hbm, kv_ref, sems):
    width = k_hbm.shape[1]
    copies = [
        pltpu.make_async_copy(k_hbm, kv_ref.at[:, :width], sems.at[0]),
        pltpu.make_async_copy(v_hbm, kv_ref.at[:, width:], sems.at[1]),
    ]
    for copy in copies:
        copy.start()
    for copy in copies:
        copy.wait()


def pack_kernel(token_ref, *refs, chips):
    out_ref = refs[chips]
    size = refs[0].shape[0]
    _, key_group, chip, _ = place()
    level = chips // 4
    turn = (chip // level % 2) ^ key_group
    for spot in range(chips // 2):
        flip = spot // level * (2 * level) + spot % level
        for turned in range(2):

            @pl.when(turn == turned)
            def _():
                out_ref[spot * size : (spot + 1) * size, :] = refs[flip ^ turned * level][...]


def prep_kernel(
    seg_hbm, q_hbm, g_hbm, q_ref, g_ref, gt_ref, bias_ref, token_ref, seg_ref, sems, *, dims
):
    heads, rows, width, held, ctx_count = dims
    head_group = place()[0]
    seg_copy = pltpu.make_async_copy(seg_hbm, seg_ref, sems.at[2, 0])
    seg_copy.start()
    copies = []
    for head in range(heads):
        source = head_columns(head_group * heads + head, width)
        target = slice(head * width, (head + 1) * width)
        for k, (full, part) in enumerate(((g_hbm, g_ref), (q_hbm, q_ref))):
            copies.append(
                pltpu.make_async_copy(full.at[:, source], part.at[:, target], sems.at[k, head])
            )
            copies[-1].start()
    token_ref[...] = jnp.zeros_like(token_ref)
    seg_copy.wait()
    for k, block in enumerate(mask_bias(seg_ref, rows, held)):
        bias_ref[k * rows : (k + 1) * rows, :] = block
    for head in range(heads):
        cols = slice(head * width, (head + 1) * width)
        copies[2 * head].wait()
        gt_ref[cols, :] = g_ref[:, cols].astype(jnp.float32).T.astype(jnp.bfloat16)
    for head in range(heads):
        copies[2 * head + 1].wait()


def head_columns(head, width):
    return pl.ds(pl.multiple_of(head * width, width), width)


def forward_kernel(
    q_ref, gt_ref, bias_ref, near_ref, far_ref, stats_ref, kv_ref, scores_ref, *refs, dims
):
    heads, rows, width, held, ctx_count = dims
    outs, vt_ref = refs[:KEY_GROUPS], refs[KEY_GROUPS]
    pair = heads // KEY_GROUPS
    key_group = place()[1]
    unit = width**-0.5 * LOG2E
    kv_ref[: held // 2, :] = near_ref[...]
    kv_ref[held // 2 :, :] = far_ref[...]
    vt_ref[...] = kv_ref[:, width:].astype(jnp.float32).T.astype(jnp.bfloat16)
    for head in range(heads):
        cols = slice(head * width, (head + 1) * width)
        raw = lax.dot_general(
            kv_ref[:, :width], q_ref[:, cols], NT, preferred_element_type=jnp.float32
        )
        scores = raw * unit + bias_ref[...]
        scores_ref[head] = scores
        stats_ref[head : head + 1, :] = jnp.max(scores, axis=0, keepdims=True)
    for slot in range(KEY_GROUPS):
        for part in range(pair):
            head = (key_group ^ slot) * pair + part
            expd = jnp.exp2(scores_ref[head] - stats_ref[pl.ds(head, 1), :])
            total = jnp.sum(expd, axis=0, keepdims=True)
            accum = jnp.dot(
                vt_ref[...], expd.astype(jnp.bfloat16), preferred_element_type=jnp.float32
            )
            grad_t = gt_ref[head_columns(head, width), :].astype(jnp.float32)
            delta = jnp.sum(accum * grad_t, axis=0, keepdims=True)
            outs[slot][part * width : (part + 1) * width, :] = accum.astype(jnp.bfloat16)
            stats_ref[pl.ds(heads + head, 1), :] = total
            stats_ref[pl.ds(2 * heads + head, 1), :] = delta


def merged_stats(stats, heads):
    top = functools.reduce(jnp.maximum, [s[:heads] for s in stats])
    shares = [jnp.exp2(s[:heads] - top) for s in stats]
    total = sum(f * s[heads : 2 * heads] for f, s in zip(shares, stats))
    delta = sum(f * s[2 * heads :] for f, s in zip(shares, stats)) / total
    return top, shares, total, delta


def backward_kernel(q_ref, g_ref, kv_ref, scores_ref, *refs, dims):
    heads, rows, width, held, ctx_count = dims
    stats = refs[:KEY_GROUPS]
    ds_ref, keep_ref, send_ref, acc_ref = refs[KEY_GROUPS:]
    scale = width**-0.5
    top, _, total, delta = merged_stats([s[...] for s in stats], heads)
    lse = top + jnp.log2(total)
    for head in range(heads):
        cols = slice(head * width, (head + 1) * width)
        query, grad = q_ref[:, cols], g_ref[:, cols]
        probs = jnp.exp2(scores_ref[head] - lse[head : head + 1])
        dprobs = lax.dot_general(kv_ref[:, width:], grad, NT, preferred_element_type=jnp.float32)
        dscores = (probs * (dprobs - delta[head : head + 1])).astype(jnp.bfloat16)
        ds_ref[head] = dscores
        dv = jnp.dot(probs.astype(jnp.bfloat16), grad, preferred_element_type=jnp.float32)
        dk = jnp.dot(dscores, query, preferred_element_type=jnp.float32)
        if head == 0:
            acc_ref[:, :width] = dk
            acc_ref[:, width:] = dv
        else:
            acc_ref[:, :width] += dk
            acc_ref[:, width:] += dv
    head_group, key_group, chip, core = place()
    chips, piece = ctx_count // 2, rows // 4
    level = chips // 4
    for spot in range(2 * chips):
        here = slice(spot * piece, (spot + 1) * piece)
        target = chip ^ (spot % chips)
        group = head_group ^ (spot // chips)
        block = group * (ctx_count // 2) + key_group * (ctx_count // 4) + target // 2
        flip = block // 2 ^ chip
        line = ((block % 2 ^ core) * (chips // 2) + flip // (2 * level) * level + flip % level) * rows
        for ref, side in ((keep_ref, core), (send_ref, 1 - core)):
            mine = pl.ds(pl.multiple_of(line + (target % 2 * 2 + side) * piece, piece), piece)
            ref[here, :width] = (acc_ref[mine, :width] * scale).astype(ref.dtype)
            ref[here, width:] = acc_ref[mine, width:].astype(ref.dtype)


def query_kernel(kv_ref, ds_ref, after_ref, *refs, dims):
    heads, rows, width, held, ctx_count = dims
    outs, kt_ref = refs[:KEY_GROUPS], refs[KEY_GROUPS]
    pair = heads // KEY_GROUPS
    key_group = place()[1]
    scale = width**-0.5
    kt_ref[...] = kv_ref[:, :width].astype(jnp.float32).T.astype(jnp.bfloat16)
    for slot in range(KEY_GROUPS):
        for part in range(pair):
            head = (key_group ^ slot) * pair + part
            dq = jnp.dot(kt_ref[...], ds_ref[head], preferred_element_type=jnp.float32)
            outs[slot][part * width : (part + 1) * width, :] = (dq * scale).astype(jnp.bfloat16)


def join_kernel(keep_ref, got_ref, *refs, after):
    start = 0
    for out_ref in refs[after:]:
        here = slice(start, start + out_ref.shape[0])
        total = keep_ref[here, :] + got_ref[here, :].astype(jnp.float32)
        out_ref[...] = total.astype(out_ref.dtype)
        start = start + out_ref.shape[0]


def finish_out_kernel(*refs, dims):
    heads, rows, width, held, ctx_count = dims
    stats, outs = refs[:KEY_GROUPS], refs[KEY_GROUPS : 2 * KEY_GROUPS]
    attn_ref, token_ref = refs[2 * KEY_GROUPS :]
    token_ref[...] = jnp.zeros_like(token_ref)
    pair = heads // KEY_GROUPS
    top, shares, total, _ = merged_stats([s[...] for s in stats], heads)
    own = place()[1] * pair
    row = lax.broadcasted_iota(jnp.int32, (heads, 1), 0)
    for part in range(pair):
        here = slice(part * width, (part + 1) * width)

        def pick(array):
            return jnp.sum(jnp.where(row == own + part, array, 0.0), axis=0, keepdims=True)

        joined = sum(o[here, :].astype(jnp.float32) * pick(f) for o, f in zip(outs, shares))
        attn_ref[:, here] = (joined / pick(total)).T.astype(jnp.bfloat16)


def finish_kernel(*refs):
    *sources, gq_ref, gk_ref, gv_ref = refs
    dqs, terms = sources[:KEY_GROUPS], sources[KEY_GROUPS:]
    width = gk_ref.shape[1]
    gq_ref[...] = sum(r[...].astype(jnp.float32) for r in dqs).T.astype(jnp.bfloat16)
    both = sum(r[...].astype(jnp.float32) for r in terms)
    gk_ref[...] = both[:, :width].astype(jnp.bfloat16)
    gv_ref[...] = both[:, width:].astype(jnp.bfloat16)


def on_device(queries, keys, values, out_grad, segment_ids):
    rows = queries.shape[0]
    width = keys.shape[1]
    seq = segment_ids.shape[0]
    dp_count, ctx_count = lax.axis_size("dp"), lax.axis_size("ctx")
    head_groups = dp_count // KEY_GROUPS
    heads = queries.shape[1] // width // head_groups
    pair = heads // KEY_GROUPS
    chips = ctx_count // 2
    held = rows * ctx_count // KEY_GROUPS
    piece = rows // dp_count
    dims = (heads, rows, width, held, ctx_count)
    seg = segment_ids.reshape(seq // 128, 128)
    params = pltpu.CompilerParams(
        vmem_limit_bytes=min(56 * MIB, 12 * MIB + 12 * 4 * held * rows)
    )
    vmem = pl.BlockSpec(memory_space=pltpu.VMEM)
    bf16, f32 = jnp.bfloat16, jnp.float32

    def call(kernel, outs, ins, name, scratch=(), work=0, **static):
        specs = [a[1] if isinstance(a, tuple) else vmem for a in ins]
        arrays = [a[0] if isinstance(a, tuple) else a for a in ins]
        return pl.pallas_call(
            functools.partial(kernel, **static),
            out_shape=[jax.ShapeDtypeStruct(*o) for o in outs],
            in_specs=specs,
            out_specs=[vmem] * len(outs),
            scratch_shapes=list(scratch),
            compiler_params=params,
            cost_estimate=pl.CostEstimate(
                flops=work * 2 * heads * rows * held * width,
                bytes_accessed=sum(math.prod(o[0]) * 2 for o in outs),
                transcendentals=0,
            ),
            name=name,
        )(*arrays)

    def in_hbm(array):
        return pltpu.with_memory_space_constraint(array, pltpu.HBM), pl.BlockSpec(
            memory_space=pltpu.HBM
        )

    def over_dp(array, flip):
        return lax.ppermute(array, "dp", [(d, d ^ flip) for d in range(dp_count)])

    def over_ctx(array, flip):
        return lax.ppermute(array, "ctx", [(c, c ^ flip) for c in range(ctx_count)])

    def to_group(array, flip):
        moves = []
        for d in range(dp_count):
            for c in range(ctx_count):
                chip, core = divmod(c, 2)
                later = chip ^ flip
                if chip // (chips // 4) % 2 == d % KEY_GROUPS and later > chip:
                    moves.append((d * ctx_count + c, d * ctx_count + later * 2 + core))
        return lax.ppermute(array, ("dp", "ctx"), moves)

    (own_kv,) = call(
        load_kernel,
        [((rows, 2 * width), bf16)],
        [in_hbm(keys), in_hbm(values)],
        "load",
        scratch=[pltpu.SemaphoreType.DMA((2,))],
    )
    query_v, grad_v, grad_t, bias, token = call(
        prep_kernel,
        [
            ((rows, heads * width), bf16),
            ((rows, heads * width), bf16),
            ((heads * width, rows), bf16),
            ((held, rows), f32),
            ((8, 128), f32),
        ],
        [in_hbm(seg), in_hbm(queries), in_hbm(out_grad)],
        "prepare",
        scratch=[pltpu.VMEM(seg.shape, seg.dtype), pltpu.SemaphoreType.DMA((3, heads))],
        work=1,
        dims=dims,
    )
    (near,) = call(
        pack_kernel,
        [((held // 2, 2 * width), bf16)],
        [token, own_kv] + [to_group(own_kv, t) for t in range(1, chips)],
        "pack",
        chips=chips,
    )
    far = over_ctx(near, 1)
    stats, kv, scores, *outs = call(
        forward_kernel,
        [
            ((3 * heads, rows), f32),
            ((held, 2 * width), bf16),
            ((heads, held, rows), f32),
        ]
        + [((pair * width, rows), bf16)] * KEY_GROUPS,
        [query_v, grad_t, bias, near, far],
        "attend",
        scratch=[pltpu.VMEM((width, held), bf16)],
        work=2,
        dims=dims,
    )
    all_stats = [stats, over_dp(stats, 1)]
    all_outs = [outs[0], over_dp(outs[1], 1)]

    dscores, keep, send = call(
        backward_kernel,
        [
            ((heads, held, rows), bf16),
            ((held // 2, 2 * width), f32),
            ((held // 2, 2 * width), bf16),
        ],
        [query_v, grad_v, kv, scores] + all_stats,
        "differentiate",
        scratch=[pltpu.VMEM((held, 2 * width), f32)],
        work=4,
        dims=dims,
    )
    got = over_ctx(send, 1)
    dqs = call(
        query_kernel,
        [((pair * width, rows), bf16)] * KEY_GROUPS,
        [kv, dscores, all_outs[1]],
        "query_terms",
        scratch=[pltpu.VMEM((width, held), bf16)],
        work=1,
        dims=dims,
    )
    all_dqs = [dqs[0], over_dp(dqs[1], 1)]
    attn_out, token = call(
        finish_out_kernel,
        [((rows, pair * width), bf16), ((8, 128), f32)],
        all_stats + all_outs,
        "finish_out",
        dims=dims,
    )
    quarter = held // 4
    keep, send = call(
        join_kernel,
        [((quarter, 2 * width), f32), ((quarter, 2 * width), bf16)],
        [keep, got],
        "join_cores",
        after=0,
    )
    pieces = call(
        join_kernel,
        [((piece, 2 * width), bf16)] * chips,
        [keep, over_dp(send, 2), token],
        "join_heads",
        after=1,
    )
    grad_kv = [pieces[0]] + [over_ctx(pieces[t], 2 * t) for t in range(1, chips)]

    grad_q, grad_k, grad_values = call(
        finish_kernel,
        [((rows, pair * width), bf16)] + [((piece, width), bf16)] * 2,
        all_dqs + grad_kv,
        "finish",
    )
    return attn_out, grad_q, grad_k, grad_values


def solution(mesh):
    return jax.shard_map(
        on_device,
        mesh=mesh,
        in_specs=(P("ctx", None), P("ctx", None), P("ctx", None), P("ctx", None), P()),
        out_specs=(P("ctx", "dp"), P("ctx", "dp"), P(("dp", "ctx"), None), P(("dp", "ctx"), None)),
        check_vma=False,
    )
```

```python
import functools
import math

import jax
import jax.numpy as jnp
from jax import lax
from jax.experimental import pallas as pl
from jax.experimental.pallas import tpu as pltpu
from jax.sharding import PartitionSpec as P

NEG = -1e30
LOG2E = 1.4426950408889634
DOC_NUMBERS = 4
KEY_GROUPS = 2
MIB = 1024 * 1024


def place():
    dp_index, ctx_index = lax.axis_index("dp"), lax.axis_index("ctx")
    return dp_index // KEY_GROUPS, dp_index % KEY_GROUPS, ctx_index // 2, ctx_index % 2

NT = (((1,), (1,)), ((), ()))


def home_chip(spot, key_group, chip, chips):
    level = chips // 4
    flip = spot // level * (2 * level) + spot % level
    home = chip ^ flip
    return home ^ ((home // level % 2) ^ key_group) * level


def mask_bias(seg_ref, rows, held):
    _, key_group, chip, core = place()
    seg = seg_ref[...]
    lines = rows // 128
    seg_own = seg_ref[pl.ds((chip * 2 + core) * lines, lines), :]
    start = jnp.zeros((lines, 128), jnp.int32)
    for number in range(1, DOC_NUMBERS):
        before = jnp.sum((seg < number).astype(jnp.float32), axis=(0, 1), keepdims=True)
        start = jnp.where(seg_own == number, before.astype(jnp.int32), start)
    start = jnp.concatenate([start[k : k + 1] for k in range(lines)], axis=1)
    query_pos = (chip * 2 + core) * rows + lax.broadcasted_iota(jnp.int32, (1, rows), 1)
    blocks = held // rows
    bias = []
    for block in range(blocks):
        spot, side = block % (blocks // 2), block // (blocks // 2)
        home = home_chip(spot, key_group, chip, blocks) * 2 + (core ^ side)
        key_pos = home * rows + lax.broadcasted_iota(jnp.int32, (rows, rows), 0)
        allowed = (key_pos >= start) & (key_pos <= query_pos)
        bias.append(jnp.where(allowed, 0.0, NEG))
    return bias


def load_kernel(k_hbm, v_hbm, kv_ref, sems):
    width = k_hbm.shape[1]
    copies = [
        pltpu.make_async_copy(k_hbm, kv_ref.at[:, :width], sems.at[0]),
        pltpu.make_async_copy(v_hbm, kv_ref.at[:, width:], sems.at[1]),
    ]
    for copy in copies:
        copy.start()
    for copy in copies:
        copy.wait()


def pack_kernel(token_ref, *refs, chips):
    refs, out_ref = refs[:1] + refs[1:chips][::-1], refs[chips]
    size = refs[0].shape[0]
    _, key_group, chip, _ = place()
    level = chips // 4
    turn = (chip // level % 2) ^ key_group
    for spot in range(chips // 2):
        flip = spot // level * (2 * level) + spot % level
        for turned in range(2):

            @pl.when(turn == turned)
            def _():
                out_ref[spot * size : (spot + 1) * size, :] = refs[flip ^ turned * level][...]


def prep_kernel(
    seg_hbm, q_hbm, g_hbm, q_ref, g_ref, gt_ref, bias_ref, token_ref, seg_ref, sems, *, dims
):
    heads, rows, width, held, ctx_count = dims
    head_group = place()[0]
    seg_copy = pltpu.make_async_copy(seg_hbm, seg_ref, sems.at[2, 0])
    seg_copy.start()
    copies = []
    for head in range(heads):
        source = head_columns(head_group * heads + head, width)
        target = slice(head * width, (head + 1) * width)
        for k, (full, part) in enumerate(((g_hbm, g_ref), (q_hbm, q_ref))):
            copies.append(
                pltpu.make_async_copy(full.at[:, source], part.at[:, target], sems.at[k, head])
            )
            copies[-1].start()
    token_ref[...] = jnp.zeros_like(token_ref)
    seg_copy.wait()
    for k, block in enumerate(mask_bias(seg_ref, rows, held)):
        bias_ref[k * rows : (k + 1) * rows, :] = block
    for head in range(heads):
        cols = slice(head * width, (head + 1) * width)
        copies[2 * head].wait()
        gt_ref[cols, :] = g_ref[:, cols].astype(jnp.float32).T.astype(jnp.bfloat16)
    for head in range(heads):
        copies[2 * head + 1].wait()


def head_columns(head, width):
    return pl.ds(pl.multiple_of(head * width, width), width)


def score_block(key_value_ref, query, bias, unit):
    width = query.shape[1]
    raw = lax.dot_general(
        key_value_ref[:, :width], query, NT, preferred_element_type=jnp.float32
    )
    return raw * unit + bias


def near_kernel(q_ref, bias_ref, near_ref, scores_ref, top_ref, vt_ref, *, dims):
    heads, rows, width, held, ctx_count = dims
    vt_ref[...] = near_ref[:, width:].astype(jnp.float32).T.astype(jnp.bfloat16)
    for head in range(heads):
        cols = slice(head * width, (head + 1) * width)
        bias = bias_ref[: held // 2, :]
        scores = score_block(near_ref, q_ref[:, cols], bias, width**-0.5 * LOG2E)
        scores_ref[head] = scores
        top_ref[head : head + 1, :] = jnp.max(scores, axis=0, keepdims=True)


def forward_kernel(
    q_ref, gt_ref, bias_ref, near_scores_ref, top_ref, near_vt_ref, far_ref, stats_ref, *refs, dims
):
    heads, rows, width, held, ctx_count = dims
    far_scores_ref, *outs, far_vt_ref = refs
    pair = heads // KEY_GROUPS
    key_group = place()[1]
    far_vt_ref[...] = far_ref[:, width:].astype(jnp.float32).T.astype(jnp.bfloat16)
    for head in range(heads):
        cols = slice(head * width, (head + 1) * width)
        bias = bias_ref[held // 2 :, :]
        scores = score_block(far_ref, q_ref[:, cols], bias, width**-0.5 * LOG2E)
        far_scores_ref[head] = scores
        row = slice(head, head + 1)
        stats_ref[row, :] = jnp.maximum(top_ref[row, :], jnp.max(scores, axis=0, keepdims=True))
    for slot in range(KEY_GROUPS):
        for part in range(pair):
            head = (key_group ^ slot) * pair + part
            top = stats_ref[pl.ds(head, 1), :]
            total, accum = 0.0, 0.0
            for scores_ref, vt_ref in ((near_scores_ref, near_vt_ref), (far_scores_ref, far_vt_ref)):
                expd = jnp.exp2(scores_ref[head] - top)
                total = total + jnp.sum(expd, axis=0, keepdims=True)
                accum = accum + jnp.dot(
                    vt_ref[...], expd.astype(jnp.bfloat16), preferred_element_type=jnp.float32
                )
            grad_t = gt_ref[head_columns(head, width), :].astype(jnp.float32)
            delta = jnp.sum(accum * grad_t, axis=0, keepdims=True)
            outs[slot][part * width : (part + 1) * width, :] = accum.astype(jnp.bfloat16)
            stats_ref[pl.ds(heads + head, 1), :] = total
            stats_ref[pl.ds(2 * heads + head, 1), :] = delta


def dprobs_kernel(g_ref, near_ref, far_ref, dprobs_ref, *, dims):
    heads, rows, width, held, ctx_count = dims
    for head in range(heads):
        grad = g_ref[:, head * width : (head + 1) * width]
        for side, ref in enumerate((near_ref, far_ref)):
            here = slice(side * held // 2, (side + 1) * held // 2)
            dprobs_ref[head, here, :] = lax.dot_general(
                ref[:, width:], grad, NT, preferred_element_type=jnp.float32
            )


def merged_stats(stats, heads):
    top = functools.reduce(jnp.maximum, [s[:heads] for s in stats])
    shares = [jnp.exp2(s[:heads] - top) for s in stats]
    total = sum(f * s[heads : 2 * heads] for f, s in zip(shares, stats))
    delta = sum(f * s[2 * heads :] for f, s in zip(shares, stats)) / total
    return top, shares, total, delta


def backward_kernel(q_ref, g_ref, near_ref, far_ref, *refs, dims, ahead):
    heads, rows, width, held, ctx_count = dims
    scores, refs = refs[:2], refs[2:]
    dprobs_ref, refs = (refs[0], refs[1:]) if ahead else (None, refs)
    stats = refs[:KEY_GROUPS]
    ds_ref, keep_ref, send_ref, acc_ref = refs[KEY_GROUPS:]
    scale = width**-0.5
    top, _, total, delta = merged_stats([s[...] for s in stats], heads)
    lse = top + jnp.log2(total)
    for head in range(heads):
        cols = slice(head * width, (head + 1) * width)
        query, grad = q_ref[:, cols], g_ref[:, cols]
        for side, ref in enumerate((near_ref, far_ref)):
            here = slice(side * held // 2, (side + 1) * held // 2)
            probs = jnp.exp2(scores[side][head] - lse[head : head + 1])
            if ahead:
                dprobs = dprobs_ref[head, here, :]
            else:
                dprobs = lax.dot_general(
                    ref[:, width:], grad, NT, preferred_element_type=jnp.float32
                )
            dscores = (probs * (dprobs - delta[head : head + 1])).astype(jnp.bfloat16)
            ds_ref[head, here, :] = dscores
            dv = jnp.dot(probs.astype(jnp.bfloat16), grad, preferred_element_type=jnp.float32)
            dk = jnp.dot(dscores, query, preferred_element_type=jnp.float32)
            if head == 0:
                acc_ref[here, :width] = dk
                acc_ref[here, width:] = dv
            else:
                acc_ref[here, :width] += dk
                acc_ref[here, width:] += dv
    head_group, key_group, chip, core = place()
    chips, piece = ctx_count // 2, rows // 4
    level = chips // 4
    for spot in range(2 * chips):
        here = slice(spot * piece, (spot + 1) * piece)
        target = chip ^ (spot % chips)
        group = head_group ^ (spot // chips)
        block = group * (ctx_count // 2) + key_group * (ctx_count // 4) + target // 2
        flip = block // 2 ^ chip
        line = ((block % 2 ^ core) * (chips // 2) + flip // (2 * level) * level + flip % level) * rows
        for ref, side in ((keep_ref, core), (send_ref, 1 - core)):
            mine = pl.ds(pl.multiple_of(line + (target % 2 * 2 + side) * piece, piece), piece)
            ref[here, :width] = (acc_ref[mine, :width] * scale).astype(ref.dtype)
            ref[here, width:] = acc_ref[mine, width:].astype(ref.dtype)


def query_kernel(near_ref, far_ref, ds_ref, after_ref, *refs, dims):
    heads, rows, width, held, ctx_count = dims
    outs, kt_ref = refs[:KEY_GROUPS], refs[KEY_GROUPS]
    pair = heads // KEY_GROUPS
    key_group = place()[1]
    scale = width**-0.5
    for side, ref in enumerate((near_ref, far_ref)):
        here = slice(side * held // 2, (side + 1) * held // 2)
        kt_ref[:, here] = ref[:, :width].astype(jnp.float32).T.astype(jnp.bfloat16)
    for slot in range(KEY_GROUPS):
        for part in range(pair):
            head = (key_group ^ slot) * pair + part
            dq = jnp.dot(kt_ref[...], ds_ref[head], preferred_element_type=jnp.float32)
            outs[slot][part * width : (part + 1) * width, :] = (dq * scale).astype(jnp.bfloat16)


def join_kernel(keep_ref, got_ref, *refs, after):
    start = 0
    for out_ref in refs[after:]:
        here = slice(start, start + out_ref.shape[0])
        total = keep_ref[here, :] + got_ref[here, :].astype(jnp.float32)
        out_ref[...] = total.astype(out_ref.dtype)
        start = start + out_ref.shape[0]


def finish_out_kernel(*refs, dims):
    heads, rows, width, held, ctx_count = dims
    stats, outs = refs[:KEY_GROUPS], refs[KEY_GROUPS : 2 * KEY_GROUPS]
    attn_ref, token_ref = refs[2 * KEY_GROUPS :]
    token_ref[...] = jnp.zeros_like(token_ref)
    pair = heads // KEY_GROUPS
    top, shares, total, _ = merged_stats([s[...] for s in stats], heads)
    own = place()[1] * pair
    row = lax.broadcasted_iota(jnp.int32, (heads, 1), 0)
    for part in range(pair):
        here = slice(part * width, (part + 1) * width)

        def pick(array):
            return jnp.sum(jnp.where(row == own + part, array, 0.0), axis=0, keepdims=True)

        joined = sum(o[here, :].astype(jnp.float32) * pick(f) for o, f in zip(outs, shares))
        attn_ref[:, here] = (joined / pick(total)).T.astype(jnp.bfloat16)


def finish_kernel(*refs):
    *sources, gq_ref, gk_ref, gv_ref = refs
    dqs, terms = sources[:KEY_GROUPS], sources[KEY_GROUPS:]
    width = gk_ref.shape[1]
    gq_ref[...] = sum(r[...].astype(jnp.float32) for r in dqs).T.astype(jnp.bfloat16)
    both = sum(r[...].astype(jnp.float32) for r in terms)
    gk_ref[...] = both[:, :width].astype(jnp.bfloat16)
    gv_ref[...] = both[:, width:].astype(jnp.bfloat16)


def on_device(queries, keys, values, out_grad, segment_ids):
    rows = queries.shape[0]
    width = keys.shape[1]
    seq = segment_ids.shape[0]
    dp_count, ctx_count = lax.axis_size("dp"), lax.axis_size("ctx")
    head_groups = dp_count // KEY_GROUPS
    heads = queries.shape[1] // width // head_groups
    pair = heads // KEY_GROUPS
    chips = ctx_count // 2
    held = rows * ctx_count // KEY_GROUPS
    piece = rows // dp_count
    dims = (heads, rows, width, held, ctx_count)
    seg = segment_ids.reshape(seq // 128, 128)
    params = pltpu.CompilerParams(
        vmem_limit_bytes=min(56 * MIB, 12 * MIB + 12 * 4 * held * rows)
    )
    vmem = pl.BlockSpec(memory_space=pltpu.VMEM)
    bf16, f32 = jnp.bfloat16, jnp.float32

    def call(kernel, outs, ins, name, scratch=(), work=0, **static):
        specs = [a[1] if isinstance(a, tuple) else vmem for a in ins]
        arrays = [a[0] if isinstance(a, tuple) else a for a in ins]
        return pl.pallas_call(
            functools.partial(kernel, **static),
            out_shape=[jax.ShapeDtypeStruct(*o) for o in outs],
            in_specs=specs,
            out_specs=[vmem] * len(outs),
            scratch_shapes=list(scratch),
            compiler_params=params,
            cost_estimate=pl.CostEstimate(
                flops=work * 2 * heads * rows * held * width,
                bytes_accessed=sum(math.prod(o[0]) * 2 for o in outs),
                transcendentals=0,
            ),
            name=name,
        )(*arrays)

    def in_hbm(array):
        return pltpu.with_memory_space_constraint(array, pltpu.HBM), pl.BlockSpec(
            memory_space=pltpu.HBM
        )

    def over_dp(array, flip):
        return lax.ppermute(array, "dp", [(d, d ^ flip) for d in range(dp_count)])

    def over_ctx(array, flip):
        return lax.ppermute(array, "ctx", [(c, c ^ flip) for c in range(ctx_count)])

    def to_group(array, flip):
        moves = []
        for d in range(dp_count):
            for c in range(ctx_count):
                chip, core = divmod(c, 2)
                later = chip ^ flip
                if chip // (chips // 4) % 2 == d % KEY_GROUPS and later > chip:
                    moves.append((d * ctx_count + c, d * ctx_count + later * 2 + core))
        return lax.ppermute(array, ("dp", "ctx"), moves)

    (own_kv,) = call(
        load_kernel,
        [((rows, 2 * width), bf16)],
        [in_hbm(keys), in_hbm(values)],
        "load",
        scratch=[pltpu.SemaphoreType.DMA((2,))],
    )
    query_v, grad_v, grad_t, bias, token = call(
        prep_kernel,
        [
            ((rows, heads * width), bf16),
            ((rows, heads * width), bf16),
            ((heads * width, rows), bf16),
            ((held, rows), f32),
            ((8, 128), f32),
        ],
        [in_hbm(seg), in_hbm(queries), in_hbm(out_grad)],
        "prepare",
        scratch=[pltpu.VMEM(seg.shape, seg.dtype), pltpu.SemaphoreType.DMA((3, heads))],
        work=1,
        dims=dims,
    )
    (near,) = call(
        pack_kernel,
        [((held // 2, 2 * width), bf16)],
        [token, own_kv] + [to_group(own_kv, t) for t in range(chips - 1, 0, -1)],
        "pack",
        chips=chips,
    )
    far = over_ctx(near, 1)
    near_scores, top, near_vt = call(
        near_kernel,
        [((heads, held // 2, rows), f32), ((heads, rows), f32), ((width, held // 2), bf16)],
        [query_v, bias, near],
        "score_near",
        work=1,
        dims=dims,
    )
    stats, far_scores, *outs = call(
        forward_kernel,
        [((3 * heads, rows), f32), ((heads, held // 2, rows), f32)]
        + [((pair * width, rows), bf16)] * KEY_GROUPS,
        [query_v, grad_t, bias, near_scores, top, near_vt, far],
        "attend",
        scratch=[pltpu.VMEM((width, held // 2), bf16)],
        work=2,
        dims=dims,
    )
    all_stats = [stats, over_dp(stats, 1)]
    all_outs = [outs[0], over_dp(outs[1], 1)]
    ahead = 4 * heads * held * rows <= 8 * MIB
    dprobs = []
    if ahead:
        dprobs = call(
            dprobs_kernel,
            [((heads, held, rows), f32)],
            [grad_v, near, far],
            "dprobs",
            work=1,
            dims=dims,
        )

    dscores, keep, send = call(
        backward_kernel,
        [
            ((heads, held, rows), bf16),
            ((held // 2, 2 * width), f32),
            ((held // 2, 2 * width), bf16),
        ],
        [query_v, grad_v, near, far, near_scores, far_scores] + list(dprobs) + all_stats,
        "differentiate",
        scratch=[pltpu.VMEM((held, 2 * width), f32)],
        work=4,
        dims=dims,
        ahead=ahead,
    )
    got = over_ctx(send, 1)
    dqs = call(
        query_kernel,
        [((pair * width, rows), bf16)] * KEY_GROUPS,
        [near, far, dscores, all_outs[1]],
        "query_terms",
        scratch=[pltpu.VMEM((width, held), bf16)],
        work=1,
        dims=dims,
    )
    all_dqs = [dqs[0], over_dp(dqs[1], 1)]
    attn_out, token = call(
        finish_out_kernel,
        [((rows, pair * width), bf16), ((8, 128), f32)],
        all_stats + all_outs,
        "finish_out",
        dims=dims,
    )
    quarter = held // 4
    keep, send = call(
        join_kernel,
        [((quarter, 2 * width), f32), ((quarter, 2 * width), bf16)],
        [keep, got],
        "join_cores",
        after=0,
    )
    pieces = call(
        join_kernel,
        [((piece, 2 * width), bf16)] * chips,
        [keep, over_dp(send, 2), token],
        "join_heads",
        after=1,
    )
    grad_kv = [pieces[0]] + [over_ctx(pieces[t], 2 * t) for t in range(1, chips)]

    grad_q, grad_k, grad_values = call(
        finish_kernel,
        [((rows, pair * width), bf16)] + [((piece, width), bf16)] * 2,
        all_dqs + grad_kv,
        "finish",
    )
    return attn_out, grad_q, grad_k, grad_values


def solution(mesh):
    return jax.shard_map(
        on_device,
        mesh=mesh,
        in_specs=(P("ctx", None), P("ctx", None), P("ctx", None), P("ctx", None), P()),
        out_specs=(P("ctx", "dp"), P("ctx", "dp"), P(("dp", "ctx"), None), P(("dp", "ctx"), None)),
        check_vma=False,
    )
```

```python
import functools
import math

import jax
import jax.numpy as jnp
from jax import lax
from jax.experimental import pallas as pl
from jax.experimental.pallas import tpu as pltpu
from jax.sharding import PartitionSpec as P

NEG = -1e30
LOG2E = 1.4426950408889634
DOC_NUMBERS = 4
KEY_GROUPS = 2
MIB = 1024 * 1024


def place():
    dp_index, ctx_index = lax.axis_index("dp"), lax.axis_index("ctx")
    return dp_index // KEY_GROUPS, dp_index % KEY_GROUPS, ctx_index // 2, ctx_index % 2

NT = (((1,), (1,)), ((), ()))


def home_chip(spot, key_group, chip, chips):
    level = chips // 4
    flip = spot // level * (2 * level) + spot % level
    home = chip ^ flip
    return home ^ ((home // level % 2) ^ key_group) * level


def mask_bias(seg_ref, rows, held):
    _, key_group, chip, core = place()
    seg = seg_ref[...]
    lines = rows // 128
    seg_own = seg_ref[pl.ds((chip * 2 + core) * lines, lines), :]
    start = jnp.zeros((lines, 128), jnp.int32)
    for number in range(1, DOC_NUMBERS):
        before = jnp.sum((seg < number).astype(jnp.float32), axis=(0, 1), keepdims=True)
        start = jnp.where(seg_own == number, before.astype(jnp.int32), start)
    start = jnp.concatenate([start[k : k + 1] for k in range(lines)], axis=1)
    query_pos = (chip * 2 + core) * rows + lax.broadcasted_iota(jnp.int32, (1, rows), 1)
    blocks = held // rows
    bias = []
    for block in range(blocks):
        spot, side = block % (blocks // 2), block // (blocks // 2)
        home = home_chip(spot, key_group, chip, blocks) * 2 + (core ^ side)
        key_pos = home * rows + lax.broadcasted_iota(jnp.int32, (rows, rows), 0)
        allowed = (key_pos >= start) & (key_pos <= query_pos)
        bias.append(jnp.where(allowed, 0.0, NEG))
    return bias


def load_kernel(k_hbm, v_hbm, kv_ref, sems):
    width = k_hbm.shape[1]
    copies = [
        pltpu.make_async_copy(k_hbm, kv_ref.at[:, :width], sems.at[0]),
        pltpu.make_async_copy(v_hbm, kv_ref.at[:, width:], sems.at[1]),
    ]
    for copy in copies:
        copy.start()
    for copy in copies:
        copy.wait()


def pack_kernel(token_ref, *refs, chips):
    out_ref = refs[chips]
    size = refs[0].shape[0]
    _, key_group, chip, _ = place()
    level = chips // 4
    turn = (chip // level % 2) ^ key_group
    for spot in range(chips // 2):
        flip = spot // level * (2 * level) + spot % level
        for turned in range(2):

            @pl.when(turn == turned)
            def _():
                out_ref[spot * size : (spot + 1) * size, :] = refs[flip ^ turned * level][...]


def prep_kernel(
    seg_hbm, q_hbm, g_hbm, q_ref, g_ref, gt_ref, bias_ref, token_ref, seg_ref, sems, *, dims
):
    heads, rows, width, held, ctx_count = dims
    head_group = place()[0]
    seg_copy = pltpu.make_async_copy(seg_hbm, seg_ref, sems.at[2, 0])
    seg_copy.start()
    copies = []
    for head in range(heads):
        source = head_columns(head_group * heads + head, width)
        target = slice(head * width, (head + 1) * width)
        for k, (full, part) in enumerate(((g_hbm, g_ref), (q_hbm, q_ref))):
            copies.append(
                pltpu.make_async_copy(full.at[:, source], part.at[:, target], sems.at[k, head])
            )
            copies[-1].start()
    token_ref[...] = jnp.zeros_like(token_ref)
    seg_copy.wait()
    for k, block in enumerate(mask_bias(seg_ref, rows, held)):
        bias_ref[k * rows : (k + 1) * rows, :] = block
    for head in range(heads):
        cols = slice(head * width, (head + 1) * width)
        copies[2 * head].wait()
        gt_ref[cols, :] = g_ref[:, cols].astype(jnp.float32).T.astype(jnp.bfloat16)
    for head in range(heads):
        copies[2 * head + 1].wait()


def head_columns(head, width):
    return pl.ds(pl.multiple_of(head * width, width), width)


def score_block(key_value_ref, query, bias, unit):
    width = query.shape[1]
    raw = lax.dot_general(
        key_value_ref[:, :width], query, NT, preferred_element_type=jnp.float32
    )
    return raw * unit + bias


def near_kernel(q_ref, bias_ref, near_ref, scores_ref, top_ref, vt_ref, *, dims):
    heads, rows, width, held, ctx_count = dims
    vt_ref[...] = near_ref[:, width:].astype(jnp.float32).T.astype(jnp.bfloat16)
    for head in range(heads):
        cols = slice(head * width, (head + 1) * width)
        bias = bias_ref[: held // 2, :]
        scores = score_block(near_ref, q_ref[:, cols], bias, width**-0.5 * LOG2E)
        scores_ref[head] = scores
        top_ref[head : head + 1, :] = jnp.max(scores, axis=0, keepdims=True)


def forward_kernel(
    q_ref, gt_ref, bias_ref, near_scores_ref, top_ref, near_vt_ref, far_ref, stats_ref, *refs, dims
):
    heads, rows, width, held, ctx_count = dims
    far_scores_ref, *outs, far_vt_ref = refs
    pair = heads // KEY_GROUPS
    key_group = place()[1]
    far_vt_ref[...] = far_ref[:, width:].astype(jnp.float32).T.astype(jnp.bfloat16)
    for head in range(heads):
        cols = slice(head * width, (head + 1) * width)
        bias = bias_ref[held // 2 :, :]
        scores = score_block(far_ref, q_ref[:, cols], bias, width**-0.5 * LOG2E)
        far_scores_ref[head] = scores
        row = slice(head, head + 1)
        stats_ref[row, :] = jnp.maximum(top_ref[row, :], jnp.max(scores, axis=0, keepdims=True))
    for slot in range(KEY_GROUPS):
        for part in range(pair):
            head = (key_group ^ slot) * pair + part
            top = stats_ref[pl.ds(head, 1), :]
            total, accum = 0.0, 0.0
            for scores_ref, vt_ref in ((near_scores_ref, near_vt_ref), (far_scores_ref, far_vt_ref)):
                expd = jnp.exp2(scores_ref[head] - top)
                total = total + jnp.sum(expd, axis=0, keepdims=True)
                accum = accum + jnp.dot(
                    vt_ref[...], expd.astype(jnp.bfloat16), preferred_element_type=jnp.float32
                )
            grad_t = gt_ref[head_columns(head, width), :].astype(jnp.float32)
            delta = jnp.sum(accum * grad_t, axis=0, keepdims=True)
            outs[slot][part * width : (part + 1) * width, :] = accum.astype(jnp.bfloat16)
            stats_ref[pl.ds(heads + head, 1), :] = total
            stats_ref[pl.ds(2 * heads + head, 1), :] = delta


def dprobs_kernel(g_ref, near_ref, far_ref, dprobs_ref, *, dims):
    heads, rows, width, held, ctx_count = dims
    for head in range(heads):
        grad = g_ref[:, head * width : (head + 1) * width]
        for side, ref in enumerate((near_ref, far_ref)):
            here = slice(side * held // 2, (side + 1) * held // 2)
            dprobs_ref[head, here, :] = lax.dot_general(
                ref[:, width:], grad, NT, preferred_element_type=jnp.float32
            )


def merged_stats(stats, heads):
    top = functools.reduce(jnp.maximum, [s[:heads] for s in stats])
    shares = [jnp.exp2(s[:heads] - top) for s in stats]
    total = sum(f * s[heads : 2 * heads] for f, s in zip(shares, stats))
    delta = sum(f * s[2 * heads :] for f, s in zip(shares, stats)) / total
    return top, shares, total, delta


def backward_kernel(q_ref, g_ref, near_ref, far_ref, *refs, dims, ahead):
    heads, rows, width, held, ctx_count = dims
    scores, refs = refs[:2], refs[2:]
    dprobs_ref, refs = (refs[0], refs[1:]) if ahead else (None, refs)
    stats = refs[:KEY_GROUPS]
    ds_ref, keep_ref, send_ref, acc_ref = refs[KEY_GROUPS:]
    scale = width**-0.5
    top, _, total, delta = merged_stats([s[...] for s in stats], heads)
    lse = top + jnp.log2(total)
    for head in range(heads):
        cols = slice(head * width, (head + 1) * width)
        query, grad = q_ref[:, cols], g_ref[:, cols]
        for side, ref in enumerate((near_ref, far_ref)):
            here = slice(side * held // 2, (side + 1) * held // 2)
            probs = jnp.exp2(scores[side][head] - lse[head : head + 1])
            if ahead:
                dprobs = dprobs_ref[head, here, :]
            else:
                dprobs = lax.dot_general(
                    ref[:, width:], grad, NT, preferred_element_type=jnp.float32
                )
            dscores = (probs * (dprobs - delta[head : head + 1])).astype(jnp.bfloat16)
            ds_ref[head, here, :] = dscores
            dv = jnp.dot(probs.astype(jnp.bfloat16), grad, preferred_element_type=jnp.float32)
            dk = jnp.dot(dscores, query, preferred_element_type=jnp.float32)
            if head == 0:
                acc_ref[here, :width] = dk
                acc_ref[here, width:] = dv
            else:
                acc_ref[here, :width] += dk
                acc_ref[here, width:] += dv
    head_group, key_group, chip, core = place()
    chips, piece = ctx_count // 2, rows // 4
    level = chips // 4
    for spot in range(2 * chips):
        here = slice(spot * piece, (spot + 1) * piece)
        target = chip ^ (spot % chips)
        group = head_group ^ (spot // chips)
        block = group * (ctx_count // 2) + key_group * (ctx_count // 4) + target // 2
        flip = block // 2 ^ chip
        line = ((block % 2 ^ core) * (chips // 2) + flip // (2 * level) * level + flip % level) * rows
        for ref, side in ((keep_ref, core), (send_ref, 1 - core)):
            mine = pl.ds(pl.multiple_of(line + (target % 2 * 2 + side) * piece, piece), piece)
            ref[here, :width] = (acc_ref[mine, :width] * scale).astype(ref.dtype)
            ref[here, width:] = acc_ref[mine, width:].astype(ref.dtype)


def query_kernel(near_ref, far_ref, ds_ref, after_ref, *refs, dims):
    heads, rows, width, held, ctx_count = dims
    outs, kt_ref = refs[:KEY_GROUPS], refs[KEY_GROUPS]
    pair = heads // KEY_GROUPS
    key_group = place()[1]
    scale = width**-0.5
    for side, ref in enumerate((near_ref, far_ref)):
        here = slice(side * held // 2, (side + 1) * held // 2)
        kt_ref[:, here] = ref[:, :width].astype(jnp.float32).T.astype(jnp.bfloat16)
    for slot in range(KEY_GROUPS):
        for part in range(pair):
            head = (key_group ^ slot) * pair + part
            dq = jnp.dot(kt_ref[...], ds_ref[head], preferred_element_type=jnp.float32)
            outs[slot][part * width : (part + 1) * width, :] = (dq * scale).astype(jnp.bfloat16)


def join_kernel(keep_ref, got_ref, *refs, after):
    start = 0
    for out_ref in refs[after:]:
        here = slice(start, start + out_ref.shape[0])
        total = keep_ref[here, :] + got_ref[here, :].astype(jnp.float32)
        out_ref[...] = total.astype(out_ref.dtype)
        start = start + out_ref.shape[0]


def finish_out_kernel(*refs, dims):
    heads, rows, width, held, ctx_count = dims
    stats, outs = refs[:KEY_GROUPS], refs[KEY_GROUPS : 2 * KEY_GROUPS]
    attn_ref, token_ref = refs[2 * KEY_GROUPS :]
    token_ref[...] = jnp.zeros_like(token_ref)
    pair = heads // KEY_GROUPS
    top, shares, total, _ = merged_stats([s[...] for s in stats], heads)
    own = place()[1] * pair
    row = lax.broadcasted_iota(jnp.int32, (heads, 1), 0)
    for part in range(pair):
        here = slice(part * width, (part + 1) * width)

        def pick(array):
            return jnp.sum(jnp.where(row == own + part, array, 0.0), axis=0, keepdims=True)

        joined = sum(o[here, :].astype(jnp.float32) * pick(f) for o, f in zip(outs, shares))
        attn_ref[:, here] = (joined / pick(total)).T.astype(jnp.bfloat16)


def finish_kernel(*refs):
    *sources, gq_ref, gk_ref, gv_ref = refs
    dqs, terms = sources[:KEY_GROUPS], sources[KEY_GROUPS:]
    width = gk_ref.shape[1]
    gq_ref[...] = sum(r[...].astype(jnp.float32) for r in dqs).T.astype(jnp.bfloat16)
    both = sum(r[...].astype(jnp.float32) for r in terms)
    gk_ref[...] = both[:, :width].astype(jnp.bfloat16)
    gv_ref[...] = both[:, width:].astype(jnp.bfloat16)


def on_device(queries, keys, values, out_grad, segment_ids):
    rows = queries.shape[0]
    width = keys.shape[1]
    seq = segment_ids.shape[0]
    dp_count, ctx_count = lax.axis_size("dp"), lax.axis_size("ctx")
    head_groups = dp_count // KEY_GROUPS
    heads = queries.shape[1] // width // head_groups
    pair = heads // KEY_GROUPS
    chips = ctx_count // 2
    held = rows * ctx_count // KEY_GROUPS
    piece = rows // dp_count
    dims = (heads, rows, width, held, ctx_count)
    seg = segment_ids.reshape(seq // 128, 128)
    params = pltpu.CompilerParams(
        vmem_limit_bytes=min(56 * MIB, 12 * MIB + 12 * 4 * held * rows)
    )
    vmem = pl.BlockSpec(memory_space=pltpu.VMEM)
    bf16, f32 = jnp.bfloat16, jnp.float32

    def call(kernel, outs, ins, name, scratch=(), work=0, **static):
        specs = [a[1] if isinstance(a, tuple) else vmem for a in ins]
        arrays = [a[0] if isinstance(a, tuple) else a for a in ins]
        return pl.pallas_call(
            functools.partial(kernel, **static),
            out_shape=[jax.ShapeDtypeStruct(*o) for o in outs],
            in_specs=specs,
            out_specs=[vmem] * len(outs),
            scratch_shapes=list(scratch),
            compiler_params=params,
            cost_estimate=pl.CostEstimate(
                flops=work * 2 * heads * rows * held * width,
                bytes_accessed=sum(math.prod(o[0]) * 2 for o in outs),
                transcendentals=0,
            ),
            name=name,
        )(*arrays)

    def in_hbm(array):
        return pltpu.with_memory_space_constraint(array, pltpu.HBM), pl.BlockSpec(
            memory_space=pltpu.HBM
        )

    def over_dp(array, flip):
        return lax.ppermute(array, "dp", [(d, d ^ flip) for d in range(dp_count)])

    def over_ctx(array, flip):
        return lax.ppermute(array, "ctx", [(c, c ^ flip) for c in range(ctx_count)])

    def to_group(array, flip):
        moves = []
        for d in range(dp_count):
            for c in range(ctx_count):
                chip, core = divmod(c, 2)
                later = chip ^ flip
                if chip // (chips // 4) % 2 == d % KEY_GROUPS and later > chip:
                    moves.append((d * ctx_count + c, d * ctx_count + later * 2 + core))
        return lax.ppermute(array, ("dp", "ctx"), moves)

    (own_kv,) = call(
        load_kernel,
        [((rows, 2 * width), bf16)],
        [in_hbm(keys), in_hbm(values)],
        "load",
        scratch=[pltpu.SemaphoreType.DMA((2,))],
    )
    query_v, grad_v, grad_t, bias, token = call(
        prep_kernel,
        [
            ((rows, heads * width), bf16),
            ((rows, heads * width), bf16),
            ((heads * width, rows), bf16),
            ((held, rows), f32),
            ((8, 128), f32),
        ],
        [in_hbm(seg), in_hbm(queries), in_hbm(out_grad)],
        "prepare",
        scratch=[pltpu.VMEM(seg.shape, seg.dtype), pltpu.SemaphoreType.DMA((3, heads))],
        work=1,
        dims=dims,
    )
    (near,) = call(
        pack_kernel,
        [((held // 2, 2 * width), bf16)],
        [token, own_kv] + [to_group(own_kv, t) for t in range(1, chips)],
        "pack",
        chips=chips,
    )
    far = over_ctx(near, 1)
    near_scores, top, near_vt = call(
        near_kernel,
        [((heads, held // 2, rows), f32), ((heads, rows), f32), ((width, held // 2), bf16)],
        [query_v, bias, near],
        "score_near",
        work=1,
        dims=dims,
    )
    stats, far_scores, *outs = call(
        forward_kernel,
        [((3 * heads, rows), f32), ((heads, held // 2, rows), f32)]
        + [((pair * width, rows), bf16)] * KEY_GROUPS,
        [query_v, grad_t, bias, near_scores, top, near_vt, far],
        "attend",
        scratch=[pltpu.VMEM((width, held // 2), bf16)],
        work=2,
        dims=dims,
    )
    all_stats = [stats, over_dp(stats, 1)]
    all_outs = [outs[0], over_dp(outs[1], 1)]
    ahead = 4 * heads * held * rows <= 8 * MIB
    dprobs = []
    if ahead:
        dprobs = call(
            dprobs_kernel,
            [((heads, held, rows), f32)],
            [grad_v, near, far],
            "dprobs",
            work=1,
            dims=dims,
        )

    dscores, keep, send = call(
        backward_kernel,
        [
            ((heads, held, rows), bf16),
            ((held // 2, 2 * width), f32),
            ((held // 2, 2 * width), bf16),
        ],
        [query_v, grad_v, near, far, near_scores, far_scores] + list(dprobs) + all_stats,
        "differentiate",
        scratch=[pltpu.VMEM((held, 2 * width), f32)],
        work=4,
        dims=dims,
        ahead=ahead,
    )
    got = over_ctx(send, 1)
    dqs = call(
        query_kernel,
        [((pair * width, rows), bf16)] * KEY_GROUPS,
        [near, far, dscores, all_outs[1]],
        "query_terms",
        scratch=[pltpu.VMEM((width, held), bf16)],
        work=1,
        dims=dims,
    )
    all_dqs = [dqs[0], over_dp(dqs[1], 1)]
    attn_out, token = call(
        finish_out_kernel,
        [((rows, pair * width), bf16), ((8, 128), f32)],
        all_stats + all_outs,
        "finish_out",
        dims=dims,
    )
    quarter = held // 4
    keep, send = call(
        join_kernel,
        [((quarter, 2 * width), f32), ((quarter, 2 * width), bf16)],
        [keep, got],
        "join_cores",
        after=0,
    )
    pieces = call(
        join_kernel,
        [((piece, 2 * width), bf16)] * chips,
        [keep, over_dp(send, 2), token],
        "join_heads",
        after=1,
    )
    grad_kv = [pieces[0]] + [over_ctx(pieces[t], 2 * t) for t in range(1, chips)]

    grad_q, grad_k, grad_values = call(
        finish_kernel,
        [((rows, pair * width), bf16)] + [((piece, width), bf16)] * 2,
        all_dqs + grad_kv,
        "finish",
    )
    return attn_out, grad_q, grad_k, grad_values


def solution(mesh):
    return jax.shard_map(
        on_device,
        mesh=mesh,
        in_specs=(P("ctx", None), P("ctx", None), P("ctx", None), P("ctx", None), P()),
        out_specs=(P("ctx", "dp"), P("ctx", "dp"), P(("dp", "ctx"), None), P(("dp", "ctx"), None)),
        check_vma=False,
    )
```

```python
import functools
import math

import jax
import jax.numpy as jnp
from jax import lax
from jax.experimental import pallas as pl
from jax.experimental.pallas import tpu as pltpu
from jax.sharding import PartitionSpec as P

NEG = -1e30
LOG2E = 1.4426950408889634
DOC_NUMBERS = 4
KEY_GROUPS = 2
MIB = 1024 * 1024


def place():
    dp_index, ctx_index = lax.axis_index("dp"), lax.axis_index("ctx")
    return dp_index // KEY_GROUPS, dp_index % KEY_GROUPS, ctx_index // 2, ctx_index % 2

NT = (((1,), (1,)), ((), ()))


def home_chip(spot, key_group, chip, chips):
    level = chips // 4
    flip = spot // level * (2 * level) + spot % level
    home = chip ^ flip
    return home ^ ((home // level % 2) ^ key_group) * level


def mask_bias(seg_ref, rows, held):
    _, key_group, chip, core = place()
    seg = seg_ref[...]
    lines = rows // 128
    seg_own = seg_ref[pl.ds((chip * 2 + core) * lines, lines), :]
    start = jnp.zeros((lines, 128), jnp.int32)
    for number in range(1, DOC_NUMBERS):
        before = jnp.sum((seg < number).astype(jnp.float32), axis=(0, 1), keepdims=True)
        start = jnp.where(seg_own == number, before.astype(jnp.int32), start)
    start = jnp.concatenate([start[k : k + 1] for k in range(lines)], axis=1)
    query_pos = (chip * 2 + core) * rows + lax.broadcasted_iota(jnp.int32, (1, rows), 1)
    blocks = held // rows
    bias = []
    for block in range(blocks):
        spot, side = block % (blocks // 2), block // (blocks // 2)
        home = home_chip(spot, key_group, chip, blocks) * 2 + (core ^ side)
        key_pos = home * rows + lax.broadcasted_iota(jnp.int32, (rows, rows), 0)
        allowed = (key_pos >= start) & (key_pos <= query_pos)
        bias.append(jnp.where(allowed, 0.0, NEG))
    return bias


def load_kernel(k_hbm, v_hbm, kv_ref, sems):
    width = k_hbm.shape[1]
    copies = [
        pltpu.make_async_copy(k_hbm, kv_ref.at[:, :width], sems.at[0]),
        pltpu.make_async_copy(v_hbm, kv_ref.at[:, width:], sems.at[1]),
    ]
    for copy in copies:
        copy.start()
    for copy in copies:
        copy.wait()


def pack_kernel(token_ref, *refs, flips):
    out_ref, chips = refs[-1], len(flips) + 1
    refs = [refs[0]] + [refs[1 + flips.index(t)] for t in range(1, chips)]
    size = refs[0].shape[0]
    _, key_group, chip, _ = place()
    level = chips // 4
    turn = (chip // level % 2) ^ key_group
    for spot in range(chips // 2):
        flip = spot // level * (2 * level) + spot % level
        for turned in range(2):

            @pl.when(turn == turned)
            def _():
                out_ref[spot * size : (spot + 1) * size, :] = refs[flip ^ turned * level][...]


def prep_kernel(
    seg_hbm, q_hbm, g_hbm, q_ref, g_ref, gt_ref, bias_ref, token_ref, seg_ref, sems, *, dims
):
    heads, rows, width, held, ctx_count = dims
    head_group = place()[0]
    seg_copy = pltpu.make_async_copy(seg_hbm, seg_ref, sems.at[2, 0])
    seg_copy.start()
    copies = []
    for head in range(heads):
        source = head_columns(head_group * heads + head, width)
        target = slice(head * width, (head + 1) * width)
        for k, (full, part) in enumerate(((g_hbm, g_ref), (q_hbm, q_ref))):
            copies.append(
                pltpu.make_async_copy(full.at[:, source], part.at[:, target], sems.at[k, head])
            )
            copies[-1].start()
    token_ref[...] = jnp.zeros_like(token_ref)
    seg_copy.wait()
    for k, block in enumerate(mask_bias(seg_ref, rows, held)):
        bias_ref[k * rows : (k + 1) * rows, :] = block
    for head in range(heads):
        cols = slice(head * width, (head + 1) * width)
        copies[2 * head].wait()
        gt_ref[cols, :] = g_ref[:, cols].astype(jnp.float32).T.astype(jnp.bfloat16)
    for head in range(heads):
        copies[2 * head + 1].wait()


def head_columns(head, width):
    return pl.ds(pl.multiple_of(head * width, width), width)


def score_block(key_value_ref, query, bias, unit):
    width = query.shape[1]
    raw = lax.dot_general(
        key_value_ref[:, :width], query, NT, preferred_element_type=jnp.float32
    )
    return raw * unit + bias


def near_kernel(q_ref, bias_ref, near_ref, scores_ref, top_ref, vt_ref, *, dims):
    heads, rows, width, held, ctx_count = dims
    vt_ref[...] = near_ref[:, width:].astype(jnp.float32).T.astype(jnp.bfloat16)
    for head in range(heads):
        cols = slice(head * width, (head + 1) * width)
        bias = bias_ref[: held // 2, :]
        scores = score_block(near_ref, q_ref[:, cols], bias, width**-0.5 * LOG2E)
        scores_ref[head] = scores
        top_ref[head : head + 1, :] = jnp.max(scores, axis=0, keepdims=True)


def forward_kernel(
    q_ref, gt_ref, bias_ref, near_scores_ref, top_ref, near_vt_ref, far_ref, stats_ref, *refs, dims
):
    heads, rows, width, held, ctx_count = dims
    far_scores_ref, *outs, far_vt_ref = refs
    pair = heads // KEY_GROUPS
    key_group = place()[1]
    far_vt_ref[...] = far_ref[:, width:].astype(jnp.float32).T.astype(jnp.bfloat16)
    for head in range(heads):
        cols = slice(head * width, (head + 1) * width)
        bias = bias_ref[held // 2 :, :]
        scores = score_block(far_ref, q_ref[:, cols], bias, width**-0.5 * LOG2E)
        far_scores_ref[head] = scores
        row = slice(head, head + 1)
        stats_ref[row, :] = jnp.maximum(top_ref[row, :], jnp.max(scores, axis=0, keepdims=True))
    for slot in range(KEY_GROUPS):
        for part in range(pair):
            head = (key_group ^ slot) * pair + part
            top = stats_ref[pl.ds(head, 1), :]
            total, accum = 0.0, 0.0
            for scores_ref, vt_ref in ((near_scores_ref, near_vt_ref), (far_scores_ref, far_vt_ref)):
                expd = jnp.exp2(scores_ref[head] - top)
                total = total + jnp.sum(expd, axis=0, keepdims=True)
                accum = accum + jnp.dot(
                    vt_ref[...], expd.astype(jnp.bfloat16), preferred_element_type=jnp.float32
                )
            grad_t = gt_ref[head_columns(head, width), :].astype(jnp.float32)
            delta = jnp.sum(accum * grad_t, axis=0, keepdims=True)
            outs[slot][part * width : (part + 1) * width, :] = accum.astype(jnp.bfloat16)
            stats_ref[pl.ds(heads + head, 1), :] = total
            stats_ref[pl.ds(2 * heads + head, 1), :] = delta


def dprobs_kernel(g_ref, near_ref, far_ref, dprobs_ref, *, dims):
    heads, rows, width, held, ctx_count = dims
    for head in range(heads):
        grad = g_ref[:, head * width : (head + 1) * width]
        for side, ref in enumerate((near_ref, far_ref)):
            here = slice(side * held // 2, (side + 1) * held // 2)
            dprobs_ref[head, here, :] = lax.dot_general(
                ref[:, width:], grad, NT, preferred_element_type=jnp.float32
            )


def merged_stats(stats, heads):
    top = functools.reduce(jnp.maximum, [s[:heads] for s in stats])
    shares = [jnp.exp2(s[:heads] - top) for s in stats]
    total = sum(f * s[heads : 2 * heads] for f, s in zip(shares, stats))
    delta = sum(f * s[2 * heads :] for f, s in zip(shares, stats)) / total
    return top, shares, total, delta


def backward_kernel(q_ref, g_ref, near_ref, far_ref, *refs, dims, ahead):
    heads, rows, width, held, ctx_count = dims
    scores, refs = refs[:2], refs[2:]
    dprobs_ref, refs = (refs[0], refs[1:]) if ahead else (None, refs)
    stats = refs[:KEY_GROUPS]
    ds_ref, keep_ref, send_ref, acc_ref = refs[KEY_GROUPS:]
    scale = width**-0.5
    top, _, total, delta = merged_stats([s[...] for s in stats], heads)
    lse = top + jnp.log2(total)
    for head in range(heads):
        cols = slice(head * width, (head + 1) * width)
        query, grad = q_ref[:, cols], g_ref[:, cols]
        for side, ref in enumerate((near_ref, far_ref)):
            here = slice(side * held // 2, (side + 1) * held // 2)
            probs = jnp.exp2(scores[side][head] - lse[head : head + 1])
            if ahead:
                dprobs = dprobs_ref[head, here, :]
            else:
                dprobs = lax.dot_general(
                    ref[:, width:], grad, NT, preferred_element_type=jnp.float32
                )
            dscores = (probs * (dprobs - delta[head : head + 1])).astype(jnp.bfloat16)
            ds_ref[head, here, :] = dscores
            dv = jnp.dot(probs.astype(jnp.bfloat16), grad, preferred_element_type=jnp.float32)
            dk = jnp.dot(dscores, query, preferred_element_type=jnp.float32)
            if head == 0:
                acc_ref[here, :width] = dk
                acc_ref[here, width:] = dv
            else:
                acc_ref[here, :width] += dk
                acc_ref[here, width:] += dv
    head_group, key_group, chip, core = place()
    chips, piece = ctx_count // 2, rows // 4
    level = chips // 4
    for spot in range(2 * chips):
        here = slice(spot * piece, (spot + 1) * piece)
        target = chip ^ (spot % chips)
        group = head_group ^ (spot // chips)
        block = group * (ctx_count // 2) + key_group * (ctx_count // 4) + target // 2
        flip = block // 2 ^ chip
        line = ((block % 2 ^ core) * (chips // 2) + flip // (2 * level) * level + flip % level) * rows
        for ref, side in ((keep_ref, core), (send_ref, 1 - core)):
            mine = pl.ds(pl.multiple_of(line + (target % 2 * 2 + side) * piece, piece), piece)
            ref[here, :width] = (acc_ref[mine, :width] * scale).astype(ref.dtype)
            ref[here, width:] = acc_ref[mine, width:].astype(ref.dtype)


def query_kernel(near_ref, far_ref, ds_ref, after_ref, *refs, dims):
    heads, rows, width, held, ctx_count = dims
    outs, kt_ref = refs[:KEY_GROUPS], refs[KEY_GROUPS]
    pair = heads // KEY_GROUPS
    key_group = place()[1]
    scale = width**-0.5
    for side, ref in enumerate((near_ref, far_ref)):
        here = slice(side * held // 2, (side + 1) * held // 2)
        kt_ref[:, here] = ref[:, :width].astype(jnp.float32).T.astype(jnp.bfloat16)
    for slot in range(KEY_GROUPS):
        for part in range(pair):
            head = (key_group ^ slot) * pair + part
            dq = jnp.dot(kt_ref[...], ds_ref[head], preferred_element_type=jnp.float32)
            outs[slot][part * width : (part + 1) * width, :] = (dq * scale).astype(jnp.bfloat16)


def join_kernel(keep_ref, got_ref, *refs, after):
    start = 0
    for out_ref in refs[after:]:
        here = slice(start, start + out_ref.shape[0])
        total = keep_ref[here, :] + got_ref[here, :].astype(jnp.float32)
        out_ref[...] = total.astype(out_ref.dtype)
        start = start + out_ref.shape[0]


def finish_out_kernel(*refs, dims):
    heads, rows, width, held, ctx_count = dims
    stats, outs = refs[:KEY_GROUPS], refs[KEY_GROUPS : 2 * KEY_GROUPS]
    attn_ref, token_ref = refs[2 * KEY_GROUPS :]
    token_ref[...] = jnp.zeros_like(token_ref)
    pair = heads // KEY_GROUPS
    top, shares, total, _ = merged_stats([s[...] for s in stats], heads)
    own = place()[1] * pair
    row = lax.broadcasted_iota(jnp.int32, (heads, 1), 0)
    for part in range(pair):
        here = slice(part * width, (part + 1) * width)

        def pick(array):
            return jnp.sum(jnp.where(row == own + part, array, 0.0), axis=0, keepdims=True)

        joined = sum(o[here, :].astype(jnp.float32) * pick(f) for o, f in zip(outs, shares))
        attn_ref[:, here] = (joined / pick(total)).T.astype(jnp.bfloat16)


def finish_kernel(*refs):
    *sources, gq_ref, gk_ref, gv_ref = refs
    dqs, terms = sources[:KEY_GROUPS], sources[KEY_GROUPS:]
    width = gk_ref.shape[1]
    gq_ref[...] = sum(r[...].astype(jnp.float32) for r in dqs).T.astype(jnp.bfloat16)
    both = sum(r[...].astype(jnp.float32) for r in terms)
    gk_ref[...] = both[:, :width].astype(jnp.bfloat16)
    gv_ref[...] = both[:, width:].astype(jnp.bfloat16)


def on_device(queries, keys, values, out_grad, segment_ids):
    rows = queries.shape[0]
    width = keys.shape[1]
    seq = segment_ids.shape[0]
    dp_count, ctx_count = lax.axis_size("dp"), lax.axis_size("ctx")
    head_groups = dp_count // KEY_GROUPS
    heads = queries.shape[1] // width // head_groups
    pair = heads // KEY_GROUPS
    chips = ctx_count // 2
    held = rows * ctx_count // KEY_GROUPS
    piece = rows // dp_count
    dims = (heads, rows, width, held, ctx_count)
    seg = segment_ids.reshape(seq // 128, 128)
    params = pltpu.CompilerParams(
        vmem_limit_bytes=min(56 * MIB, 12 * MIB + 12 * 4 * held * rows)
    )
    vmem = pl.BlockSpec(memory_space=pltpu.VMEM)
    bf16, f32 = jnp.bfloat16, jnp.float32

    def call(kernel, outs, ins, name, scratch=(), work=0, **static):
        specs = [a[1] if isinstance(a, tuple) else vmem for a in ins]
        arrays = [a[0] if isinstance(a, tuple) else a for a in ins]
        return pl.pallas_call(
            functools.partial(kernel, **static),
            out_shape=[jax.ShapeDtypeStruct(*o) for o in outs],
            in_specs=specs,
            out_specs=[vmem] * len(outs),
            scratch_shapes=list(scratch),
            compiler_params=params,
            cost_estimate=pl.CostEstimate(
                flops=work * 2 * heads * rows * held * width,
                bytes_accessed=sum(math.prod(o[0]) * 2 for o in outs),
                transcendentals=0,
            ),
            name=name,
        )(*arrays)

    def in_hbm(array):
        return pltpu.with_memory_space_constraint(array, pltpu.HBM), pl.BlockSpec(
            memory_space=pltpu.HBM
        )

    def over_dp(array, flip):
        return lax.ppermute(array, "dp", [(d, d ^ flip) for d in range(dp_count)])

    def over_ctx(array, flip):
        return lax.ppermute(array, "ctx", [(c, c ^ flip) for c in range(ctx_count)])

    def to_group(array, flip):
        moves = []
        for d in range(dp_count):
            for c in range(ctx_count):
                chip, core = divmod(c, 2)
                later = chip ^ flip
                if chip // (chips // 4) % 2 == d % KEY_GROUPS and later > chip:
                    moves.append((d * ctx_count + c, d * ctx_count + later * 2 + core))
        return lax.ppermute(array, ("dp", "ctx"), moves)

    (own_kv,) = call(
        load_kernel,
        [((rows, 2 * width), bf16)],
        [in_hbm(keys), in_hbm(values)],
        "load",
        scratch=[pltpu.SemaphoreType.DMA((2,))],
    )
    query_v, grad_v, grad_t, bias, token = call(
        prep_kernel,
        [
            ((rows, heads * width), bf16),
            ((rows, heads * width), bf16),
            ((heads * width, rows), bf16),
            ((held, rows), f32),
            ((8, 128), f32),
        ],
        [in_hbm(seg), in_hbm(queries), in_hbm(out_grad)],
        "prepare",
        scratch=[pltpu.VMEM(seg.shape, seg.dtype), pltpu.SemaphoreType.DMA((3, heads))],
        work=1,
        dims=dims,
    )
    flips = sorted(range(1, chips), key=lambda t: (t % (chips // 2) != 0, t))[::-1]
    (near,) = call(
        pack_kernel,
        [((held // 2, 2 * width), bf16)],
        [token, own_kv] + [to_group(own_kv, t) for t in flips],
        "pack",
        flips=flips,
    )
    far = over_ctx(near, 1)
    near_scores, top, near_vt = call(
        near_kernel,
        [((heads, held // 2, rows), f32), ((heads, rows), f32), ((width, held // 2), bf16)],
        [query_v, bias, near],
        "score_near",
        work=1,
        dims=dims,
    )
    stats, far_scores, *outs = call(
        forward_kernel,
        [((3 * heads, rows), f32), ((heads, held // 2, rows), f32)]
        + [((pair * width, rows), bf16)] * KEY_GROUPS,
        [query_v, grad_t, bias, near_scores, top, near_vt, far],
        "attend",
        scratch=[pltpu.VMEM((width, held // 2), bf16)],
        work=2,
        dims=dims,
    )
    all_stats = [stats, over_dp(stats, 1)]
    all_outs = [outs[0], over_dp(outs[1], 1)]
    ahead = 4 * heads * held * rows <= 8 * MIB
    dprobs = []
    if ahead:
        dprobs = call(
            dprobs_kernel,
            [((heads, held, rows), f32)],
            [grad_v, near, far],
            "dprobs",
            work=1,
            dims=dims,
        )

    dscores, keep, send = call(
        backward_kernel,
        [
            ((heads, held, rows), bf16),
            ((held // 2, 2 * width), f32),
            ((held // 2, 2 * width), bf16),
        ],
        [query_v, grad_v, near, far, near_scores, far_scores] + list(dprobs) + all_stats,
        "differentiate",
        scratch=[pltpu.VMEM((held, 2 * width), f32)],
        work=4,
        dims=dims,
        ahead=ahead,
    )
    got = over_ctx(send, 1)
    attn_out, token = call(
        finish_out_kernel,
        [((rows, pair * width), bf16), ((8, 128), f32)],
        all_stats + all_outs,
        "finish_out",
        dims=dims,
    )
    quarter = held // 4
    keep, send = call(
        join_kernel,
        [((quarter, 2 * width), f32), ((quarter, 2 * width), bf16)],
        [keep, got],
        "join_cores",
        after=0,
    )
    dqs = call(
        query_kernel,
        [((pair * width, rows), bf16)] * KEY_GROUPS,
        [near, far, dscores, keep],
        "query_terms",
        scratch=[pltpu.VMEM((width, held), bf16)],
        work=1,
        dims=dims,
    )
    all_dqs = [dqs[0], over_dp(dqs[1], 1)]
    pieces = call(
        join_kernel,
        [((piece, 2 * width), bf16)] * chips,
        [keep, over_dp(send, 2), token],
        "join_heads",
        after=1,
    )
    grad_kv = [pieces[0]] + [over_ctx(pieces[t], 2 * t) for t in range(1, chips)]

    grad_q, grad_k, grad_values = call(
        finish_kernel,
        [((rows, pair * width), bf16)] + [((piece, width), bf16)] * 2,
        all_dqs + grad_kv,
        "finish",
    )
    return attn_out, grad_q, grad_k, grad_values


def solution(mesh):
    return jax.shard_map(
        on_device,
        mesh=mesh,
        in_specs=(P("ctx", None), P("ctx", None), P("ctx", None), P("ctx", None), P()),
        out_specs=(P("ctx", "dp"), P("ctx", "dp"), P(("dp", "ctx"), None), P(("dp", "ctx"), None)),
        check_vma=False,
    )
```

```python
import functools
import math

import jax
import jax.numpy as jnp
from jax import lax
from jax.experimental import pallas as pl
from jax.experimental.pallas import tpu as pltpu
from jax.sharding import PartitionSpec as P

NEG = -1e30
LOG2E = 1.4426950408889634
DOC_NUMBERS = 4
KEY_GROUPS = 2
MIB = 1024 * 1024


def place():
    dp_index, ctx_index = lax.axis_index("dp"), lax.axis_index("ctx")
    return dp_index // KEY_GROUPS, dp_index % KEY_GROUPS, ctx_index // 2, ctx_index % 2

NT = (((1,), (1,)), ((), ()))


def home_chip(spot, key_group, chip, chips):
    level = chips // 4
    flip = spot // level * (2 * level) + spot % level
    home = chip ^ flip
    return home ^ ((home // level % 2) ^ key_group) * level


def mask_bias(seg_ref, rows, held):
    _, key_group, chip, core = place()
    seg = seg_ref[...]
    lines = rows // 128
    seg_own = seg_ref[pl.ds((chip * 2 + core) * lines, lines), :]
    start = jnp.zeros((lines, 128), jnp.int32)
    for number in range(1, DOC_NUMBERS):
        before = jnp.sum((seg < number).astype(jnp.float32), axis=(0, 1), keepdims=True)
        start = jnp.where(seg_own == number, before.astype(jnp.int32), start)
    start = jnp.concatenate([start[k : k + 1] for k in range(lines)], axis=1)
    query_pos = (chip * 2 + core) * rows + lax.broadcasted_iota(jnp.int32, (1, rows), 1)
    blocks = held // rows
    bias = []
    for block in range(blocks):
        spot, side = block % (blocks // 2), block // (blocks // 2)
        home = home_chip(spot, key_group, chip, blocks) * 2 + (core ^ side)
        key_pos = home * rows + lax.broadcasted_iota(jnp.int32, (rows, rows), 0)
        allowed = (key_pos >= start) & (key_pos <= query_pos)
        bias.append(jnp.where(allowed, 0.0, NEG))
    return bias


def load_kernel(k_hbm, v_hbm, kv_ref, sems):
    width = k_hbm.shape[1]
    copies = [
        pltpu.make_async_copy(k_hbm, kv_ref.at[:, :width], sems.at[0]),
        pltpu.make_async_copy(v_hbm, kv_ref.at[:, width:], sems.at[1]),
    ]
    for copy in copies:
        copy.start()
    for copy in copies:
        copy.wait()


def pack_kernel(token_ref, *refs, flips):
    out_ref, chips = refs[-1], len(flips) + 1
    refs = [refs[0]] + [refs[1 + flips.index(t)] for t in range(1, chips)]
    size = refs[0].shape[0]
    _, key_group, chip, _ = place()
    level = chips // 4
    turn = (chip // level % 2) ^ key_group
    for spot in range(chips // 2):
        flip = spot // level * (2 * level) + spot % level
        for turned in range(2):

            @pl.when(turn == turned)
            def _():
                out_ref[spot * size : (spot + 1) * size, :] = refs[flip ^ turned * level][...]


def prep_kernel(
    seg_hbm, q_hbm, g_hbm, q_ref, g_ref, gt_ref, bias_ref, token_ref, seg_ref, sems, *, dims
):
    heads, rows, width, held, ctx_count = dims
    head_group = place()[0]
    seg_copy = pltpu.make_async_copy(seg_hbm, seg_ref, sems.at[2, 0])
    seg_copy.start()
    copies = []
    for head in range(heads):
        source = head_columns(head_group * heads + head, width)
        target = slice(head * width, (head + 1) * width)
        for k, (full, part) in enumerate(((g_hbm, g_ref), (q_hbm, q_ref))):
            copies.append(
                pltpu.make_async_copy(full.at[:, source], part.at[:, target], sems.at[k, head])
            )
            copies[-1].start()
    token_ref[...] = jnp.zeros_like(token_ref)
    seg_copy.wait()
    for k, block in enumerate(mask_bias(seg_ref, rows, held)):
        bias_ref[k * rows : (k + 1) * rows, :] = block
    for head in range(heads):
        cols = slice(head * width, (head + 1) * width)
        copies[2 * head].wait()
        gt_ref[cols, :] = g_ref[:, cols].astype(jnp.float32).T.astype(jnp.bfloat16)
    for head in range(heads):
        copies[2 * head + 1].wait()


def head_columns(head, width):
    return pl.ds(pl.multiple_of(head * width, width), width)


def score_block(key_value_ref, query, bias, unit):
    width = query.shape[1]
    raw = lax.dot_general(
        key_value_ref[:, :width], query, NT, preferred_element_type=jnp.float32
    )
    return raw * unit + bias


def near_kernel(q_ref, bias_ref, near_ref, scores_ref, top_ref, vt_ref, *, dims):
    heads, rows, width, held, ctx_count = dims
    vt_ref[...] = near_ref[:, width:].astype(jnp.float32).T.astype(jnp.bfloat16)
    for head in range(heads):
        cols = slice(head * width, (head + 1) * width)
        bias = bias_ref[: held // 2, :]
        scores = score_block(near_ref, q_ref[:, cols], bias, width**-0.5 * LOG2E)
        scores_ref[head] = scores
        top_ref[head : head + 1, :] = jnp.max(scores, axis=0, keepdims=True)


def forward_kernel(
    q_ref, gt_ref, bias_ref, near_scores_ref, top_ref, near_vt_ref, far_ref, stats_ref, *refs, dims
):
    heads, rows, width, held, ctx_count = dims
    far_scores_ref, *outs, far_vt_ref = refs
    pair = heads // KEY_GROUPS
    key_group = place()[1]
    far_vt_ref[...] = far_ref[:, width:].astype(jnp.float32).T.astype(jnp.bfloat16)
    for head in range(heads):
        cols = slice(head * width, (head + 1) * width)
        bias = bias_ref[held // 2 :, :]
        scores = score_block(far_ref, q_ref[:, cols], bias, width**-0.5 * LOG2E)
        far_scores_ref[head] = scores
        row = slice(head, head + 1)
        stats_ref[row, :] = jnp.maximum(top_ref[row, :], jnp.max(scores, axis=0, keepdims=True))
    for slot in range(KEY_GROUPS):
        for part in range(pair):
            head = (key_group ^ slot) * pair + part
            top = stats_ref[pl.ds(head, 1), :]
            total, accum = 0.0, 0.0
            for scores_ref, vt_ref in ((near_scores_ref, near_vt_ref), (far_scores_ref, far_vt_ref)):
                expd = jnp.exp2(scores_ref[head] - top)
                total = total + jnp.sum(expd, axis=0, keepdims=True)
                accum = accum + jnp.dot(
                    vt_ref[...], expd.astype(jnp.bfloat16), preferred_element_type=jnp.float32
                )
            grad_t = gt_ref[head_columns(head, width), :].astype(jnp.float32)
            delta = jnp.sum(accum * grad_t, axis=0, keepdims=True)
            outs[slot][part * width : (part + 1) * width, :] = accum.astype(jnp.bfloat16)
            stats_ref[pl.ds(heads + head, 1), :] = total
            stats_ref[pl.ds(2 * heads + head, 1), :] = delta


def dprobs_kernel(g_ref, near_ref, far_ref, dprobs_ref, *, dims):
    heads, rows, width, held, ctx_count = dims
    for head in range(heads):
        grad = g_ref[:, head * width : (head + 1) * width]
        for side, ref in enumerate((near_ref, far_ref)):
            here = slice(side * held // 2, (side + 1) * held // 2)
            dprobs_ref[head, here, :] = lax.dot_general(
                ref[:, width:], grad, NT, preferred_element_type=jnp.float32
            )


def merged_stats(stats, heads):
    top = functools.reduce(jnp.maximum, [s[:heads] for s in stats])
    shares = [jnp.exp2(s[:heads] - top) for s in stats]
    total = sum(f * s[heads : 2 * heads] for f, s in zip(shares, stats))
    delta = sum(f * s[2 * heads :] for f, s in zip(shares, stats)) / total
    return top, shares, total, delta


def backward_kernel(q_ref, g_ref, near_ref, far_ref, *refs, dims, ahead):
    heads, rows, width, held, ctx_count = dims
    scores, refs = refs[:2], refs[2:]
    dprobs_ref, refs = (refs[0], refs[1:]) if ahead else (None, refs)
    stats = refs[:KEY_GROUPS]
    ds_ref, keep_ref, send_ref, acc_ref = refs[KEY_GROUPS:]
    scale = width**-0.5
    top, _, total, delta = merged_stats([s[...] for s in stats], heads)
    lse = top + jnp.log2(total)
    for head in range(heads):
        cols = slice(head * width, (head + 1) * width)
        query, grad = q_ref[:, cols], g_ref[:, cols]
        for side, ref in enumerate((near_ref, far_ref)):
            here = slice(side * held // 2, (side + 1) * held // 2)
            probs = jnp.exp2(scores[side][head] - lse[head : head + 1])
            if ahead:
                dprobs = dprobs_ref[head, here, :]
            else:
                dprobs = lax.dot_general(
                    ref[:, width:], grad, NT, preferred_element_type=jnp.float32
                )
            dscores = (probs * (dprobs - delta[head : head + 1])).astype(jnp.bfloat16)
            ds_ref[head, here, :] = dscores
            dv = jnp.dot(probs.astype(jnp.bfloat16), grad, preferred_element_type=jnp.float32)
            dk = jnp.dot(dscores, query, preferred_element_type=jnp.float32)
            if head == 0:
                acc_ref[here, :width] = dk
                acc_ref[here, width:] = dv
            else:
                acc_ref[here, :width] += dk
                acc_ref[here, width:] += dv
    head_group, key_group, chip, core = place()
    chips, piece = ctx_count // 2, rows // 4
    level = chips // 4
    for spot in range(2 * chips):
        here = slice(spot * piece, (spot + 1) * piece)
        target = chip ^ (spot % chips)
        group = head_group ^ (spot // chips)
        block = group * (ctx_count // 2) + key_group * (ctx_count // 4) + target // 2
        flip = block // 2 ^ chip
        line = ((block % 2 ^ core) * (chips // 2) + flip // (2 * level) * level + flip % level) * rows
        for ref, side in ((keep_ref, core), (send_ref, 1 - core)):
            mine = pl.ds(pl.multiple_of(line + (target % 2 * 2 + side) * piece, piece), piece)
            ref[here, :width] = (acc_ref[mine, :width] * scale).astype(ref.dtype)
            ref[here, width:] = acc_ref[mine, width:].astype(ref.dtype)


def query_kernel(near_ref, far_ref, ds_ref, after_ref, *refs, dims):
    heads, rows, width, held, ctx_count = dims
    outs, kt_ref = refs[:KEY_GROUPS], refs[KEY_GROUPS]
    pair = heads // KEY_GROUPS
    key_group = place()[1]
    scale = width**-0.5
    for side, ref in enumerate((near_ref, far_ref)):
        here = slice(side * held // 2, (side + 1) * held // 2)
        kt_ref[:, here] = ref[:, :width].astype(jnp.float32).T.astype(jnp.bfloat16)
    for slot in range(KEY_GROUPS):
        for part in range(pair):
            head = (key_group ^ slot) * pair + part
            dq = jnp.dot(kt_ref[...], ds_ref[head], preferred_element_type=jnp.float32)
            outs[slot][part * width : (part + 1) * width, :] = (dq * scale).astype(jnp.bfloat16)


def join_kernel(keep_ref, got_ref, *refs, after):
    start = 0
    for out_ref in refs[after:]:
        here = slice(start, start + out_ref.shape[0])
        total = keep_ref[here, :] + got_ref[here, :].astype(jnp.float32)
        out_ref[...] = total.astype(out_ref.dtype)
        start = start + out_ref.shape[0]


def finish_out_kernel(*refs, dims):
    heads, rows, width, held, ctx_count = dims
    stats, outs = refs[:KEY_GROUPS], refs[KEY_GROUPS : 2 * KEY_GROUPS]
    attn_ref, token_ref = refs[2 * KEY_GROUPS :]
    token_ref[...] = jnp.zeros_like(token_ref)
    pair = heads // KEY_GROUPS
    top, shares, total, _ = merged_stats([s[...] for s in stats], heads)
    own = place()[1] * pair
    row = lax.broadcasted_iota(jnp.int32, (heads, 1), 0)
    for part in range(pair):
        here = slice(part * width, (part + 1) * width)

        def pick(array):
            return jnp.sum(jnp.where(row == own + part, array, 0.0), axis=0, keepdims=True)

        joined = sum(o[here, :].astype(jnp.float32) * pick(f) for o, f in zip(outs, shares))
        attn_ref[:, here] = (joined / pick(total)).T.astype(jnp.bfloat16)


def finish_kernel(*refs):
    *sources, gq_ref, gk_ref, gv_ref = refs
    dqs, terms = sources[:KEY_GROUPS], sources[KEY_GROUPS:]
    width = gk_ref.shape[1]
    gq_ref[...] = sum(r[...].astype(jnp.float32) for r in dqs).T.astype(jnp.bfloat16)
    both = sum(r[...].astype(jnp.float32) for r in terms)
    gk_ref[...] = both[:, :width].astype(jnp.bfloat16)
    gv_ref[...] = both[:, width:].astype(jnp.bfloat16)


def on_device(queries, keys, values, out_grad, segment_ids):
    rows = queries.shape[0]
    width = keys.shape[1]
    seq = segment_ids.shape[0]
    dp_count, ctx_count = lax.axis_size("dp"), lax.axis_size("ctx")
    head_groups = dp_count // KEY_GROUPS
    heads = queries.shape[1] // width // head_groups
    pair = heads // KEY_GROUPS
    chips = ctx_count // 2
    held = rows * ctx_count // KEY_GROUPS
    piece = rows // dp_count
    dims = (heads, rows, width, held, ctx_count)
    seg = segment_ids.reshape(seq // 128, 128)
    params = pltpu.CompilerParams(
        vmem_limit_bytes=min(56 * MIB, 12 * MIB + 12 * 4 * held * rows)
    )
    vmem = pl.BlockSpec(memory_space=pltpu.VMEM)
    bf16, f32 = jnp.bfloat16, jnp.float32

    def call(kernel, outs, ins, name, scratch=(), work=0, **static):
        specs = [a[1] if isinstance(a, tuple) else vmem for a in ins]
        arrays = [a[0] if isinstance(a, tuple) else a for a in ins]
        return pl.pallas_call(
            functools.partial(kernel, **static),
            out_shape=[jax.ShapeDtypeStruct(*o) for o in outs],
            in_specs=specs,
            out_specs=[vmem] * len(outs),
            scratch_shapes=list(scratch),
            compiler_params=params,
            cost_estimate=pl.CostEstimate(
                flops=work * 2 * heads * rows * held * width,
                bytes_accessed=sum(math.prod(o[0]) * 2 for o in outs),
                transcendentals=0,
            ),
            name=name,
        )(*arrays)

    def in_hbm(array):
        return pltpu.with_memory_space_constraint(array, pltpu.HBM), pl.BlockSpec(
            memory_space=pltpu.HBM
        )

    def over_dp(array, flip):
        return lax.ppermute(array, "dp", [(d, d ^ flip) for d in range(dp_count)])

    def over_ctx(array, flip):
        return lax.ppermute(array, "ctx", [(c, c ^ flip) for c in range(ctx_count)])

    def to_group(array, flip):
        moves = []
        for d in range(dp_count):
            for c in range(ctx_count):
                chip, core = divmod(c, 2)
                later = chip ^ flip
                if chip // (chips // 4) % 2 == d % KEY_GROUPS and later > chip:
                    source = d ^ 1 if chip == 0 and later == 1 else d
                    moves.append((source * ctx_count + c, d * ctx_count + later * 2 + core))
        return lax.ppermute(array, ("dp", "ctx"), moves)

    (own_kv,) = call(
        load_kernel,
        [((rows, 2 * width), bf16)],
        [in_hbm(keys), in_hbm(values)],
        "load",
        scratch=[pltpu.SemaphoreType.DMA((2,))],
    )
    query_v, grad_v, grad_t, bias, token = call(
        prep_kernel,
        [
            ((rows, heads * width), bf16),
            ((rows, heads * width), bf16),
            ((heads * width, rows), bf16),
            ((held, rows), f32),
            ((8, 128), f32),
        ],
        [in_hbm(seg), in_hbm(queries), in_hbm(out_grad)],
        "prepare",
        scratch=[pltpu.VMEM(seg.shape, seg.dtype), pltpu.SemaphoreType.DMA((3, heads))],
        work=1,
        dims=dims,
    )
    flips = sorted(range(1, chips), key=lambda t: (t % (chips // 2) != 0, t))[::-1]
    (near,) = call(
        pack_kernel,
        [((held // 2, 2 * width), bf16)],
        [token, own_kv] + [to_group(own_kv, t) for t in flips],
        "pack",
        flips=flips,
    )
    far = over_ctx(near, 1)
    near_scores, top, near_vt = call(
        near_kernel,
        [((heads, held // 2, rows), f32), ((heads, rows), f32), ((width, held // 2), bf16)],
        [query_v, bias, near],
        "score_near",
        work=1,
        dims=dims,
    )
    stats, far_scores, *outs = call(
        forward_kernel,
        [((3 * heads, rows), f32), ((heads, held // 2, rows), f32)]
        + [((pair * width, rows), bf16)] * KEY_GROUPS,
        [query_v, grad_t, bias, near_scores, top, near_vt, far],
        "attend",
        scratch=[pltpu.VMEM((width, held // 2), bf16)],
        work=2,
        dims=dims,
    )
    all_stats = [stats, over_dp(stats, 1)]
    all_outs = [outs[0], over_dp(outs[1], 1)]
    ahead = 4 * heads * held * rows <= 8 * MIB
    dprobs = []
    if ahead:
        dprobs = call(
            dprobs_kernel,
            [((heads, held, rows), f32)],
            [grad_v, near, far],
            "dprobs",
            work=1,
            dims=dims,
        )

    dscores, keep, send = call(
        backward_kernel,
        [
            ((heads, held, rows), bf16),
            ((held // 2, 2 * width), f32),
            ((held // 2, 2 * width), bf16),
        ],
        [query_v, grad_v, near, far, near_scores, far_scores] + list(dprobs) + all_stats,
        "differentiate",
        scratch=[pltpu.VMEM((held, 2 * width), f32)],
        work=4,
        dims=dims,
        ahead=ahead,
    )
    got = over_ctx(send, 1)
    attn_out, token = call(
        finish_out_kernel,
        [((rows, pair * width), bf16), ((8, 128), f32)],
        all_stats + all_outs,
        "finish_out",
        dims=dims,
    )
    quarter = held // 4
    keep, send = call(
        join_kernel,
        [((quarter, 2 * width), f32), ((quarter, 2 * width), bf16)],
        [keep, got],
        "join_cores",
        after=0,
    )
    dqs = call(
        query_kernel,
        [((pair * width, rows), bf16)] * KEY_GROUPS,
        [near, far, dscores, keep],
        "query_terms",
        scratch=[pltpu.VMEM((width, held), bf16)],
        work=1,
        dims=dims,
    )
    all_dqs = [dqs[0], over_dp(dqs[1], 1)]
    pieces = call(
        join_kernel,
        [((piece, 2 * width), bf16)] * chips,
        [keep, over_dp(send, 2), token],
        "join_heads",
        after=1,
    )
    grad_kv = [over_ctx(pieces[t], 2 * t) for t in range(chips - 1, 0, -1)] + [pieces[0]]

    grad_q, grad_k, grad_values = call(
        finish_kernel,
        [((rows, pair * width), bf16)] + [((piece, width), bf16)] * 2,
        all_dqs + grad_kv,
        "finish",
    )
    return attn_out, grad_q, grad_k, grad_values


def solution(mesh):
    return jax.shard_map(
        on_device,
        mesh=mesh,
        in_specs=(P("ctx", None), P("ctx", None), P("ctx", None), P("ctx", None), P()),
        out_specs=(P("ctx", "dp"), P("ctx", "dp"), P(("dp", "ctx"), None), P(("dp", "ctx"), None)),
        check_vma=False,
    )
```

```python
import functools
import math

import jax
import jax.numpy as jnp
from jax import lax
from jax.experimental import pallas as pl
from jax.experimental.pallas import tpu as pltpu
from jax.sharding import PartitionSpec as P

NEG = -1e30
LOG2E = 1.4426950408889634
DOC_NUMBERS = 4
KEY_GROUPS = 2
MIB = 1024 * 1024


def place():
    dp_index, ctx_index = lax.axis_index("dp"), lax.axis_index("ctx")
    return dp_index // KEY_GROUPS, dp_index % KEY_GROUPS, ctx_index // 2, ctx_index % 2

NT = (((1,), (1,)), ((), ()))


def home_chip(spot, key_group, chip, chips):
    level = chips // 4
    flip = spot // level * (2 * level) + spot % level
    home = chip ^ flip
    return home ^ ((home // level % 2) ^ key_group) * level


def mask_bias(seg_ref, rows, held):
    _, key_group, chip, core = place()
    seg = seg_ref[...]
    lines = rows // 128
    seg_own = seg_ref[pl.ds((chip * 2 + core) * lines, lines), :]
    start = jnp.zeros((lines, 128), jnp.int32)
    for number in range(1, DOC_NUMBERS):
        before = jnp.sum((seg < number).astype(jnp.float32), axis=(0, 1), keepdims=True)
        start = jnp.where(seg_own == number, before.astype(jnp.int32), start)
    start = jnp.concatenate([start[k : k + 1] for k in range(lines)], axis=1)
    query_pos = (chip * 2 + core) * rows + lax.broadcasted_iota(jnp.int32, (1, rows), 1)
    blocks = held // rows
    bias = []
    for block in range(blocks):
        spot, side = block % (blocks // 2), block // (blocks // 2)
        home = home_chip(spot, key_group, chip, blocks) * 2 + (core ^ side)
        key_pos = home * rows + lax.broadcasted_iota(jnp.int32, (rows, rows), 0)
        allowed = (key_pos >= start) & (key_pos <= query_pos)
        bias.append(jnp.where(allowed, 0.0, NEG))
    return bias


def load_kernel(k_hbm, v_hbm, kv_ref, sems):
    width = k_hbm.shape[1]
    copies = [
        pltpu.make_async_copy(k_hbm, kv_ref.at[:, :width], sems.at[0]),
        pltpu.make_async_copy(v_hbm, kv_ref.at[:, width:], sems.at[1]),
    ]
    for copy in copies:
        copy.start()
    for copy in copies:
        copy.wait()


def pick_kernel(plain_ref, turned_ref, *refs, chips):
    _, key_group, chip, _ = place()
    same = (chip // (chips // 4) % 2) == key_group
    out_ref = refs[-1]

    @pl.when(same)
    def _():
        out_ref[...] = plain_ref[...]

    @pl.when(jnp.logical_not(same))
    def _():
        out_ref[...] = turned_ref[...]


def pass_kernel(*refs):
    refs[-1][...] = refs[0][:8, :128]


def prep_kernel(
    seg_hbm, q_hbm, g_hbm, q_ref, g_ref, gt_ref, bias_ref, token_ref, seg_ref, sems, *, dims
):
    heads, rows, width, held, ctx_count = dims
    head_group = place()[0]
    seg_copy = pltpu.make_async_copy(seg_hbm, seg_ref, sems.at[2, 0])
    seg_copy.start()
    copies = []
    for head in range(heads):
        source = head_columns(head_group * heads + head, width)
        target = slice(head * width, (head + 1) * width)
        for k, (full, part) in enumerate(((g_hbm, g_ref), (q_hbm, q_ref))):
            copies.append(
                pltpu.make_async_copy(full.at[:, source], part.at[:, target], sems.at[k, head])
            )
            copies[-1].start()
    token_ref[...] = jnp.zeros_like(token_ref)
    seg_copy.wait()
    for k, block in enumerate(mask_bias(seg_ref, rows, held)):
        bias_ref[k * rows : (k + 1) * rows, :] = block
    for head in range(heads):
        cols = slice(head * width, (head + 1) * width)
        copies[2 * head].wait()
        gt_ref[cols, :] = g_ref[:, cols].astype(jnp.float32).T.astype(jnp.bfloat16)
    for head in range(heads):
        copies[2 * head + 1].wait()


def head_columns(head, width):
    return pl.ds(pl.multiple_of(head * width, width), width)


def part_scores(q_ref, bias_ref, kv_ref, scores_ref, stats_ref, *, dims, part):
    heads, rows, width, held, ctx_count = dims
    here = slice(part * rows, (part + 1) * rows)
    for head in range(heads):
        raw = lax.dot_general(
            kv_ref[:, :width],
            q_ref[:, head * width : (head + 1) * width],
            NT,
            preferred_element_type=jnp.float32,
        )
        scores = raw * (width**-0.5 * LOG2E) + bias_ref[here, :]
        scores_ref[head] = scores
        stats_ref[head : head + 1, :] = jnp.max(scores, axis=0, keepdims=True)


def part_sums(values_t, scores_ref, stats_ref, head, heads):
    expd = jnp.exp2(scores_ref[head] - stats_ref[head : head + 1, :])
    stats_ref[heads + head : heads + head + 1, :] = jnp.sum(expd, axis=0, keepdims=True)
    return jnp.dot(values_t, expd.astype(jnp.bfloat16), preferred_element_type=jnp.float32)


def part_kernel(q_ref, bias_ref, kv_ref, scores_ref, stats_ref, sums_ref, *, dims, part):
    heads, rows, width, held, ctx_count = dims
    part_scores(q_ref, bias_ref, kv_ref, scores_ref, stats_ref, dims=dims, part=part)
    values_t = kv_ref[:, width:].astype(jnp.float32).T.astype(jnp.bfloat16)
    for head in range(heads):
        sums_ref[head] = part_sums(values_t, scores_ref, stats_ref, head, heads)


def forward_kernel(q_ref, gt_ref, bias_ref, kv_ref, *refs, dims, part):
    heads, rows, width, held, ctx_count = dims
    others, refs = refs[: 2 * part], refs[2 * part :]
    stats_ref, scores_ref, *outs, own_ref = refs
    pair = heads // KEY_GROUPS
    key_group = place()[1]
    part_scores(q_ref, bias_ref, kv_ref, scores_ref, own_ref, dims=dims, part=part)
    values_t = kv_ref[:, width:].astype(jnp.float32).T.astype(jnp.bfloat16)
    for head in range(heads):
        cols = slice(head * width, (head + 1) * width)
        sums = part_sums(values_t, scores_ref, own_ref, head, heads)
        parts = [(own_ref, sums)] + [(others[2 * k], others[2 * k + 1][head]) for k in range(part)]
        top = functools.reduce(jnp.maximum, [s[head : head + 1, :] for s, _ in parts])
        total, accum = 0.0, 0.0
        for part_stats, part_sum in parts:
            share = jnp.exp2(part_stats[head : head + 1, :] - top)
            total = total + share * part_stats[heads + head : heads + head + 1, :]
            accum = accum + share * part_sum
        delta = jnp.sum(accum * gt_ref[cols, :].astype(jnp.float32), axis=0, keepdims=True)
        for row, value in enumerate((top, total, delta)):
            stats_ref[row * heads + head : row * heads + head + 1, :] = value
        where = slice(head % pair * width, (head % pair + 1) * width)
        sums_bf = accum.astype(jnp.bfloat16)
        for slot in range(KEY_GROUPS):

            @pl.when((key_group ^ slot) == head // pair)
            def _():
                outs[slot][where, :] = sums_bf


def dprobs_kernel(g_ref, *refs, dims):
    heads, rows, width, held, ctx_count = dims
    *blocks, dprobs_ref = refs
    for head in range(heads):
        grad = g_ref[:, head * width : (head + 1) * width]
        for part, ref in enumerate(blocks):
            dprobs_ref[head, part * rows : (part + 1) * rows, :] = lax.dot_general(
                ref[:, width:], grad, NT, preferred_element_type=jnp.float32
            )


def merged_stats(stats, heads):
    top = functools.reduce(jnp.maximum, [s[:heads] for s in stats])
    shares = [jnp.exp2(s[:heads] - top) for s in stats]
    total = sum(f * s[heads : 2 * heads] for f, s in zip(shares, stats))
    delta = sum(f * s[2 * heads :] for f, s in zip(shares, stats)) / total
    return top, shares, total, delta


def backward_kernel(q_ref, g_ref, *refs, dims, ahead):
    heads, rows, width, held, ctx_count = dims
    parts = held // rows
    blocks, scores, refs = refs[:parts], refs[parts : 2 * parts], refs[2 * parts :]
    dprobs_ref, refs = (refs[0], refs[1:]) if ahead else (None, refs)
    stats = refs[:KEY_GROUPS]
    ds_ref, keep_ref, send_ref, acc_ref = refs[KEY_GROUPS:]
    scale = width**-0.5
    top, _, total, delta = merged_stats([s[...] for s in stats], heads)
    lse = top + jnp.log2(total)
    for head in range(heads):
        cols = slice(head * width, (head + 1) * width)
        query, grad = q_ref[:, cols], g_ref[:, cols]
        for part, ref in enumerate(blocks):
            here = slice(part * rows, (part + 1) * rows)
            probs = jnp.exp2(scores[part][head] - lse[head : head + 1])
            if ahead:
                dprobs = dprobs_ref[head, here, :]
            else:
                dprobs = lax.dot_general(
                    ref[:, width:], grad, NT, preferred_element_type=jnp.float32
                )
            dscores = (probs * (dprobs - delta[head : head + 1])).astype(jnp.bfloat16)
            ds_ref[head, here, :] = dscores
            dv = jnp.dot(probs.astype(jnp.bfloat16), grad, preferred_element_type=jnp.float32)
            dk = jnp.dot(dscores, query, preferred_element_type=jnp.float32)
            if head == 0:
                acc_ref[here, :width] = dk
                acc_ref[here, width:] = dv
            else:
                acc_ref[here, :width] += dk
                acc_ref[here, width:] += dv
    head_group, key_group, chip, core = place()
    chips, piece = ctx_count // 2, rows // 4
    level = chips // 4
    for spot in range(2 * chips):
        here = slice(spot * piece, (spot + 1) * piece)
        target = chip ^ (spot % chips)
        group = head_group ^ (spot // chips)
        block = group * (ctx_count // 2) + key_group * (ctx_count // 4) + target // 2
        flip = block // 2 ^ chip
        line = ((block % 2 ^ core) * (chips // 2) + flip // (2 * level) * level + flip % level) * rows
        for ref, side in ((keep_ref, core), (send_ref, 1 - core)):
            mine = pl.ds(pl.multiple_of(line + (target % 2 * 2 + side) * piece, piece), piece)
            ref[here, :width] = (acc_ref[mine, :width] * scale).astype(ref.dtype)
            ref[here, width:] = acc_ref[mine, width:].astype(ref.dtype)


def query_kernel(*refs, dims):
    heads, rows, width, held, ctx_count = dims
    parts = held // rows
    blocks, ds_ref, refs = refs[:parts], refs[parts], refs[parts + 2 :]
    outs, kt_ref = refs[:KEY_GROUPS], refs[KEY_GROUPS]
    pair = heads // KEY_GROUPS
    key_group = place()[1]
    scale = width**-0.5
    for part, ref in enumerate(blocks):
        here = slice(part * rows, (part + 1) * rows)
        kt_ref[:, here] = ref[:, :width].astype(jnp.float32).T.astype(jnp.bfloat16)
    for slot in range(KEY_GROUPS):
        for part in range(pair):
            head = (key_group ^ slot) * pair + part
            dq = jnp.dot(kt_ref[...], ds_ref[head], preferred_element_type=jnp.float32)
            outs[slot][part * width : (part + 1) * width, :] = (dq * scale).astype(jnp.bfloat16)


def join_kernel(keep_ref, got_ref, *refs, after):
    start = 0
    for out_ref in refs[after:]:
        here = slice(start, start + out_ref.shape[0])
        total = keep_ref[here, :] + got_ref[here, :].astype(jnp.float32)
        out_ref[...] = total.astype(out_ref.dtype)
        start = start + out_ref.shape[0]


def finish_out_kernel(*refs, dims):
    heads, rows, width, held, ctx_count = dims
    stats, outs = refs[:KEY_GROUPS], refs[KEY_GROUPS : 2 * KEY_GROUPS]
    attn_ref, token_ref = refs[2 * KEY_GROUPS :]
    token_ref[...] = jnp.zeros_like(token_ref)
    pair = heads // KEY_GROUPS
    top, shares, total, _ = merged_stats([s[...] for s in stats], heads)
    own = place()[1] * pair
    row = lax.broadcasted_iota(jnp.int32, (heads, 1), 0)
    for part in range(pair):
        here = slice(part * width, (part + 1) * width)

        def pick(array):
            return jnp.sum(jnp.where(row == own + part, array, 0.0), axis=0, keepdims=True)

        joined = sum(o[here, :].astype(jnp.float32) * pick(f) for o, f in zip(outs, shares))
        attn_ref[:, here] = (joined / pick(total)).T.astype(jnp.bfloat16)


def finish_query_kernel(own_ref, got_ref, gq_ref, token_ref):
    total = own_ref[...].astype(jnp.float32) + got_ref[...].astype(jnp.float32)
    gq_ref[...] = total.T.astype(jnp.bfloat16)
    token_ref[...] = jnp.zeros_like(token_ref)


def finish_kernel(token_ref, *refs):
    *terms, gk_ref, gv_ref = refs
    width = gk_ref.shape[1]
    both = sum(r[...].astype(jnp.float32) for r in terms)
    gk_ref[...] = both[:, :width].astype(jnp.bfloat16)
    gv_ref[...] = both[:, width:].astype(jnp.bfloat16)


def on_device(queries, keys, values, out_grad, segment_ids):
    rows = queries.shape[0]
    width = keys.shape[1]
    seq = segment_ids.shape[0]
    dp_count, ctx_count = lax.axis_size("dp"), lax.axis_size("ctx")
    head_groups = dp_count // KEY_GROUPS
    heads = queries.shape[1] // width // head_groups
    pair = heads // KEY_GROUPS
    chips = ctx_count // 2
    held = rows * ctx_count // KEY_GROUPS
    piece = rows // dp_count
    dims = (heads, rows, width, held, ctx_count)
    seg = segment_ids.reshape(seq // 128, 128)
    params = pltpu.CompilerParams(
        vmem_limit_bytes=min(56 * MIB, 12 * MIB + 12 * 4 * held * rows)
    )
    vmem = pl.BlockSpec(memory_space=pltpu.VMEM)
    bf16, f32 = jnp.bfloat16, jnp.float32

    def call(kernel, outs, ins, name, scratch=(), work=0, **static):
        specs = [a[1] if isinstance(a, tuple) else vmem for a in ins]
        arrays = [a[0] if isinstance(a, tuple) else a for a in ins]
        return pl.pallas_call(
            functools.partial(kernel, **static),
            out_shape=[jax.ShapeDtypeStruct(*o) for o in outs],
            in_specs=specs,
            out_specs=[vmem] * len(outs),
            scratch_shapes=list(scratch),
            compiler_params=params,
            cost_estimate=pl.CostEstimate(
                flops=work * 2 * heads * rows * held * width,
                bytes_accessed=sum(math.prod(o[0]) * 2 for o in outs),
                transcendentals=0,
            ),
            name=name,
        )(*arrays)

    def in_hbm(array):
        return pltpu.with_memory_space_constraint(array, pltpu.HBM), pl.BlockSpec(
            memory_space=pltpu.HBM
        )

    def over_dp(array, flip):
        return lax.ppermute(array, "dp", [(d, d ^ flip) for d in range(dp_count)])

    def over_ctx(array, flip):
        return lax.ppermute(array, "ctx", [(c, c ^ flip) for c in range(ctx_count)])

    def to_group(array, flip):
        moves = []
        for d in range(dp_count):
            for c in range(ctx_count):
                chip, core = divmod(c, 2)
                later = chip ^ flip
                if chip // (chips // 4) % 2 == d % KEY_GROUPS and later > chip:
                    source = d ^ 1 if chip == 0 and later == 1 else d
                    moves.append((source * ctx_count + c, d * ctx_count + later * 2 + core))
        return lax.ppermute(array, ("dp", "ctx"), moves)

    (own_kv,) = call(
        load_kernel,
        [((rows, 2 * width), bf16)],
        [in_hbm(keys), in_hbm(values)],
        "load",
        scratch=[pltpu.SemaphoreType.DMA((2,))],
    )
    query_v, grad_v, grad_t, bias, token = call(
        prep_kernel,
        [
            ((rows, heads * width), bf16),
            ((rows, heads * width), bf16),
            ((heads * width, rows), bf16),
            ((held, rows), f32),
            ((8, 128), f32),
        ],
        [in_hbm(seg), in_hbm(queries), in_hbm(out_grad)],
        "prepare",
        scratch=[pltpu.VMEM(seg.shape, seg.dtype), pltpu.SemaphoreType.DMA((3, heads))],
        work=1,
        dims=dims,
    )
    level, slots = chips // 4, chips // 2
    flips = [slot // level * (2 * level) + slot % level for slot in range(slots)]
    sent = {t: to_group(own_kv, t) for t in range(1, chips)}
    first = call(pass_kernel, [((8, 128), bf16)], [sent[t] for t in flips[1:]], "pass")
    blocks, done = {}, {}
    for slot, flip in enumerate(flips):
        (blocks[slot],) = call(
            pick_kernel,
            [((rows, 2 * width), bf16)],
            [sent[flip] if flip else own_kv, sent[flip ^ level], token] + (list(first) if slot == 0 else []),
            "pick",
            chips=chips,
        )
        blocks[slot + slots] = over_ctx(blocks[slot], 1)
        for part in (slot, slot + slots)[: 1 + (slot < slots - 1)]:
            done[part] = call(
                part_kernel,
                [((heads, rows, rows), f32), ((2 * heads, rows), f32), ((heads, width, rows), f32)],
                [query_v, bias, blocks[part]],
                "attend_part",
                work=1,
                dims=dims,
                part=part,
            )
    blocks = [blocks[part] for part in range(2 * slots)]
    last = 2 * slots - 1
    others = [a for part in range(last) for a in done[part][1:]]
    stats, last_scores, *outs = call(
        forward_kernel,
        [((3 * heads, rows), f32), ((heads, rows, rows), f32)]
        + [((pair * width, rows), bf16)] * KEY_GROUPS,
        [query_v, grad_t, bias, blocks[last]] + others,
        "attend",
        scratch=[pltpu.VMEM((2 * heads, rows), f32)],
        work=1,
        dims=dims,
        part=last,
    )
    scores = [done[part][0] for part in range(last)] + [last_scores]
    all_stats = [stats, over_dp(stats, 1)]
    all_outs = [outs[0], over_dp(outs[1], 1)]
    ahead = 4 * heads * held * rows <= 8 * MIB
    dprobs = []
    if ahead:
        dprobs = call(
            dprobs_kernel,
            [((heads, held, rows), f32)],
            [grad_v] + blocks,
            "dprobs",
            work=1,
            dims=dims,
        )

    dscores, keep, send = call(
        backward_kernel,
        [
            ((heads, held, rows), bf16),
            ((held // 2, 2 * width), f32),
            ((held // 2, 2 * width), bf16),
        ],
        [query_v, grad_v] + blocks + scores + list(dprobs) + all_stats,
        "differentiate",
        scratch=[pltpu.VMEM((held, 2 * width), f32)],
        work=4,
        dims=dims,
        ahead=ahead,
    )
    got = over_ctx(send, 1)
    attn_out, token = call(
        finish_out_kernel,
        [((rows, pair * width), bf16), ((8, 128), f32)],
        all_stats + all_outs,
        "finish_out",
        dims=dims,
    )
    quarter = held // 4
    keep, send = call(
        join_kernel,
        [((quarter, 2 * width), f32), ((quarter, 2 * width), bf16)],
        [keep, got],
        "join_cores",
        after=0,
    )
    dqs = call(
        query_kernel,
        [((pair * width, rows), bf16)] * KEY_GROUPS,
        blocks + [dscores, keep],
        "query_terms",
        scratch=[pltpu.VMEM((width, held), bf16)],
        work=1,
        dims=dims,
    )
    all_dqs = [dqs[0], over_dp(dqs[1], 1)]
    pieces = call(
        join_kernel,
        [((piece, 2 * width), bf16)] * chips,
        [keep, over_dp(send, 2), token],
        "join_heads",
        after=1,
    )
    grad_kv = [over_ctx(pieces[t], 2 * t) for t in range(chips - 1, 0, -1)] + [pieces[0]]

    grad_q, token = call(
        finish_query_kernel,
        [((rows, pair * width), bf16), ((8, 128), f32)],
        all_dqs,
        "finish_query",
    )
    grad_k, grad_values = call(
        finish_kernel, [((piece, width), bf16)] * 2, [token] + grad_kv, "finish"
    )
    return attn_out, grad_q, grad_k, grad_values


def solution(mesh):
    return jax.shard_map(
        on_device,
        mesh=mesh,
        in_specs=(P("ctx", None), P("ctx", None), P("ctx", None), P("ctx", None), P()),
        out_specs=(P("ctx", "dp"), P("ctx", "dp"), P(("dp", "ctx"), None), P(("dp", "ctx"), None)),
        check_vma=False,
    )
```

```python
import functools
import math

import jax
import jax.numpy as jnp
from jax import lax
from jax.experimental import pallas as pl
from jax.experimental.pallas import tpu as pltpu
from jax.sharding import PartitionSpec as P

NEG = -1e30
LOG2E = 1.4426950408889634
DOC_NUMBERS = 4
KEY_GROUPS = 2
MIB = 1024 * 1024


def place():
    dp_index, ctx_index = lax.axis_index("dp"), lax.axis_index("ctx")
    return dp_index // KEY_GROUPS, dp_index % KEY_GROUPS, ctx_index // 2, ctx_index % 2

NT = (((1,), (1,)), ((), ()))


def home_chip(spot, key_group, chip, chips):
    level = chips // 4
    flip = spot // level * (2 * level) + spot % level
    home = chip ^ flip
    return home ^ ((home // level % 2) ^ key_group) * level


def gather_rounds(chips):
    if chips == 4:
        first = {(0, 1): (1, 0), (0, 2): (0, 0), (1, 2): (1, 1), (0, 3): (0, 2)}
        return [first, {(0, 3): (0, 0), (1, 3): (1, 1)}]
    rounds = [{} for _ in range(1, chips)]
    for flip, moves in enumerate(rounds, 1):
        for home in range(chips):
            group = home // (chips // 4) % 2
            if home ^ flip > home:
                moves[group, home ^ flip] = (group, home)
    return rounds


def spread_rounds(chips):
    if chips == 4:
        return [{3: 0, 0: 1, 1: 2}, {2: 0, 3: 1, 0: 2, 1: 3}, {1: 0, 2: 1, 3: 2, 0: 3}, {2: 3}]
    return [{chip: chip ^ flip for chip in range(chips)} for flip in range(1, chips)]


def mask_bias(seg_ref, rows, held):
    _, key_group, chip, core = place()
    seg = seg_ref[...]
    lines = rows // 128
    seg_own = seg_ref[pl.ds((chip * 2 + core) * lines, lines), :]
    start = jnp.zeros((lines, 128), jnp.int32)
    for number in range(1, DOC_NUMBERS):
        before = jnp.sum((seg < number).astype(jnp.float32), axis=(0, 1), keepdims=True)
        start = jnp.where(seg_own == number, before.astype(jnp.int32), start)
    start = jnp.concatenate([start[k : k + 1] for k in range(lines)], axis=1)
    query_pos = (chip * 2 + core) * rows + lax.broadcasted_iota(jnp.int32, (1, rows), 1)
    blocks = held // rows
    bias = []
    for block in range(blocks):
        home = home_chip(block // 2, key_group, chip, blocks) * 2 + (core ^ block % 2)
        key_pos = home * rows + lax.broadcasted_iota(jnp.int32, (rows, rows), 0)
        allowed = (key_pos >= start) & (key_pos <= query_pos)
        bias.append(jnp.where(allowed, 0.0, NEG))
    return bias


def load_kernel(k_hbm, v_hbm, kv_ref, sems):
    width = k_hbm.shape[1]
    copies = [
        pltpu.make_async_copy(k_hbm, kv_ref.at[:, :width], sems.at[0]),
        pltpu.make_async_copy(v_hbm, kv_ref.at[:, width:], sems.at[1]),
    ]
    for copy in copies:
        copy.start()
    for copy in copies:
        copy.wait()


def pick_kernel(*refs, choices):
    out_ref = refs[-1]
    _, key_group, chip, _ = place()
    spot = key_group * (len(choices) // 2) + chip
    for choice in sorted(set(choices)):
        wanted = functools.reduce(
            jnp.logical_or, [spot == k for k, c in enumerate(choices) if c == choice]
        )

        @pl.when(wanted)
        def _():
            out_ref[...] = jnp.zeros_like(out_ref) if choice < 0 else refs[choice][...]


def prep_kernel(
    seg_hbm, q_hbm, g_hbm, q_ref, g_ref, gt_ref, bias_ref, token_ref, seg_ref, sems, *, dims
):
    heads, rows, width, held, ctx_count = dims
    head_group = place()[0]
    seg_copy = pltpu.make_async_copy(seg_hbm, seg_ref, sems.at[2, 0])
    seg_copy.start()
    copies = []
    for head in range(heads):
        source = head_columns(head_group * heads + head, width)
        target = slice(head * width, (head + 1) * width)
        for k, (full, part) in enumerate(((g_hbm, g_ref), (q_hbm, q_ref))):
            copies.append(
                pltpu.make_async_copy(full.at[:, source], part.at[:, target], sems.at[k, head])
            )
            copies[-1].start()
    token_ref[...] = jnp.zeros_like(token_ref)
    seg_copy.wait()
    for k, block in enumerate(mask_bias(seg_ref, rows, held)):
        bias_ref[k * rows : (k + 1) * rows, :] = block
    for head in range(heads):
        cols = slice(head * width, (head + 1) * width)
        copies[2 * head].wait()
        gt_ref[cols, :] = g_ref[:, cols].astype(jnp.float32).T.astype(jnp.bfloat16)
    for head in range(heads):
        copies[2 * head + 1].wait()


def head_columns(head, width):
    return pl.ds(pl.multiple_of(head * width, width), width)


def scores_pass(q_ref, bias_ref, blocks, scores_ref, top_ref, *, dims, first):
    heads, rows, width, held, ctx_count = dims
    for head in range(heads):
        query = q_ref[:, head * width : (head + 1) * width]
        top = None
        for k, kv_ref in enumerate(blocks):
            bias = bias_ref[(first + k) * rows : (first + k + 1) * rows, :]
            raw = lax.dot_general(kv_ref[:, :width], query, NT, preferred_element_type=jnp.float32)
            scores = raw * (width**-0.5 * LOG2E) + bias
            scores_ref[head, k * rows : (k + 1) * rows, :] = scores
            here = jnp.max(scores, axis=0, keepdims=True)
            top = here if top is None else jnp.maximum(top, here)
        top_ref[head : head + 1, :] = top


def transpose_values(blocks, vt_ref, width):
    size = blocks[0].shape[0]
    for k, kv_ref in enumerate(blocks):
        vt = kv_ref[:, width:].astype(jnp.float32).T.astype(jnp.bfloat16)
        vt_ref[:, k * size : (k + 1) * size] = vt


def sums_pass(vt_ref, scores_ref, top, head):
    expd = jnp.exp2(scores_ref[head] - top)
    total = jnp.sum(expd, axis=0, keepdims=True)
    sums = jnp.dot(vt_ref[...], expd.astype(jnp.bfloat16), preferred_element_type=jnp.float32)
    return total, sums


def part_kernel(q_ref, bias_ref, *refs, dims):
    heads, rows, width, held, ctx_count = dims
    *blocks, scores_ref, stats_ref, sums_ref, vt_ref = refs
    transpose_values(blocks, vt_ref, width)
    scores_pass(q_ref, bias_ref, blocks, scores_ref, stats_ref, dims=dims, first=0)
    for head in range(heads):
        total, sums_ref[head] = sums_pass(
            vt_ref, scores_ref, stats_ref[head : head + 1, :], head
        )
        stats_ref[heads + head : heads + head + 1, :] = total


def forward_kernel(
    q_ref, gt_ref, bias_ref, kv_ref, part_ref, part_sums_ref, stats_ref, scores_ref, *refs, dims
):
    heads, rows, width, held, ctx_count = dims
    *outs, top_ref, vt_ref = refs
    pair = heads // KEY_GROUPS
    key_group = place()[1]
    transpose_values([kv_ref], vt_ref, width)
    scores_pass(q_ref, bias_ref, [kv_ref], scores_ref, top_ref, dims=dims, first=held // rows - 1)
    for head in range(heads):
        cols = slice(head * width, (head + 1) * width)
        before = part_ref[head : head + 1, :]
        top = jnp.maximum(top_ref[head : head + 1, :], before)
        share = jnp.exp2(before - top)
        total, accum = sums_pass(vt_ref, scores_ref, top, head)
        total = total + share * part_ref[heads + head : heads + head + 1, :]
        accum = accum + share * part_sums_ref[head]
        delta = jnp.sum(accum * gt_ref[cols, :].astype(jnp.float32), axis=0, keepdims=True)
        for row, value in enumerate((top, total, delta)):
            stats_ref[row * heads + head : row * heads + head + 1, :] = value
        where = slice(head % pair * width, (head % pair + 1) * width)
        sums_bf = accum.astype(jnp.bfloat16)
        for slot in range(KEY_GROUPS):

            @pl.when((key_group ^ slot) == head // pair)
            def _():
                outs[slot][where, :] = sums_bf


def dprobs_kernel(g_ref, *refs, dims):
    heads, rows, width, held, ctx_count = dims
    *blocks, dprobs_ref = refs
    for head in range(heads):
        grad = g_ref[:, head * width : (head + 1) * width]
        for part, ref in enumerate(blocks):
            dprobs_ref[head, part * rows : (part + 1) * rows, :] = lax.dot_general(
                ref[:, width:], grad, NT, preferred_element_type=jnp.float32
            )


def merged_stats(stats, heads):
    top = functools.reduce(jnp.maximum, [s[:heads] for s in stats])
    shares = [jnp.exp2(s[:heads] - top) for s in stats]
    total = sum(f * s[heads : 2 * heads] for f, s in zip(shares, stats))
    delta = sum(f * s[2 * heads :] for f, s in zip(shares, stats)) / total
    return top, shares, total, delta


def backward_kernel(q_ref, g_ref, *refs, dims, ahead):
    heads, rows, width, held, ctx_count = dims
    parts = held // rows
    blocks, scores, last_scores, refs = refs[:parts], refs[parts], refs[parts + 1], refs[parts + 2 :]
    dprobs_ref, refs = (refs[0], refs[1:]) if ahead else (None, refs)
    stats = refs[:KEY_GROUPS]
    ds_ref, keep_ref, send_ref, acc_ref = refs[KEY_GROUPS:]
    scale = width**-0.5
    top, _, total, delta = merged_stats([s[...] for s in stats], heads)
    lse = top + jnp.log2(total)
    for head in range(heads):
        cols = slice(head * width, (head + 1) * width)
        query, grad = q_ref[:, cols], g_ref[:, cols]
        for part, ref in enumerate(blocks):
            here = slice(part * rows, (part + 1) * rows)
            row = last_scores[head] if part == parts - 1 else scores[head, here, :]
            probs = jnp.exp2(row - lse[head : head + 1])
            if ahead:
                dprobs = dprobs_ref[head, here, :]
            else:
                dprobs = lax.dot_general(
                    ref[:, width:], grad, NT, preferred_element_type=jnp.float32
                )
            dscores = (probs * (dprobs - delta[head : head + 1])).astype(jnp.bfloat16)
            ds_ref[head, here, :] = dscores
            dv = jnp.dot(probs.astype(jnp.bfloat16), grad, preferred_element_type=jnp.float32)
            dk = jnp.dot(dscores, query, preferred_element_type=jnp.float32)
            if head == 0:
                acc_ref[here, :width] = dk
                acc_ref[here, width:] = dv
            else:
                acc_ref[here, :width] += dk
                acc_ref[here, width:] += dv
    head_group, key_group, chip, core = place()
    chips, piece = ctx_count // 2, rows // 4
    level = chips // 4
    for spot in range(2 * chips):
        here = slice(spot * piece, (spot + 1) * piece)
        target = chip ^ (spot % chips)
        group = head_group ^ (spot // chips)
        block = group * (ctx_count // 2) + key_group * (ctx_count // 4) + target // 2
        flip = block // 2 ^ chip
        slot = flip // (2 * level) * level + flip % level
        line = (slot * 2 + (block % 2 ^ core)) * rows
        for ref, side in ((keep_ref, core), (send_ref, 1 - core)):
            mine = pl.ds(pl.multiple_of(line + (target % 2 * 2 + side) * piece, piece), piece)
            ref[here, :width] = (acc_ref[mine, :width] * scale).astype(ref.dtype)
            ref[here, width:] = acc_ref[mine, width:].astype(ref.dtype)


def query_kernel(*refs, dims):
    heads, rows, width, held, ctx_count = dims
    parts = held // rows
    blocks, ds_ref, refs = refs[:parts], refs[parts], refs[parts + 2 :]
    outs, kt_ref = refs[:KEY_GROUPS], refs[KEY_GROUPS]
    pair = heads // KEY_GROUPS
    key_group = place()[1]
    scale = width**-0.5
    for part, ref in enumerate(blocks):
        here = slice(part * rows, (part + 1) * rows)
        kt_ref[:, here] = ref[:, :width].astype(jnp.float32).T.astype(jnp.bfloat16)
    for slot in range(KEY_GROUPS):
        for part in range(pair):
            head = (key_group ^ slot) * pair + part
            dq = jnp.dot(kt_ref[...], ds_ref[head], preferred_element_type=jnp.float32)
            outs[slot][part * width : (part + 1) * width, :] = (dq * scale).astype(jnp.bfloat16)


def join_kernel(keep_ref, got_ref, kept_ref, send_ref):
    half = kept_ref.shape[0]
    kept_ref[...] = keep_ref[:half, :] + got_ref[:half, :].astype(jnp.float32)
    send = keep_ref[half:, :] + got_ref[half:, :].astype(jnp.float32)
    send_ref[...] = send.astype(jnp.bfloat16)


def spread_kernel(keep_ref, got_ref, token_ref, own_ref, *outs, rounds):
    piece = own_ref.shape[0]
    chip = place()[2]
    own_ref[...] = keep_ref[:piece, :] + got_ref[:piece, :].astype(jnp.float32)
    for out_ref, moves in zip(outs, rounds):
        flip = 0
        for source, target in moves.items():
            flip = jnp.where(chip == source, source ^ target, flip)
        mine = pl.ds(pl.multiple_of(flip * piece, piece), piece)
        out_ref[...] = (keep_ref[mine, :] + got_ref[mine, :].astype(jnp.float32)).astype(
            jnp.bfloat16
        )


def add_kernel(first_ref, second_ref, out_ref):
    out_ref[...] = first_ref[...] + second_ref[...].astype(jnp.float32)


def finish_out_kernel(*refs, dims):
    heads, rows, width, held, ctx_count = dims
    stats, outs = refs[:KEY_GROUPS], refs[KEY_GROUPS : 2 * KEY_GROUPS]
    attn_ref, token_ref = refs[2 * KEY_GROUPS :]
    token_ref[...] = jnp.zeros_like(token_ref)
    pair = heads // KEY_GROUPS
    top, shares, total, _ = merged_stats([s[...] for s in stats], heads)
    own = place()[1] * pair
    row = lax.broadcasted_iota(jnp.int32, (heads, 1), 0)
    for part in range(pair):
        here = slice(part * width, (part + 1) * width)

        def pick(array):
            return jnp.sum(jnp.where(row == own + part, array, 0.0), axis=0, keepdims=True)

        joined = sum(o[here, :].astype(jnp.float32) * pick(f) for o, f in zip(outs, shares))
        attn_ref[:, here] = (joined / pick(total)).T.astype(jnp.bfloat16)


def finish_query_kernel(own_ref, got_ref, gq_ref, token_ref):
    total = own_ref[...].astype(jnp.float32) + got_ref[...].astype(jnp.float32)
    gq_ref[...] = total.T.astype(jnp.bfloat16)
    token_ref[...] = jnp.zeros_like(token_ref)


def finish_kernel(token_ref, *refs):
    *terms, gk_ref, gv_ref = refs
    width = gk_ref.shape[1]
    both = sum(r[...].astype(jnp.float32) for r in terms)
    gk_ref[...] = both[:, :width].astype(jnp.bfloat16)
    gv_ref[...] = both[:, width:].astype(jnp.bfloat16)


def on_device(queries, keys, values, out_grad, segment_ids):
    rows = queries.shape[0]
    width = keys.shape[1]
    seq = segment_ids.shape[0]
    dp_count, ctx_count = lax.axis_size("dp"), lax.axis_size("ctx")
    head_groups = dp_count // KEY_GROUPS
    heads = queries.shape[1] // width // head_groups
    pair = heads // KEY_GROUPS
    chips = ctx_count // 2
    held = rows * ctx_count // KEY_GROUPS
    piece = rows // dp_count
    dims = (heads, rows, width, held, ctx_count)
    seg = segment_ids.reshape(seq // 128, 128)
    params = pltpu.CompilerParams(
        vmem_limit_bytes=min(56 * MIB, 12 * MIB + 12 * 4 * held * rows)
    )
    vmem = pl.BlockSpec(memory_space=pltpu.VMEM)
    bf16, f32 = jnp.bfloat16, jnp.float32

    def call(kernel, outs, ins, name, scratch=(), work=0, **static):
        specs = [a[1] if isinstance(a, tuple) else vmem for a in ins]
        arrays = [a[0] if isinstance(a, tuple) else a for a in ins]
        return pl.pallas_call(
            functools.partial(kernel, **static),
            out_shape=[jax.ShapeDtypeStruct(*o) for o in outs],
            in_specs=specs,
            out_specs=[vmem] * len(outs),
            scratch_shapes=list(scratch),
            compiler_params=params,
            cost_estimate=pl.CostEstimate(
                flops=work * 2 * heads * rows * held * width,
                bytes_accessed=sum(math.prod(o[0]) * 2 for o in outs),
                transcendentals=0,
            ),
            name=name,
        )(*arrays)

    def in_hbm(array):
        return pltpu.with_memory_space_constraint(array, pltpu.HBM), pl.BlockSpec(
            memory_space=pltpu.HBM
        )

    def over_dp(array, flip):
        return lax.ppermute(array, "dp", [(d, d ^ flip) for d in range(dp_count)])

    def over_cores(array):
        return lax.ppermute(array, "ctx", [(c, c ^ 1) for c in range(ctx_count)])

    def gathered(array, moves):
        pairs = []
        for d in range(0, dp_count, KEY_GROUPS):
            for (group, chip), (source, home) in moves.items():
                for core in range(2):
                    start = (d + source) * ctx_count + home * 2 + core
                    pairs.append((start, (d + group) * ctx_count + chip * 2 + core))
        return lax.ppermute(array, ("dp", "ctx"), pairs)

    def spread(array, moves):
        pairs = [(a * 2 + core, b * 2 + core) for a, b in moves.items() for core in range(2)]
        return lax.ppermute(array, "ctx", pairs)

    (own_kv,) = call(
        load_kernel,
        [((rows, 2 * width), bf16)],
        [in_hbm(keys), in_hbm(values)],
        "load",
        scratch=[pltpu.SemaphoreType.DMA((2,))],
    )
    query_v, grad_v, grad_t, bias, token = call(
        prep_kernel,
        [
            ((rows, heads * width), bf16),
            ((rows, heads * width), bf16),
            ((heads * width, rows), bf16),
            ((held, rows), f32),
            ((8, 128), f32),
        ],
        [in_hbm(seg), in_hbm(queries), in_hbm(out_grad)],
        "prepare",
        scratch=[pltpu.VMEM(seg.shape, seg.dtype), pltpu.SemaphoreType.DMA((3, heads))],
        work=1,
        dims=dims,
    )
    rounds = gather_rounds(chips)
    sent = [own_kv] + [gathered(own_kv, moves) for moves in rounds]
    blocks = []
    for spot in range(chips // 2):
        choices = []
        for group in range(KEY_GROUPS):
            for chip in range(chips):
                home = home_chip(spot, group, chip, chips)
                ways = [k for k, moves in enumerate(rounds, 1) if moves.get((group, chip), (0, chip))[1] == home]
                choices.append(0 if home == chip else ways[0] if home < chip else -1)
        used = sorted(set(choices) - {-1})
        (picked,) = call(
            pick_kernel,
            [((rows, 2 * width), bf16)],
            [sent[k] for k in used] + [token],
            "pick",
            choices=[used.index(c) if c >= 0 else -1 for c in choices],
        )
        blocks += [picked, over_cores(picked)]
    early = held - rows
    scores, part_stats, part_sums = call(
        part_kernel,
        [((heads, early, rows), f32), ((2 * heads, rows), f32), ((heads, width, rows), f32)],
        [query_v, bias] + blocks[:-1],
        "attend_most",
        scratch=[pltpu.VMEM((width, early), bf16)],
        work=2,
        dims=dims,
    )
    stats, last_scores, *outs = call(
        forward_kernel,
        [((3 * heads, rows), f32), ((heads, rows, rows), f32)]
        + [((pair * width, rows), bf16)] * KEY_GROUPS,
        [query_v, grad_t, bias, blocks[-1], part_stats, part_sums],
        "attend",
        scratch=[pltpu.VMEM((heads, rows), f32), pltpu.VMEM((width, rows), bf16)],
        work=1,
        dims=dims,
    )
    all_stats = [stats, over_dp(stats, 1)]
    all_outs = [outs[0], over_dp(outs[1], 1)]
    ahead = 4 * heads * held * rows <= 8 * MIB
    dprobs = []
    if ahead:
        dprobs = call(
            dprobs_kernel,
            [((heads, held, rows), f32)],
            [grad_v] + blocks,
            "dprobs",
            work=1,
            dims=dims,
        )

    dscores, keep, send = call(
        backward_kernel,
        [
            ((heads, held, rows), bf16),
            ((held // 2, 2 * width), f32),
            ((held // 2, 2 * width), bf16),
        ],
        [query_v, grad_v] + blocks + [scores, last_scores] + list(dprobs) + all_stats,
        "differentiate",
        scratch=[pltpu.VMEM((held, 2 * width), f32)],
        work=4,
        dims=dims,
        ahead=ahead,
    )
    got = over_cores(send)
    attn_out, token = call(
        finish_out_kernel,
        [((rows, pair * width), bf16), ((8, 128), f32)],
        all_stats + all_outs,
        "finish_out",
        dims=dims,
    )
    quarter = held // 4
    keep, send = call(
        join_kernel,
        [((quarter, 2 * width), f32), ((quarter, 2 * width), bf16)],
        [keep, got],
        "join_cores",
    )
    dqs = call(
        query_kernel,
        [((pair * width, rows), bf16)] * KEY_GROUPS,
        blocks + [dscores, keep],
        "query_terms",
        scratch=[pltpu.VMEM((width, held), bf16)],
        work=1,
        dims=dims,
    )
    all_dqs = [dqs[0], over_dp(dqs[1], 1)]
    rounds = spread_rounds(chips)
    terms, *pieces = call(
        spread_kernel,
        [((piece, 2 * width), f32)] + [((piece, 2 * width), bf16)] * len(rounds),
        [keep, over_dp(send, 2), token],
        "join_heads",
        rounds=rounds,
    )
    got = [spread(p, moves) for p, moves in zip(pieces, rounds)]
    for array in got[:-1]:
        (terms,) = call(add_kernel, [((piece, 2 * width), f32)], [terms, array], "add_terms")

    grad_q, token = call(
        finish_query_kernel,
        [((rows, pair * width), bf16), ((8, 128), f32)],
        all_dqs,
        "finish_query",
    )
    grad_k, grad_values = call(
        finish_kernel, [((piece, width), bf16)] * 2, [token, terms, got[-1]], "finish"
    )
    return attn_out, grad_q, grad_k, grad_values


def solution(mesh):
    return jax.shard_map(
        on_device,
        mesh=mesh,
        in_specs=(P("ctx", None), P("ctx", None), P("ctx", None), P("ctx", None), P()),
        out_specs=(P("ctx", "dp"), P("ctx", "dp"), P(("dp", "ctx"), None), P(("dp", "ctx"), None)),
        check_vma=False,
    )
```

```python
import functools
import math

import jax
import jax.numpy as jnp
from jax import lax
from jax.experimental import pallas as pl
from jax.experimental.pallas import tpu as pltpu
from jax.sharding import PartitionSpec as P

NEG = -1e30
LOG2E = 1.4426950408889634
DOC_NUMBERS = 4
KEY_GROUPS = 2
MIB = 1024 * 1024


def place():
    dp_index, ctx_index = lax.axis_index("dp"), lax.axis_index("ctx")
    return dp_index // KEY_GROUPS, dp_index % KEY_GROUPS, ctx_index // 2, ctx_index % 2

NT = (((1,), (1,)), ((), ()))


def home_chip(spot, key_group, chip, chips):
    level = chips // 4
    flip = spot // level * (2 * level) + spot % level
    home = chip ^ flip
    return home ^ ((home // level % 2) ^ key_group) * level


def gather_rounds(chips):
    rounds = [{} for _ in range(2 if chips == 4 else chips - 1)]
    for core in range(2):
        if chips == 4:
            rounds[0][0, 1, core] = (1, 0)
            rounds[0][0, 2, core] = (0, 0)
            rounds[0][1, 2, core] = (1, 1)
            rounds[0][0, 3, core] = (core, 2)
            rounds[1][0, 3, core] = (0, 0)
            rounds[1][1, 3, core] = (1, 1)
            continue
        for flip, moves in enumerate(rounds, 1):
            for home in range(chips):
                group = home // (chips // 4) % 2
                if home ^ flip > home:
                    moves[group, home ^ flip, core] = (group, home)
    return rounds


def spread_rounds(chips):
    return [{chip: (chip + step) % chips for chip in range(chips)} for step in range(1, chips)]


def mask_bias(seg_ref, rows, held):
    _, key_group, chip, core = place()
    seg = seg_ref[...]
    lines = rows // 128
    seg_own = seg_ref[pl.ds((chip * 2 + core) * lines, lines), :]
    start = jnp.zeros((lines, 128), jnp.int32)
    for number in range(1, DOC_NUMBERS):
        before = jnp.sum((seg < number).astype(jnp.float32), axis=(0, 1), keepdims=True)
        start = jnp.where(seg_own == number, before.astype(jnp.int32), start)
    start = jnp.concatenate([start[k : k + 1] for k in range(lines)], axis=1)
    query_pos = (chip * 2 + core) * rows + lax.broadcasted_iota(jnp.int32, (1, rows), 1)
    blocks = held // rows
    bias = []
    for block in range(blocks):
        home = home_chip(block // 2, key_group, chip, blocks) * 2 + (core ^ block % 2)
        key_pos = home * rows + lax.broadcasted_iota(jnp.int32, (rows, rows), 0)
        allowed = (key_pos >= start) & (key_pos <= query_pos)
        bias.append(jnp.where(allowed, 0.0, NEG))
    return bias


def load_kernel(k_hbm, v_hbm, kv_ref, sems):
    width = k_hbm.shape[1]
    copies = [
        pltpu.make_async_copy(k_hbm, kv_ref.at[:, :width], sems.at[0]),
        pltpu.make_async_copy(v_hbm, kv_ref.at[:, width:], sems.at[1]),
    ]
    for copy in copies:
        copy.start()
    for copy in copies:
        copy.wait()


def pick_kernel(*refs, choices):
    out_ref = refs[-1]
    _, key_group, chip, _ = place()
    spot = key_group * (len(choices) // 2) + chip
    for choice in sorted(set(choices)):
        wanted = functools.reduce(
            jnp.logical_or, [spot == k for k, c in enumerate(choices) if c == choice]
        )

        @pl.when(wanted)
        def _():
            out_ref[...] = jnp.zeros_like(out_ref) if choice < 0 else refs[choice][...]


def prep_kernel(
    seg_hbm, q_hbm, g_hbm, q_ref, g_ref, gt_ref, bias_ref, token_ref, seg_ref, sems, *, dims
):
    heads, rows, width, held, ctx_count = dims
    head_group = place()[0]
    seg_copy = pltpu.make_async_copy(seg_hbm, seg_ref, sems.at[2, 0])
    seg_copy.start()
    copies = []
    for head in range(heads):
        source = head_columns(head_group * heads + head, width)
        target = slice(head * width, (head + 1) * width)
        for k, (full, part) in enumerate(((g_hbm, g_ref), (q_hbm, q_ref))):
            copies.append(
                pltpu.make_async_copy(full.at[:, source], part.at[:, target], sems.at[k, head])
            )
            copies[-1].start()
    token_ref[...] = jnp.zeros_like(token_ref)
    seg_copy.wait()
    for k, block in enumerate(mask_bias(seg_ref, rows, held)):
        bias_ref[k * rows : (k + 1) * rows, :] = block
    for head in range(heads):
        cols = slice(head * width, (head + 1) * width)
        copies[2 * head].wait()
        gt_ref[cols, :] = g_ref[:, cols].astype(jnp.float32).T.astype(jnp.bfloat16)
    for head in range(heads):
        copies[2 * head + 1].wait()


def head_columns(head, width):
    return pl.ds(pl.multiple_of(head * width, width), width)


def scores_pass(q_ref, bias_ref, blocks, scores_ref, top_ref, *, dims, first):
    heads, rows, width, held, ctx_count = dims
    for head in range(heads):
        query = q_ref[:, head * width : (head + 1) * width]
        top = None
        for k, kv_ref in enumerate(blocks):
            bias = bias_ref[(first + k) * rows : (first + k + 1) * rows, :]
            raw = lax.dot_general(kv_ref[:, :width], query, NT, preferred_element_type=jnp.float32)
            scores = raw * (width**-0.5 * LOG2E) + bias
            scores_ref[head, k * rows : (k + 1) * rows, :] = scores
            here = jnp.max(scores, axis=0, keepdims=True)
            top = here if top is None else jnp.maximum(top, here)
        top_ref[head : head + 1, :] = top


def transpose_values(blocks, vt_ref, width):
    size = blocks[0].shape[0]
    for k, kv_ref in enumerate(blocks):
        vt = kv_ref[:, width:].astype(jnp.float32).T.astype(jnp.bfloat16)
        vt_ref[:, k * size : (k + 1) * size] = vt


def sums_pass(vt_ref, scores_ref, top, head):
    expd = jnp.exp2(scores_ref[head] - top)
    total = jnp.sum(expd, axis=0, keepdims=True)
    sums = jnp.dot(vt_ref[...], expd.astype(jnp.bfloat16), preferred_element_type=jnp.float32)
    return total, sums


def part_kernel(q_ref, bias_ref, *refs, dims):
    heads, rows, width, held, ctx_count = dims
    *blocks, scores_ref, stats_ref, sums_ref, vt_ref = refs
    transpose_values(blocks, vt_ref, width)
    scores_pass(q_ref, bias_ref, blocks, scores_ref, stats_ref, dims=dims, first=0)
    for head in range(heads):
        total, sums_ref[head] = sums_pass(
            vt_ref, scores_ref, stats_ref[head : head + 1, :], head
        )
        stats_ref[heads + head : heads + head + 1, :] = total


def forward_kernel(
    q_ref, gt_ref, bias_ref, kv_ref, part_ref, part_sums_ref, stats_ref, scores_ref, *refs, dims
):
    heads, rows, width, held, ctx_count = dims
    *outs, top_ref, vt_ref, sums_ref = refs
    pair = heads // KEY_GROUPS
    key_group = place()[1]
    transpose_values([kv_ref], vt_ref, width)
    scores_pass(q_ref, bias_ref, [kv_ref], scores_ref, top_ref, dims=dims, first=held // rows - 1)
    for head in range(heads):
        cols = slice(head * width, (head + 1) * width)
        before = part_ref[head : head + 1, :]
        top = jnp.maximum(top_ref[head : head + 1, :], before)
        share = jnp.exp2(before - top)
        total, accum = sums_pass(vt_ref, scores_ref, top, head)
        total = total + share * part_ref[heads + head : heads + head + 1, :]
        accum = accum + share * part_sums_ref[head]
        delta = jnp.sum(accum * gt_ref[cols, :].astype(jnp.float32), axis=0, keepdims=True)
        for row, value in enumerate((top, total, delta)):
            stats_ref[row * heads + head : row * heads + head + 1, :] = value
        sums_ref[cols, :] = accum.astype(jnp.bfloat16)
    for slot, out_ref in enumerate(outs):
        out_ref[...] = sums_ref[head_columns(key_group ^ slot, pair * width), :]


def dprobs_kernel(g_ref, *refs, dims):
    heads, rows, width, held, ctx_count = dims
    *blocks, dprobs_ref = refs
    for head in range(heads):
        grad = g_ref[:, head * width : (head + 1) * width]
        for part, ref in enumerate(blocks):
            dprobs_ref[head, part * rows : (part + 1) * rows, :] = lax.dot_general(
                ref[:, width:], grad, NT, preferred_element_type=jnp.float32
            )


def merged_stats(stats, heads):
    top = functools.reduce(jnp.maximum, [s[:heads] for s in stats])
    shares = [jnp.exp2(s[:heads] - top) for s in stats]
    total = sum(f * s[heads : 2 * heads] for f, s in zip(shares, stats))
    delta = sum(f * s[2 * heads :] for f, s in zip(shares, stats)) / total
    return top, shares, total, delta


def backward_kernel(q_ref, g_ref, *refs, dims, ahead):
    heads, rows, width, held, ctx_count = dims
    parts = held // rows
    blocks, scores, last_scores, refs = refs[:parts], refs[parts], refs[parts + 1], refs[parts + 2 :]
    dprobs_ref, refs = (refs[0], refs[1:]) if ahead else (None, refs)
    stats = refs[:KEY_GROUPS]
    ds_ref, keep_ref, send_ref, acc_ref = refs[KEY_GROUPS:]
    scale = width**-0.5
    top, _, total, delta = merged_stats([s[...] for s in stats], heads)
    lse = top + jnp.log2(total)
    for head in range(heads):
        cols = slice(head * width, (head + 1) * width)
        query, grad = q_ref[:, cols], g_ref[:, cols]
        for part, ref in enumerate(blocks):
            here = slice(part * rows, (part + 1) * rows)
            row = last_scores[head] if part == parts - 1 else scores[head, here, :]
            probs = jnp.exp2(row - lse[head : head + 1])
            if ahead:
                dprobs = dprobs_ref[head, here, :]
            else:
                dprobs = lax.dot_general(
                    ref[:, width:], grad, NT, preferred_element_type=jnp.float32
                )
            dscores = (probs * (dprobs - delta[head : head + 1])).astype(jnp.bfloat16)
            ds_ref[head, here, :] = dscores
            dv = jnp.dot(probs.astype(jnp.bfloat16), grad, preferred_element_type=jnp.float32)
            dk = jnp.dot(dscores, query, preferred_element_type=jnp.float32)
            if head == 0:
                acc_ref[here, :width] = dk
                acc_ref[here, width:] = dv
            else:
                acc_ref[here, :width] += dk
                acc_ref[here, width:] += dv
    head_group, key_group, chip, core = place()
    chips, piece = ctx_count // 2, rows // 4
    level = chips // 4
    for spot in range(2 * chips):
        here = slice(spot * piece, (spot + 1) * piece)
        target = chip ^ (spot % chips)
        group = head_group ^ (spot // chips)
        block = group * (ctx_count // 2) + key_group * (ctx_count // 4) + target // 2
        flip = block // 2 ^ chip
        slot = flip // (2 * level) * level + flip % level
        line = (slot * 2 + (block % 2 ^ core)) * rows
        for ref, side in ((keep_ref, core), (send_ref, 1 - core)):
            mine = pl.ds(pl.multiple_of(line + (target % 2 * 2 + side) * piece, piece), piece)
            ref[here, :width] = (acc_ref[mine, :width] * scale).astype(ref.dtype)
            ref[here, width:] = acc_ref[mine, width:].astype(ref.dtype)


def query_kernel(*refs, dims):
    heads, rows, width, held, ctx_count = dims
    parts = held // rows
    blocks, ds_ref, refs = refs[:parts], refs[parts], refs[parts + 2 :]
    outs, kt_ref = refs[:KEY_GROUPS], refs[KEY_GROUPS]
    pair = heads // KEY_GROUPS
    key_group = place()[1]
    scale = width**-0.5
    for part, ref in enumerate(blocks):
        here = slice(part * rows, (part + 1) * rows)
        kt_ref[:, here] = ref[:, :width].astype(jnp.float32).T.astype(jnp.bfloat16)
    for slot in range(KEY_GROUPS):
        for part in range(pair):
            head = (key_group ^ slot) * pair + part
            dq = jnp.dot(kt_ref[...], ds_ref[head], preferred_element_type=jnp.float32)
            outs[slot][part * width : (part + 1) * width, :] = (dq * scale).astype(jnp.bfloat16)


def join_kernel(keep_ref, got_ref, kept_ref, send_ref):
    half = kept_ref.shape[0]
    kept_ref[...] = keep_ref[:half, :] + got_ref[:half, :].astype(jnp.float32)
    send = keep_ref[half:, :] + got_ref[half:, :].astype(jnp.float32)
    send_ref[...] = send.astype(jnp.bfloat16)


def spread_kernel(keep_ref, got_ref, token_ref, own_ref, *outs, rounds):
    piece = own_ref.shape[0]
    chip = place()[2]
    own_ref[...] = keep_ref[:piece, :] + got_ref[:piece, :].astype(jnp.float32)
    for out_ref, moves in zip(outs, rounds):
        flip = 0
        for source, target in moves.items():
            flip = jnp.where(chip == source, source ^ target, flip)
        mine = pl.ds(pl.multiple_of(flip * piece, piece), piece)
        out_ref[...] = (keep_ref[mine, :] + got_ref[mine, :].astype(jnp.float32)).astype(
            jnp.bfloat16
        )


def add_kernel(first_ref, second_ref, out_ref):
    out_ref[...] = first_ref[...] + second_ref[...].astype(jnp.float32)


def finish_out_kernel(*refs, dims):
    heads, rows, width, held, ctx_count = dims
    stats, outs = refs[:KEY_GROUPS], refs[KEY_GROUPS : 2 * KEY_GROUPS]
    attn_ref, token_ref = refs[2 * KEY_GROUPS :]
    token_ref[...] = jnp.zeros_like(token_ref)
    pair = heads // KEY_GROUPS
    top, shares, total, _ = merged_stats([s[...] for s in stats], heads)
    own = place()[1] * pair
    row = lax.broadcasted_iota(jnp.int32, (heads, 1), 0)
    for part in range(pair):
        here = slice(part * width, (part + 1) * width)

        def pick(array):
            return jnp.sum(jnp.where(row == own + part, array, 0.0), axis=0, keepdims=True)

        joined = sum(o[here, :].astype(jnp.float32) * pick(f) for o, f in zip(outs, shares))
        attn_ref[:, here] = (joined / pick(total)).T.astype(jnp.bfloat16)


def finish_query_kernel(own_ref, got_ref, piece_ref, gq_ref, passed_ref):
    total = own_ref[...].astype(jnp.float32) + got_ref[...].astype(jnp.float32)
    gq_ref[...] = total.T.astype(jnp.bfloat16)
    passed_ref[...] = piece_ref[...]


def finish_kernel(*refs):
    *terms, gk_ref, gv_ref = refs
    width = gk_ref.shape[1]
    both = sum(r[...].astype(jnp.float32) for r in terms)
    gk_ref[...] = both[:, :width].astype(jnp.bfloat16)
    gv_ref[...] = both[:, width:].astype(jnp.bfloat16)


def on_device(queries, keys, values, out_grad, segment_ids):
    rows = queries.shape[0]
    width = keys.shape[1]
    seq = segment_ids.shape[0]
    dp_count, ctx_count = lax.axis_size("dp"), lax.axis_size("ctx")
    head_groups = dp_count // KEY_GROUPS
    heads = queries.shape[1] // width // head_groups
    pair = heads // KEY_GROUPS
    chips = ctx_count // 2
    held = rows * ctx_count // KEY_GROUPS
    piece = rows // dp_count
    dims = (heads, rows, width, held, ctx_count)
    seg = segment_ids.reshape(seq // 128, 128)
    params = pltpu.CompilerParams(
        vmem_limit_bytes=min(56 * MIB, 12 * MIB + 12 * 4 * held * rows)
    )
    vmem = pl.BlockSpec(memory_space=pltpu.VMEM)
    bf16, f32 = jnp.bfloat16, jnp.float32

    def call(kernel, outs, ins, name, scratch=(), work=0, **static):
        specs = [a[1] if isinstance(a, tuple) else vmem for a in ins]
        arrays = [a[0] if isinstance(a, tuple) else a for a in ins]
        return pl.pallas_call(
            functools.partial(kernel, **static),
            out_shape=[jax.ShapeDtypeStruct(*o) for o in outs],
            in_specs=specs,
            out_specs=[vmem] * len(outs),
            scratch_shapes=list(scratch),
            compiler_params=params,
            cost_estimate=pl.CostEstimate(
                flops=work * 2 * heads * rows * held * width,
                bytes_accessed=sum(math.prod(o[0]) * 2 for o in outs),
                transcendentals=0,
            ),
            name=name,
        )(*arrays)

    def in_hbm(array):
        return pltpu.with_memory_space_constraint(array, pltpu.HBM), pl.BlockSpec(
            memory_space=pltpu.HBM
        )

    def over_dp(array, flip):
        return lax.ppermute(array, "dp", [(d, d ^ flip) for d in range(dp_count)])

    def over_cores(array):
        return lax.ppermute(array, "ctx", [(c, c ^ 1) for c in range(ctx_count)])

    def gathered(array, moves):
        pairs = []
        for d in range(0, dp_count, KEY_GROUPS):
            for (group, chip, core), (source, home) in moves.items():
                start = (d + source) * ctx_count + home * 2 + core
                pairs.append((start, (d + group) * ctx_count + chip * 2 + core))
        return lax.ppermute(array, ("dp", "ctx"), pairs)

    def spread(array, moves):
        pairs = [(a * 2 + core, b * 2 + core) for a, b in moves.items() for core in range(2)]
        return lax.ppermute(array, "ctx", pairs)

    (own_kv,) = call(
        load_kernel,
        [((rows, 2 * width), bf16)],
        [in_hbm(keys), in_hbm(values)],
        "load",
        scratch=[pltpu.SemaphoreType.DMA((2,))],
    )
    query_v, grad_v, grad_t, bias, token = call(
        prep_kernel,
        [
            ((rows, heads * width), bf16),
            ((rows, heads * width), bf16),
            ((heads * width, rows), bf16),
            ((held, rows), f32),
            ((8, 128), f32),
        ],
        [in_hbm(seg), in_hbm(queries), in_hbm(out_grad)],
        "prepare",
        scratch=[pltpu.VMEM(seg.shape, seg.dtype), pltpu.SemaphoreType.DMA((3, heads))],
        work=1,
        dims=dims,
    )
    rounds = gather_rounds(chips)
    sent = [own_kv] + [gathered(own_kv, moves) for moves in rounds]
    blocks = []
    for spot in range(chips // 2):
        choices = []
        for group in range(KEY_GROUPS):
            for chip in range(chips):
                home = home_chip(spot, group, chip, chips)
                spot_key = (group, chip, 0)
                ways = [k for k, m in enumerate(rounds, 1) if m.get(spot_key, (0, -1))[1] == home]
                choices.append(0 if home == chip else ways[0] if home < chip else -1)
        used = sorted(set(choices) - {-1})
        (picked,) = call(
            pick_kernel,
            [((rows, 2 * width), bf16)],
            [sent[k] for k in used] + [token],
            "pick",
            choices=[used.index(c) if c >= 0 else -1 for c in choices],
        )
        blocks += [picked, over_cores(picked)]
    early = held - rows
    scores, part_stats, part_sums = call(
        part_kernel,
        [((heads, early, rows), f32), ((2 * heads, rows), f32), ((heads, width, rows), f32)],
        [query_v, bias] + blocks[:-1],
        "attend_most",
        scratch=[pltpu.VMEM((width, early), bf16)],
        work=2,
        dims=dims,
    )
    stats, last_scores, *outs = call(
        forward_kernel,
        [((3 * heads, rows), f32), ((heads, rows, rows), f32)]
        + [((pair * width, rows), bf16)] * KEY_GROUPS,
        [query_v, grad_t, bias, blocks[-1], part_stats, part_sums],
        "attend",
        scratch=[
            pltpu.VMEM((heads, rows), f32),
            pltpu.VMEM((width, rows), bf16),
            pltpu.VMEM((heads * width, rows), bf16),
        ],
        work=1,
        dims=dims,
    )
    all_stats = [stats, over_dp(stats, 1)]
    all_outs = [outs[0], over_dp(outs[1], 1)]
    ahead = 4 * heads * held * rows <= 8 * MIB
    dprobs = []
    if ahead:
        dprobs = call(
            dprobs_kernel,
            [((heads, held, rows), f32)],
            [grad_v] + blocks,
            "dprobs",
            work=1,
            dims=dims,
        )

    dscores, keep, send = call(
        backward_kernel,
        [
            ((heads, held, rows), bf16),
            ((held // 2, 2 * width), f32),
            ((held // 2, 2 * width), bf16),
        ],
        [query_v, grad_v] + blocks + [scores, last_scores] + list(dprobs) + all_stats,
        "differentiate",
        scratch=[pltpu.VMEM((held, 2 * width), f32)],
        work=4,
        dims=dims,
        ahead=ahead,
    )
    got = over_cores(send)
    attn_out, token = call(
        finish_out_kernel,
        [((rows, pair * width), bf16), ((8, 128), f32)],
        all_stats + all_outs,
        "finish_out",
        dims=dims,
    )
    quarter = held // 4
    keep, send = call(
        join_kernel,
        [((quarter, 2 * width), f32), ((quarter, 2 * width), bf16)],
        [keep, got],
        "join_cores",
    )
    dqs = call(
        query_kernel,
        [((pair * width, rows), bf16)] * KEY_GROUPS,
        blocks + [dscores, keep],
        "query_terms",
        scratch=[pltpu.VMEM((width, held), bf16)],
        work=1,
        dims=dims,
    )
    all_dqs = [dqs[0], over_dp(dqs[1], 1)]
    rounds = spread_rounds(chips)
    terms, *pieces = call(
        spread_kernel,
        [((piece, 2 * width), f32)] + [((piece, 2 * width), bf16)] * len(rounds),
        [keep, over_dp(send, 2), token],
        "join_heads",
        rounds=rounds,
    )
    grad_q, pieces[-1] = call(
        finish_query_kernel,
        [((rows, pair * width), bf16), ((piece, 2 * width), bf16)],
        all_dqs + pieces[-1:],
        "finish_query",
    )
    got = [spread(p, moves) for p, moves in zip(pieces, rounds)]
    for array in got[:-1]:
        (terms,) = call(add_kernel, [((piece, 2 * width), f32)], [terms, array], "add_terms")
    grad_k, grad_values = call(
        finish_kernel, [((piece, width), bf16)] * 2, [terms, got[-1]], "finish"
    )
    return attn_out, grad_q, grad_k, grad_values


def solution(mesh):
    return jax.shard_map(
        on_device,
        mesh=mesh,
        in_specs=(P("ctx", None), P("ctx", None), P("ctx", None), P("ctx", None), P()),
        out_specs=(P("ctx", "dp"), P("ctx", "dp"), P(("dp", "ctx"), None), P(("dp", "ctx"), None)),
        check_vma=False,
    )
```

```python
import functools
import math

import jax
import jax.numpy as jnp
from jax import lax
from jax.experimental import pallas as pl
from jax.experimental.pallas import tpu as pltpu
from jax.sharding import PartitionSpec as P

NEG = -1e30
LOG2E = 1.4426950408889634
DOC_NUMBERS = 4
KEY_GROUPS = 2
MIB = 1024 * 1024


def place():
    dp_index, ctx_index = lax.axis_index("dp"), lax.axis_index("ctx")
    return dp_index // KEY_GROUPS, dp_index % KEY_GROUPS, ctx_index // 2, ctx_index % 2

NT = (((1,), (1,)), ((), ()))


def home_chip(spot, key_group, chip, chips):
    level = chips // 4
    flip = spot // level * (2 * level) + spot % level
    home = chip ^ flip
    return home ^ ((home // level % 2) ^ key_group) * level


def gather_rounds(chips):
    rounds = [{} for _ in range(2 if chips == 4 else chips - 1)]
    for core in range(2):
        if chips == 4:
            rounds[0][0, 1, core] = (1, 0)
            rounds[0][0, 2, core] = (0, 0)
            rounds[0][1, 2, core] = (1, 1)
            rounds[0][0, 3, core] = (core, 2)
            rounds[1][0, 3, core] = (0, 0)
            rounds[1][1, 3, core] = (1, 1)
            continue
        for flip, moves in enumerate(rounds, 1):
            for home in range(chips):
                group = home // (chips // 4) % 2
                if home ^ flip > home:
                    moves[group, home ^ flip, core] = (group, home)
    return rounds


def spread_rounds(chips):
    if chips == 4:
        return [{3: 0, 0: 1, 1: 2}, {2: 0, 3: 1, 0: 2, 1: 3}, {1: 0, 2: 1, 3: 2, 0: 3}, {2: 3}]
    return [{chip: (chip + step) % chips for chip in range(chips)} for step in range(1, chips)]


def mask_bias(seg_ref, rows, held):
    _, key_group, chip, core = place()
    seg = seg_ref[...]
    lines = rows // 128
    seg_own = seg_ref[pl.ds((chip * 2 + core) * lines, lines), :]
    start = jnp.zeros((lines, 128), jnp.int32)
    for number in range(1, DOC_NUMBERS):
        before = jnp.sum((seg < number).astype(jnp.float32), axis=(0, 1), keepdims=True)
        start = jnp.where(seg_own == number, before.astype(jnp.int32), start)
    start = jnp.concatenate([start[k : k + 1] for k in range(lines)], axis=1)
    query_pos = (chip * 2 + core) * rows + lax.broadcasted_iota(jnp.int32, (1, rows), 1)
    blocks = held // rows
    bias = []
    for block in range(blocks):
        home = home_chip(block // 2, key_group, chip, blocks) * 2 + (core ^ block % 2)
        key_pos = home * rows + lax.broadcasted_iota(jnp.int32, (rows, rows), 0)
        allowed = (key_pos >= start) & (key_pos <= query_pos)
        bias.append(jnp.where(allowed, 0.0, NEG))
    return bias


def load_kernel(k_hbm, v_hbm, kv_ref, sems):
    width = k_hbm.shape[1]
    copies = [
        pltpu.make_async_copy(k_hbm, kv_ref.at[:, :width], sems.at[0]),
        pltpu.make_async_copy(v_hbm, kv_ref.at[:, width:], sems.at[1]),
    ]
    for copy in copies:
        copy.start()
    for copy in copies:
        copy.wait()


def pick_kernel(*refs, choices):
    out_ref = refs[-1]
    _, key_group, chip, _ = place()
    spot = key_group * (len(choices) // 2) + chip
    for choice in sorted(set(choices)):
        wanted = functools.reduce(
            jnp.logical_or, [spot == k for k, c in enumerate(choices) if c == choice]
        )

        @pl.when(wanted)
        def _():
            out_ref[...] = jnp.zeros_like(out_ref) if choice < 0 else refs[choice][...]


def prep_kernel(
    seg_hbm, q_hbm, g_hbm, q_ref, g_ref, gt_ref, bias_ref, token_ref, seg_ref, sems, *, dims
):
    heads, rows, width, held, ctx_count = dims
    head_group = place()[0]
    seg_copy = pltpu.make_async_copy(seg_hbm, seg_ref, sems.at[2, 0])
    seg_copy.start()
    copies = []
    for head in range(heads):
        source = head_columns(head_group * heads + head, width)
        target = slice(head * width, (head + 1) * width)
        for k, (full, part) in enumerate(((g_hbm, g_ref), (q_hbm, q_ref))):
            copies.append(
                pltpu.make_async_copy(full.at[:, source], part.at[:, target], sems.at[k, head])
            )
            copies[-1].start()
    token_ref[...] = jnp.zeros_like(token_ref)
    seg_copy.wait()
    for k, block in enumerate(mask_bias(seg_ref, rows, held)):
        bias_ref[k * rows : (k + 1) * rows, :] = block
    for head in range(heads):
        cols = slice(head * width, (head + 1) * width)
        copies[2 * head].wait()
        gt_ref[cols, :] = g_ref[:, cols].astype(jnp.float32).T.astype(jnp.bfloat16)
    for head in range(heads):
        copies[2 * head + 1].wait()


def head_columns(head, width):
    return pl.ds(pl.multiple_of(head * width, width), width)


def scores_pass(q_ref, bias_ref, blocks, scores_ref, top_ref, *, dims, first):
    heads, rows, width, held, ctx_count = dims
    for head in range(heads):
        query = q_ref[:, head * width : (head + 1) * width]
        top = None
        for k, kv_ref in enumerate(blocks):
            bias = bias_ref[(first + k) * rows : (first + k + 1) * rows, :]
            raw = lax.dot_general(kv_ref[:, :width], query, NT, preferred_element_type=jnp.float32)
            scores = raw * (width**-0.5 * LOG2E) + bias
            scores_ref[head, k * rows : (k + 1) * rows, :] = scores
            here = jnp.max(scores, axis=0, keepdims=True)
            top = here if top is None else jnp.maximum(top, here)
        top_ref[head : head + 1, :] = top


def transpose_values(blocks, vt_ref, width):
    size = blocks[0].shape[0]
    for k, kv_ref in enumerate(blocks):
        vt = kv_ref[:, width:].astype(jnp.float32).T.astype(jnp.bfloat16)
        vt_ref[:, k * size : (k + 1) * size] = vt


def sums_pass(vt_ref, scores_ref, top, head):
    expd = jnp.exp2(scores_ref[head] - top)
    total = jnp.sum(expd, axis=0, keepdims=True)
    sums = jnp.dot(vt_ref[...], expd.astype(jnp.bfloat16), preferred_element_type=jnp.float32)
    return total, sums


def part_kernel(q_ref, bias_ref, *refs, dims):
    heads, rows, width, held, ctx_count = dims
    *blocks, scores_ref, stats_ref, sums_ref, vt_ref = refs
    transpose_values(blocks, vt_ref, width)
    scores_pass(q_ref, bias_ref, blocks, scores_ref, stats_ref, dims=dims, first=0)
    for head in range(heads):
        total, sums_ref[head] = sums_pass(
            vt_ref, scores_ref, stats_ref[head : head + 1, :], head
        )
        stats_ref[heads + head : heads + head + 1, :] = total


def forward_kernel(
    q_ref, gt_ref, bias_ref, kv_ref, part_ref, part_sums_ref, stats_ref, scores_ref, *refs, dims
):
    heads, rows, width, held, ctx_count = dims
    *outs, top_ref, vt_ref, sums_ref = refs
    pair = heads // KEY_GROUPS
    key_group = place()[1]
    transpose_values([kv_ref], vt_ref, width)
    scores_pass(q_ref, bias_ref, [kv_ref], scores_ref, top_ref, dims=dims, first=held // rows - 1)
    for head in range(heads):
        cols = slice(head * width, (head + 1) * width)
        before = part_ref[head : head + 1, :]
        top = jnp.maximum(top_ref[head : head + 1, :], before)
        share = jnp.exp2(before - top)
        total, accum = sums_pass(vt_ref, scores_ref, top, head)
        total = total + share * part_ref[heads + head : heads + head + 1, :]
        accum = accum + share * part_sums_ref[head]
        delta = jnp.sum(accum * gt_ref[cols, :].astype(jnp.float32), axis=0, keepdims=True)
        for row, value in enumerate((top, total, delta)):
            stats_ref[row * heads + head : row * heads + head + 1, :] = value
        sums_ref[cols, :] = accum.astype(jnp.bfloat16)
    for slot, out_ref in enumerate(outs):
        out_ref[...] = sums_ref[head_columns(key_group ^ slot, pair * width), :]


def dprobs_kernel(g_ref, *refs, dims):
    heads, rows, width, held, ctx_count = dims
    *blocks, dprobs_ref = refs
    for head in range(heads):
        grad = g_ref[:, head * width : (head + 1) * width]
        for part, ref in enumerate(blocks):
            dprobs_ref[head, part * rows : (part + 1) * rows, :] = lax.dot_general(
                ref[:, width:], grad, NT, preferred_element_type=jnp.float32
            )


def merged_stats(stats, heads):
    top = functools.reduce(jnp.maximum, [s[:heads] for s in stats])
    shares = [jnp.exp2(s[:heads] - top) for s in stats]
    total = sum(f * s[heads : 2 * heads] for f, s in zip(shares, stats))
    delta = sum(f * s[2 * heads :] for f, s in zip(shares, stats)) / total
    return top, shares, total, delta


def backward_kernel(q_ref, g_ref, *refs, dims, ahead):
    heads, rows, width, held, ctx_count = dims
    parts = held // rows
    blocks, scores, last_scores, refs = refs[:parts], refs[parts], refs[parts + 1], refs[parts + 2 :]
    dprobs_ref, refs = (refs[0], refs[1:]) if ahead else (None, refs)
    stats = refs[:KEY_GROUPS]
    ds_ref, keep_ref, send_ref, acc_ref = refs[KEY_GROUPS:]
    scale = width**-0.5
    top, _, total, delta = merged_stats([s[...] for s in stats], heads)
    lse = top + jnp.log2(total)
    for head in range(heads):
        cols = slice(head * width, (head + 1) * width)
        query, grad = q_ref[:, cols], g_ref[:, cols]
        for part, ref in enumerate(blocks):
            here = slice(part * rows, (part + 1) * rows)
            row = last_scores[head] if part == parts - 1 else scores[head, here, :]
            probs = jnp.exp2(row - lse[head : head + 1])
            if ahead:
                dprobs = dprobs_ref[head, here, :]
            else:
                dprobs = lax.dot_general(
                    ref[:, width:], grad, NT, preferred_element_type=jnp.float32
                )
            dscores = (probs * (dprobs - delta[head : head + 1])).astype(jnp.bfloat16)
            ds_ref[head, here, :] = dscores
            dv = jnp.dot(probs.astype(jnp.bfloat16), grad, preferred_element_type=jnp.float32)
            dk = jnp.dot(dscores, query, preferred_element_type=jnp.float32)
            if head == 0:
                acc_ref[here, :width] = dk
                acc_ref[here, width:] = dv
            else:
                acc_ref[here, :width] += dk
                acc_ref[here, width:] += dv
    head_group, key_group, chip, core = place()
    chips, piece = ctx_count // 2, rows // 4
    level = chips // 4
    for spot in range(2 * chips):
        here = slice(spot * piece, (spot + 1) * piece)
        target = chip ^ (spot % chips)
        group = head_group ^ (spot // chips)
        block = group * (ctx_count // 2) + key_group * (ctx_count // 4) + target // 2
        flip = block // 2 ^ chip
        slot = flip // (2 * level) * level + flip % level
        line = (slot * 2 + (block % 2 ^ core)) * rows
        for ref, side in ((keep_ref, core), (send_ref, 1 - core)):
            mine = pl.ds(pl.multiple_of(line + (target % 2 * 2 + side) * piece, piece), piece)
            ref[here, :width] = (acc_ref[mine, :width] * scale).astype(ref.dtype)
            ref[here, width:] = acc_ref[mine, width:].astype(ref.dtype)


def query_kernel(*refs, dims):
    heads, rows, width, held, ctx_count = dims
    parts = held // rows
    blocks, ds_ref, refs = refs[:parts], refs[parts], refs[parts + 2 :]
    outs, kt_ref = refs[:KEY_GROUPS], refs[KEY_GROUPS]
    pair = heads // KEY_GROUPS
    key_group = place()[1]
    scale = width**-0.5
    for part, ref in enumerate(blocks):
        here = slice(part * rows, (part + 1) * rows)
        kt_ref[:, here] = ref[:, :width].astype(jnp.float32).T.astype(jnp.bfloat16)
    for slot in range(KEY_GROUPS):
        for part in range(pair):
            head = (key_group ^ slot) * pair + part
            dq = jnp.dot(kt_ref[...], ds_ref[head], preferred_element_type=jnp.float32)
            outs[slot][part * width : (part + 1) * width, :] = (dq * scale).astype(jnp.bfloat16)


def join_kernel(keep_ref, got_ref, kept_ref, send_ref):
    half = kept_ref.shape[0]
    kept_ref[...] = keep_ref[:half, :] + got_ref[:half, :].astype(jnp.float32)
    send = keep_ref[half:, :] + got_ref[half:, :].astype(jnp.float32)
    send_ref[...] = send.astype(jnp.bfloat16)


def spread_kernel(keep_ref, got_ref, token_ref, own_ref, *outs, rounds):
    piece = own_ref.shape[0]
    chip = place()[2]
    own_ref[...] = keep_ref[:piece, :] + got_ref[:piece, :].astype(jnp.float32)
    for out_ref, moves in zip(outs, rounds):
        flip = 0
        for source, target in moves.items():
            flip = jnp.where(chip == source, source ^ target, flip)
        mine = pl.ds(pl.multiple_of(flip * piece, piece), piece)
        out_ref[...] = (keep_ref[mine, :] + got_ref[mine, :].astype(jnp.float32)).astype(
            jnp.bfloat16
        )


def add_kernel(first_ref, second_ref, out_ref):
    out_ref[...] = first_ref[...] + second_ref[...].astype(jnp.float32)


def finish_out_kernel(*refs, dims):
    heads, rows, width, held, ctx_count = dims
    stats, outs = refs[:KEY_GROUPS], refs[KEY_GROUPS : 2 * KEY_GROUPS]
    attn_ref, token_ref = refs[2 * KEY_GROUPS :]
    token_ref[...] = jnp.zeros_like(token_ref)
    pair = heads // KEY_GROUPS
    top, shares, total, _ = merged_stats([s[...] for s in stats], heads)
    own = place()[1] * pair
    row = lax.broadcasted_iota(jnp.int32, (heads, 1), 0)
    for part in range(pair):
        here = slice(part * width, (part + 1) * width)

        def pick(array):
            return jnp.sum(jnp.where(row == own + part, array, 0.0), axis=0, keepdims=True)

        joined = sum(o[here, :].astype(jnp.float32) * pick(f) for o, f in zip(outs, shares))
        attn_ref[:, here] = (joined / pick(total)).T.astype(jnp.bfloat16)


def finish_query_kernel(own_ref, got_ref, gq_ref, token_ref):
    total = own_ref[...].astype(jnp.float32) + got_ref[...].astype(jnp.float32)
    gq_ref[...] = total.T.astype(jnp.bfloat16)
    token_ref[...] = jnp.zeros_like(token_ref)


def finish_kernel(token_ref, *refs):
    *terms, gk_ref, gv_ref = refs
    width = gk_ref.shape[1]
    both = sum(r[...].astype(jnp.float32) for r in terms)
    gk_ref[...] = both[:, :width].astype(jnp.bfloat16)
    gv_ref[...] = both[:, width:].astype(jnp.bfloat16)


def on_device(queries, keys, values, out_grad, segment_ids):
    rows = queries.shape[0]
    width = keys.shape[1]
    seq = segment_ids.shape[0]
    dp_count, ctx_count = lax.axis_size("dp"), lax.axis_size("ctx")
    head_groups = dp_count // KEY_GROUPS
    heads = queries.shape[1] // width // head_groups
    pair = heads // KEY_GROUPS
    chips = ctx_count // 2
    held = rows * ctx_count // KEY_GROUPS
    piece = rows // dp_count
    dims = (heads, rows, width, held, ctx_count)
    seg = segment_ids.reshape(seq // 128, 128)
    params = pltpu.CompilerParams(
        vmem_limit_bytes=min(56 * MIB, 12 * MIB + 12 * 4 * held * rows)
    )
    vmem = pl.BlockSpec(memory_space=pltpu.VMEM)
    bf16, f32 = jnp.bfloat16, jnp.float32

    def call(kernel, outs, ins, name, scratch=(), work=0, **static):
        specs = [a[1] if isinstance(a, tuple) else vmem for a in ins]
        arrays = [a[0] if isinstance(a, tuple) else a for a in ins]
        return pl.pallas_call(
            functools.partial(kernel, **static),
            out_shape=[jax.ShapeDtypeStruct(*o) for o in outs],
            in_specs=specs,
            out_specs=[vmem] * len(outs),
            scratch_shapes=list(scratch),
            compiler_params=params,
            cost_estimate=pl.CostEstimate(
                flops=work * 2 * heads * rows * held * width,
                bytes_accessed=sum(math.prod(o[0]) * 2 for o in outs),
                transcendentals=0,
            ),
            name=name,
        )(*arrays)

    def in_hbm(array):
        return pltpu.with_memory_space_constraint(array, pltpu.HBM), pl.BlockSpec(
            memory_space=pltpu.HBM
        )

    def over_dp(array, flip):
        return lax.ppermute(array, "dp", [(d, d ^ flip) for d in range(dp_count)])

    def over_cores(array):
        return lax.ppermute(array, "ctx", [(c, c ^ 1) for c in range(ctx_count)])

    def gathered(array, moves):
        pairs = []
        for d in range(0, dp_count, KEY_GROUPS):
            for (group, chip, core), (source, home) in moves.items():
                start = (d + source) * ctx_count + home * 2 + core
                pairs.append((start, (d + group) * ctx_count + chip * 2 + core))
        return lax.ppermute(array, ("dp", "ctx"), pairs)

    def spread(array, moves):
        pairs = [(a * 2 + core, b * 2 + core) for a, b in moves.items() for core in range(2)]
        return lax.ppermute(array, "ctx", pairs)

    (own_kv,) = call(
        load_kernel,
        [((rows, 2 * width), bf16)],
        [in_hbm(keys), in_hbm(values)],
        "load",
        scratch=[pltpu.SemaphoreType.DMA((2,))],
    )
    query_v, grad_v, grad_t, bias, token = call(
        prep_kernel,
        [
            ((rows, heads * width), bf16),
            ((rows, heads * width), bf16),
            ((heads * width, rows), bf16),
            ((held, rows), f32),
            ((8, 128), f32),
        ],
        [in_hbm(seg), in_hbm(queries), in_hbm(out_grad)],
        "prepare",
        scratch=[pltpu.VMEM(seg.shape, seg.dtype), pltpu.SemaphoreType.DMA((3, heads))],
        work=1,
        dims=dims,
    )
    rounds = gather_rounds(chips)
    sent = [own_kv] + [gathered(own_kv, moves) for moves in rounds]
    blocks = []
    for spot in range(chips // 2):
        choices = []
        for group in range(KEY_GROUPS):
            for chip in range(chips):
                home = home_chip(spot, group, chip, chips)
                spot_key = (group, chip, 0)
                ways = [k for k, m in enumerate(rounds, 1) if m.get(spot_key, (0, -1))[1] == home]
                choices.append(0 if home == chip else ways[0] if home < chip else -1)
        used = sorted(set(choices) - {-1})
        (picked,) = call(
            pick_kernel,
            [((rows, 2 * width), bf16)],
            [sent[k] for k in used] + [token],
            "pick",
            choices=[used.index(c) if c >= 0 else -1 for c in choices],
        )
        blocks += [picked, over_cores(picked)]
    early = held - rows
    scores, part_stats, part_sums = call(
        part_kernel,
        [((heads, early, rows), f32), ((2 * heads, rows), f32), ((heads, width, rows), f32)],
        [query_v, bias] + blocks[:-1],
        "attend_most",
        scratch=[pltpu.VMEM((width, early), bf16)],
        work=2,
        dims=dims,
    )
    stats, last_scores, *outs = call(
        forward_kernel,
        [((3 * heads, rows), f32), ((heads, rows, rows), f32)]
        + [((pair * width, rows), bf16)] * KEY_GROUPS,
        [query_v, grad_t, bias, blocks[-1], part_stats, part_sums],
        "attend",
        scratch=[
            pltpu.VMEM((heads, rows), f32),
            pltpu.VMEM((width, rows), bf16),
            pltpu.VMEM((heads * width, rows), bf16),
        ],
        work=1,
        dims=dims,
    )
    all_stats = [stats, over_dp(stats, 1)]
    all_outs = [outs[0], over_dp(outs[1], 1)]
    ahead = 4 * heads * held * rows <= 8 * MIB
    dprobs = []
    if ahead:
        dprobs = call(
            dprobs_kernel,
            [((heads, held, rows), f32)],
            [grad_v] + blocks,
            "dprobs",
            work=1,
            dims=dims,
        )

    dscores, keep, send = call(
        backward_kernel,
        [
            ((heads, held, rows), bf16),
            ((held // 2, 2 * width), f32),
            ((held // 2, 2 * width), bf16),
        ],
        [query_v, grad_v] + blocks + [scores, last_scores] + list(dprobs) + all_stats,
        "differentiate",
        scratch=[pltpu.VMEM((held, 2 * width), f32)],
        work=4,
        dims=dims,
        ahead=ahead,
    )
    got = over_cores(send)
    attn_out, token = call(
        finish_out_kernel,
        [((rows, pair * width), bf16), ((8, 128), f32)],
        all_stats + all_outs,
        "finish_out",
        dims=dims,
    )
    quarter = held // 4
    keep, send = call(
        join_kernel,
        [((quarter, 2 * width), f32), ((quarter, 2 * width), bf16)],
        [keep, got],
        "join_cores",
    )
    dqs = call(
        query_kernel,
        [((pair * width, rows), bf16)] * KEY_GROUPS,
        blocks + [dscores, keep],
        "query_terms",
        scratch=[pltpu.VMEM((width, held), bf16)],
        work=1,
        dims=dims,
    )
    all_dqs = [dqs[0], over_dp(dqs[1], 1)]
    rounds = spread_rounds(chips)
    terms, *pieces = call(
        spread_kernel,
        [((piece, 2 * width), f32)] + [((piece, 2 * width), bf16)] * len(rounds),
        [keep, over_dp(send, 2), token],
        "join_heads",
        rounds=rounds,
    )
    grad_q, token = call(
        finish_query_kernel,
        [((rows, pair * width), bf16), ((8, 128), f32)],
        all_dqs,
        "finish_query",
    )
    got = [spread(p, moves) for p, moves in zip(pieces, rounds)]
    for array in got[:-1]:
        (terms,) = call(add_kernel, [((piece, 2 * width), f32)], [terms, array], "add_terms")
    grad_k, grad_values = call(
        finish_kernel, [((piece, width), bf16)] * 2, [token, terms, got[-1]], "finish"
    )
    return attn_out, grad_q, grad_k, grad_values


def solution(mesh):
    return jax.shard_map(
        on_device,
        mesh=mesh,
        in_specs=(P("ctx", None), P("ctx", None), P("ctx", None), P("ctx", None), P()),
        out_specs=(P("ctx", "dp"), P("ctx", "dp"), P(("dp", "ctx"), None), P(("dp", "ctx"), None)),
        check_vma=False,
    )
```

```python
import functools
import math

import jax
import jax.numpy as jnp
from jax import lax
from jax.experimental import pallas as pl
from jax.experimental.pallas import tpu as pltpu
from jax.sharding import PartitionSpec as P

NEG = -1e30
LOG2E = 1.4426950408889634
DOC_NUMBERS = 4
KEY_GROUPS = 2
MIB = 1024 * 1024


def place():
    dp_index, ctx_index = lax.axis_index("dp"), lax.axis_index("ctx")
    return dp_index // KEY_GROUPS, dp_index % KEY_GROUPS, ctx_index // 2, ctx_index % 2

NT = (((1,), (1,)), ((), ()))


def home_chip(spot, key_group, chip, chips):
    level = chips // 4
    flip = spot // level * (2 * level) + spot % level
    home = chip ^ flip
    return home ^ ((home // level % 2) ^ key_group) * level


def gather_rounds(chips):
    rounds = [{} for _ in range(2 if chips == 4 else chips - 1)]
    for core in range(2):
        if chips == 4:
            rounds[0][0, 1, core] = (1, 0)
            rounds[0][0, 2, core] = (0, 0)
            rounds[0][1, 2, core] = (1, 1)
            rounds[0][0, 3, core] = (core, 2)
            rounds[1][0, 3, core] = (0, 0)
            rounds[1][1, 3, core] = (1, 1)
            continue
        for flip, moves in enumerate(rounds, 1):
            for home in range(chips):
                group = home // (chips // 4) % 2
                if home ^ flip > home:
                    moves[group, home ^ flip, core] = (group, home)
    return rounds


def spread_rounds(chips):
    steps = sorted(range(1, chips), key=lambda step: min(step, chips - step))
    return [{chip: (chip + step) % chips for chip in range(chips)} for step in steps]


def mask_bias(seg_ref, rows, held):
    _, key_group, chip, core = place()
    seg = seg_ref[...]
    lines = rows // 128
    seg_own = seg_ref[pl.ds((chip * 2 + core) * lines, lines), :]
    start = jnp.zeros((lines, 128), jnp.int32)
    for number in range(1, DOC_NUMBERS):
        before = jnp.sum((seg < number).astype(jnp.float32), axis=(0, 1), keepdims=True)
        start = jnp.where(seg_own == number, before.astype(jnp.int32), start)
    start = jnp.concatenate([start[k : k + 1] for k in range(lines)], axis=1)
    query_pos = (chip * 2 + core) * rows + lax.broadcasted_iota(jnp.int32, (1, rows), 1)
    blocks = held // rows
    bias = []
    for block in range(blocks):
        home = home_chip(block // 2, key_group, chip, blocks) * 2 + (core ^ block % 2)
        key_pos = home * rows + lax.broadcasted_iota(jnp.int32, (rows, rows), 0)
        allowed = (key_pos >= start) & (key_pos <= query_pos)
        bias.append(jnp.where(allowed, 0.0, NEG))
    return bias


def load_kernel(k_hbm, v_hbm, kv_ref, sems):
    width = k_hbm.shape[1]
    copies = [
        pltpu.make_async_copy(k_hbm, kv_ref.at[:, :width], sems.at[0]),
        pltpu.make_async_copy(v_hbm, kv_ref.at[:, width:], sems.at[1]),
    ]
    for copy in copies:
        copy.start()
    for copy in copies:
        copy.wait()


def pick_kernel(*refs, choices):
    out_ref = refs[-1]
    _, key_group, chip, _ = place()
    spot = key_group * (len(choices) // 2) + chip
    for choice in sorted(set(choices)):
        wanted = functools.reduce(
            jnp.logical_or, [spot == k for k, c in enumerate(choices) if c == choice]
        )

        @pl.when(wanted)
        def _():
            out_ref[...] = jnp.zeros_like(out_ref) if choice < 0 else refs[choice][...]


def prep_kernel(
    seg_hbm, q_hbm, g_hbm, q_ref, g_ref, gt_ref, bias_ref, token_ref, seg_ref, sems, *, dims
):
    heads, rows, width, held, ctx_count = dims
    head_group = place()[0]
    seg_copy = pltpu.make_async_copy(seg_hbm, seg_ref, sems.at[2, 0])
    seg_copy.start()
    copies = []
    for head in range(heads):
        source = head_columns(head_group * heads + head, width)
        target = slice(head * width, (head + 1) * width)
        for k, (full, part) in enumerate(((g_hbm, g_ref), (q_hbm, q_ref))):
            copies.append(
                pltpu.make_async_copy(full.at[:, source], part.at[:, target], sems.at[k, head])
            )
            copies[-1].start()
    token_ref[...] = jnp.zeros_like(token_ref)
    seg_copy.wait()
    for k, block in enumerate(mask_bias(seg_ref, rows, held)):
        bias_ref[k * rows : (k + 1) * rows, :] = block
    for head in range(heads):
        cols = slice(head * width, (head + 1) * width)
        copies[2 * head].wait()
        gt_ref[cols, :] = g_ref[:, cols].astype(jnp.float32).T.astype(jnp.bfloat16)
    for head in range(heads):
        copies[2 * head + 1].wait()


def head_columns(head, width):
    return pl.ds(pl.multiple_of(head * width, width), width)


def scores_pass(q_ref, bias_ref, blocks, scores_ref, top_ref, *, dims, first):
    heads, rows, width, held, ctx_count = dims
    for head in range(heads):
        query = q_ref[:, head * width : (head + 1) * width]
        top = None
        for k, kv_ref in enumerate(blocks):
            bias = bias_ref[(first + k) * rows : (first + k + 1) * rows, :]
            raw = lax.dot_general(kv_ref[:, :width], query, NT, preferred_element_type=jnp.float32)
            scores = raw * (width**-0.5 * LOG2E) + bias
            scores_ref[head, k * rows : (k + 1) * rows, :] = scores
            here = jnp.max(scores, axis=0, keepdims=True)
            top = here if top is None else jnp.maximum(top, here)
        top_ref[head : head + 1, :] = top


def transpose_values(blocks, vt_ref, width):
    size = blocks[0].shape[0]
    for k, kv_ref in enumerate(blocks):
        vt = kv_ref[:, width:].astype(jnp.float32).T.astype(jnp.bfloat16)
        vt_ref[:, k * size : (k + 1) * size] = vt


def sums_pass(vt_ref, scores_ref, top, head):
    expd = jnp.exp2(scores_ref[head] - top)
    total = jnp.sum(expd, axis=0, keepdims=True)
    sums = jnp.dot(vt_ref[...], expd.astype(jnp.bfloat16), preferred_element_type=jnp.float32)
    return total, sums


def part_kernel(q_ref, bias_ref, *refs, dims):
    heads, rows, width, held, ctx_count = dims
    *blocks, scores_ref, stats_ref, sums_ref, vt_ref = refs
    transpose_values(blocks, vt_ref, width)
    scores_pass(q_ref, bias_ref, blocks, scores_ref, stats_ref, dims=dims, first=0)
    for head in range(heads):
        total, sums_ref[head] = sums_pass(
            vt_ref, scores_ref, stats_ref[head : head + 1, :], head
        )
        stats_ref[heads + head : heads + head + 1, :] = total


def forward_kernel(
    q_ref, gt_ref, bias_ref, kv_ref, part_ref, part_sums_ref, stats_ref, scores_ref, *refs, dims
):
    heads, rows, width, held, ctx_count = dims
    *outs, top_ref, vt_ref, sums_ref = refs
    pair = heads // KEY_GROUPS
    key_group = place()[1]
    transpose_values([kv_ref], vt_ref, width)
    scores_pass(q_ref, bias_ref, [kv_ref], scores_ref, top_ref, dims=dims, first=held // rows - 1)
    for head in range(heads):
        cols = slice(head * width, (head + 1) * width)
        before = part_ref[head : head + 1, :]
        top = jnp.maximum(top_ref[head : head + 1, :], before)
        share = jnp.exp2(before - top)
        total, accum = sums_pass(vt_ref, scores_ref, top, head)
        total = total + share * part_ref[heads + head : heads + head + 1, :]
        accum = accum + share * part_sums_ref[head]
        delta = jnp.sum(accum * gt_ref[cols, :].astype(jnp.float32), axis=0, keepdims=True)
        for row, value in enumerate((top, total, delta)):
            stats_ref[row * heads + head : row * heads + head + 1, :] = value
        sums_ref[cols, :] = accum.astype(jnp.bfloat16)
    for slot, out_ref in enumerate(outs):
        out_ref[...] = sums_ref[head_columns(key_group ^ slot, pair * width), :]


def dprobs_kernel(g_ref, *refs, dims):
    heads, rows, width, held, ctx_count = dims
    *blocks, dprobs_ref = refs
    for head in range(heads):
        grad = g_ref[:, head * width : (head + 1) * width]
        for part, ref in enumerate(blocks):
            dprobs_ref[head, part * rows : (part + 1) * rows, :] = lax.dot_general(
                ref[:, width:], grad, NT, preferred_element_type=jnp.float32
            )


def merged_stats(stats, heads):
    top = functools.reduce(jnp.maximum, [s[:heads] for s in stats])
    shares = [jnp.exp2(s[:heads] - top) for s in stats]
    total = sum(f * s[heads : 2 * heads] for f, s in zip(shares, stats))
    delta = sum(f * s[2 * heads :] for f, s in zip(shares, stats)) / total
    return top, shares, total, delta


def backward_kernel(q_ref, g_ref, *refs, dims, ahead):
    heads, rows, width, held, ctx_count = dims
    parts = held // rows
    blocks, scores, last_scores, refs = refs[:parts], refs[parts], refs[parts + 1], refs[parts + 2 :]
    dprobs_ref, refs = (refs[0], refs[1:]) if ahead else (None, refs)
    stats = refs[:KEY_GROUPS]
    ds_ref, keep_ref, send_ref, acc_ref = refs[KEY_GROUPS:]
    scale = width**-0.5
    top, _, total, delta = merged_stats([s[...] for s in stats], heads)
    lse = top + jnp.log2(total)
    for head in range(heads):
        cols = slice(head * width, (head + 1) * width)
        query, grad = q_ref[:, cols], g_ref[:, cols]
        for part, ref in enumerate(blocks):
            here = slice(part * rows, (part + 1) * rows)
            row = last_scores[head] if part == parts - 1 else scores[head, here, :]
            probs = jnp.exp2(row - lse[head : head + 1])
            if ahead:
                dprobs = dprobs_ref[head, here, :]
            else:
                dprobs = lax.dot_general(
                    ref[:, width:], grad, NT, preferred_element_type=jnp.float32
                )
            dscores = (probs * (dprobs - delta[head : head + 1])).astype(jnp.bfloat16)
            ds_ref[head, here, :] = dscores
            dv = jnp.dot(probs.astype(jnp.bfloat16), grad, preferred_element_type=jnp.float32)
            dk = jnp.dot(dscores, query, preferred_element_type=jnp.float32)
            if head == 0:
                acc_ref[here, :width] = dk
                acc_ref[here, width:] = dv
            else:
                acc_ref[here, :width] += dk
                acc_ref[here, width:] += dv
    head_group, key_group, chip, core = place()
    chips, piece = ctx_count // 2, rows // 4
    level = chips // 4
    for spot in range(2 * chips):
        here = slice(spot * piece, (spot + 1) * piece)
        target = chip ^ (spot % chips)
        group = head_group ^ (spot // chips)
        block = group * (ctx_count // 2) + key_group * (ctx_count // 4) + target // 2
        flip = block // 2 ^ chip
        slot = flip // (2 * level) * level + flip % level
        line = (slot * 2 + (block % 2 ^ core)) * rows
        for ref, side in ((keep_ref, core), (send_ref, 1 - core)):
            mine = pl.ds(pl.multiple_of(line + (target % 2 * 2 + side) * piece, piece), piece)
            ref[here, :width] = (acc_ref[mine, :width] * scale).astype(ref.dtype)
            ref[here, width:] = acc_ref[mine, width:].astype(ref.dtype)


def query_kernel(*refs, dims):
    heads, rows, width, held, ctx_count = dims
    parts = held // rows
    blocks, ds_ref, refs = refs[:parts], refs[parts], refs[parts + 2 :]
    outs, kt_ref = refs[:KEY_GROUPS], refs[KEY_GROUPS]
    pair = heads // KEY_GROUPS
    key_group = place()[1]
    scale = width**-0.5
    for part, ref in enumerate(blocks):
        here = slice(part * rows, (part + 1) * rows)
        kt_ref[:, here] = ref[:, :width].astype(jnp.float32).T.astype(jnp.bfloat16)
    for slot in range(KEY_GROUPS):
        for part in range(pair):
            head = (key_group ^ slot) * pair + part
            dq = jnp.dot(kt_ref[...], ds_ref[head], preferred_element_type=jnp.float32)
            outs[slot][part * width : (part + 1) * width, :] = (dq * scale).astype(jnp.bfloat16)


def join_kernel(keep_ref, got_ref, kept_ref, send_ref):
    half = kept_ref.shape[0]
    kept_ref[...] = keep_ref[:half, :] + got_ref[:half, :].astype(jnp.float32)
    send = keep_ref[half:, :] + got_ref[half:, :].astype(jnp.float32)
    send_ref[...] = send.astype(jnp.bfloat16)


def spread_kernel(keep_ref, got_ref, token_ref, own_ref, *outs, rounds):
    piece = own_ref.shape[0]
    chip = place()[2]
    own_ref[...] = keep_ref[:piece, :] + got_ref[:piece, :].astype(jnp.float32)
    for out_ref, moves in zip(outs, rounds):
        flip = 0
        for source, target in moves.items():
            flip = jnp.where(chip == source, source ^ target, flip)
        mine = pl.ds(pl.multiple_of(flip * piece, piece), piece)
        out_ref[...] = (keep_ref[mine, :] + got_ref[mine, :].astype(jnp.float32)).astype(
            jnp.bfloat16
        )


def add_kernel(first_ref, second_ref, out_ref):
    out_ref[...] = first_ref[...] + second_ref[...].astype(jnp.float32)


def finish_out_kernel(*refs, dims):
    heads, rows, width, held, ctx_count = dims
    stats, outs = refs[:KEY_GROUPS], refs[KEY_GROUPS : 2 * KEY_GROUPS]
    attn_ref, token_ref = refs[2 * KEY_GROUPS :]
    token_ref[...] = jnp.zeros_like(token_ref)
    pair = heads // KEY_GROUPS
    top, shares, total, _ = merged_stats([s[...] for s in stats], heads)
    own = place()[1] * pair
    row = lax.broadcasted_iota(jnp.int32, (heads, 1), 0)
    for part in range(pair):
        here = slice(part * width, (part + 1) * width)

        def pick(array):
            return jnp.sum(jnp.where(row == own + part, array, 0.0), axis=0, keepdims=True)

        joined = sum(o[here, :].astype(jnp.float32) * pick(f) for o, f in zip(outs, shares))
        attn_ref[:, here] = (joined / pick(total)).T.astype(jnp.bfloat16)


def finish_query_kernel(own_ref, got_ref, gq_ref, token_ref):
    total = own_ref[...].astype(jnp.float32) + got_ref[...].astype(jnp.float32)
    gq_ref[...] = total.T.astype(jnp.bfloat16)
    token_ref[...] = jnp.zeros_like(token_ref)


def finish_kernel(token_ref, *refs):
    *terms, gk_ref, gv_ref = refs
    width = gk_ref.shape[1]
    both = sum(r[...].astype(jnp.float32) for r in terms)
    gk_ref[...] = both[:, :width].astype(jnp.bfloat16)
    gv_ref[...] = both[:, width:].astype(jnp.bfloat16)


def on_device(queries, keys, values, out_grad, segment_ids):
    rows = queries.shape[0]
    width = keys.shape[1]
    seq = segment_ids.shape[0]
    dp_count, ctx_count = lax.axis_size("dp"), lax.axis_size("ctx")
    head_groups = dp_count // KEY_GROUPS
    heads = queries.shape[1] // width // head_groups
    pair = heads // KEY_GROUPS
    chips = ctx_count // 2
    held = rows * ctx_count // KEY_GROUPS
    piece = rows // dp_count
    dims = (heads, rows, width, held, ctx_count)
    seg = segment_ids.reshape(seq // 128, 128)
    params = pltpu.CompilerParams(
        vmem_limit_bytes=min(56 * MIB, 12 * MIB + 12 * 4 * held * rows)
    )
    vmem = pl.BlockSpec(memory_space=pltpu.VMEM)
    bf16, f32 = jnp.bfloat16, jnp.float32

    def call(kernel, outs, ins, name, scratch=(), work=0, **static):
        specs = [a[1] if isinstance(a, tuple) else vmem for a in ins]
        arrays = [a[0] if isinstance(a, tuple) else a for a in ins]
        return pl.pallas_call(
            functools.partial(kernel, **static),
            out_shape=[jax.ShapeDtypeStruct(*o) for o in outs],
            in_specs=specs,
            out_specs=[vmem] * len(outs),
            scratch_shapes=list(scratch),
            compiler_params=params,
            cost_estimate=pl.CostEstimate(
                flops=work * 2 * heads * rows * held * width,
                bytes_accessed=sum(math.prod(o[0]) * 2 for o in outs),
                transcendentals=0,
            ),
            name=name,
        )(*arrays)

    def in_hbm(array):
        return pltpu.with_memory_space_constraint(array, pltpu.HBM), pl.BlockSpec(
            memory_space=pltpu.HBM
        )

    def over_dp(array, flip):
        return lax.ppermute(array, "dp", [(d, d ^ flip) for d in range(dp_count)])

    def over_cores(array):
        return lax.ppermute(array, "ctx", [(c, c ^ 1) for c in range(ctx_count)])

    def gathered(array, moves):
        pairs = []
        for d in range(0, dp_count, KEY_GROUPS):
            for (group, chip, core), (source, home) in moves.items():
                start = (d + source) * ctx_count + home * 2 + core
                pairs.append((start, (d + group) * ctx_count + chip * 2 + core))
        return lax.ppermute(array, ("dp", "ctx"), pairs)

    def spread(array, moves):
        pairs = [(a * 2 + core, b * 2 + core) for a, b in moves.items() for core in range(2)]
        return lax.ppermute(array, "ctx", pairs)

    (own_kv,) = call(
        load_kernel,
        [((rows, 2 * width), bf16)],
        [in_hbm(keys), in_hbm(values)],
        "load",
        scratch=[pltpu.SemaphoreType.DMA((2,))],
    )
    query_v, grad_v, grad_t, bias, token = call(
        prep_kernel,
        [
            ((rows, heads * width), bf16),
            ((rows, heads * width), bf16),
            ((heads * width, rows), bf16),
            ((held, rows), f32),
            ((8, 128), f32),
        ],
        [in_hbm(seg), in_hbm(queries), in_hbm(out_grad)],
        "prepare",
        scratch=[pltpu.VMEM(seg.shape, seg.dtype), pltpu.SemaphoreType.DMA((3, heads))],
        work=1,
        dims=dims,
    )
    rounds = gather_rounds(chips)
    sent = [own_kv] + [gathered(own_kv, moves) for moves in rounds]
    blocks = []
    for spot in range(chips // 2):
        choices = []
        for group in range(KEY_GROUPS):
            for chip in range(chips):
                home = home_chip(spot, group, chip, chips)
                spot_key = (group, chip, 0)
                ways = [k for k, m in enumerate(rounds, 1) if m.get(spot_key, (0, -1))[1] == home]
                choices.append(0 if home == chip else ways[0] if home < chip else -1)
        used = sorted(set(choices) - {-1})
        (picked,) = call(
            pick_kernel,
            [((rows, 2 * width), bf16)],
            [sent[k] for k in used] + [token],
            "pick",
            choices=[used.index(c) if c >= 0 else -1 for c in choices],
        )
        blocks += [picked, over_cores(picked)]
    early = held - rows
    scores, part_stats, part_sums = call(
        part_kernel,
        [((heads, early, rows), f32), ((2 * heads, rows), f32), ((heads, width, rows), f32)],
        [query_v, bias] + blocks[:-1],
        "attend_most",
        scratch=[pltpu.VMEM((width, early), bf16)],
        work=2,
        dims=dims,
    )
    stats, last_scores, *outs = call(
        forward_kernel,
        [((3 * heads, rows), f32), ((heads, rows, rows), f32)]
        + [((pair * width, rows), bf16)] * KEY_GROUPS,
        [query_v, grad_t, bias, blocks[-1], part_stats, part_sums],
        "attend",
        scratch=[
            pltpu.VMEM((heads, rows), f32),
            pltpu.VMEM((width, rows), bf16),
            pltpu.VMEM((heads * width, rows), bf16),
        ],
        work=1,
        dims=dims,
    )
    all_stats = [stats, over_dp(stats, 1)]
    all_outs = [outs[0], over_dp(outs[1], 1)]
    ahead = 4 * heads * held * rows <= 8 * MIB
    dprobs = []
    if ahead:
        dprobs = call(
            dprobs_kernel,
            [((heads, held, rows), f32)],
            [grad_v] + blocks,
            "dprobs",
            work=1,
            dims=dims,
        )

    dscores, keep, send = call(
        backward_kernel,
        [
            ((heads, held, rows), bf16),
            ((held // 2, 2 * width), f32),
            ((held // 2, 2 * width), bf16),
        ],
        [query_v, grad_v] + blocks + [scores, last_scores] + list(dprobs) + all_stats,
        "differentiate",
        scratch=[pltpu.VMEM((held, 2 * width), f32)],
        work=4,
        dims=dims,
        ahead=ahead,
    )
    got = over_cores(send)
    attn_out, token = call(
        finish_out_kernel,
        [((rows, pair * width), bf16), ((8, 128), f32)],
        all_stats + all_outs,
        "finish_out",
        dims=dims,
    )
    quarter = held // 4
    keep, send = call(
        join_kernel,
        [((quarter, 2 * width), f32), ((quarter, 2 * width), bf16)],
        [keep, got],
        "join_cores",
    )
    dqs = call(
        query_kernel,
        [((pair * width, rows), bf16)] * KEY_GROUPS,
        blocks + [dscores, keep],
        "query_terms",
        scratch=[pltpu.VMEM((width, held), bf16)],
        work=1,
        dims=dims,
    )
    all_dqs = [dqs[0], over_dp(dqs[1], 1)]
    rounds = spread_rounds(chips)
    terms, *pieces = call(
        spread_kernel,
        [((piece, 2 * width), f32)] + [((piece, 2 * width), bf16)] * len(rounds),
        [keep, over_dp(send, 2), token],
        "join_heads",
        rounds=rounds,
    )
    grad_q, token = call(
        finish_query_kernel,
        [((rows, pair * width), bf16), ((8, 128), f32)],
        all_dqs,
        "finish_query",
    )
    got = [spread(p, moves) for p, moves in zip(pieces, rounds)]
    for array in got[:-1]:
        (terms,) = call(add_kernel, [((piece, 2 * width), f32)], [terms, array], "add_terms")
    grad_k, grad_values = call(
        finish_kernel, [((piece, width), bf16)] * 2, [token, terms, got[-1]], "finish"
    )
    return attn_out, grad_q, grad_k, grad_values


def solution(mesh):
    return jax.shard_map(
        on_device,
        mesh=mesh,
        in_specs=(P("ctx", None), P("ctx", None), P("ctx", None), P("ctx", None), P()),
        out_specs=(P("ctx", "dp"), P("ctx", "dp"), P(("dp", "ctx"), None), P(("dp", "ctx"), None)),
        check_vma=False,
    )
```

```python
import functools
import math

import jax
import jax.numpy as jnp
from jax import lax
from jax.experimental import pallas as pl
from jax.experimental.pallas import tpu as pltpu
from jax.sharding import PartitionSpec as P

NEG = -1e30
LOG2E = 1.4426950408889634
DOC_NUMBERS = 4
KEY_GROUPS = 2
MIB = 1024 * 1024


def place():
    dp_index, ctx_index = lax.axis_index("dp"), lax.axis_index("ctx")
    return dp_index // KEY_GROUPS, dp_index % KEY_GROUPS, ctx_index // 2, ctx_index % 2

NT = (((1,), (1,)), ((), ()))


def home_chip(spot, key_group, chip, chips):
    level = chips // 4
    flip = spot // level * (2 * level) + spot % level
    home = chip ^ flip
    return home ^ ((home // level % 2) ^ key_group) * level


def gather_rounds(chips):
    rounds = [{} for _ in range(2 if chips == 4 else chips - 1)]
    for core in range(2):
        if chips == 4:
            rounds[0][0, 1, core] = (1, 0)
            rounds[0][0, 2, core] = (0, 0)
            rounds[0][1, 2, core] = (1, 1)
            rounds[0][0, 3, core] = (core, 2)
            rounds[1][0, 3, core] = (0, 0)
            rounds[1][1, 3, core] = (1, 1)
            continue
        for flip, moves in enumerate(rounds, 1):
            for home in range(chips):
                group = home // (chips // 4) % 2
                if home ^ flip > home:
                    moves[group, home ^ flip, core] = (group, home)
    return rounds


def spread_rounds(chips):
    flips = list(range(2, chips)) + [1]
    return [{chip: chip ^ flip for chip in range(chips)} for flip in flips]


def mask_bias(seg_ref, rows, held):
    _, key_group, chip, core = place()
    seg = seg_ref[...]
    lines = rows // 128
    seg_own = seg_ref[pl.ds((chip * 2 + core) * lines, lines), :]
    start = jnp.zeros((lines, 128), jnp.int32)
    for number in range(1, DOC_NUMBERS):
        before = jnp.sum((seg < number).astype(jnp.float32), axis=(0, 1), keepdims=True)
        start = jnp.where(seg_own == number, before.astype(jnp.int32), start)
    start = jnp.concatenate([start[k : k + 1] for k in range(lines)], axis=1)
    query_pos = (chip * 2 + core) * rows + lax.broadcasted_iota(jnp.int32, (1, rows), 1)
    blocks = held // rows
    bias = []
    for block in range(blocks):
        home = home_chip(block // 2, key_group, chip, blocks) * 2 + (core ^ block % 2)
        key_pos = home * rows + lax.broadcasted_iota(jnp.int32, (rows, rows), 0)
        allowed = (key_pos >= start) & (key_pos <= query_pos)
        bias.append(jnp.where(allowed, 0.0, NEG))
    return bias


def load_kernel(k_hbm, v_hbm, kv_ref, sems):
    width = k_hbm.shape[1]
    copies = [
        pltpu.make_async_copy(k_hbm, kv_ref.at[:, :width], sems.at[0]),
        pltpu.make_async_copy(v_hbm, kv_ref.at[:, width:], sems.at[1]),
    ]
    for copy in copies:
        copy.start()
    for copy in copies:
        copy.wait()


def pick_kernel(*refs, choices):
    out_ref = refs[-1]
    _, key_group, chip, _ = place()
    spot = key_group * (len(choices) // 2) + chip
    for choice in sorted(set(choices)):
        wanted = functools.reduce(
            jnp.logical_or, [spot == k for k, c in enumerate(choices) if c == choice]
        )

        @pl.when(wanted)
        def _():
            out_ref[...] = jnp.zeros_like(out_ref) if choice < 0 else refs[choice][...]


def prep_kernel(
    seg_hbm, q_hbm, g_hbm, q_ref, g_ref, gt_ref, bias_ref, token_ref, seg_ref, sems, *, dims
):
    heads, rows, width, held, ctx_count = dims
    head_group = place()[0]
    seg_copy = pltpu.make_async_copy(seg_hbm, seg_ref, sems.at[2, 0])
    seg_copy.start()
    copies = []
    for head in range(heads):
        source = head_columns(head_group * heads + head, width)
        target = slice(head * width, (head + 1) * width)
        for k, (full, part) in enumerate(((g_hbm, g_ref), (q_hbm, q_ref))):
            copies.append(
                pltpu.make_async_copy(full.at[:, source], part.at[:, target], sems.at[k, head])
            )
            copies[-1].start()
    token_ref[...] = jnp.zeros_like(token_ref)
    seg_copy.wait()
    for k, block in enumerate(mask_bias(seg_ref, rows, held)):
        bias_ref[k * rows : (k + 1) * rows, :] = block
    for head in range(heads):
        cols = slice(head * width, (head + 1) * width)
        copies[2 * head].wait()
        gt_ref[cols, :] = g_ref[:, cols].astype(jnp.float32).T.astype(jnp.bfloat16)
    for head in range(heads):
        copies[2 * head + 1].wait()


def head_columns(head, width):
    return pl.ds(pl.multiple_of(head * width, width), width)


def scores_pass(q_ref, bias_ref, blocks, scores_ref, top_ref, *, dims, first):
    heads, rows, width, held, ctx_count = dims
    for head in range(heads):
        query = q_ref[:, head * width : (head + 1) * width]
        top = None
        for k, kv_ref in enumerate(blocks):
            bias = bias_ref[(first + k) * rows : (first + k + 1) * rows, :]
            raw = lax.dot_general(kv_ref[:, :width], query, NT, preferred_element_type=jnp.float32)
            scores = raw * (width**-0.5 * LOG2E) + bias
            scores_ref[head, k * rows : (k + 1) * rows, :] = scores
            here = jnp.max(scores, axis=0, keepdims=True)
            top = here if top is None else jnp.maximum(top, here)
        top_ref[head : head + 1, :] = top


def transpose_values(blocks, vt_ref, width):
    size = blocks[0].shape[0]
    for k, kv_ref in enumerate(blocks):
        vt = kv_ref[:, width:].astype(jnp.float32).T.astype(jnp.bfloat16)
        vt_ref[:, k * size : (k + 1) * size] = vt


def sums_pass(vt_ref, scores_ref, top, head):
    expd = jnp.exp2(scores_ref[head] - top)
    total = jnp.sum(expd, axis=0, keepdims=True)
    sums = jnp.dot(vt_ref[...], expd.astype(jnp.bfloat16), preferred_element_type=jnp.float32)
    return total, sums


def part_kernel(q_ref, bias_ref, *refs, dims):
    heads, rows, width, held, ctx_count = dims
    *blocks, scores_ref, stats_ref, sums_ref, vt_ref = refs
    transpose_values(blocks, vt_ref, width)
    scores_pass(q_ref, bias_ref, blocks, scores_ref, stats_ref, dims=dims, first=0)
    for head in range(heads):
        total, sums_ref[head] = sums_pass(
            vt_ref, scores_ref, stats_ref[head : head + 1, :], head
        )
        stats_ref[heads + head : heads + head + 1, :] = total


def forward_kernel(
    q_ref, gt_ref, bias_ref, kv_ref, part_ref, part_sums_ref, stats_ref, scores_ref, *refs, dims
):
    heads, rows, width, held, ctx_count = dims
    *outs, top_ref, vt_ref, sums_ref = refs
    pair = heads // KEY_GROUPS
    key_group = place()[1]
    transpose_values([kv_ref], vt_ref, width)
    scores_pass(q_ref, bias_ref, [kv_ref], scores_ref, top_ref, dims=dims, first=held // rows - 1)
    for head in range(heads):
        cols = slice(head * width, (head + 1) * width)
        before = part_ref[head : head + 1, :]
        top = jnp.maximum(top_ref[head : head + 1, :], before)
        share = jnp.exp2(before - top)
        total, accum = sums_pass(vt_ref, scores_ref, top, head)
        total = total + share * part_ref[heads + head : heads + head + 1, :]
        accum = accum + share * part_sums_ref[head]
        delta = jnp.sum(accum * gt_ref[cols, :].astype(jnp.float32), axis=0, keepdims=True)
        for row, value in enumerate((top, total, delta)):
            stats_ref[row * heads + head : row * heads + head + 1, :] = value
        sums_ref[cols, :] = accum.astype(jnp.bfloat16)
    for slot, out_ref in enumerate(outs):
        out_ref[...] = sums_ref[head_columns(key_group ^ slot, pair * width), :]


def dprobs_kernel(g_ref, *refs, dims):
    heads, rows, width, held, ctx_count = dims
    *blocks, dprobs_ref = refs
    for head in range(heads):
        grad = g_ref[:, head * width : (head + 1) * width]
        for part, ref in enumerate(blocks):
            dprobs_ref[head, part * rows : (part + 1) * rows, :] = lax.dot_general(
                ref[:, width:], grad, NT, preferred_element_type=jnp.float32
            )


def merged_stats(stats, heads):
    top = functools.reduce(jnp.maximum, [s[:heads] for s in stats])
    shares = [jnp.exp2(s[:heads] - top) for s in stats]
    total = sum(f * s[heads : 2 * heads] for f, s in zip(shares, stats))
    delta = sum(f * s[2 * heads :] for f, s in zip(shares, stats)) / total
    return top, shares, total, delta


def backward_kernel(q_ref, g_ref, *refs, dims, ahead):
    heads, rows, width, held, ctx_count = dims
    parts = held // rows
    blocks, scores, last_scores, refs = refs[:parts], refs[parts], refs[parts + 1], refs[parts + 2 :]
    dprobs_ref, refs = (refs[0], refs[1:]) if ahead else (None, refs)
    stats = refs[:KEY_GROUPS]
    ds_ref, keep_ref, send_ref, acc_ref = refs[KEY_GROUPS:]
    scale = width**-0.5
    top, _, total, delta = merged_stats([s[...] for s in stats], heads)
    lse = top + jnp.log2(total)
    for head in range(heads):
        cols = slice(head * width, (head + 1) * width)
        query, grad = q_ref[:, cols], g_ref[:, cols]
        for part, ref in enumerate(blocks):
            here = slice(part * rows, (part + 1) * rows)
            row = last_scores[head] if part == parts - 1 else scores[head, here, :]
            probs = jnp.exp2(row - lse[head : head + 1])
            if ahead:
                dprobs = dprobs_ref[head, here, :]
            else:
                dprobs = lax.dot_general(
                    ref[:, width:], grad, NT, preferred_element_type=jnp.float32
                )
            dscores = (probs * (dprobs - delta[head : head + 1])).astype(jnp.bfloat16)
            ds_ref[head, here, :] = dscores
            dv = jnp.dot(probs.astype(jnp.bfloat16), grad, preferred_element_type=jnp.float32)
            dk = jnp.dot(dscores, query, preferred_element_type=jnp.float32)
            if head == 0:
                acc_ref[here, :width] = dk
                acc_ref[here, width:] = dv
            else:
                acc_ref[here, :width] += dk
                acc_ref[here, width:] += dv
    head_group, key_group, chip, core = place()
    chips, piece = ctx_count // 2, rows // 4
    level = chips // 4
    for spot in range(2 * chips):
        here = slice(spot * piece, (spot + 1) * piece)
        target = chip ^ (spot % chips)
        group = head_group ^ (spot // chips)
        block = group * (ctx_count // 2) + key_group * (ctx_count // 4) + target // 2
        flip = block // 2 ^ chip
        slot = flip // (2 * level) * level + flip % level
        line = (slot * 2 + (block % 2 ^ core)) * rows
        for ref, side in ((keep_ref, core), (send_ref, 1 - core)):
            mine = pl.ds(pl.multiple_of(line + (target % 2 * 2 + side) * piece, piece), piece)
            ref[here, :width] = (acc_ref[mine, :width] * scale).astype(ref.dtype)
            ref[here, width:] = acc_ref[mine, width:].astype(ref.dtype)


def query_kernel(*refs, dims):
    heads, rows, width, held, ctx_count = dims
    parts = held // rows
    blocks, ds_ref, refs = refs[:parts], refs[parts], refs[parts + 2 :]
    outs, kt_ref = refs[:KEY_GROUPS], refs[KEY_GROUPS]
    pair = heads // KEY_GROUPS
    key_group = place()[1]
    scale = width**-0.5
    for part, ref in enumerate(blocks):
        here = slice(part * rows, (part + 1) * rows)
        kt_ref[:, here] = ref[:, :width].astype(jnp.float32).T.astype(jnp.bfloat16)
    for slot in range(KEY_GROUPS):
        for part in range(pair):
            head = (key_group ^ slot) * pair + part
            dq = jnp.dot(kt_ref[...], ds_ref[head], preferred_element_type=jnp.float32)
            outs[slot][part * width : (part + 1) * width, :] = (dq * scale).astype(jnp.bfloat16)


def join_kernel(keep_ref, got_ref, kept_ref, send_ref):
    half = kept_ref.shape[0]
    kept_ref[...] = keep_ref[:half, :] + got_ref[:half, :].astype(jnp.float32)
    send = keep_ref[half:, :] + got_ref[half:, :].astype(jnp.float32)
    send_ref[...] = send.astype(jnp.bfloat16)


def spread_kernel(keep_ref, got_ref, token_ref, own_ref, *outs, rounds):
    piece = own_ref.shape[0]
    chip = place()[2]
    own_ref[...] = keep_ref[:piece, :] + got_ref[:piece, :].astype(jnp.float32)
    for out_ref, moves in zip(outs, rounds):
        flip = 0
        for source, target in moves.items():
            flip = jnp.where(chip == source, source ^ target, flip)
        mine = pl.ds(pl.multiple_of(flip * piece, piece), piece)
        out_ref[...] = (keep_ref[mine, :] + got_ref[mine, :].astype(jnp.float32)).astype(
            jnp.bfloat16
        )


def add_kernel(first_ref, second_ref, out_ref):
    out_ref[...] = first_ref[...] + second_ref[...].astype(jnp.float32)


def finish_out_kernel(*refs, dims):
    heads, rows, width, held, ctx_count = dims
    stats, outs = refs[:KEY_GROUPS], refs[KEY_GROUPS : 2 * KEY_GROUPS]
    attn_ref, token_ref = refs[2 * KEY_GROUPS :]
    token_ref[...] = jnp.zeros_like(token_ref)
    pair = heads // KEY_GROUPS
    top, shares, total, _ = merged_stats([s[...] for s in stats], heads)
    own = place()[1] * pair
    row = lax.broadcasted_iota(jnp.int32, (heads, 1), 0)
    for part in range(pair):
        here = slice(part * width, (part + 1) * width)

        def pick(array):
            return jnp.sum(jnp.where(row == own + part, array, 0.0), axis=0, keepdims=True)

        joined = sum(o[here, :].astype(jnp.float32) * pick(f) for o, f in zip(outs, shares))
        attn_ref[:, here] = (joined / pick(total)).T.astype(jnp.bfloat16)


def finish_query_kernel(own_ref, got_ref, gq_ref, token_ref):
    total = own_ref[...].astype(jnp.float32) + got_ref[...].astype(jnp.float32)
    gq_ref[...] = total.T.astype(jnp.bfloat16)
    token_ref[...] = jnp.zeros_like(token_ref)


def finish_kernel(token_ref, *refs):
    *terms, gk_ref, gv_ref = refs
    width = gk_ref.shape[1]
    both = sum(r[...].astype(jnp.float32) for r in terms)
    gk_ref[...] = both[:, :width].astype(jnp.bfloat16)
    gv_ref[...] = both[:, width:].astype(jnp.bfloat16)


def on_device(queries, keys, values, out_grad, segment_ids):
    rows = queries.shape[0]
    width = keys.shape[1]
    seq = segment_ids.shape[0]
    dp_count, ctx_count = lax.axis_size("dp"), lax.axis_size("ctx")
    head_groups = dp_count // KEY_GROUPS
    heads = queries.shape[1] // width // head_groups
    pair = heads // KEY_GROUPS
    chips = ctx_count // 2
    held = rows * ctx_count // KEY_GROUPS
    piece = rows // dp_count
    dims = (heads, rows, width, held, ctx_count)
    seg = segment_ids.reshape(seq // 128, 128)
    params = pltpu.CompilerParams(
        vmem_limit_bytes=min(56 * MIB, 12 * MIB + 12 * 4 * held * rows)
    )
    vmem = pl.BlockSpec(memory_space=pltpu.VMEM)
    bf16, f32 = jnp.bfloat16, jnp.float32

    def call(kernel, outs, ins, name, scratch=(), work=0, **static):
        specs = [a[1] if isinstance(a, tuple) else vmem for a in ins]
        arrays = [a[0] if isinstance(a, tuple) else a for a in ins]
        return pl.pallas_call(
            functools.partial(kernel, **static),
            out_shape=[jax.ShapeDtypeStruct(*o) for o in outs],
            in_specs=specs,
            out_specs=[vmem] * len(outs),
            scratch_shapes=list(scratch),
            compiler_params=params,
            cost_estimate=pl.CostEstimate(
                flops=work * 2 * heads * rows * held * width,
                bytes_accessed=sum(math.prod(o[0]) * 2 for o in outs),
                transcendentals=0,
            ),
            name=name,
        )(*arrays)

    def in_hbm(array):
        return pltpu.with_memory_space_constraint(array, pltpu.HBM), pl.BlockSpec(
            memory_space=pltpu.HBM
        )

    def over_dp(array, flip):
        return lax.ppermute(array, "dp", [(d, d ^ flip) for d in range(dp_count)])

    def over_cores(array):
        return lax.ppermute(array, "ctx", [(c, c ^ 1) for c in range(ctx_count)])

    def gathered(array, moves):
        pairs = []
        for d in range(0, dp_count, KEY_GROUPS):
            for (group, chip, core), (source, home) in moves.items():
                start = (d + source) * ctx_count + home * 2 + core
                pairs.append((start, (d + group) * ctx_count + chip * 2 + core))
        return lax.ppermute(array, ("dp", "ctx"), pairs)

    def spread(array, moves):
        pairs = [(a * 2 + core, b * 2 + core) for a, b in moves.items() for core in range(2)]
        return lax.ppermute(array, "ctx", pairs)

    (own_kv,) = call(
        load_kernel,
        [((rows, 2 * width), bf16)],
        [in_hbm(keys), in_hbm(values)],
        "load",
        scratch=[pltpu.SemaphoreType.DMA((2,))],
    )
    query_v, grad_v, grad_t, bias, token = call(
        prep_kernel,
        [
            ((rows, heads * width), bf16),
            ((rows, heads * width), bf16),
            ((heads * width, rows), bf16),
            ((held, rows), f32),
            ((8, 128), f32),
        ],
        [in_hbm(seg), in_hbm(queries), in_hbm(out_grad)],
        "prepare",
        scratch=[pltpu.VMEM(seg.shape, seg.dtype), pltpu.SemaphoreType.DMA((3, heads))],
        work=1,
        dims=dims,
    )
    rounds = gather_rounds(chips)
    sent = [own_kv] + [gathered(own_kv, moves) for moves in rounds]
    blocks = []
    for spot in range(chips // 2):
        choices = []
        for group in range(KEY_GROUPS):
            for chip in range(chips):
                home = home_chip(spot, group, chip, chips)
                spot_key = (group, chip, 0)
                ways = [k for k, m in enumerate(rounds, 1) if m.get(spot_key, (0, -1))[1] == home]
                choices.append(0 if home == chip else ways[0] if home < chip else -1)
        used = sorted(set(choices) - {-1})
        (picked,) = call(
            pick_kernel,
            [((rows, 2 * width), bf16)],
            [sent[k] for k in used] + [token],
            "pick",
            choices=[used.index(c) if c >= 0 else -1 for c in choices],
        )
        blocks += [picked, over_cores(picked)]
    early = held - rows
    scores, part_stats, part_sums = call(
        part_kernel,
        [((heads, early, rows), f32), ((2 * heads, rows), f32), ((heads, width, rows), f32)],
        [query_v, bias] + blocks[:-1],
        "attend_most",
        scratch=[pltpu.VMEM((width, early), bf16)],
        work=2,
        dims=dims,
    )
    stats, last_scores, *outs = call(
        forward_kernel,
        [((3 * heads, rows), f32), ((heads, rows, rows), f32)]
        + [((pair * width, rows), bf16)] * KEY_GROUPS,
        [query_v, grad_t, bias, blocks[-1], part_stats, part_sums],
        "attend",
        scratch=[
            pltpu.VMEM((heads, rows), f32),
            pltpu.VMEM((width, rows), bf16),
            pltpu.VMEM((heads * width, rows), bf16),
        ],
        work=1,
        dims=dims,
    )
    all_stats = [stats, over_dp(stats, 1)]
    all_outs = [outs[0], over_dp(outs[1], 1)]
    ahead = 4 * heads * held * rows <= 8 * MIB
    dprobs = []
    if ahead:
        dprobs = call(
            dprobs_kernel,
            [((heads, held, rows), f32)],
            [grad_v] + blocks,
            "dprobs",
            work=1,
            dims=dims,
        )

    dscores, keep, send = call(
        backward_kernel,
        [
            ((heads, held, rows), bf16),
            ((held // 2, 2 * width), f32),
            ((held // 2, 2 * width), bf16),
        ],
        [query_v, grad_v] + blocks + [scores, last_scores] + list(dprobs) + all_stats,
        "differentiate",
        scratch=[pltpu.VMEM((held, 2 * width), f32)],
        work=4,
        dims=dims,
        ahead=ahead,
    )
    got = over_cores(send)
    attn_out, token = call(
        finish_out_kernel,
        [((rows, pair * width), bf16), ((8, 128), f32)],
        all_stats + all_outs,
        "finish_out",
        dims=dims,
    )
    quarter = held // 4
    keep, send = call(
        join_kernel,
        [((quarter, 2 * width), f32), ((quarter, 2 * width), bf16)],
        [keep, got],
        "join_cores",
    )
    dqs = call(
        query_kernel,
        [((pair * width, rows), bf16)] * KEY_GROUPS,
        blocks + [dscores, keep],
        "query_terms",
        scratch=[pltpu.VMEM((width, held), bf16)],
        work=1,
        dims=dims,
    )
    all_dqs = [dqs[0], over_dp(dqs[1], 1)]
    rounds = spread_rounds(chips)
    terms, *pieces = call(
        spread_kernel,
        [((piece, 2 * width), f32)] + [((piece, 2 * width), bf16)] * len(rounds),
        [keep, over_dp(send, 2), token],
        "join_heads",
        rounds=rounds,
    )
    grad_q, token = call(
        finish_query_kernel,
        [((rows, pair * width), bf16), ((8, 128), f32)],
        all_dqs,
        "finish_query",
    )
    got = [spread(p, moves) for p, moves in zip(pieces, rounds)]
    for array in got[:-1]:
        (terms,) = call(add_kernel, [((piece, 2 * width), f32)], [terms, array], "add_terms")
    grad_k, grad_values = call(
        finish_kernel, [((piece, width), bf16)] * 2, [token, terms, got[-1]], "finish"
    )
    return attn_out, grad_q, grad_k, grad_values


def solution(mesh):
    return jax.shard_map(
        on_device,
        mesh=mesh,
        in_specs=(P("ctx", None), P("ctx", None), P("ctx", None), P("ctx", None), P()),
        out_specs=(P("ctx", "dp"), P("ctx", "dp"), P(("dp", "ctx"), None), P(("dp", "ctx"), None)),
        check_vma=False,
    )
```

```python
import functools
import math

import jax
import jax.numpy as jnp
from jax import lax
from jax.experimental import pallas as pl
from jax.experimental.pallas import tpu as pltpu
from jax.sharding import PartitionSpec as P

NEG = -1e30
LOG2E = 1.4426950408889634
DOC_NUMBERS = 4
KEY_GROUPS = 2
MIB = 1024 * 1024


def place():
    dp_index, ctx_index = lax.axis_index("dp"), lax.axis_index("ctx")
    return dp_index // KEY_GROUPS, dp_index % KEY_GROUPS, ctx_index // 2, ctx_index % 2

NT = (((1,), (1,)), ((), ()))


def home_chip(spot, key_group, chip, chips):
    level = chips // 4
    flip = spot // level * (2 * level) + spot % level
    home = chip ^ flip
    return home ^ ((home // level % 2) ^ key_group) * level


def gather_rounds(chips):
    rounds = [{} for _ in range(2 if chips == 4 else chips - 1)]
    for core in range(2):
        if chips == 4:
            rounds[0][0, 1, core] = (1, 0)
            rounds[0][0, 2, core] = (0, 0)
            rounds[0][1, 2, core] = (1, 1)
            rounds[0][0, 3, core] = (core, 2)
            rounds[1][0, 3, core] = (1, 0)
            rounds[1][1, 3, core] = (0, 1)
            continue
        for flip, moves in enumerate(rounds, 1):
            for home in range(chips):
                group = home // (chips // 4) % 2
                if home ^ flip > home:
                    moves[group, home ^ flip, core] = (group, home)
    return rounds


def spread_rounds(chips):
    flips = list(range(2, chips)) + [1]
    return [{chip: chip ^ flip for chip in range(chips)} for flip in flips]


def mask_bias(seg_ref, rows, held):
    _, key_group, chip, core = place()
    seg = seg_ref[...]
    lines = rows // 128
    seg_own = seg_ref[pl.ds((chip * 2 + core) * lines, lines), :]
    start = jnp.zeros((lines, 128), jnp.int32)
    for number in range(1, DOC_NUMBERS):
        before = jnp.sum((seg < number).astype(jnp.float32), axis=(0, 1), keepdims=True)
        start = jnp.where(seg_own == number, before.astype(jnp.int32), start)
    start = jnp.concatenate([start[k : k + 1] for k in range(lines)], axis=1)
    query_pos = (chip * 2 + core) * rows + lax.broadcasted_iota(jnp.int32, (1, rows), 1)
    blocks = held // rows
    bias = []
    for block in range(blocks):
        home = home_chip(block // 2, key_group, chip, blocks) * 2 + (core ^ block % 2)
        key_pos = home * rows + lax.broadcasted_iota(jnp.int32, (rows, rows), 0)
        allowed = (key_pos >= start) & (key_pos <= query_pos)
        bias.append(jnp.where(allowed, 0.0, NEG))
    return bias


def load_kernel(k_hbm, v_hbm, kv_ref, sems):
    width = k_hbm.shape[1]
    copies = [
        pltpu.make_async_copy(k_hbm, kv_ref.at[:, :width], sems.at[0]),
        pltpu.make_async_copy(v_hbm, kv_ref.at[:, width:], sems.at[1]),
    ]
    for copy in copies:
        copy.start()
    for copy in copies:
        copy.wait()


def pick_kernel(*refs, choices):
    out_ref = refs[-1]
    _, key_group, chip, _ = place()
    spot = key_group * (len(choices) // 2) + chip
    for choice in sorted(set(choices)):
        wanted = functools.reduce(
            jnp.logical_or, [spot == k for k, c in enumerate(choices) if c == choice]
        )

        @pl.when(wanted)
        def _():
            out_ref[...] = jnp.zeros_like(out_ref) if choice < 0 else refs[choice][...]


def prep_kernel(
    seg_hbm, q_hbm, g_hbm, q_ref, g_ref, gt_ref, bias_ref, token_ref, seg_ref, sems, *, dims
):
    heads, rows, width, held, ctx_count = dims
    head_group = place()[0]
    seg_copy = pltpu.make_async_copy(seg_hbm, seg_ref, sems.at[2, 0])
    seg_copy.start()
    copies = []
    for head in range(heads):
        source = head_columns(head_group * heads + head, width)
        target = slice(head * width, (head + 1) * width)
        for k, (full, part) in enumerate(((g_hbm, g_ref), (q_hbm, q_ref))):
            copies.append(
                pltpu.make_async_copy(full.at[:, source], part.at[:, target], sems.at[k, head])
            )
            copies[-1].start()
    token_ref[...] = jnp.zeros_like(token_ref)
    seg_copy.wait()
    for k, block in enumerate(mask_bias(seg_ref, rows, held)):
        bias_ref[k * rows : (k + 1) * rows, :] = block
    for head in range(heads):
        cols = slice(head * width, (head + 1) * width)
        copies[2 * head].wait()
        gt_ref[cols, :] = g_ref[:, cols].astype(jnp.float32).T.astype(jnp.bfloat16)
    for head in range(heads):
        copies[2 * head + 1].wait()


def head_columns(head, width):
    return pl.ds(pl.multiple_of(head * width, width), width)


def scores_pass(q_ref, bias_ref, blocks, scores_ref, top_ref, *, dims, first):
    heads, rows, width, held, ctx_count = dims
    for head in range(heads):
        query = q_ref[:, head * width : (head + 1) * width]
        top = None
        for k, kv_ref in enumerate(blocks):
            bias = bias_ref[(first + k) * rows : (first + k + 1) * rows, :]
            raw = lax.dot_general(kv_ref[:, :width], query, NT, preferred_element_type=jnp.float32)
            scores = raw * (width**-0.5 * LOG2E) + bias
            scores_ref[head, k * rows : (k + 1) * rows, :] = scores
            here = jnp.max(scores, axis=0, keepdims=True)
            top = here if top is None else jnp.maximum(top, here)
        top_ref[head : head + 1, :] = top


def transpose_values(blocks, vt_ref, width):
    size = blocks[0].shape[0]
    for k, kv_ref in enumerate(blocks):
        vt = kv_ref[:, width:].astype(jnp.float32).T.astype(jnp.bfloat16)
        vt_ref[:, k * size : (k + 1) * size] = vt


def sums_pass(vt_ref, scores_ref, top, head):
    expd = jnp.exp2(scores_ref[head] - top)
    total = jnp.sum(expd, axis=0, keepdims=True)
    sums = jnp.dot(vt_ref[...], expd.astype(jnp.bfloat16), preferred_element_type=jnp.float32)
    return total, sums


def part_kernel(q_ref, bias_ref, *refs, dims):
    heads, rows, width, held, ctx_count = dims
    *blocks, scores_ref, stats_ref, sums_ref, vt_ref = refs
    transpose_values(blocks, vt_ref, width)
    scores_pass(q_ref, bias_ref, blocks, scores_ref, stats_ref, dims=dims, first=0)
    for head in range(heads):
        total, sums_ref[head] = sums_pass(
            vt_ref, scores_ref, stats_ref[head : head + 1, :], head
        )
        stats_ref[heads + head : heads + head + 1, :] = total


def forward_kernel(
    q_ref, gt_ref, bias_ref, kv_ref, part_ref, part_sums_ref, stats_ref, scores_ref, *refs, dims
):
    heads, rows, width, held, ctx_count = dims
    *outs, top_ref, vt_ref, sums_ref = refs
    pair = heads // KEY_GROUPS
    key_group = place()[1]
    transpose_values([kv_ref], vt_ref, width)
    scores_pass(q_ref, bias_ref, [kv_ref], scores_ref, top_ref, dims=dims, first=held // rows - 1)
    for head in range(heads):
        cols = slice(head * width, (head + 1) * width)
        before = part_ref[head : head + 1, :]
        top = jnp.maximum(top_ref[head : head + 1, :], before)
        share = jnp.exp2(before - top)
        total, accum = sums_pass(vt_ref, scores_ref, top, head)
        total = total + share * part_ref[heads + head : heads + head + 1, :]
        accum = accum + share * part_sums_ref[head]
        delta = jnp.sum(accum * gt_ref[cols, :].astype(jnp.float32), axis=0, keepdims=True)
        for row, value in enumerate((top, total, delta)):
            stats_ref[row * heads + head : row * heads + head + 1, :] = value
        sums_ref[cols, :] = accum.astype(jnp.bfloat16)
    for slot, out_ref in enumerate(outs):
        out_ref[...] = sums_ref[head_columns(key_group ^ slot, pair * width), :]


def dprobs_kernel(g_ref, *refs, dims):
    heads, rows, width, held, ctx_count = dims
    *blocks, dprobs_ref = refs
    for head in range(heads):
        grad = g_ref[:, head * width : (head + 1) * width]
        for part, ref in enumerate(blocks):
            dprobs_ref[head, part * rows : (part + 1) * rows, :] = lax.dot_general(
                ref[:, width:], grad, NT, preferred_element_type=jnp.float32
            )


def merged_stats(stats, heads):
    top = functools.reduce(jnp.maximum, [s[:heads] for s in stats])
    shares = [jnp.exp2(s[:heads] - top) for s in stats]
    total = sum(f * s[heads : 2 * heads] for f, s in zip(shares, stats))
    delta = sum(f * s[2 * heads :] for f, s in zip(shares, stats)) / total
    return top, shares, total, delta


def backward_kernel(q_ref, g_ref, *refs, dims, ahead):
    heads, rows, width, held, ctx_count = dims
    parts = held // rows
    blocks, scores, last_scores, refs = refs[:parts], refs[parts], refs[parts + 1], refs[parts + 2 :]
    dprobs_ref, refs = (refs[0], refs[1:]) if ahead else (None, refs)
    stats = refs[:KEY_GROUPS]
    ds_ref, keep_ref, send_ref, acc_ref = refs[KEY_GROUPS:]
    scale = width**-0.5
    top, _, total, delta = merged_stats([s[...] for s in stats], heads)
    lse = top + jnp.log2(total)
    for head in range(heads):
        cols = slice(head * width, (head + 1) * width)
        query, grad = q_ref[:, cols], g_ref[:, cols]
        for part, ref in enumerate(blocks):
            here = slice(part * rows, (part + 1) * rows)
            row = last_scores[head] if part == parts - 1 else scores[head, here, :]
            probs = jnp.exp2(row - lse[head : head + 1])
            if ahead:
                dprobs = dprobs_ref[head, here, :]
            else:
                dprobs = lax.dot_general(
                    ref[:, width:], grad, NT, preferred_element_type=jnp.float32
                )
            dscores = (probs * (dprobs - delta[head : head + 1])).astype(jnp.bfloat16)
            ds_ref[head, here, :] = dscores
            dv = jnp.dot(probs.astype(jnp.bfloat16), grad, preferred_element_type=jnp.float32)
            dk = jnp.dot(dscores, query, preferred_element_type=jnp.float32)
            if head == 0:
                acc_ref[here, :width] = dk
                acc_ref[here, width:] = dv
            else:
                acc_ref[here, :width] += dk
                acc_ref[here, width:] += dv
    head_group, key_group, chip, core = place()
    chips, piece = ctx_count // 2, rows // 4
    level = chips // 4
    for spot in range(2 * chips):
        here = slice(spot * piece, (spot + 1) * piece)
        target = chip ^ (spot % chips)
        group = head_group ^ (spot // chips)
        block = group * (ctx_count // 2) + key_group * (ctx_count // 4) + target // 2
        flip = block // 2 ^ chip
        slot = flip // (2 * level) * level + flip % level
        line = (slot * 2 + (block % 2 ^ core)) * rows
        for ref, side in ((keep_ref, core), (send_ref, 1 - core)):
            mine = pl.ds(pl.multiple_of(line + (target % 2 * 2 + side) * piece, piece), piece)
            ref[here, :width] = (acc_ref[mine, :width] * scale).astype(ref.dtype)
            ref[here, width:] = acc_ref[mine, width:].astype(ref.dtype)


def query_kernel(*refs, dims):
    heads, rows, width, held, ctx_count = dims
    parts = held // rows
    blocks, ds_ref, refs = refs[:parts], refs[parts], refs[parts + 2 :]
    outs, kt_ref = refs[:KEY_GROUPS], refs[KEY_GROUPS]
    pair = heads // KEY_GROUPS
    key_group = place()[1]
    scale = width**-0.5
    for part, ref in enumerate(blocks):
        here = slice(part * rows, (part + 1) * rows)
        kt_ref[:, here] = ref[:, :width].astype(jnp.float32).T.astype(jnp.bfloat16)
    for slot in range(KEY_GROUPS):
        for part in range(pair):
            head = (key_group ^ slot) * pair + part
            dq = jnp.dot(kt_ref[...], ds_ref[head], preferred_element_type=jnp.float32)
            outs[slot][part * width : (part + 1) * width, :] = (dq * scale).astype(jnp.bfloat16)


def join_kernel(keep_ref, got_ref, kept_ref, send_ref):
    half = kept_ref.shape[0]
    kept_ref[...] = keep_ref[:half, :] + got_ref[:half, :].astype(jnp.float32)
    send = keep_ref[half:, :] + got_ref[half:, :].astype(jnp.float32)
    send_ref[...] = send.astype(jnp.bfloat16)


def spread_kernel(keep_ref, got_ref, token_ref, own_ref, *outs, rounds):
    piece = own_ref.shape[0]
    chip = place()[2]
    own_ref[...] = keep_ref[:piece, :] + got_ref[:piece, :].astype(jnp.float32)
    for out_ref, moves in zip(outs, rounds):
        flip = 0
        for source, target in moves.items():
            flip = jnp.where(chip == source, source ^ target, flip)
        mine = pl.ds(pl.multiple_of(flip * piece, piece), piece)
        out_ref[...] = (keep_ref[mine, :] + got_ref[mine, :].astype(jnp.float32)).astype(
            jnp.bfloat16
        )


def add_kernel(first_ref, second_ref, out_ref):
    out_ref[...] = first_ref[...] + second_ref[...].astype(jnp.float32)


def finish_out_kernel(*refs, dims):
    heads, rows, width, held, ctx_count = dims
    stats, outs = refs[:KEY_GROUPS], refs[KEY_GROUPS : 2 * KEY_GROUPS]
    attn_ref, token_ref = refs[2 * KEY_GROUPS :]
    token_ref[...] = jnp.zeros_like(token_ref)
    pair = heads // KEY_GROUPS
    top, shares, total, _ = merged_stats([s[...] for s in stats], heads)
    own = place()[1] * pair
    row = lax.broadcasted_iota(jnp.int32, (heads, 1), 0)
    for part in range(pair):
        here = slice(part * width, (part + 1) * width)

        def pick(array):
            return jnp.sum(jnp.where(row == own + part, array, 0.0), axis=0, keepdims=True)

        joined = sum(o[here, :].astype(jnp.float32) * pick(f) for o, f in zip(outs, shares))
        attn_ref[:, here] = (joined / pick(total)).T.astype(jnp.bfloat16)


def finish_query_kernel(own_ref, got_ref, gq_ref, token_ref):
    total = own_ref[...].astype(jnp.float32) + got_ref[...].astype(jnp.float32)
    gq_ref[...] = total.T.astype(jnp.bfloat16)
    token_ref[...] = jnp.zeros_like(token_ref)


def finish_kernel(token_ref, *refs):
    *terms, gk_ref, gv_ref = refs
    width = gk_ref.shape[1]
    both = sum(r[...].astype(jnp.float32) for r in terms)
    gk_ref[...] = both[:, :width].astype(jnp.bfloat16)
    gv_ref[...] = both[:, width:].astype(jnp.bfloat16)


def on_device(queries, keys, values, out_grad, segment_ids):
    rows = queries.shape[0]
    width = keys.shape[1]
    seq = segment_ids.shape[0]
    dp_count, ctx_count = lax.axis_size("dp"), lax.axis_size("ctx")
    head_groups = dp_count // KEY_GROUPS
    heads = queries.shape[1] // width // head_groups
    pair = heads // KEY_GROUPS
    chips = ctx_count // 2
    held = rows * ctx_count // KEY_GROUPS
    piece = rows // dp_count
    dims = (heads, rows, width, held, ctx_count)
    seg = segment_ids.reshape(seq // 128, 128)
    params = pltpu.CompilerParams(
        vmem_limit_bytes=min(56 * MIB, 12 * MIB + 12 * 4 * held * rows)
    )
    vmem = pl.BlockSpec(memory_space=pltpu.VMEM)
    bf16, f32 = jnp.bfloat16, jnp.float32

    def call(kernel, outs, ins, name, scratch=(), work=0, **static):
        specs = [a[1] if isinstance(a, tuple) else vmem for a in ins]
        arrays = [a[0] if isinstance(a, tuple) else a for a in ins]
        return pl.pallas_call(
            functools.partial(kernel, **static),
            out_shape=[jax.ShapeDtypeStruct(*o) for o in outs],
            in_specs=specs,
            out_specs=[vmem] * len(outs),
            scratch_shapes=list(scratch),
            compiler_params=params,
            cost_estimate=pl.CostEstimate(
                flops=work * 2 * heads * rows * held * width,
                bytes_accessed=sum(math.prod(o[0]) * 2 for o in outs),
                transcendentals=0,
            ),
            name=name,
        )(*arrays)

    def in_hbm(array):
        return pltpu.with_memory_space_constraint(array, pltpu.HBM), pl.BlockSpec(
            memory_space=pltpu.HBM
        )

    def over_dp(array, flip):
        return lax.ppermute(array, "dp", [(d, d ^ flip) for d in range(dp_count)])

    def over_cores(array):
        return lax.ppermute(array, "ctx", [(c, c ^ 1) for c in range(ctx_count)])

    def gathered(array, moves):
        pairs = []
        for d in range(0, dp_count, KEY_GROUPS):
            for (group, chip, core), (source, home) in moves.items():
                start = (d + source) * ctx_count + home * 2 + core
                pairs.append((start, (d + group) * ctx_count + chip * 2 + core))
        return lax.ppermute(array, ("dp", "ctx"), pairs)

    def spread(array, moves):
        pairs = [(a * 2 + core, b * 2 + core) for a, b in moves.items() for core in range(2)]
        return lax.ppermute(array, "ctx", pairs)

    (own_kv,) = call(
        load_kernel,
        [((rows, 2 * width), bf16)],
        [in_hbm(keys), in_hbm(values)],
        "load",
        scratch=[pltpu.SemaphoreType.DMA((2,))],
    )
    query_v, grad_v, grad_t, bias, token = call(
        prep_kernel,
        [
            ((rows, heads * width), bf16),
            ((rows, heads * width), bf16),
            ((heads * width, rows), bf16),
            ((held, rows), f32),
            ((8, 128), f32),
        ],
        [in_hbm(seg), in_hbm(queries), in_hbm(out_grad)],
        "prepare",
        scratch=[pltpu.VMEM(seg.shape, seg.dtype), pltpu.SemaphoreType.DMA((3, heads))],
        work=1,
        dims=dims,
    )
    rounds = gather_rounds(chips)
    sent = [own_kv] + [gathered(own_kv, moves) for moves in rounds]
    blocks = []
    for spot in range(chips // 2):
        choices = []
        for group in range(KEY_GROUPS):
            for chip in range(chips):
                home = home_chip(spot, group, chip, chips)
                spot_key = (group, chip, 0)
                ways = [k for k, m in enumerate(rounds, 1) if m.get(spot_key, (0, -1))[1] == home]
                choices.append(0 if home == chip else ways[0] if home < chip else -1)
        used = sorted(set(choices) - {-1})
        (picked,) = call(
            pick_kernel,
            [((rows, 2 * width), bf16)],
            [sent[k] for k in used] + [token],
            "pick",
            choices=[used.index(c) if c >= 0 else -1 for c in choices],
        )
        blocks += [picked, over_cores(picked)]
    early = held - rows
    scores, part_stats, part_sums = call(
        part_kernel,
        [((heads, early, rows), f32), ((2 * heads, rows), f32), ((heads, width, rows), f32)],
        [query_v, bias] + blocks[:-1],
        "attend_most",
        scratch=[pltpu.VMEM((width, early), bf16)],
        work=2,
        dims=dims,
    )
    stats, last_scores, *outs = call(
        forward_kernel,
        [((3 * heads, rows), f32), ((heads, rows, rows), f32)]
        + [((pair * width, rows), bf16)] * KEY_GROUPS,
        [query_v, grad_t, bias, blocks[-1], part_stats, part_sums],
        "attend",
        scratch=[
            pltpu.VMEM((heads, rows), f32),
            pltpu.VMEM((width, rows), bf16),
            pltpu.VMEM((heads * width, rows), bf16),
        ],
        work=1,
        dims=dims,
    )
    all_stats = [stats, over_dp(stats, 1)]
    all_outs = [outs[0], over_dp(outs[1], 1)]
    ahead = 4 * heads * held * rows <= 8 * MIB
    dprobs = []
    if ahead:
        dprobs = call(
            dprobs_kernel,
            [((heads, held, rows), f32)],
            [grad_v] + blocks,
            "dprobs",
            work=1,
            dims=dims,
        )

    dscores, keep, send = call(
        backward_kernel,
        [
            ((heads, held, rows), bf16),
            ((held // 2, 2 * width), f32),
            ((held // 2, 2 * width), bf16),
        ],
        [query_v, grad_v] + blocks + [scores, last_scores] + list(dprobs) + all_stats,
        "differentiate",
        scratch=[pltpu.VMEM((held, 2 * width), f32)],
        work=4,
        dims=dims,
        ahead=ahead,
    )
    got = over_cores(send)
    attn_out, token = call(
        finish_out_kernel,
        [((rows, pair * width), bf16), ((8, 128), f32)],
        all_stats + all_outs,
        "finish_out",
        dims=dims,
    )
    quarter = held // 4
    keep, send = call(
        join_kernel,
        [((quarter, 2 * width), f32), ((quarter, 2 * width), bf16)],
        [keep, got],
        "join_cores",
    )
    dqs = call(
        query_kernel,
        [((pair * width, rows), bf16)] * KEY_GROUPS,
        blocks + [dscores, keep],
        "query_terms",
        scratch=[pltpu.VMEM((width, held), bf16)],
        work=1,
        dims=dims,
    )
    all_dqs = [dqs[0], over_dp(dqs[1], 1)]
    rounds = spread_rounds(chips)
    terms, *pieces = call(
        spread_kernel,
        [((piece, 2 * width), f32)] + [((piece, 2 * width), bf16)] * len(rounds),
        [keep, over_dp(send, 2), token],
        "join_heads",
        rounds=rounds,
    )
    grad_q, token = call(
        finish_query_kernel,
        [((rows, pair * width), bf16), ((8, 128), f32)],
        all_dqs,
        "finish_query",
    )
    got = [spread(p, moves) for p, moves in zip(pieces, rounds)]
    for array in got[:-1]:
        (terms,) = call(add_kernel, [((piece, 2 * width), f32)], [terms, array], "add_terms")
    grad_k, grad_values = call(
        finish_kernel, [((piece, width), bf16)] * 2, [token, terms, got[-1]], "finish"
    )
    return attn_out, grad_q, grad_k, grad_values


def solution(mesh):
    return jax.shard_map(
        on_device,
        mesh=mesh,
        in_specs=(P("ctx", None), P("ctx", None), P("ctx", None), P("ctx", None), P()),
        out_specs=(P("ctx", "dp"), P("ctx", "dp"), P(("dp", "ctx"), None), P(("dp", "ctx"), None)),
        check_vma=False,
    )
```

```python
import functools
import math

import jax
import jax.numpy as jnp
from jax import lax
from jax.experimental import pallas as pl
from jax.experimental.pallas import tpu as pltpu
from jax.sharding import PartitionSpec as P

NEG = -1e30
LOG2E = 1.4426950408889634
DOC_NUMBERS = 4
KEY_GROUPS = 2
MIB = 1024 * 1024


def place():
    dp_index, ctx_index = lax.axis_index("dp"), lax.axis_index("ctx")
    return dp_index // KEY_GROUPS, dp_index % KEY_GROUPS, ctx_index // 2, ctx_index % 2

NT = (((1,), (1,)), ((), ()))


def home_chip(spot, key_group, chip, chips):
    level = chips // 4
    flip = spot // level * (2 * level) + spot % level
    home = chip ^ flip
    return home ^ ((home // level % 2) ^ key_group) * level


def gather_rounds(chips):
    rounds = [{} for _ in range(2 if chips == 4 else chips - 1)]
    for core in range(2):
        if chips == 4:
            rounds[0][0, 1, core] = (1, 0)
            rounds[0][0, 2, core] = (0, 0)
            rounds[0][1, 2, core] = (1, 1)
            rounds[0][0, 3, core] = (core, 2)
            rounds[1][0, 3, core] = (0, 0)
            rounds[1][1, 3, core] = (1, 1)
            continue
        for flip, moves in enumerate(rounds, 1):
            for home in range(chips):
                group = home // (chips // 4) % 2
                if home ^ flip > home:
                    moves[group, home ^ flip, core] = (group, home)
    return rounds


def spread_rounds(chips):
    flips = [1] + list(range(chips - 1, 1, -1))
    return [{chip: chip ^ flip for chip in range(chips)} for flip in flips]


def mask_bias(seg_ref, rows, held):
    _, key_group, chip, core = place()
    seg = seg_ref[...]
    lines = rows // 128
    seg_own = seg_ref[pl.ds((chip * 2 + core) * lines, lines), :]
    start = jnp.zeros((lines, 128), jnp.int32)
    for number in range(1, DOC_NUMBERS):
        before = jnp.sum((seg < number).astype(jnp.float32), axis=(0, 1), keepdims=True)
        start = jnp.where(seg_own == number, before.astype(jnp.int32), start)
    start = jnp.concatenate([start[k : k + 1] for k in range(lines)], axis=1)
    query_pos = (chip * 2 + core) * rows + lax.broadcasted_iota(jnp.int32, (1, rows), 1)
    blocks = held // rows
    bias = []
    for block in range(blocks):
        home = home_chip(block // 2, key_group, chip, blocks) * 2 + (core ^ block % 2)
        key_pos = home * rows + lax.broadcasted_iota(jnp.int32, (rows, rows), 0)
        allowed = (key_pos >= start) & (key_pos <= query_pos)
        bias.append(jnp.where(allowed, 0.0, NEG))
    return bias


def load_kernel(k_hbm, v_hbm, kv_ref, sems):
    width = k_hbm.shape[1]
    copies = [
        pltpu.make_async_copy(k_hbm, kv_ref.at[:, :width], sems.at[0]),
        pltpu.make_async_copy(v_hbm, kv_ref.at[:, width:], sems.at[1]),
    ]
    for copy in copies:
        copy.start()
    for copy in copies:
        copy.wait()


def pick_kernel(*refs, choices):
    out_ref = refs[-1]
    _, key_group, chip, _ = place()
    spot = key_group * (len(choices) // 2) + chip
    for choice in sorted(set(choices)):
        wanted = functools.reduce(
            jnp.logical_or, [spot == k for k, c in enumerate(choices) if c == choice]
        )

        @pl.when(wanted)
        def _():
            out_ref[...] = jnp.zeros_like(out_ref) if choice < 0 else refs[choice][...]


def prep_kernel(
    seg_hbm, q_hbm, g_hbm, q_ref, g_ref, gt_ref, bias_ref, token_ref, seg_ref, sems, *, dims
):
    heads, rows, width, held, ctx_count = dims
    head_group = place()[0]
    seg_copy = pltpu.make_async_copy(seg_hbm, seg_ref, sems.at[2, 0])
    seg_copy.start()
    copies = []
    for head in range(heads):
        source = head_columns(head_group * heads + head, width)
        target = slice(head * width, (head + 1) * width)
        for k, (full, part) in enumerate(((g_hbm, g_ref), (q_hbm, q_ref))):
            copies.append(
                pltpu.make_async_copy(full.at[:, source], part.at[:, target], sems.at[k, head])
            )
            copies[-1].start()
    token_ref[...] = jnp.zeros_like(token_ref)
    seg_copy.wait()
    for k, block in enumerate(mask_bias(seg_ref, rows, held)):
        bias_ref[k * rows : (k + 1) * rows, :] = block
    for head in range(heads):
        cols = slice(head * width, (head + 1) * width)
        copies[2 * head].wait()
        gt_ref[cols, :] = g_ref[:, cols].astype(jnp.float32).T.astype(jnp.bfloat16)
    for head in range(heads):
        copies[2 * head + 1].wait()


def head_columns(head, width):
    return pl.ds(pl.multiple_of(head * width, width), width)


def scores_pass(q_ref, bias_ref, blocks, scores_ref, top_ref, *, dims, first):
    heads, rows, width, held, ctx_count = dims
    for head in range(heads):
        query = q_ref[:, head * width : (head + 1) * width]
        top = None
        for k, kv_ref in enumerate(blocks):
            bias = bias_ref[(first + k) * rows : (first + k + 1) * rows, :]
            raw = lax.dot_general(kv_ref[:, :width], query, NT, preferred_element_type=jnp.float32)
            scores = raw * (width**-0.5 * LOG2E) + bias
            scores_ref[head, k * rows : (k + 1) * rows, :] = scores
            here = jnp.max(scores, axis=0, keepdims=True)
            top = here if top is None else jnp.maximum(top, here)
        top_ref[head : head + 1, :] = top


def transpose_values(blocks, vt_ref, width):
    size = blocks[0].shape[0]
    for k, kv_ref in enumerate(blocks):
        vt = kv_ref[:, width:].astype(jnp.float32).T.astype(jnp.bfloat16)
        vt_ref[:, k * size : (k + 1) * size] = vt


def sums_pass(vt_ref, scores_ref, top, head):
    expd = jnp.exp2(scores_ref[head] - top)
    total = jnp.sum(expd, axis=0, keepdims=True)
    sums = jnp.dot(vt_ref[...], expd.astype(jnp.bfloat16), preferred_element_type=jnp.float32)
    return total, sums


def part_kernel(q_ref, bias_ref, *refs, dims):
    heads, rows, width, held, ctx_count = dims
    *blocks, scores_ref, stats_ref, sums_ref, vt_ref = refs
    transpose_values(blocks, vt_ref, width)
    scores_pass(q_ref, bias_ref, blocks, scores_ref, stats_ref, dims=dims, first=0)
    for head in range(heads):
        total, sums_ref[head] = sums_pass(
            vt_ref, scores_ref, stats_ref[head : head + 1, :], head
        )
        stats_ref[heads + head : heads + head + 1, :] = total


def forward_kernel(
    q_ref, gt_ref, bias_ref, kv_ref, part_ref, part_sums_ref, stats_ref, scores_ref, *refs, dims
):
    heads, rows, width, held, ctx_count = dims
    *outs, top_ref, vt_ref, sums_ref = refs
    pair = heads // KEY_GROUPS
    key_group = place()[1]
    transpose_values([kv_ref], vt_ref, width)
    scores_pass(q_ref, bias_ref, [kv_ref], scores_ref, top_ref, dims=dims, first=held // rows - 1)
    for head in range(heads):
        cols = slice(head * width, (head + 1) * width)
        before = part_ref[head : head + 1, :]
        top = jnp.maximum(top_ref[head : head + 1, :], before)
        share = jnp.exp2(before - top)
        total, accum = sums_pass(vt_ref, scores_ref, top, head)
        total = total + share * part_ref[heads + head : heads + head + 1, :]
        accum = accum + share * part_sums_ref[head]
        delta = jnp.sum(accum * gt_ref[cols, :].astype(jnp.float32), axis=0, keepdims=True)
        for row, value in enumerate((top, total, delta)):
            stats_ref[row * heads + head : row * heads + head + 1, :] = value
        sums_ref[cols, :] = accum.astype(jnp.bfloat16)
    for slot, out_ref in enumerate(outs):
        out_ref[...] = sums_ref[head_columns(key_group ^ slot, pair * width), :]


def dprobs_kernel(g_ref, *refs, dims):
    heads, rows, width, held, ctx_count = dims
    *blocks, dprobs_ref = refs
    for head in range(heads):
        grad = g_ref[:, head * width : (head + 1) * width]
        for part, ref in enumerate(blocks):
            dprobs_ref[head, part * rows : (part + 1) * rows, :] = lax.dot_general(
                ref[:, width:], grad, NT, preferred_element_type=jnp.float32
            )


def merged_stats(stats, heads):
    top = functools.reduce(jnp.maximum, [s[:heads] for s in stats])
    shares = [jnp.exp2(s[:heads] - top) for s in stats]
    total = sum(f * s[heads : 2 * heads] for f, s in zip(shares, stats))
    delta = sum(f * s[2 * heads :] for f, s in zip(shares, stats)) / total
    return top, shares, total, delta


def backward_kernel(q_ref, g_ref, *refs, dims, ahead):
    heads, rows, width, held, ctx_count = dims
    parts = held // rows
    blocks, scores, last_scores, refs = refs[:parts], refs[parts], refs[parts + 1], refs[parts + 2 :]
    dprobs_ref, refs = (refs[0], refs[1:]) if ahead else (None, refs)
    stats = refs[:KEY_GROUPS]
    ds_ref, keep_ref, send_ref, acc_ref = refs[KEY_GROUPS:]
    scale = width**-0.5
    top, _, total, delta = merged_stats([s[...] for s in stats], heads)
    lse = top + jnp.log2(total)
    for head in range(heads):
        cols = slice(head * width, (head + 1) * width)
        query, grad = q_ref[:, cols], g_ref[:, cols]
        for part, ref in enumerate(blocks):
            here = slice(part * rows, (part + 1) * rows)
            row = last_scores[head] if part == parts - 1 else scores[head, here, :]
            probs = jnp.exp2(row - lse[head : head + 1])
            if ahead:
                dprobs = dprobs_ref[head, here, :]
            else:
                dprobs = lax.dot_general(
                    ref[:, width:], grad, NT, preferred_element_type=jnp.float32
                )
            dscores = (probs * (dprobs - delta[head : head + 1])).astype(jnp.bfloat16)
            ds_ref[head, here, :] = dscores
            dv = jnp.dot(probs.astype(jnp.bfloat16), grad, preferred_element_type=jnp.float32)
            dk = jnp.dot(dscores, query, preferred_element_type=jnp.float32)
            if head == 0:
                acc_ref[here, :width] = dk
                acc_ref[here, width:] = dv
            else:
                acc_ref[here, :width] += dk
                acc_ref[here, width:] += dv
    head_group, key_group, chip, core = place()
    chips, piece = ctx_count // 2, rows // 4
    level = chips // 4
    for spot in range(2 * chips):
        here = slice(spot * piece, (spot + 1) * piece)
        target = chip ^ (spot % chips)
        group = head_group ^ (spot // chips)
        block = group * (ctx_count // 2) + key_group * (ctx_count // 4) + target // 2
        flip = block // 2 ^ chip
        slot = flip // (2 * level) * level + flip % level
        line = (slot * 2 + (block % 2 ^ core)) * rows
        for ref, side in ((keep_ref, core), (send_ref, 1 - core)):
            mine = pl.ds(pl.multiple_of(line + (target % 2 * 2 + side) * piece, piece), piece)
            ref[here, :width] = (acc_ref[mine, :width] * scale).astype(ref.dtype)
            ref[here, width:] = acc_ref[mine, width:].astype(ref.dtype)


def query_kernel(*refs, dims):
    heads, rows, width, held, ctx_count = dims
    parts = held // rows
    blocks, ds_ref, refs = refs[:parts], refs[parts], refs[parts + 2 :]
    outs, kt_ref = refs[:KEY_GROUPS], refs[KEY_GROUPS]
    pair = heads // KEY_GROUPS
    key_group = place()[1]
    scale = width**-0.5
    for part, ref in enumerate(blocks):
        here = slice(part * rows, (part + 1) * rows)
        kt_ref[:, here] = ref[:, :width].astype(jnp.float32).T.astype(jnp.bfloat16)
    for slot in range(KEY_GROUPS):
        for part in range(pair):
            head = (key_group ^ slot) * pair + part
            dq = jnp.dot(kt_ref[...], ds_ref[head], preferred_element_type=jnp.float32)
            outs[slot][part * width : (part + 1) * width, :] = (dq * scale).astype(jnp.bfloat16)


def join_kernel(keep_ref, got_ref, kept_ref, send_ref):
    half = kept_ref.shape[0]
    kept_ref[...] = keep_ref[:half, :] + got_ref[:half, :].astype(jnp.float32)
    send = keep_ref[half:, :] + got_ref[half:, :].astype(jnp.float32)
    send_ref[...] = send.astype(jnp.bfloat16)


def spread_kernel(keep_ref, got_ref, token_ref, own_ref, *outs, rounds):
    piece = own_ref.shape[0]
    chip = place()[2]
    own_ref[...] = keep_ref[:piece, :] + got_ref[:piece, :].astype(jnp.float32)
    for out_ref, moves in zip(outs, rounds):
        flip = 0
        for source, target in moves.items():
            flip = jnp.where(chip == source, source ^ target, flip)
        mine = pl.ds(pl.multiple_of(flip * piece, piece), piece)
        out_ref[...] = (keep_ref[mine, :] + got_ref[mine, :].astype(jnp.float32)).astype(
            jnp.bfloat16
        )


def add_kernel(first_ref, second_ref, out_ref):
    out_ref[...] = first_ref[...] + second_ref[...].astype(jnp.float32)


def finish_out_kernel(*refs, dims):
    heads, rows, width, held, ctx_count = dims
    stats, outs = refs[:KEY_GROUPS], refs[KEY_GROUPS : 2 * KEY_GROUPS]
    attn_ref, token_ref = refs[2 * KEY_GROUPS :]
    token_ref[...] = jnp.zeros_like(token_ref)
    pair = heads // KEY_GROUPS
    top, shares, total, _ = merged_stats([s[...] for s in stats], heads)
    own = place()[1] * pair
    row = lax.broadcasted_iota(jnp.int32, (heads, 1), 0)
    for part in range(pair):
        here = slice(part * width, (part + 1) * width)

        def pick(array):
            return jnp.sum(jnp.where(row == own + part, array, 0.0), axis=0, keepdims=True)

        joined = sum(o[here, :].astype(jnp.float32) * pick(f) for o, f in zip(outs, shares))
        attn_ref[:, here] = (joined / pick(total)).T.astype(jnp.bfloat16)


def finish_query_kernel(own_ref, got_ref, gq_ref, token_ref):
    total = own_ref[...].astype(jnp.float32) + got_ref[...].astype(jnp.float32)
    gq_ref[...] = total.T.astype(jnp.bfloat16)
    token_ref[...] = jnp.zeros_like(token_ref)


def finish_kernel(token_ref, *refs):
    *terms, gk_ref, gv_ref = refs
    width = gk_ref.shape[1]
    both = sum(r[...].astype(jnp.float32) for r in terms)
    gk_ref[...] = both[:, :width].astype(jnp.bfloat16)
    gv_ref[...] = both[:, width:].astype(jnp.bfloat16)


def on_device(queries, keys, values, out_grad, segment_ids):
    rows = queries.shape[0]
    width = keys.shape[1]
    seq = segment_ids.shape[0]
    dp_count, ctx_count = lax.axis_size("dp"), lax.axis_size("ctx")
    head_groups = dp_count // KEY_GROUPS
    heads = queries.shape[1] // width // head_groups
    pair = heads // KEY_GROUPS
    chips = ctx_count // 2
    held = rows * ctx_count // KEY_GROUPS
    piece = rows // dp_count
    dims = (heads, rows, width, held, ctx_count)
    seg = segment_ids.reshape(seq // 128, 128)
    params = pltpu.CompilerParams(
        vmem_limit_bytes=min(56 * MIB, 12 * MIB + 12 * 4 * held * rows)
    )
    vmem = pl.BlockSpec(memory_space=pltpu.VMEM)
    bf16, f32 = jnp.bfloat16, jnp.float32

    def call(kernel, outs, ins, name, scratch=(), work=0, **static):
        specs = [a[1] if isinstance(a, tuple) else vmem for a in ins]
        arrays = [a[0] if isinstance(a, tuple) else a for a in ins]
        return pl.pallas_call(
            functools.partial(kernel, **static),
            out_shape=[jax.ShapeDtypeStruct(*o) for o in outs],
            in_specs=specs,
            out_specs=[vmem] * len(outs),
            scratch_shapes=list(scratch),
            compiler_params=params,
            cost_estimate=pl.CostEstimate(
                flops=work * 2 * heads * rows * held * width,
                bytes_accessed=sum(math.prod(o[0]) * 2 for o in outs),
                transcendentals=0,
            ),
            name=name,
        )(*arrays)

    def in_hbm(array):
        return pltpu.with_memory_space_constraint(array, pltpu.HBM), pl.BlockSpec(
            memory_space=pltpu.HBM
        )

    def over_dp(array, flip):
        return lax.ppermute(array, "dp", [(d, d ^ flip) for d in range(dp_count)])

    def over_cores(array):
        return lax.ppermute(array, "ctx", [(c, c ^ 1) for c in range(ctx_count)])

    def gathered(array, moves):
        pairs = []
        for d in range(0, dp_count, KEY_GROUPS):
            for (group, chip, core), (source, home) in moves.items():
                start = (d + source) * ctx_count + home * 2 + core
                pairs.append((start, (d + group) * ctx_count + chip * 2 + core))
        return lax.ppermute(array, ("dp", "ctx"), pairs)

    def spread(array, moves):
        pairs = [(a * 2 + core, b * 2 + core) for a, b in moves.items() for core in range(2)]
        return lax.ppermute(array, "ctx", pairs)

    (own_kv,) = call(
        load_kernel,
        [((rows, 2 * width), bf16)],
        [in_hbm(keys), in_hbm(values)],
        "load",
        scratch=[pltpu.SemaphoreType.DMA((2,))],
    )
    query_v, grad_v, grad_t, bias, token = call(
        prep_kernel,
        [
            ((rows, heads * width), bf16),
            ((rows, heads * width), bf16),
            ((heads * width, rows), bf16),
            ((held, rows), f32),
            ((8, 128), f32),
        ],
        [in_hbm(seg), in_hbm(queries), in_hbm(out_grad)],
        "prepare",
        scratch=[pltpu.VMEM(seg.shape, seg.dtype), pltpu.SemaphoreType.DMA((3, heads))],
        work=1,
        dims=dims,
    )
    rounds = gather_rounds(chips)
    sent = [own_kv] + [gathered(own_kv, moves) for moves in rounds]
    blocks = []
    for spot in range(chips // 2):
        choices = []
        for group in range(KEY_GROUPS):
            for chip in range(chips):
                home = home_chip(spot, group, chip, chips)
                spot_key = (group, chip, 0)
                ways = [k for k, m in enumerate(rounds, 1) if m.get(spot_key, (0, -1))[1] == home]
                choices.append(0 if home == chip else ways[0] if home < chip else -1)
        used = sorted(set(choices) - {-1})
        (picked,) = call(
            pick_kernel,
            [((rows, 2 * width), bf16)],
            [sent[k] for k in used] + [token],
            "pick",
            choices=[used.index(c) if c >= 0 else -1 for c in choices],
        )
        blocks += [picked, over_cores(picked)]
    early = held - rows
    scores, part_stats, part_sums = call(
        part_kernel,
        [((heads, early, rows), f32), ((2 * heads, rows), f32), ((heads, width, rows), f32)],
        [query_v, bias] + blocks[:-1],
        "attend_most",
        scratch=[pltpu.VMEM((width, early), bf16)],
        work=2,
        dims=dims,
    )
    stats, last_scores, *outs = call(
        forward_kernel,
        [((3 * heads, rows), f32), ((heads, rows, rows), f32)]
        + [((pair * width, rows), bf16)] * KEY_GROUPS,
        [query_v, grad_t, bias, blocks[-1], part_stats, part_sums],
        "attend",
        scratch=[
            pltpu.VMEM((heads, rows), f32),
            pltpu.VMEM((width, rows), bf16),
            pltpu.VMEM((heads * width, rows), bf16),
        ],
        work=1,
        dims=dims,
    )
    all_stats = [stats, over_dp(stats, 1)]
    all_outs = [outs[0], over_dp(outs[1], 1)]
    ahead = 4 * heads * held * rows <= 8 * MIB
    dprobs = []
    if ahead:
        dprobs = call(
            dprobs_kernel,
            [((heads, held, rows), f32)],
            [grad_v] + blocks,
            "dprobs",
            work=1,
            dims=dims,
        )

    dscores, keep, send = call(
        backward_kernel,
        [
            ((heads, held, rows), bf16),
            ((held // 2, 2 * width), f32),
            ((held // 2, 2 * width), bf16),
        ],
        [query_v, grad_v] + blocks + [scores, last_scores] + list(dprobs) + all_stats,
        "differentiate",
        scratch=[pltpu.VMEM((held, 2 * width), f32)],
        work=4,
        dims=dims,
        ahead=ahead,
    )
    got = over_cores(send)
    attn_out, token = call(
        finish_out_kernel,
        [((rows, pair * width), bf16), ((8, 128), f32)],
        all_stats + all_outs,
        "finish_out",
        dims=dims,
    )
    quarter = held // 4
    keep, send = call(
        join_kernel,
        [((quarter, 2 * width), f32), ((quarter, 2 * width), bf16)],
        [keep, got],
        "join_cores",
    )
    dqs = call(
        query_kernel,
        [((pair * width, rows), bf16)] * KEY_GROUPS,
        blocks + [dscores, keep],
        "query_terms",
        scratch=[pltpu.VMEM((width, held), bf16)],
        work=1,
        dims=dims,
    )
    all_dqs = [dqs[0], over_dp(dqs[1], 1)]
    rounds = spread_rounds(chips)
    terms, *pieces = call(
        spread_kernel,
        [((piece, 2 * width), f32)] + [((piece, 2 * width), bf16)] * len(rounds),
        [keep, over_dp(send, 2), token],
        "join_heads",
        rounds=rounds,
    )
    grad_q, token = call(
        finish_query_kernel,
        [((rows, pair * width), bf16), ((8, 128), f32)],
        all_dqs,
        "finish_query",
    )
    got = [spread(p, moves) for p, moves in zip(pieces, rounds)]
    for array in got[:-1]:
        (terms,) = call(add_kernel, [((piece, 2 * width), f32)], [terms, array], "add_terms")
    grad_k, grad_values = call(
        finish_kernel, [((piece, width), bf16)] * 2, [token, terms, got[-1]], "finish"
    )
    return attn_out, grad_q, grad_k, grad_values


def solution(mesh):
    return jax.shard_map(
        on_device,
        mesh=mesh,
        in_specs=(P("ctx", None), P("ctx", None), P("ctx", None), P("ctx", None), P()),
        out_specs=(P("ctx", "dp"), P("ctx", "dp"), P(("dp", "ctx"), None), P(("dp", "ctx"), None)),
        check_vma=False,
    )
```

```python
import functools
import math

import jax
import jax.numpy as jnp
from jax import lax
from jax.experimental import pallas as pl
from jax.experimental.pallas import tpu as pltpu
from jax.sharding import PartitionSpec as P

NEG = -1e30
LOG2E = 1.4426950408889634
DOC_NUMBERS = 4
KEY_GROUPS = 2
MIB = 1024 * 1024


def place():
    dp_index, ctx_index = lax.axis_index("dp"), lax.axis_index("ctx")
    return dp_index // KEY_GROUPS, dp_index % KEY_GROUPS, ctx_index // 2, ctx_index % 2

NT = (((1,), (1,)), ((), ()))


def home_chip(spot, key_group, chip, chips):
    level = chips // 4
    flip = spot // level * (2 * level) + spot % level
    home = chip ^ flip
    return home ^ ((home // level % 2) ^ key_group) * level


def gather_rounds(chips):
    rounds = [{} for _ in range(2 if chips == 4 else chips - 1)]
    for core in range(2):
        if chips == 4:
            rounds[0][0, 1, core] = (1, 0)
            rounds[0][0, 2, core] = (0, 0)
            rounds[0][1, 2, core] = (1, 1)
            rounds[0][0, 3, core] = (core, 2)
            rounds[1][0, 3, core] = (0, 0)
            rounds[1][1, 3, core] = (1, 1)
            continue
        for flip, moves in enumerate(rounds, 1):
            for home in range(chips):
                group = home // (chips // 4) % 2
                if home ^ flip > home:
                    moves[group, home ^ flip, core] = (group, home)
    return rounds


def spread_rounds(chips):
    flips = list(range(2, chips)) + [1]
    return [{chip: chip ^ flip for chip in range(chips)} for flip in flips]


def mask_bias(seg_ref, rows, held):
    _, key_group, chip, core = place()
    seg = seg_ref[...]
    lines = rows // 128
    seg_own = seg_ref[pl.ds((chip * 2 + core) * lines, lines), :]
    start = jnp.zeros((lines, 128), jnp.int32)
    for number in range(1, DOC_NUMBERS):
        before = jnp.sum((seg < number).astype(jnp.float32), axis=(0, 1), keepdims=True)
        start = jnp.where(seg_own == number, before.astype(jnp.int32), start)
    start = jnp.concatenate([start[k : k + 1] for k in range(lines)], axis=1)
    query_pos = (chip * 2 + core) * rows + lax.broadcasted_iota(jnp.int32, (1, rows), 1)
    blocks = held // rows
    size = rows // 4
    line = lax.broadcasted_iota(jnp.int32, (rows, rows), 0)
    place_of = line // size
    row = (place_of % 2 * 2 + place_of // 2) * size + line % size
    bias = []
    for block in range(blocks):
        home = home_chip(block // 2, key_group, chip, blocks) * 2 + (core ^ block % 2)
        key_pos = home * rows + row
        allowed = (key_pos >= start) & (key_pos <= query_pos)
        bias.append(jnp.where(allowed, 0.0, NEG))
    return bias


def row_order(pieces):
    return list(range(0, pieces, 2)) + list(range(1, pieces, 2))


def load_kernel(k_hbm, v_hbm, kv_ref, sems, *, pieces):
    rows, width = k_hbm.shape
    size = rows // pieces
    copies = []
    for spot, piece in enumerate(row_order(pieces)):
        source, target = (slice(k * size, (k + 1) * size) for k in (piece, spot))
        for k, array in enumerate((k_hbm, v_hbm)):
            columns = slice(k * width, (k + 1) * width)
            copies.append(
                pltpu.make_async_copy(
                    array.at[source, :], kv_ref.at[target, columns], sems.at[k, spot]
                )
            )
    for copy in copies:
        copy.start()
    for copy in copies:
        copy.wait()


def pick_kernel(*refs, choices):
    out_ref = refs[-1]
    _, key_group, chip, _ = place()
    spot = key_group * (len(choices) // 2) + chip
    for choice in sorted(set(choices)):
        wanted = functools.reduce(
            jnp.logical_or, [spot == k for k, c in enumerate(choices) if c == choice]
        )

        @pl.when(wanted)
        def _():
            out_ref[...] = jnp.zeros_like(out_ref) if choice < 0 else refs[choice][...]


def prep_kernel(
    seg_hbm, q_hbm, g_hbm, q_ref, g_ref, gt_ref, bias_ref, token_ref, seg_ref, sems, *, dims
):
    heads, rows, width, held, ctx_count = dims
    head_group = place()[0]
    seg_copy = pltpu.make_async_copy(seg_hbm, seg_ref, sems.at[2, 0])
    seg_copy.start()
    copies = []
    for head in range(heads):
        source = head_columns(head_group * heads + head, width)
        target = slice(head * width, (head + 1) * width)
        for k, (full, part) in enumerate(((g_hbm, g_ref), (q_hbm, q_ref))):
            copies.append(
                pltpu.make_async_copy(full.at[:, source], part.at[:, target], sems.at[k, head])
            )
            copies[-1].start()
    token_ref[...] = jnp.zeros_like(token_ref)
    seg_copy.wait()
    for k, block in enumerate(mask_bias(seg_ref, rows, held)):
        bias_ref[k * rows : (k + 1) * rows, :] = block
    for head in range(heads):
        cols = slice(head * width, (head + 1) * width)
        copies[2 * head].wait()
        gt_ref[cols, :] = g_ref[:, cols].astype(jnp.float32).T.astype(jnp.bfloat16)
    for head in range(heads):
        copies[2 * head + 1].wait()


def head_columns(head, width):
    return pl.ds(pl.multiple_of(head * width, width), width)


def scores_pass(q_ref, bias_ref, blocks, scores_ref, top_ref, *, dims, first):
    heads, rows, width, held, ctx_count = dims
    for head in range(heads):
        query = q_ref[:, head * width : (head + 1) * width]
        top = None
        for k, kv_ref in enumerate(blocks):
            bias = bias_ref[(first + k) * rows : (first + k + 1) * rows, :]
            raw = lax.dot_general(kv_ref[:, :width], query, NT, preferred_element_type=jnp.float32)
            scores = raw * (width**-0.5 * LOG2E) + bias
            scores_ref[head, k * rows : (k + 1) * rows, :] = scores
            here = jnp.max(scores, axis=0, keepdims=True)
            top = here if top is None else jnp.maximum(top, here)
        top_ref[head : head + 1, :] = top


def transpose_values(blocks, vt_ref, width):
    size = blocks[0].shape[0]
    for k, kv_ref in enumerate(blocks):
        vt = kv_ref[:, width:].astype(jnp.float32).T.astype(jnp.bfloat16)
        vt_ref[:, k * size : (k + 1) * size] = vt


def sums_pass(vt_ref, scores_ref, top, head):
    expd = jnp.exp2(scores_ref[head] - top)
    total = jnp.sum(expd, axis=0, keepdims=True)
    sums = jnp.dot(vt_ref[...], expd.astype(jnp.bfloat16), preferred_element_type=jnp.float32)
    return total, sums


def part_kernel(q_ref, bias_ref, *refs, dims):
    heads, rows, width, held, ctx_count = dims
    *blocks, scores_ref, stats_ref, sums_ref, vt_ref = refs
    transpose_values(blocks, vt_ref, width)
    scores_pass(q_ref, bias_ref, blocks, scores_ref, stats_ref, dims=dims, first=0)
    for head in range(heads):
        total, sums_ref[head] = sums_pass(
            vt_ref, scores_ref, stats_ref[head : head + 1, :], head
        )
        stats_ref[heads + head : heads + head + 1, :] = total


def forward_kernel(
    q_ref, gt_ref, bias_ref, kv_ref, part_ref, part_sums_ref, stats_ref, scores_ref, *refs, dims
):
    heads, rows, width, held, ctx_count = dims
    *outs, top_ref, vt_ref, sums_ref = refs
    pair = heads // KEY_GROUPS
    key_group = place()[1]
    transpose_values([kv_ref], vt_ref, width)
    scores_pass(q_ref, bias_ref, [kv_ref], scores_ref, top_ref, dims=dims, first=held // rows - 1)
    for head in range(heads):
        cols = slice(head * width, (head + 1) * width)
        before = part_ref[head : head + 1, :]
        top = jnp.maximum(top_ref[head : head + 1, :], before)
        share = jnp.exp2(before - top)
        total, accum = sums_pass(vt_ref, scores_ref, top, head)
        total = total + share * part_ref[heads + head : heads + head + 1, :]
        accum = accum + share * part_sums_ref[head]
        delta = jnp.sum(accum * gt_ref[cols, :].astype(jnp.float32), axis=0, keepdims=True)
        for row, value in enumerate((top, total, delta)):
            stats_ref[row * heads + head : row * heads + head + 1, :] = value
        sums_ref[cols, :] = accum.astype(jnp.bfloat16)
    for slot, out_ref in enumerate(outs):
        out_ref[...] = sums_ref[head_columns(key_group ^ slot, pair * width), :]


def dprobs_kernel(g_ref, *refs, dims):
    heads, rows, width, held, ctx_count = dims
    *blocks, dprobs_ref = refs
    for head in range(heads):
        grad = g_ref[:, head * width : (head + 1) * width]
        for part, ref in enumerate(blocks):
            dprobs_ref[head, part * rows : (part + 1) * rows, :] = lax.dot_general(
                ref[:, width:], grad, NT, preferred_element_type=jnp.float32
            )


def merged_stats(stats, heads):
    top = functools.reduce(jnp.maximum, [s[:heads] for s in stats])
    shares = [jnp.exp2(s[:heads] - top) for s in stats]
    total = sum(f * s[heads : 2 * heads] for f, s in zip(shares, stats))
    delta = sum(f * s[2 * heads :] for f, s in zip(shares, stats)) / total
    return top, shares, total, delta


def core_rows(base, side, half):
    return pl.ds(pl.multiple_of(base + side * half, half), half)


def backward_kernel(q_ref, g_ref, *refs, dims, ahead, own):
    heads, rows, width, held, ctx_count = dims
    parts, half = held // rows, rows // 2
    blocks, scores, last_scores, refs = refs[:parts], refs[parts], refs[parts + 1], refs[parts + 2 :]
    dprobs_ref, refs = (refs[0], refs[1:]) if ahead else (None, refs)
    stats = refs[:KEY_GROUPS]
    ds_ref, terms_ref, acc_ref = refs[-3:]
    head_group, key_group, chip, core = place()
    side = core if own else 1 - core
    scale = width**-0.5
    top, _, total, delta = merged_stats([s[...] for s in stats], heads)
    lse = top + jnp.log2(total)
    for head in range(heads):
        cols = slice(head * width, (head + 1) * width)
        query, grad = q_ref[:, cols], g_ref[:, cols]
        for part, ref in enumerate(blocks):
            held_rows, block_rows = core_rows(part * rows, side, half), core_rows(0, side, half)
            if part == parts - 1:
                row = last_scores[head, block_rows, :]
            else:
                row = scores[head, held_rows, :]
            probs = jnp.exp2(row - lse[head : head + 1])
            if ahead:
                dprobs = dprobs_ref[head, held_rows, :]
            else:
                dprobs = lax.dot_general(
                    ref[block_rows, width:], grad, NT, preferred_element_type=jnp.float32
                )
            dscores = (probs * (dprobs - delta[head : head + 1])).astype(jnp.bfloat16)
            here = slice(part * half, (part + 1) * half)
            ds_ref[head, here, :] = dscores
            dv = jnp.dot(probs.astype(jnp.bfloat16), grad, preferred_element_type=jnp.float32)
            dk = jnp.dot(dscores, query, preferred_element_type=jnp.float32)
            if head == 0:
                acc_ref[here, :width] = dk
                acc_ref[here, width:] = dv
            else:
                acc_ref[here, :width] += dk
                acc_ref[here, width:] += dv
    chips, piece = ctx_count // 2, rows // 4
    level = chips // 4
    for spot in range(2 * chips):
        here = slice(spot * piece, (spot + 1) * piece)
        target = chip ^ (spot % chips)
        group = head_group ^ (spot // chips)
        block = group * (ctx_count // 2) + key_group * (ctx_count // 4) + target // 2
        flip = block // 2 ^ chip
        slot = flip // (2 * level) * level + flip % level
        line = (slot * 2 + (block % 2 ^ core)) * half + target % 2 * piece
        mine = pl.ds(pl.multiple_of(line, piece), piece)
        terms_ref[here, :width] = (acc_ref[mine, :width] * scale).astype(terms_ref.dtype)
        terms_ref[here, width:] = acc_ref[mine, width:].astype(terms_ref.dtype)


def query_kernel(*refs, dims):
    heads, rows, width, held, ctx_count = dims
    parts, half = held // rows, rows // 2
    blocks, dscores, refs = refs[:parts], refs[parts : parts + 2], refs[parts + 3 :]
    outs, kts = refs[:KEY_GROUPS], refs[KEY_GROUPS:]
    pair = heads // KEY_GROUPS
    _, key_group, _, core = place()
    scale = width**-0.5
    for kt_ref, side in zip(kts, (core, 1 - core)):
        for part, ref in enumerate(blocks):
            keys = ref[core_rows(0, side, half), :width].astype(jnp.float32)
            kt_ref[:, part * half : (part + 1) * half] = keys.T.astype(jnp.bfloat16)
    for slot in range(KEY_GROUPS):
        for part in range(pair):
            head = (key_group ^ slot) * pair + part
            dq = sum(
                jnp.dot(kt_ref[...], ds_ref[head], preferred_element_type=jnp.float32)
                for kt_ref, ds_ref in zip(kts, dscores)
            )
            outs[slot][part * width : (part + 1) * width, :] = (dq * scale).astype(jnp.bfloat16)


def join_kernel(keep_ref, got_ref, kept_ref, send_ref):
    half = kept_ref.shape[0]
    kept_ref[...] = keep_ref[:half, :] + got_ref[:half, :].astype(jnp.float32)
    send = keep_ref[half:, :] + got_ref[half:, :].astype(jnp.float32)
    send_ref[...] = send.astype(jnp.bfloat16)


def spread_kernel(keep_ref, got_ref, token_ref, own_ref, *outs, rounds):
    piece = own_ref.shape[0]
    chip = place()[2]
    own_ref[...] = keep_ref[:piece, :] + got_ref[:piece, :].astype(jnp.float32)
    for out_ref, moves in zip(outs, rounds):
        flip = 0
        for source, target in moves.items():
            flip = jnp.where(chip == source, source ^ target, flip)
        mine = pl.ds(pl.multiple_of(flip * piece, piece), piece)
        out_ref[...] = (keep_ref[mine, :] + got_ref[mine, :].astype(jnp.float32)).astype(
            jnp.bfloat16
        )


def add_kernel(first_ref, second_ref, out_ref):
    out_ref[...] = first_ref[...] + second_ref[...].astype(jnp.float32)


def finish_out_kernel(*refs, dims):
    heads, rows, width, held, ctx_count = dims
    stats, outs = refs[:KEY_GROUPS], refs[KEY_GROUPS : 2 * KEY_GROUPS]
    attn_ref, token_ref = refs[2 * KEY_GROUPS :]
    token_ref[...] = jnp.zeros_like(token_ref)
    pair = heads // KEY_GROUPS
    top, shares, total, _ = merged_stats([s[...] for s in stats], heads)
    own = place()[1] * pair
    row = lax.broadcasted_iota(jnp.int32, (heads, 1), 0)
    for part in range(pair):
        here = slice(part * width, (part + 1) * width)

        def pick(array):
            return jnp.sum(jnp.where(row == own + part, array, 0.0), axis=0, keepdims=True)

        joined = sum(o[here, :].astype(jnp.float32) * pick(f) for o, f in zip(outs, shares))
        attn_ref[:, here] = (joined / pick(total)).T.astype(jnp.bfloat16)


def finish_query_kernel(own_ref, got_ref, gq_ref, token_ref):
    total = own_ref[...].astype(jnp.float32) + got_ref[...].astype(jnp.float32)
    gq_ref[...] = total.T.astype(jnp.bfloat16)
    token_ref[...] = jnp.zeros_like(token_ref)


def finish_kernel(token_ref, *refs):
    *terms, gk_ref, gv_ref = refs
    width = gk_ref.shape[1]
    both = sum(r[...].astype(jnp.float32) for r in terms)
    gk_ref[...] = both[:, :width].astype(jnp.bfloat16)
    gv_ref[...] = both[:, width:].astype(jnp.bfloat16)


def on_device(queries, keys, values, out_grad, segment_ids):
    rows = queries.shape[0]
    width = keys.shape[1]
    seq = segment_ids.shape[0]
    dp_count, ctx_count = lax.axis_size("dp"), lax.axis_size("ctx")
    head_groups = dp_count // KEY_GROUPS
    heads = queries.shape[1] // width // head_groups
    pair = heads // KEY_GROUPS
    chips = ctx_count // 2
    held = rows * ctx_count // KEY_GROUPS
    piece = rows // dp_count
    dims = (heads, rows, width, held, ctx_count)
    seg = segment_ids.reshape(seq // 128, 128)
    params = pltpu.CompilerParams(
        vmem_limit_bytes=min(56 * MIB, 12 * MIB + 12 * 4 * held * rows)
    )
    vmem = pl.BlockSpec(memory_space=pltpu.VMEM)
    bf16, f32 = jnp.bfloat16, jnp.float32

    def call(kernel, outs, ins, name, scratch=(), work=0, **static):
        specs = [a[1] if isinstance(a, tuple) else vmem for a in ins]
        arrays = [a[0] if isinstance(a, tuple) else a for a in ins]
        return pl.pallas_call(
            functools.partial(kernel, **static),
            out_shape=[jax.ShapeDtypeStruct(*o) for o in outs],
            in_specs=specs,
            out_specs=[vmem] * len(outs),
            scratch_shapes=list(scratch),
            compiler_params=params,
            cost_estimate=pl.CostEstimate(
                flops=work * 2 * heads * rows * held * width,
                bytes_accessed=sum(math.prod(o[0]) * 2 for o in outs),
                transcendentals=0,
            ),
            name=name,
        )(*arrays)

    def in_hbm(array):
        return pltpu.with_memory_space_constraint(array, pltpu.HBM), pl.BlockSpec(
            memory_space=pltpu.HBM
        )

    def over_dp(array, flip):
        return lax.ppermute(array, "dp", [(d, d ^ flip) for d in range(dp_count)])

    def over_cores(array):
        return lax.ppermute(array, "ctx", [(c, c ^ 1) for c in range(ctx_count)])

    def gathered(array, moves):
        pairs = []
        for d in range(0, dp_count, KEY_GROUPS):
            for (group, chip, core), (source, home) in moves.items():
                start = (d + source) * ctx_count + home * 2 + core
                pairs.append((start, (d + group) * ctx_count + chip * 2 + core))
        return lax.ppermute(array, ("dp", "ctx"), pairs)

    def spread(array, moves):
        pairs = [(a * 2 + core, b * 2 + core) for a, b in moves.items() for core in range(2)]
        return lax.ppermute(array, "ctx", pairs)

    (own_kv,) = call(
        load_kernel,
        [((rows, 2 * width), bf16)],
        [in_hbm(keys), in_hbm(values)],
        "load",
        scratch=[pltpu.SemaphoreType.DMA((2, dp_count))],
        pieces=dp_count,
    )
    query_v, grad_v, grad_t, bias, token = call(
        prep_kernel,
        [
            ((rows, heads * width), bf16),
            ((rows, heads * width), bf16),
            ((heads * width, rows), bf16),
            ((held, rows), f32),
            ((8, 128), f32),
        ],
        [in_hbm(seg), in_hbm(queries), in_hbm(out_grad)],
        "prepare",
        scratch=[pltpu.VMEM(seg.shape, seg.dtype), pltpu.SemaphoreType.DMA((3, heads))],
        work=1,
        dims=dims,
    )
    rounds = gather_rounds(chips)
    sent = [own_kv] + [gathered(own_kv, moves) for moves in rounds]
    blocks = []
    for spot in range(chips // 2):
        choices = []
        for group in range(KEY_GROUPS):
            for chip in range(chips):
                home = home_chip(spot, group, chip, chips)
                spot_key = (group, chip, 0)
                ways = [k for k, m in enumerate(rounds, 1) if m.get(spot_key, (0, -1))[1] == home]
                choices.append(0 if home == chip else ways[0] if home < chip else -1)
        used = sorted(set(choices) - {-1})
        (picked,) = call(
            pick_kernel,
            [((rows, 2 * width), bf16)],
            [sent[k] for k in used] + [token],
            "pick",
            choices=[used.index(c) if c >= 0 else -1 for c in choices],
        )
        blocks += [picked, over_cores(picked)]
    early = held - rows
    scores, part_stats, part_sums = call(
        part_kernel,
        [((heads, early, rows), f32), ((2 * heads, rows), f32), ((heads, width, rows), f32)],
        [query_v, bias] + blocks[:-1],
        "attend_most",
        scratch=[pltpu.VMEM((width, early), bf16)],
        work=2,
        dims=dims,
    )
    stats, last_scores, *outs = call(
        forward_kernel,
        [((3 * heads, rows), f32), ((heads, rows, rows), f32)]
        + [((pair * width, rows), bf16)] * KEY_GROUPS,
        [query_v, grad_t, bias, blocks[-1], part_stats, part_sums],
        "attend",
        scratch=[
            pltpu.VMEM((heads, rows), f32),
            pltpu.VMEM((width, rows), bf16),
            pltpu.VMEM((heads * width, rows), bf16),
        ],
        work=1,
        dims=dims,
    )
    all_stats = [stats, over_dp(stats, 1)]
    all_outs = [outs[0], over_dp(outs[1], 1)]
    ahead = 4 * heads * held * rows <= 8 * MIB
    dprobs = []
    if ahead:
        dprobs = call(
            dprobs_kernel,
            [((heads, held, rows), f32)],
            [grad_v] + blocks,
            "dprobs",
            work=1,
            dims=dims,
        )

    inputs = [query_v, grad_v] + blocks + [scores, last_scores] + list(dprobs) + all_stats

    def differentiate(own, dtype, after):
        return call(
            backward_kernel,
            [((heads, held // 2, rows), bf16), ((held // 2, 2 * width), dtype)],
            inputs + after,
            "differentiate_own" if own else "differentiate_other",
            scratch=[pltpu.VMEM((held // 2, 2 * width), f32)],
            work=2,
            dims=dims,
            ahead=ahead,
            own=own,
        )

    other_scores, send = differentiate(False, bf16, [])
    got = over_cores(send)
    own_scores, keep = differentiate(True, f32, [other_scores])
    attn_out, token = call(
        finish_out_kernel,
        [((rows, pair * width), bf16), ((8, 128), f32)],
        all_stats + all_outs,
        "finish_out",
        dims=dims,
    )
    quarter = held // 4
    keep, send = call(
        join_kernel,
        [((quarter, 2 * width), f32), ((quarter, 2 * width), bf16)],
        [keep, got],
        "join_cores",
    )
    dqs = call(
        query_kernel,
        [((pair * width, rows), bf16)] * KEY_GROUPS,
        blocks + [own_scores, other_scores, keep],
        "query_terms",
        scratch=[pltpu.VMEM((width, held // 2), bf16)] * 2,
        work=1,
        dims=dims,
    )
    all_dqs = [dqs[0], over_dp(dqs[1], 1)]
    rounds = spread_rounds(chips)
    terms, *pieces = call(
        spread_kernel,
        [((piece, 2 * width), f32)] + [((piece, 2 * width), bf16)] * len(rounds),
        [keep, over_dp(send, 2), token],
        "join_heads",
        rounds=rounds,
    )
    grad_q, token = call(
        finish_query_kernel,
        [((rows, pair * width), bf16), ((8, 128), f32)],
        all_dqs,
        "finish_query",
    )
    got = [spread(p, moves) for p, moves in zip(pieces, rounds)]
    for array in got[:-1]:
        (terms,) = call(add_kernel, [((piece, 2 * width), f32)], [terms, array], "add_terms")
    grad_k, grad_values = call(
        finish_kernel, [((piece, width), bf16)] * 2, [token, terms, got[-1]], "finish"
    )
    return attn_out, grad_q, grad_k, grad_values


def solution(mesh):
    return jax.shard_map(
        on_device,
        mesh=mesh,
        in_specs=(P("ctx", None), P("ctx", None), P("ctx", None), P("ctx", None), P()),
        out_specs=(P("ctx", "dp"), P("ctx", "dp"), P(("dp", "ctx"), None), P(("dp", "ctx"), None)),
        check_vma=False,
    )
```

```python
import functools
import math

import jax
import jax.numpy as jnp
from jax import lax
from jax.experimental import pallas as pl
from jax.experimental.pallas import tpu as pltpu
from jax.sharding import PartitionSpec as P

NEG = -1e30
LOG2E = 1.4426950408889634
DOC_NUMBERS = 4
KEY_GROUPS = 2
MIB = 1024 * 1024


def place():
    dp_index, ctx_index = lax.axis_index("dp"), lax.axis_index("ctx")
    return dp_index // KEY_GROUPS, dp_index % KEY_GROUPS, ctx_index // 2, ctx_index % 2

NT = (((1,), (1,)), ((), ()))


def home_chip(spot, key_group, chip, chips):
    level = chips // 4
    flip = spot // level * (2 * level) + spot % level
    home = chip ^ flip
    return home ^ ((home // level % 2) ^ key_group) * level


def gather_rounds(chips):
    rounds = [{} for _ in range(2 if chips == 4 else chips - 1)]
    for core in range(2):
        if chips == 4:
            rounds[0][0, 1, core] = (1, 0)
            rounds[0][0, 2, core] = (0, 0)
            rounds[0][1, 2, core] = (1, 1)
            rounds[0][0, 3, core] = (core, 2)
            rounds[1][0, 3, core] = (0, 0)
            rounds[1][1, 3, core] = (1, 1)
            continue
        for flip, moves in enumerate(rounds, 1):
            for home in range(chips):
                group = home // (chips // 4) % 2
                if home ^ flip > home:
                    moves[group, home ^ flip, core] = (group, home)
    return rounds


def spread_rounds(chips):
    flips = list(range(2, chips)) + [1]
    return [{chip: chip ^ flip for chip in range(chips)} for flip in flips]


def mask_bias(seg_ref, rows, held):
    _, key_group, chip, core = place()
    seg = seg_ref[...]
    lines = rows // 128
    seg_own = seg_ref[pl.ds((chip * 2 + core) * lines, lines), :]
    start = jnp.zeros((lines, 128), jnp.int32)
    for number in range(1, DOC_NUMBERS):
        before = jnp.sum((seg < number).astype(jnp.float32), axis=(0, 1), keepdims=True)
        start = jnp.where(seg_own == number, before.astype(jnp.int32), start)
    start = jnp.concatenate([start[k : k + 1] for k in range(lines)], axis=1)
    query_pos = (chip * 2 + core) * rows + lax.broadcasted_iota(jnp.int32, (1, rows), 1)
    blocks = held // rows
    size = rows // 4
    line = lax.broadcasted_iota(jnp.int32, (rows, rows), 0)
    place_of = line // size
    row = (place_of % 2 * 2 + place_of // 2) * size + line % size
    bias = []
    for block in range(blocks):
        home = home_chip(block // 2, key_group, chip, blocks) * 2 + (core ^ block % 2)
        key_pos = home * rows + row
        allowed = (key_pos >= start) & (key_pos <= query_pos)
        bias.append(jnp.where(allowed, 0.0, NEG))
    return bias


def row_order(pieces):
    return list(range(0, pieces, 2)) + list(range(1, pieces, 2))


def load_kernel(k_hbm, v_hbm, kv_ref, sems, *, pieces):
    rows, width = k_hbm.shape
    size = rows // pieces
    copies = []
    for spot, piece in enumerate(row_order(pieces)):
        source, target = (slice(k * size, (k + 1) * size) for k in (piece, spot))
        for k, array in enumerate((k_hbm, v_hbm)):
            columns = slice(k * width, (k + 1) * width)
            copies.append(
                pltpu.make_async_copy(
                    array.at[source, :], kv_ref.at[target, columns], sems.at[k, spot]
                )
            )
    for copy in copies:
        copy.start()
    for copy in copies:
        copy.wait()


def pick_kernel(*refs, choices):
    out_ref = refs[-1]
    _, key_group, chip, _ = place()
    spot = key_group * (len(choices) // 2) + chip
    for choice in sorted(set(choices)):
        wanted = functools.reduce(
            jnp.logical_or, [spot == k for k, c in enumerate(choices) if c == choice]
        )

        @pl.when(wanted)
        def _():
            out_ref[...] = jnp.zeros_like(out_ref) if choice < 0 else refs[choice][...]


def prep_kernel(
    seg_hbm, q_hbm, g_hbm, q_ref, g_ref, gt_ref, bias_ref, token_ref, seg_ref, sems, *, dims
):
    heads, rows, width, held, ctx_count = dims
    head_group = place()[0]
    seg_copy = pltpu.make_async_copy(seg_hbm, seg_ref, sems.at[2, 0])
    seg_copy.start()
    copies = []
    for head in range(heads):
        source = head_columns(head_group * heads + head, width)
        target = slice(head * width, (head + 1) * width)
        for k, (full, part) in enumerate(((g_hbm, g_ref), (q_hbm, q_ref))):
            copies.append(
                pltpu.make_async_copy(full.at[:, source], part.at[:, target], sems.at[k, head])
            )
            copies[-1].start()
    token_ref[...] = jnp.zeros_like(token_ref)
    seg_copy.wait()
    for k, block in enumerate(mask_bias(seg_ref, rows, held)):
        bias_ref[k * rows : (k + 1) * rows, :] = block
    for head in range(heads):
        cols = slice(head * width, (head + 1) * width)
        copies[2 * head].wait()
        gt_ref[cols, :] = g_ref[:, cols].astype(jnp.float32).T.astype(jnp.bfloat16)
    for head in range(heads):
        copies[2 * head + 1].wait()


def head_columns(head, width):
    return pl.ds(pl.multiple_of(head * width, width), width)


def scores_pass(q_ref, bias_ref, blocks, scores_ref, top_ref, *, dims, first):
    heads, rows, width, held, ctx_count = dims
    for head in range(heads):
        query = q_ref[:, head * width : (head + 1) * width]
        top = None
        for k, kv_ref in enumerate(blocks):
            bias = bias_ref[(first + k) * rows : (first + k + 1) * rows, :]
            raw = lax.dot_general(kv_ref[:, :width], query, NT, preferred_element_type=jnp.float32)
            scores = raw * (width**-0.5 * LOG2E) + bias
            scores_ref[head, k * rows : (k + 1) * rows, :] = scores
            here = jnp.max(scores, axis=0, keepdims=True)
            top = here if top is None else jnp.maximum(top, here)
        top_ref[head : head + 1, :] = top


def transpose_values(blocks, vt_ref, width):
    size = blocks[0].shape[0]
    for k, kv_ref in enumerate(blocks):
        vt = kv_ref[:, width:].astype(jnp.float32).T.astype(jnp.bfloat16)
        vt_ref[:, k * size : (k + 1) * size] = vt


def sums_pass(vt_ref, scores_ref, top, head):
    expd = jnp.exp2(scores_ref[head] - top)
    total = jnp.sum(expd, axis=0, keepdims=True)
    sums = jnp.dot(vt_ref[...], expd.astype(jnp.bfloat16), preferred_element_type=jnp.float32)
    return total, sums


def part_kernel(q_ref, bias_ref, *refs, dims):
    heads, rows, width, held, ctx_count = dims
    *blocks, scores_ref, stats_ref, sums_ref, vt_ref = refs
    transpose_values(blocks, vt_ref, width)
    scores_pass(q_ref, bias_ref, blocks, scores_ref, stats_ref, dims=dims, first=0)
    for head in range(heads):
        total, sums_ref[head] = sums_pass(
            vt_ref, scores_ref, stats_ref[head : head + 1, :], head
        )
        stats_ref[heads + head : heads + head + 1, :] = total


def forward_kernel(
    q_ref, gt_ref, bias_ref, kv_ref, part_ref, part_sums_ref, stats_ref, scores_ref, *refs, dims
):
    heads, rows, width, held, ctx_count = dims
    *outs, top_ref, vt_ref, sums_ref = refs
    pair = heads // KEY_GROUPS
    key_group = place()[1]
    transpose_values([kv_ref], vt_ref, width)
    scores_pass(q_ref, bias_ref, [kv_ref], scores_ref, top_ref, dims=dims, first=held // rows - 1)
    for head in range(heads):
        cols = slice(head * width, (head + 1) * width)
        before = part_ref[head : head + 1, :]
        top = jnp.maximum(top_ref[head : head + 1, :], before)
        share = jnp.exp2(before - top)
        total, accum = sums_pass(vt_ref, scores_ref, top, head)
        total = total + share * part_ref[heads + head : heads + head + 1, :]
        accum = accum + share * part_sums_ref[head]
        delta = jnp.sum(accum * gt_ref[cols, :].astype(jnp.float32), axis=0, keepdims=True)
        for row, value in enumerate((top, total, delta)):
            stats_ref[row * heads + head : row * heads + head + 1, :] = value
        sums_ref[cols, :] = accum.astype(jnp.bfloat16)
    for slot, out_ref in enumerate(outs):
        out_ref[...] = sums_ref[head_columns(key_group ^ slot, pair * width), :]


def weights_kernel(g_ref, stats_ref, *refs, dims):
    heads, rows, width, held, ctx_count = dims
    *blocks, scores, last_scores, weights_ref, centred_ref = refs
    for head in range(heads):
        grad = g_ref[:, head * width : (head + 1) * width]
        top, total, delta = (stats_ref[k * heads + head : k * heads + head + 1, :] for k in range(3))
        mean = delta / total
        for part, ref in enumerate(blocks):
            here = slice(part * rows, (part + 1) * rows)
            row = last_scores[head] if part == len(blocks) - 1 else scores[head, here, :]
            weights = jnp.exp2(row - top)
            dprobs = lax.dot_general(ref[:, width:], grad, NT, preferred_element_type=jnp.float32)
            weights_ref[head, here, :] = weights.astype(jnp.bfloat16)
            centred_ref[head, here, :] = (weights * (dprobs - mean)).astype(jnp.bfloat16)


def merged_stats(stats, heads):
    top = functools.reduce(jnp.maximum, [s[:heads] for s in stats])
    shares = [jnp.exp2(s[:heads] - top) for s in stats]
    total = sum(f * s[heads : 2 * heads] for f, s in zip(shares, stats))
    delta = sum(f * s[2 * heads :] for f, s in zip(shares, stats)) / total
    return top, shares, total, delta


def query_factors(stats, heads):
    own = stats[0]
    _, shares, total, delta = merged_stats(stats, heads)
    return shares[0] / total, delta - own[2 * heads :] / own[heads : 2 * heads]


def core_rows(base, side, half):
    return pl.ds(pl.multiple_of(base + side * half, half), half)


def backward_kernel(q_ref, g_ref, weights_ref, centred_ref, *refs, dims, own):
    heads, rows, width, held, ctx_count = dims
    parts, half = held // rows, rows // 2
    stats, (terms_ref, acc_ref) = refs[:KEY_GROUPS], refs[-2:]
    head_group, key_group, chip, core = place()
    side = core if own else 1 - core
    scale = width**-0.5
    share, shift = query_factors([s[...] for s in stats], heads)
    factors = jnp.concatenate([share, share * shift], axis=0).T
    for head in range(heads):
        cols = slice(head * width, (head + 1) * width)
        by_share, by_both = factors[:, head : head + 1], factors[:, heads + head : heads + head + 1]
        query, grad = q_ref[:, cols].astype(jnp.float32), g_ref[:, cols].astype(jnp.float32)
        scaled = (query * by_share).astype(jnp.bfloat16)
        joint = jnp.concatenate([query * -by_both, grad * by_share], axis=1).astype(jnp.bfloat16)
        for part in range(parts):
            held_rows = core_rows(part * rows, side, half)
            both = jnp.dot(
                weights_ref[head, held_rows, :], joint, preferred_element_type=jnp.float32
            )
            dk = jnp.dot(
                centred_ref[head, held_rows, :], scaled, preferred_element_type=jnp.float32
            )
            here = slice(part * half, (part + 1) * half)
            if head == 0:
                acc_ref[here, :width] = dk + both[:, :width]
                acc_ref[here, width:] = both[:, width:]
            else:
                acc_ref[here, :width] += dk + both[:, :width]
                acc_ref[here, width:] += both[:, width:]
    chips, piece = ctx_count // 2, rows // 4
    level = chips // 4
    for spot in range(2 * chips):
        here = slice(spot * piece, (spot + 1) * piece)
        target = chip ^ (spot % chips)
        group = head_group ^ (spot // chips)
        block = group * (ctx_count // 2) + key_group * (ctx_count // 4) + target // 2
        flip = block // 2 ^ chip
        slot = flip // (2 * level) * level + flip % level
        line = (slot * 2 + (block % 2 ^ core)) * half + target % 2 * piece
        mine = pl.ds(pl.multiple_of(line, piece), piece)
        terms_ref[here, :width] = (acc_ref[mine, :width] * scale).astype(terms_ref.dtype)
        terms_ref[here, width:] = acc_ref[mine, width:].astype(terms_ref.dtype)


def query_kernel(*refs, dims):
    heads, rows, width, held, ctx_count = dims
    parts = held // rows
    blocks, (weights_ref, centred_ref), refs = refs[:parts], refs[parts : parts + 2], refs[parts + 2 :]
    stats, refs = refs[:KEY_GROUPS], refs[KEY_GROUPS + 1 :]
    outs, (kt_ref, share_ref, shift_ref) = refs[:KEY_GROUPS], refs[KEY_GROUPS:]
    pair = heads // KEY_GROUPS
    key_group = place()[1]
    share, shift_ref[...] = query_factors([s[...] for s in stats], heads)
    share_ref[...] = share * width**-0.5
    for part, ref in enumerate(blocks):
        keys = ref[:, :width].astype(jnp.float32)
        kt_ref[:, part * rows : (part + 1) * rows] = keys.T.astype(jnp.bfloat16)
    for slot in range(KEY_GROUPS):
        for part in range(pair):
            head = (key_group ^ slot) * pair + part
            centred = jnp.dot(kt_ref[...], centred_ref[head], preferred_element_type=jnp.float32)
            plain = jnp.dot(kt_ref[...], weights_ref[head], preferred_element_type=jnp.float32)
            dq = (centred - shift_ref[pl.ds(head, 1), :] * plain) * share_ref[pl.ds(head, 1), :]
            outs[slot][part * width : (part + 1) * width, :] = dq.astype(jnp.bfloat16)


def join_kernel(keep_ref, got_ref, kept_ref, send_ref):
    half = kept_ref.shape[0]
    kept_ref[...] = keep_ref[:half, :] + got_ref[:half, :].astype(jnp.float32)
    send = keep_ref[half:, :] + got_ref[half:, :].astype(jnp.float32)
    send_ref[...] = send.astype(jnp.bfloat16)


def spread_kernel(keep_ref, got_ref, token_ref, own_ref, *outs, rounds):
    piece = own_ref.shape[0]
    chip = place()[2]
    own_ref[...] = keep_ref[:piece, :] + got_ref[:piece, :].astype(jnp.float32)
    for out_ref, moves in zip(outs, rounds):
        flip = 0
        for source, target in moves.items():
            flip = jnp.where(chip == source, source ^ target, flip)
        mine = pl.ds(pl.multiple_of(flip * piece, piece), piece)
        out_ref[...] = (keep_ref[mine, :] + got_ref[mine, :].astype(jnp.float32)).astype(
            jnp.bfloat16
        )


def add_kernel(first_ref, second_ref, out_ref):
    out_ref[...] = first_ref[...] + second_ref[...].astype(jnp.float32)


def finish_out_kernel(*refs, dims):
    heads, rows, width, held, ctx_count = dims
    stats, outs = refs[:KEY_GROUPS], refs[KEY_GROUPS : 2 * KEY_GROUPS]
    attn_ref, token_ref = refs[2 * KEY_GROUPS :]
    token_ref[...] = jnp.zeros_like(token_ref)
    pair = heads // KEY_GROUPS
    top, shares, total, _ = merged_stats([s[...] for s in stats], heads)
    own = place()[1] * pair
    row = lax.broadcasted_iota(jnp.int32, (heads, 1), 0)
    for part in range(pair):
        here = slice(part * width, (part + 1) * width)

        def pick(array):
            return jnp.sum(jnp.where(row == own + part, array, 0.0), axis=0, keepdims=True)

        joined = sum(o[here, :].astype(jnp.float32) * pick(f) for o, f in zip(outs, shares))
        attn_ref[:, here] = (joined / pick(total)).T.astype(jnp.bfloat16)


def finish_query_kernel(own_ref, got_ref, gq_ref, token_ref):
    total = own_ref[...].astype(jnp.float32) + got_ref[...].astype(jnp.float32)
    gq_ref[...] = total.T.astype(jnp.bfloat16)
    token_ref[...] = jnp.zeros_like(token_ref)


def finish_kernel(token_ref, *refs):
    *terms, gk_ref, gv_ref = refs
    width = gk_ref.shape[1]
    both = sum(r[...].astype(jnp.float32) for r in terms)
    gk_ref[...] = both[:, :width].astype(jnp.bfloat16)
    gv_ref[...] = both[:, width:].astype(jnp.bfloat16)


def on_device(queries, keys, values, out_grad, segment_ids):
    rows = queries.shape[0]
    width = keys.shape[1]
    seq = segment_ids.shape[0]
    dp_count, ctx_count = lax.axis_size("dp"), lax.axis_size("ctx")
    head_groups = dp_count // KEY_GROUPS
    heads = queries.shape[1] // width // head_groups
    pair = heads // KEY_GROUPS
    chips = ctx_count // 2
    held = rows * ctx_count // KEY_GROUPS
    piece = rows // dp_count
    dims = (heads, rows, width, held, ctx_count)
    seg = segment_ids.reshape(seq // 128, 128)
    params = pltpu.CompilerParams(
        vmem_limit_bytes=min(56 * MIB, 12 * MIB + 12 * 4 * held * rows)
    )
    vmem = pl.BlockSpec(memory_space=pltpu.VMEM)
    bf16, f32 = jnp.bfloat16, jnp.float32

    def call(kernel, outs, ins, name, scratch=(), work=0, **static):
        specs = [a[1] if isinstance(a, tuple) else vmem for a in ins]
        arrays = [a[0] if isinstance(a, tuple) else a for a in ins]
        return pl.pallas_call(
            functools.partial(kernel, **static),
            out_shape=[jax.ShapeDtypeStruct(*o) for o in outs],
            in_specs=specs,
            out_specs=[vmem] * len(outs),
            scratch_shapes=list(scratch),
            compiler_params=params,
            cost_estimate=pl.CostEstimate(
                flops=work * 2 * heads * rows * held * width,
                bytes_accessed=sum(math.prod(o[0]) * 2 for o in outs),
                transcendentals=0,
            ),
            name=name,
        )(*arrays)

    def in_hbm(array):
        return pltpu.with_memory_space_constraint(array, pltpu.HBM), pl.BlockSpec(
            memory_space=pltpu.HBM
        )

    def over_dp(array, flip):
        return lax.ppermute(array, "dp", [(d, d ^ flip) for d in range(dp_count)])

    def over_cores(array):
        return lax.ppermute(array, "ctx", [(c, c ^ 1) for c in range(ctx_count)])

    def gathered(array, moves):
        pairs = []
        for d in range(0, dp_count, KEY_GROUPS):
            for (group, chip, core), (source, home) in moves.items():
                start = (d + source) * ctx_count + home * 2 + core
                pairs.append((start, (d + group) * ctx_count + chip * 2 + core))
        return lax.ppermute(array, ("dp", "ctx"), pairs)

    def spread(array, moves):
        pairs = [(a * 2 + core, b * 2 + core) for a, b in moves.items() for core in range(2)]
        return lax.ppermute(array, "ctx", pairs)

    (own_kv,) = call(
        load_kernel,
        [((rows, 2 * width), bf16)],
        [in_hbm(keys), in_hbm(values)],
        "load",
        scratch=[pltpu.SemaphoreType.DMA((2, dp_count))],
        pieces=dp_count,
    )
    query_v, grad_v, grad_t, bias, token = call(
        prep_kernel,
        [
            ((rows, heads * width), bf16),
            ((rows, heads * width), bf16),
            ((heads * width, rows), bf16),
            ((held, rows), f32),
            ((8, 128), f32),
        ],
        [in_hbm(seg), in_hbm(queries), in_hbm(out_grad)],
        "prepare",
        scratch=[pltpu.VMEM(seg.shape, seg.dtype), pltpu.SemaphoreType.DMA((3, heads))],
        work=1,
        dims=dims,
    )
    rounds = gather_rounds(chips)
    sent = [own_kv] + [gathered(own_kv, moves) for moves in rounds]
    blocks = []
    for spot in range(chips // 2):
        choices = []
        for group in range(KEY_GROUPS):
            for chip in range(chips):
                home = home_chip(spot, group, chip, chips)
                spot_key = (group, chip, 0)
                ways = [k for k, m in enumerate(rounds, 1) if m.get(spot_key, (0, -1))[1] == home]
                choices.append(0 if home == chip else ways[0] if home < chip else -1)
        used = sorted(set(choices) - {-1})
        (picked,) = call(
            pick_kernel,
            [((rows, 2 * width), bf16)],
            [sent[k] for k in used] + [token],
            "pick",
            choices=[used.index(c) if c >= 0 else -1 for c in choices],
        )
        blocks += [picked, over_cores(picked)]
    early = held - rows
    scores, part_stats, part_sums = call(
        part_kernel,
        [((heads, early, rows), f32), ((2 * heads, rows), f32), ((heads, width, rows), f32)],
        [query_v, bias] + blocks[:-1],
        "attend_most",
        scratch=[pltpu.VMEM((width, early), bf16)],
        work=2,
        dims=dims,
    )
    stats, last_scores, *outs = call(
        forward_kernel,
        [((3 * heads, rows), f32), ((heads, rows, rows), f32)]
        + [((pair * width, rows), bf16)] * KEY_GROUPS,
        [query_v, grad_t, bias, blocks[-1], part_stats, part_sums],
        "attend",
        scratch=[
            pltpu.VMEM((heads, rows), f32),
            pltpu.VMEM((width, rows), bf16),
            pltpu.VMEM((heads * width, rows), bf16),
        ],
        work=1,
        dims=dims,
    )
    all_stats = [stats, over_dp(stats, 1)]
    all_outs = [outs[0], over_dp(outs[1], 1)]
    weights, centred = call(
        weights_kernel,
        [((heads, held, rows), bf16)] * 2,
        [grad_v, stats] + blocks + [scores, last_scores],
        "weights",
        work=1,
        dims=dims,
    )

    def differentiate(own, dtype, after):
        return call(
            backward_kernel,
            [((held // 2, 2 * width), dtype)],
            [query_v, grad_v, weights, centred] + all_stats + after,
            "differentiate_own" if own else "differentiate_other",
            scratch=[pltpu.VMEM((held // 2, 2 * width), f32)],
            work=2,
            dims=dims,
            own=own,
        )

    (send,) = differentiate(False, bf16, [])
    got = over_cores(send)
    (keep,) = differentiate(True, f32, [send])
    attn_out, token = call(
        finish_out_kernel,
        [((rows, pair * width), bf16), ((8, 128), f32)],
        all_stats + all_outs,
        "finish_out",
        dims=dims,
    )
    quarter = held // 4
    keep, send = call(
        join_kernel,
        [((quarter, 2 * width), f32), ((quarter, 2 * width), bf16)],
        [keep, got],
        "join_cores",
    )
    dqs = call(
        query_kernel,
        [((pair * width, rows), bf16)] * KEY_GROUPS,
        blocks + [weights, centred] + all_stats + [keep],
        "query_terms",
        scratch=[pltpu.VMEM((width, held), bf16)] + [pltpu.VMEM((heads, rows), f32)] * 2,
        work=1,
        dims=dims,
    )
    all_dqs = [dqs[0], over_dp(dqs[1], 1)]
    rounds = spread_rounds(chips)
    terms, *pieces = call(
        spread_kernel,
        [((piece, 2 * width), f32)] + [((piece, 2 * width), bf16)] * len(rounds),
        [keep, over_dp(send, 2), token],
        "join_heads",
        rounds=rounds,
    )
    grad_q, token = call(
        finish_query_kernel,
        [((rows, pair * width), bf16), ((8, 128), f32)],
        all_dqs,
        "finish_query",
    )
    got = [spread(p, moves) for p, moves in zip(pieces, rounds)]
    for array in got[:-1]:
        (terms,) = call(add_kernel, [((piece, 2 * width), f32)], [terms, array], "add_terms")
    grad_k, grad_values = call(
        finish_kernel, [((piece, width), bf16)] * 2, [token, terms, got[-1]], "finish"
    )
    return attn_out, grad_q, grad_k, grad_values


def solution(mesh):
    return jax.shard_map(
        on_device,
        mesh=mesh,
        in_specs=(P("ctx", None), P("ctx", None), P("ctx", None), P("ctx", None), P()),
        out_specs=(P("ctx", "dp"), P("ctx", "dp"), P(("dp", "ctx"), None), P(("dp", "ctx"), None)),
        check_vma=False,
    )
```

```python
import functools
import math

import jax
import jax.numpy as jnp
from jax import lax
from jax.experimental import pallas as pl
from jax.experimental.pallas import tpu as pltpu
from jax.sharding import PartitionSpec as P

NEG = -1e30
LOG2E = 1.4426950408889634
DOC_NUMBERS = 4
KEY_GROUPS = 2
MIB = 1024 * 1024


def place():
    dp_index, ctx_index = lax.axis_index("dp"), lax.axis_index("ctx")
    return dp_index // KEY_GROUPS, dp_index % KEY_GROUPS, ctx_index // 2, ctx_index % 2

NT = (((1,), (1,)), ((), ()))


def home_chip(spot, key_group, chip, chips):
    level = chips // 4
    flip = spot // level * (2 * level) + spot % level
    home = chip ^ flip
    return home ^ ((home // level % 2) ^ key_group) * level


def gather_rounds(chips):
    rounds = [{} for _ in range(2 if chips == 4 else chips - 1)]
    for core in range(2):
        if chips == 4:
            rounds[0][0, 1, core] = (1, 0)
            rounds[0][0, 2, core] = (0, 0)
            rounds[0][1, 2, core] = (1, 1)
            rounds[0][0, 3, core] = (core, 2)
            rounds[1][0, 3, core] = (0, 0)
            rounds[1][1, 3, core] = (1, 1)
            continue
        for flip, moves in enumerate(rounds, 1):
            for home in range(chips):
                group = home // (chips // 4) % 2
                if home ^ flip > home:
                    moves[group, home ^ flip, core] = (group, home)
    return rounds


def spread_rounds(chips):
    flips = list(range(2, chips)) + [1]
    return [{chip: chip ^ flip for chip in range(chips)} for flip in flips]


def mask_bias(seg_ref, rows, held):
    _, key_group, chip, core = place()
    seg = seg_ref[...]
    lines = rows // 128
    seg_own = seg_ref[pl.ds((chip * 2 + core) * lines, lines), :]
    start = jnp.zeros((lines, 128), jnp.int32)
    for number in range(1, DOC_NUMBERS):
        before = jnp.sum((seg < number).astype(jnp.float32), axis=(0, 1), keepdims=True)
        start = jnp.where(seg_own == number, before.astype(jnp.int32), start)
    start = jnp.concatenate([start[k : k + 1] for k in range(lines)], axis=1)
    query_pos = (chip * 2 + core) * rows + lax.broadcasted_iota(jnp.int32, (1, rows), 1)
    blocks = held // rows
    size = rows // 4
    line = lax.broadcasted_iota(jnp.int32, (rows, rows), 0)
    place_of = line // size
    row = (place_of % 2 * 2 + place_of // 2) * size + line % size
    bias = []
    for block in range(blocks):
        home = home_chip(block // 2, key_group, chip, blocks) * 2 + (core ^ block % 2)
        key_pos = home * rows + row
        allowed = (key_pos >= start) & (key_pos <= query_pos)
        bias.append(jnp.where(allowed, 0.0, NEG))
    return bias


def row_order(pieces):
    return list(range(0, pieces, 2)) + list(range(1, pieces, 2))


def load_kernel(k_hbm, v_hbm, kv_ref, sems, *, pieces):
    rows, width = k_hbm.shape
    size = rows // pieces
    copies = []
    for spot, piece in enumerate(row_order(pieces)):
        source, target = (slice(k * size, (k + 1) * size) for k in (piece, spot))
        for k, array in enumerate((k_hbm, v_hbm)):
            columns = slice(k * width, (k + 1) * width)
            copies.append(
                pltpu.make_async_copy(
                    array.at[source, :], kv_ref.at[target, columns], sems.at[k, spot]
                )
            )
    for copy in copies:
        copy.start()
    for copy in copies:
        copy.wait()


def pick_kernel(*refs, choices):
    out_ref = refs[-1]
    _, key_group, chip, _ = place()
    spot = key_group * (len(choices) // 2) + chip
    for choice in sorted(set(choices)):
        wanted = functools.reduce(
            jnp.logical_or, [spot == k for k, c in enumerate(choices) if c == choice]
        )

        @pl.when(wanted)
        def _():
            out_ref[...] = jnp.zeros_like(out_ref) if choice < 0 else refs[choice][...]


def prep_kernel(
    seg_hbm, q_hbm, g_hbm, q_ref, g_ref, gt_ref, bias_ref, token_ref, seg_ref, sems, *, dims
):
    heads, rows, width, held, ctx_count = dims
    head_group = place()[0]
    seg_copy = pltpu.make_async_copy(seg_hbm, seg_ref, sems.at[2, 0])
    seg_copy.start()
    copies = []
    for head in range(heads):
        source = head_columns(head_group * heads + head, width)
        target = slice(head * width, (head + 1) * width)
        for k, (full, part) in enumerate(((g_hbm, g_ref), (q_hbm, q_ref))):
            copies.append(
                pltpu.make_async_copy(full.at[:, source], part.at[:, target], sems.at[k, head])
            )
            copies[-1].start()
    token_ref[...] = jnp.zeros_like(token_ref)
    seg_copy.wait()
    for k, block in enumerate(mask_bias(seg_ref, rows, held)):
        bias_ref[k * rows : (k + 1) * rows, :] = block
    for head in range(heads):
        cols = slice(head * width, (head + 1) * width)
        copies[2 * head].wait()
        gt_ref[cols, :] = g_ref[:, cols].astype(jnp.float32).T.astype(jnp.bfloat16)
    for head in range(heads):
        copies[2 * head + 1].wait()


def head_columns(head, width):
    return pl.ds(pl.multiple_of(head * width, width), width)


def scores_pass(q_ref, bias_ref, blocks, scores_ref, top_ref, *, dims, first):
    heads, rows, width, held, ctx_count = dims
    for head in range(heads):
        query = q_ref[:, head * width : (head + 1) * width]
        top = None
        for k, kv_ref in enumerate(blocks):
            bias = bias_ref[(first + k) * rows : (first + k + 1) * rows, :]
            raw = lax.dot_general(kv_ref[:, :width], query, NT, preferred_element_type=jnp.float32)
            scores = raw * (width**-0.5 * LOG2E) + bias
            scores_ref[head, k * rows : (k + 1) * rows, :] = scores
            here = jnp.max(scores, axis=0, keepdims=True)
            top = here if top is None else jnp.maximum(top, here)
        top_ref[head : head + 1, :] = top


def transpose_values(blocks, vt_ref, width):
    size = blocks[0].shape[0]
    for k, kv_ref in enumerate(blocks):
        vt = kv_ref[:, width:].astype(jnp.float32).T.astype(jnp.bfloat16)
        vt_ref[:, k * size : (k + 1) * size] = vt


def sums_pass(vt_ref, scores_ref, top, head):
    expd = jnp.exp2(scores_ref[head] - top)
    total = jnp.sum(expd, axis=0, keepdims=True)
    sums = jnp.dot(vt_ref[...], expd.astype(jnp.bfloat16), preferred_element_type=jnp.float32)
    return total, sums


def part_kernel(q_ref, bias_ref, *refs, dims):
    heads, rows, width, held, ctx_count = dims
    *blocks, scores_ref, stats_ref, sums_ref, vt_ref = refs
    transpose_values(blocks, vt_ref, width)
    scores_pass(q_ref, bias_ref, blocks, scores_ref, stats_ref, dims=dims, first=0)
    for head in range(heads):
        total, sums_ref[head] = sums_pass(
            vt_ref, scores_ref, stats_ref[head : head + 1, :], head
        )
        stats_ref[heads + head : heads + head + 1, :] = total


def forward_kernel(
    q_ref, gt_ref, bias_ref, kv_ref, part_ref, part_sums_ref, stats_ref, scores_ref, *refs, dims
):
    heads, rows, width, held, ctx_count = dims
    *outs, top_ref, vt_ref, sums_ref = refs
    pair = heads // KEY_GROUPS
    key_group = place()[1]
    transpose_values([kv_ref], vt_ref, width)
    scores_pass(q_ref, bias_ref, [kv_ref], scores_ref, top_ref, dims=dims, first=held // rows - 1)
    for head in range(heads):
        cols = slice(head * width, (head + 1) * width)
        before = part_ref[head : head + 1, :]
        top = jnp.maximum(top_ref[head : head + 1, :], before)
        share = jnp.exp2(before - top)
        total, accum = sums_pass(vt_ref, scores_ref, top, head)
        total = total + share * part_ref[heads + head : heads + head + 1, :]
        accum = accum + share * part_sums_ref[head]
        delta = jnp.sum(accum * gt_ref[cols, :].astype(jnp.float32), axis=0, keepdims=True)
        for row, value in enumerate((top, total, delta)):
            stats_ref[row * heads + head : row * heads + head + 1, :] = value
        sums_ref[cols, :] = accum.astype(jnp.bfloat16)
    for slot, out_ref in enumerate(outs):
        out_ref[...] = sums_ref[head_columns(key_group ^ slot, pair * width), :]


def dprobs_kernel(g_ref, *refs, dims):
    heads, rows, width, held, ctx_count = dims
    *blocks, dprobs_ref = refs
    for head in range(heads):
        grad = g_ref[:, head * width : (head + 1) * width]
        for part, ref in enumerate(blocks):
            dprobs_ref[head, part * rows : (part + 1) * rows, :] = lax.dot_general(
                ref[:, width:], grad, NT, preferred_element_type=jnp.float32
            )


def merged_stats(stats, heads):
    top = functools.reduce(jnp.maximum, [s[:heads] for s in stats])
    shares = [jnp.exp2(s[:heads] - top) for s in stats]
    total = sum(f * s[heads : 2 * heads] for f, s in zip(shares, stats))
    delta = sum(f * s[2 * heads :] for f, s in zip(shares, stats)) / total
    return top, shares, total, delta


def core_rows(base, side, half):
    return pl.ds(pl.multiple_of(base + side * half, half), half)


def backward_kernel(q_ref, g_ref, *refs, dims, ahead, own):
    heads, rows, width, held, ctx_count = dims
    parts, half = held // rows, rows // 2
    blocks, scores, last_scores, refs = refs[:parts], refs[parts], refs[parts + 1], refs[parts + 2 :]
    dprobs_ref, refs = (refs[0], refs[1:]) if ahead else (None, refs)
    stats = refs[:KEY_GROUPS]
    ds_ref, terms_ref, acc_ref, queries_ref, grads_ref = refs[-5:]
    head_group, key_group, chip, core = place()
    side = core if own else 1 - core
    scale = width**-0.5
    top, _, total, delta = merged_stats([s[...] for s in stats], heads)
    lse = top + jnp.log2(total)
    for head in range(heads):
        cols, here = (slice(head * size, (head + 1) * size) for size in (width, rows))
        queries_ref[here, :] = q_ref[:, cols]
        grads_ref[here, :] = g_ref[:, cols]
    for part, ref in enumerate(blocks):
        held_rows, block_rows = core_rows(part * rows, side, half), core_rows(0, side, half)
        here = slice(part * half, (part + 1) * half)
        all_probs, all_scores = [], []
        for head in range(heads):
            if part == parts - 1:
                row = last_scores[head, block_rows, :]
            else:
                row = scores[head, held_rows, :]
            probs = jnp.exp2(row - lse[head : head + 1])
            if ahead:
                dprobs = dprobs_ref[head, held_rows, :]
            else:
                dprobs = lax.dot_general(
                    ref[block_rows, width:],
                    g_ref[:, head * width : (head + 1) * width],
                    NT,
                    preferred_element_type=jnp.float32,
                )
            dscores = (probs * (dprobs - delta[head : head + 1])).astype(jnp.bfloat16)
            ds_ref[head, here, :] = dscores
            all_probs.append(probs.astype(jnp.bfloat16))
            all_scores.append(dscores)
        for columns, factors, stacked in (
            (slice(0, width), all_scores, queries_ref),
            (slice(width, 2 * width), all_probs, grads_ref),
        ):
            acc_ref[here, columns] = jnp.dot(
                jnp.concatenate(factors, axis=1), stacked[...], preferred_element_type=jnp.float32
            )
    chips, piece = ctx_count // 2, rows // 4
    level = chips // 4
    for spot in range(2 * chips):
        here = slice(spot * piece, (spot + 1) * piece)
        target = chip ^ (spot % chips)
        group = head_group ^ (spot // chips)
        block = group * (ctx_count // 2) + key_group * (ctx_count // 4) + target // 2
        flip = block // 2 ^ chip
        slot = flip // (2 * level) * level + flip % level
        line = (slot * 2 + (block % 2 ^ core)) * half + target % 2 * piece
        mine = pl.ds(pl.multiple_of(line, piece), piece)
        terms_ref[here, :width] = (acc_ref[mine, :width] * scale).astype(terms_ref.dtype)
        terms_ref[here, width:] = acc_ref[mine, width:].astype(terms_ref.dtype)


def query_kernel(*refs, dims):
    heads, rows, width, held, ctx_count = dims
    parts, half = held // rows, rows // 2
    blocks, dscores, refs = refs[:parts], refs[parts : parts + 2], refs[parts + 3 :]
    outs, kts = refs[:KEY_GROUPS], refs[KEY_GROUPS:]
    pair = heads // KEY_GROUPS
    _, key_group, _, core = place()
    scale = width**-0.5
    for kt_ref, side in zip(kts, (core, 1 - core)):
        for part, ref in enumerate(blocks):
            keys = ref[core_rows(0, side, half), :width].astype(jnp.float32)
            kt_ref[:, part * half : (part + 1) * half] = keys.T.astype(jnp.bfloat16)
    for slot in range(KEY_GROUPS):
        for part in range(pair):
            head = (key_group ^ slot) * pair + part
            dq = sum(
                jnp.dot(kt_ref[...], ds_ref[head], preferred_element_type=jnp.float32)
                for kt_ref, ds_ref in zip(kts, dscores)
            )
            outs[slot][part * width : (part + 1) * width, :] = (dq * scale).astype(jnp.bfloat16)


def join_kernel(keep_ref, got_ref, kept_ref, send_ref):
    half = kept_ref.shape[0]
    kept_ref[...] = keep_ref[:half, :] + got_ref[:half, :].astype(jnp.float32)
    send = keep_ref[half:, :] + got_ref[half:, :].astype(jnp.float32)
    send_ref[...] = send.astype(jnp.bfloat16)


def spread_kernel(keep_ref, got_ref, token_ref, own_ref, *outs, rounds):
    piece = own_ref.shape[0]
    chip = place()[2]
    own_ref[...] = keep_ref[:piece, :] + got_ref[:piece, :].astype(jnp.float32)
    for out_ref, moves in zip(outs, rounds):
        flip = 0
        for source, target in moves.items():
            flip = jnp.where(chip == source, source ^ target, flip)
        mine = pl.ds(pl.multiple_of(flip * piece, piece), piece)
        out_ref[...] = (keep_ref[mine, :] + got_ref[mine, :].astype(jnp.float32)).astype(
            jnp.bfloat16
        )


def add_kernel(first_ref, second_ref, out_ref):
    out_ref[...] = first_ref[...] + second_ref[...].astype(jnp.float32)


def finish_out_kernel(*refs, dims):
    heads, rows, width, held, ctx_count = dims
    stats, outs = refs[:KEY_GROUPS], refs[KEY_GROUPS : 2 * KEY_GROUPS]
    attn_ref, token_ref = refs[2 * KEY_GROUPS :]
    token_ref[...] = jnp.zeros_like(token_ref)
    pair = heads // KEY_GROUPS
    top, shares, total, _ = merged_stats([s[...] for s in stats], heads)
    own = place()[1] * pair
    row = lax.broadcasted_iota(jnp.int32, (heads, 1), 0)
    for part in range(pair):
        here = slice(part * width, (part + 1) * width)

        def pick(array):
            return jnp.sum(jnp.where(row == own + part, array, 0.0), axis=0, keepdims=True)

        joined = sum(o[here, :].astype(jnp.float32) * pick(f) for o, f in zip(outs, shares))
        attn_ref[:, here] = (joined / pick(total)).T.astype(jnp.bfloat16)


def finish_query_kernel(own_ref, got_ref, gq_ref, token_ref):
    total = own_ref[...].astype(jnp.float32) + got_ref[...].astype(jnp.float32)
    gq_ref[...] = total.T.astype(jnp.bfloat16)
    token_ref[...] = jnp.zeros_like(token_ref)


def finish_kernel(token_ref, *refs):
    *terms, gk_ref, gv_ref = refs
    width = gk_ref.shape[1]
    both = sum(r[...].astype(jnp.float32) for r in terms)
    gk_ref[...] = both[:, :width].astype(jnp.bfloat16)
    gv_ref[...] = both[:, width:].astype(jnp.bfloat16)


def on_device(queries, keys, values, out_grad, segment_ids):
    rows = queries.shape[0]
    width = keys.shape[1]
    seq = segment_ids.shape[0]
    dp_count, ctx_count = lax.axis_size("dp"), lax.axis_size("ctx")
    head_groups = dp_count // KEY_GROUPS
    heads = queries.shape[1] // width // head_groups
    pair = heads // KEY_GROUPS
    chips = ctx_count // 2
    held = rows * ctx_count // KEY_GROUPS
    piece = rows // dp_count
    dims = (heads, rows, width, held, ctx_count)
    seg = segment_ids.reshape(seq // 128, 128)
    params = pltpu.CompilerParams(
        vmem_limit_bytes=min(56 * MIB, 12 * MIB + 12 * 4 * held * rows)
    )
    vmem = pl.BlockSpec(memory_space=pltpu.VMEM)
    bf16, f32 = jnp.bfloat16, jnp.float32

    def call(kernel, outs, ins, name, scratch=(), work=0, **static):
        specs = [a[1] if isinstance(a, tuple) else vmem for a in ins]
        arrays = [a[0] if isinstance(a, tuple) else a for a in ins]
        return pl.pallas_call(
            functools.partial(kernel, **static),
            out_shape=[jax.ShapeDtypeStruct(*o) for o in outs],
            in_specs=specs,
            out_specs=[vmem] * len(outs),
            scratch_shapes=list(scratch),
            compiler_params=params,
            cost_estimate=pl.CostEstimate(
                flops=work * 2 * heads * rows * held * width,
                bytes_accessed=sum(math.prod(o[0]) * 2 for o in outs),
                transcendentals=0,
            ),
            name=name,
        )(*arrays)

    def in_hbm(array):
        return pltpu.with_memory_space_constraint(array, pltpu.HBM), pl.BlockSpec(
            memory_space=pltpu.HBM
        )

    def over_dp(array, flip):
        return lax.ppermute(array, "dp", [(d, d ^ flip) for d in range(dp_count)])

    def over_cores(array):
        return lax.ppermute(array, "ctx", [(c, c ^ 1) for c in range(ctx_count)])

    def gathered(array, moves):
        pairs = []
        for d in range(0, dp_count, KEY_GROUPS):
            for (group, chip, core), (source, home) in moves.items():
                start = (d + source) * ctx_count + home * 2 + core
                pairs.append((start, (d + group) * ctx_count + chip * 2 + core))
        return lax.ppermute(array, ("dp", "ctx"), pairs)

    def spread(array, moves):
        pairs = [(a * 2 + core, b * 2 + core) for a, b in moves.items() for core in range(2)]
        return lax.ppermute(array, "ctx", pairs)

    (own_kv,) = call(
        load_kernel,
        [((rows, 2 * width), bf16)],
        [in_hbm(keys), in_hbm(values)],
        "load",
        scratch=[pltpu.SemaphoreType.DMA((2, dp_count))],
        pieces=dp_count,
    )
    query_v, grad_v, grad_t, bias, token = call(
        prep_kernel,
        [
            ((rows, heads * width), bf16),
            ((rows, heads * width), bf16),
            ((heads * width, rows), bf16),
            ((held, rows), f32),
            ((8, 128), f32),
        ],
        [in_hbm(seg), in_hbm(queries), in_hbm(out_grad)],
        "prepare",
        scratch=[pltpu.VMEM(seg.shape, seg.dtype), pltpu.SemaphoreType.DMA((3, heads))],
        work=1,
        dims=dims,
    )
    rounds = gather_rounds(chips)
    sent = [own_kv] + [gathered(own_kv, moves) for moves in rounds]
    blocks = []
    for spot in range(chips // 2):
        choices = []
        for group in range(KEY_GROUPS):
            for chip in range(chips):
                home = home_chip(spot, group, chip, chips)
                spot_key = (group, chip, 0)
                ways = [k for k, m in enumerate(rounds, 1) if m.get(spot_key, (0, -1))[1] == home]
                choices.append(0 if home == chip else ways[0] if home < chip else -1)
        used = sorted(set(choices) - {-1})
        (picked,) = call(
            pick_kernel,
            [((rows, 2 * width), bf16)],
            [sent[k] for k in used] + [token],
            "pick",
            choices=[used.index(c) if c >= 0 else -1 for c in choices],
        )
        blocks += [picked, over_cores(picked)]
    early = held - rows
    scores, part_stats, part_sums = call(
        part_kernel,
        [((heads, early, rows), f32), ((2 * heads, rows), f32), ((heads, width, rows), f32)],
        [query_v, bias] + blocks[:-1],
        "attend_most",
        scratch=[pltpu.VMEM((width, early), bf16)],
        work=2,
        dims=dims,
    )
    stats, last_scores, *outs = call(
        forward_kernel,
        [((3 * heads, rows), f32), ((heads, rows, rows), f32)]
        + [((pair * width, rows), bf16)] * KEY_GROUPS,
        [query_v, grad_t, bias, blocks[-1], part_stats, part_sums],
        "attend",
        scratch=[
            pltpu.VMEM((heads, rows), f32),
            pltpu.VMEM((width, rows), bf16),
            pltpu.VMEM((heads * width, rows), bf16),
        ],
        work=1,
        dims=dims,
    )
    all_stats = [stats, over_dp(stats, 1)]
    all_outs = [outs[0], over_dp(outs[1], 1)]
    ahead = 4 * heads * held * rows <= 8 * MIB
    dprobs = []
    if ahead:
        dprobs = call(
            dprobs_kernel,
            [((heads, held, rows), f32)],
            [grad_v] + blocks,
            "dprobs",
            work=1,
            dims=dims,
        )

    inputs = [query_v, grad_v] + blocks + [scores, last_scores] + list(dprobs) + all_stats

    def differentiate(own, dtype, after):
        return call(
            backward_kernel,
            [((heads, held // 2, rows), bf16), ((held // 2, 2 * width), dtype)],
            inputs + after,
            "differentiate_own" if own else "differentiate_other",
            scratch=[pltpu.VMEM((held // 2, 2 * width), f32)]
            + [pltpu.VMEM((heads * rows, width), bf16)] * 2,
            work=2,
            dims=dims,
            ahead=ahead,
            own=own,
        )

    other_scores, send = differentiate(False, bf16, [])
    got = over_cores(send)
    own_scores, keep = differentiate(True, f32, [other_scores])
    attn_out, token = call(
        finish_out_kernel,
        [((rows, pair * width), bf16), ((8, 128), f32)],
        all_stats + all_outs,
        "finish_out",
        dims=dims,
    )
    quarter = held // 4
    keep, send = call(
        join_kernel,
        [((quarter, 2 * width), f32), ((quarter, 2 * width), bf16)],
        [keep, got],
        "join_cores",
    )
    dqs = call(
        query_kernel,
        [((pair * width, rows), bf16)] * KEY_GROUPS,
        blocks + [own_scores, other_scores, keep],
        "query_terms",
        scratch=[pltpu.VMEM((width, held // 2), bf16)] * 2,
        work=1,
        dims=dims,
    )
    all_dqs = [dqs[0], over_dp(dqs[1], 1)]
    rounds = spread_rounds(chips)
    terms, *pieces = call(
        spread_kernel,
        [((piece, 2 * width), f32)] + [((piece, 2 * width), bf16)] * len(rounds),
        [keep, over_dp(send, 2), token],
        "join_heads",
        rounds=rounds,
    )
    grad_q, token = call(
        finish_query_kernel,
        [((rows, pair * width), bf16), ((8, 128), f32)],
        all_dqs,
        "finish_query",
    )
    got = [spread(p, moves) for p, moves in zip(pieces, rounds)]
    for array in got[:-1]:
        (terms,) = call(add_kernel, [((piece, 2 * width), f32)], [terms, array], "add_terms")
    grad_k, grad_values = call(
        finish_kernel, [((piece, width), bf16)] * 2, [token, terms, got[-1]], "finish"
    )
    return attn_out, grad_q, grad_k, grad_values


def solution(mesh):
    return jax.shard_map(
        on_device,
        mesh=mesh,
        in_specs=(P("ctx", None), P("ctx", None), P("ctx", None), P("ctx", None), P()),
        out_specs=(P("ctx", "dp"), P("ctx", "dp"), P(("dp", "ctx"), None), P(("dp", "ctx"), None)),
        check_vma=False,
    )
```

```python
import functools
import math

import jax
import jax.numpy as jnp
from jax import lax
from jax.experimental import pallas as pl
from jax.experimental.pallas import tpu as pltpu
from jax.sharding import PartitionSpec as P

NEG = -1e30
LOG2E = 1.4426950408889634
DOC_NUMBERS = 4
KEY_GROUPS = 2
MIB = 1024 * 1024


def place():
    dp_index, ctx_index = lax.axis_index("dp"), lax.axis_index("ctx")
    return dp_index // KEY_GROUPS, dp_index % KEY_GROUPS, ctx_index // 2, ctx_index % 2

NT = (((1,), (1,)), ((), ()))


def home_chip(spot, key_group, chip, chips):
    level = chips // 4
    flip = spot // level * (2 * level) + spot % level
    home = chip ^ flip
    return home ^ ((home // level % 2) ^ key_group) * level


def gather_rounds(chips):
    rounds = [{} for _ in range(2 if chips == 4 else chips - 1)]
    for core in range(2):
        if chips == 4:
            rounds[0][0, 1, core] = (1, 0)
            rounds[0][0, 2, core] = (0, 0)
            rounds[0][1, 2, core] = (1, 1)
            rounds[0][0, 3, core] = (core, 2)
            rounds[1][0, 3, core] = (0, 0)
            rounds[1][1, 3, core] = (1, 1)
            continue
        for flip, moves in enumerate(rounds, 1):
            for home in range(chips):
                group = home // (chips // 4) % 2
                if home ^ flip > home:
                    moves[group, home ^ flip, core] = (group, home)
    return rounds


def spread_rounds(chips):
    return [{chip: (chip + step) % chips for chip in range(chips)} for step in range(1, chips)]


def mask_bias(seg_ref, rows, held):
    _, key_group, chip, core = place()
    seg = seg_ref[...]
    lines = rows // 128
    seg_own = seg_ref[pl.ds((chip * 2 + core) * lines, lines), :]
    start = jnp.zeros((lines, 128), jnp.int32)
    for number in range(1, DOC_NUMBERS):
        before = jnp.sum((seg < number).astype(jnp.float32), axis=(0, 1), keepdims=True)
        start = jnp.where(seg_own == number, before.astype(jnp.int32), start)
    start = jnp.concatenate([start[k : k + 1] for k in range(lines)], axis=1)
    query_pos = (chip * 2 + core) * rows + lax.broadcasted_iota(jnp.int32, (1, rows), 1)
    blocks = held // rows
    size = rows // 4
    line = lax.broadcasted_iota(jnp.int32, (rows, rows), 0)
    place_of = line // size
    row = (place_of % 2 * 2 + place_of // 2) * size + line % size
    bias = []
    for block in range(blocks):
        home = home_chip(block // 2, key_group, chip, blocks) * 2 + (core ^ block % 2)
        key_pos = home * rows + row
        allowed = (key_pos >= start) & (key_pos <= query_pos)
        bias.append(jnp.where(allowed, 0.0, NEG))
    return bias


def row_order(pieces):
    return list(range(0, pieces, 2)) + list(range(1, pieces, 2))


def load_kernel(k_hbm, v_hbm, kv_ref, sems, *, pieces):
    rows, width = k_hbm.shape
    size = rows // pieces
    copies = []
    for spot, piece in enumerate(row_order(pieces)):
        source, target = (slice(k * size, (k + 1) * size) for k in (piece, spot))
        for k, array in enumerate((k_hbm, v_hbm)):
            columns = slice(k * width, (k + 1) * width)
            copies.append(
                pltpu.make_async_copy(
                    array.at[source, :], kv_ref.at[target, columns], sems.at[k, spot]
                )
            )
    for copy in copies:
        copy.start()
    for copy in copies:
        copy.wait()


def pick_kernel(*refs, choices):
    out_ref = refs[-1]
    _, key_group, chip, _ = place()
    spot = key_group * (len(choices) // 2) + chip
    for choice in sorted(set(choices)):
        wanted = functools.reduce(
            jnp.logical_or, [spot == k for k, c in enumerate(choices) if c == choice]
        )

        @pl.when(wanted)
        def _():
            out_ref[...] = jnp.zeros_like(out_ref) if choice < 0 else refs[choice][...]


def prep_kernel(
    seg_hbm, q_hbm, g_hbm, q_ref, g_ref, gt_ref, bias_ref, token_ref, seg_ref, sems, *, dims
):
    heads, rows, width, held, ctx_count = dims
    head_group = place()[0]
    seg_copy = pltpu.make_async_copy(seg_hbm, seg_ref, sems.at[2, 0])
    seg_copy.start()
    copies = []
    for head in range(heads):
        source = head_columns(head_group * heads + head, width)
        target = slice(head * width, (head + 1) * width)
        for k, (full, part) in enumerate(((g_hbm, g_ref), (q_hbm, q_ref))):
            copies.append(
                pltpu.make_async_copy(full.at[:, source], part.at[:, target], sems.at[k, head])
            )
            copies[-1].start()
    token_ref[...] = jnp.zeros_like(token_ref)
    seg_copy.wait()
    for k, block in enumerate(mask_bias(seg_ref, rows, held)):
        bias_ref[k * rows : (k + 1) * rows, :] = block
    for head in range(heads):
        cols = slice(head * width, (head + 1) * width)
        copies[2 * head].wait()
        gt_ref[cols, :] = g_ref[:, cols].astype(jnp.float32).T.astype(jnp.bfloat16)
    for head in range(heads):
        copies[2 * head + 1].wait()


def head_columns(head, width):
    return pl.ds(pl.multiple_of(head * width, width), width)


def scores_pass(q_ref, bias_ref, blocks, scores_ref, top_ref, *, dims, first):
    heads, rows, width, held, ctx_count = dims
    for head in range(heads):
        query = q_ref[:, head * width : (head + 1) * width]
        top = None
        for k, kv_ref in enumerate(blocks):
            bias = bias_ref[(first + k) * rows : (first + k + 1) * rows, :]
            raw = lax.dot_general(kv_ref[:, :width], query, NT, preferred_element_type=jnp.float32)
            scores = raw * (width**-0.5 * LOG2E) + bias
            scores_ref[head, k * rows : (k + 1) * rows, :] = scores
            here = jnp.max(scores, axis=0, keepdims=True)
            top = here if top is None else jnp.maximum(top, here)
        top_ref[head : head + 1, :] = top


def transpose_values(blocks, vt_ref, width):
    size = blocks[0].shape[0]
    for k, kv_ref in enumerate(blocks):
        vt = kv_ref[:, width:].astype(jnp.float32).T.astype(jnp.bfloat16)
        vt_ref[:, k * size : (k + 1) * size] = vt


def sums_pass(vt_ref, scores_ref, top, head):
    expd = jnp.exp2(scores_ref[head] - top)
    total = jnp.sum(expd, axis=0, keepdims=True)
    sums = jnp.dot(vt_ref[...], expd.astype(jnp.bfloat16), preferred_element_type=jnp.float32)
    return total, sums


def part_kernel(q_ref, bias_ref, *refs, dims):
    heads, rows, width, held, ctx_count = dims
    *blocks, scores_ref, stats_ref, sums_ref, vt_ref = refs
    transpose_values(blocks, vt_ref, width)
    scores_pass(q_ref, bias_ref, blocks, scores_ref, stats_ref, dims=dims, first=0)
    for head in range(heads):
        total, sums_ref[head] = sums_pass(
            vt_ref, scores_ref, stats_ref[head : head + 1, :], head
        )
        stats_ref[heads + head : heads + head + 1, :] = total


def forward_kernel(
    q_ref, gt_ref, bias_ref, kv_ref, part_ref, part_sums_ref, stats_ref, scores_ref, *refs, dims
):
    heads, rows, width, held, ctx_count = dims
    *outs, top_ref, vt_ref, sums_ref = refs
    pair = heads // KEY_GROUPS
    key_group = place()[1]
    transpose_values([kv_ref], vt_ref, width)
    scores_pass(q_ref, bias_ref, [kv_ref], scores_ref, top_ref, dims=dims, first=held // rows - 1)
    for head in range(heads):
        cols = slice(head * width, (head + 1) * width)
        before = part_ref[head : head + 1, :]
        top = jnp.maximum(top_ref[head : head + 1, :], before)
        share = jnp.exp2(before - top)
        total, accum = sums_pass(vt_ref, scores_ref, top, head)
        total = total + share * part_ref[heads + head : heads + head + 1, :]
        accum = accum + share * part_sums_ref[head]
        delta = jnp.sum(accum * gt_ref[cols, :].astype(jnp.float32), axis=0, keepdims=True)
        for row, value in enumerate((top, total, delta)):
            stats_ref[row * heads + head : row * heads + head + 1, :] = value
        sums_ref[cols, :] = accum.astype(jnp.bfloat16)
    for slot, out_ref in enumerate(outs):
        out_ref[...] = sums_ref[head_columns(key_group ^ slot, pair * width), :]


def dprobs_kernel(g_ref, *refs, dims):
    heads, rows, width, held, ctx_count = dims
    *blocks, dprobs_ref = refs
    for head in range(heads):
        grad = g_ref[:, head * width : (head + 1) * width]
        for part, ref in enumerate(blocks):
            dprobs_ref[head, part * rows : (part + 1) * rows, :] = lax.dot_general(
                ref[:, width:], grad, NT, preferred_element_type=jnp.float32
            )


def merged_stats(stats, heads):
    top = functools.reduce(jnp.maximum, [s[:heads] for s in stats])
    shares = [jnp.exp2(s[:heads] - top) for s in stats]
    total = sum(f * s[heads : 2 * heads] for f, s in zip(shares, stats))
    delta = sum(f * s[2 * heads :] for f, s in zip(shares, stats)) / total
    return top, shares, total, delta


def core_rows(base, side, half):
    return pl.ds(pl.multiple_of(base + side * half, half), half)


def backward_kernel(q_ref, g_ref, *refs, dims, ahead, own):
    heads, rows, width, held, ctx_count = dims
    parts, half = held // rows, rows // 2
    blocks, scores, last_scores, refs = refs[:parts], refs[parts], refs[parts + 1], refs[parts + 2 :]
    dprobs_ref, refs = (refs[0], refs[1:]) if ahead else (None, refs)
    stats = refs[:KEY_GROUPS]
    ds_ref, terms_ref, acc_ref = refs[-3:]
    head_group, key_group, chip, core = place()
    side = core if own else 1 - core
    scale = width**-0.5
    top, _, total, delta = merged_stats([s[...] for s in stats], heads)
    lse = top + jnp.log2(total)
    for head in range(heads):
        cols = slice(head * width, (head + 1) * width)
        query, grad = q_ref[:, cols], g_ref[:, cols]
        for part, ref in enumerate(blocks):
            held_rows, block_rows = core_rows(part * rows, side, half), core_rows(0, side, half)
            if part == parts - 1:
                row = last_scores[head, block_rows, :]
            else:
                row = scores[head, held_rows, :]
            probs = jnp.exp2(row - lse[head : head + 1])
            if ahead:
                dprobs = dprobs_ref[head, held_rows, :]
            else:
                dprobs = lax.dot_general(
                    ref[block_rows, width:], grad, NT, preferred_element_type=jnp.float32
                )
            dscores = (probs * (dprobs - delta[head : head + 1])).astype(jnp.bfloat16)
            here = slice(part * half, (part + 1) * half)
            ds_ref[head, here, :] = dscores
            dv = jnp.dot(probs.astype(jnp.bfloat16), grad, preferred_element_type=jnp.float32)
            dk = jnp.dot(dscores, query, preferred_element_type=jnp.float32)
            if head == 0:
                acc_ref[here, :width] = dk
                acc_ref[here, width:] = dv
            else:
                acc_ref[here, :width] += dk
                acc_ref[here, width:] += dv
    chips, piece = ctx_count // 2, rows // 4
    level = chips // 4
    for spot in range(2 * chips):
        here = slice(spot * piece, (spot + 1) * piece)
        target = chip ^ (spot % chips)
        group = head_group ^ (spot // chips)
        block = group * (ctx_count // 2) + key_group * (ctx_count // 4) + target // 2
        flip = block // 2 ^ chip
        slot = flip // (2 * level) * level + flip % level
        line = (slot * 2 + (block % 2 ^ core)) * half + target % 2 * piece
        mine = pl.ds(pl.multiple_of(line, piece), piece)
        terms_ref[here, :width] = (acc_ref[mine, :width] * scale).astype(terms_ref.dtype)
        terms_ref[here, width:] = acc_ref[mine, width:].astype(terms_ref.dtype)


def query_kernel(*refs, dims):
    heads, rows, width, held, ctx_count = dims
    parts, half = held // rows, rows // 2
    blocks, dscores, refs = refs[:parts], refs[parts : parts + 2], refs[parts + 3 :]
    outs, kts = refs[:KEY_GROUPS], refs[KEY_GROUPS:]
    pair = heads // KEY_GROUPS
    _, key_group, _, core = place()
    scale = width**-0.5
    for kt_ref, side in zip(kts, (core, 1 - core)):
        for part, ref in enumerate(blocks):
            keys = ref[core_rows(0, side, half), :width].astype(jnp.float32)
            kt_ref[:, part * half : (part + 1) * half] = keys.T.astype(jnp.bfloat16)
    for slot in range(KEY_GROUPS):
        for part in range(pair):
            head = (key_group ^ slot) * pair + part
            dq = sum(
                jnp.dot(kt_ref[...], ds_ref[head], preferred_element_type=jnp.float32)
                for kt_ref, ds_ref in zip(kts, dscores)
            )
            outs[slot][part * width : (part + 1) * width, :] = (dq * scale).astype(jnp.bfloat16)


def join_kernel(keep_ref, got_ref, kept_ref, send_ref):
    half = kept_ref.shape[0]
    kept_ref[...] = keep_ref[:half, :] + got_ref[:half, :].astype(jnp.float32)
    send = keep_ref[half:, :] + got_ref[half:, :].astype(jnp.float32)
    send_ref[...] = send.astype(jnp.bfloat16)


def spread_kernel(keep_ref, got_ref, token_ref, own_ref, *outs, rounds):
    piece = own_ref.shape[0]
    chip = place()[2]
    own_ref[...] = keep_ref[:piece, :] + got_ref[:piece, :].astype(jnp.float32)
    for out_ref, moves in zip(outs, rounds):
        flip = 0
        for source, target in moves.items():
            flip = jnp.where(chip == source, source ^ target, flip)
        mine = pl.ds(pl.multiple_of(flip * piece, piece), piece)
        out_ref[...] = (keep_ref[mine, :] + got_ref[mine, :].astype(jnp.float32)).astype(
            jnp.bfloat16
        )


def add_kernel(first_ref, second_ref, out_ref):
    out_ref[...] = first_ref[...] + second_ref[...].astype(jnp.float32)


def finish_out_kernel(*refs, dims):
    heads, rows, width, held, ctx_count = dims
    stats, outs = refs[:KEY_GROUPS], refs[KEY_GROUPS : 2 * KEY_GROUPS]
    attn_ref, token_ref = refs[2 * KEY_GROUPS :]
    token_ref[...] = jnp.zeros_like(token_ref)
    pair = heads // KEY_GROUPS
    top, shares, total, _ = merged_stats([s[...] for s in stats], heads)
    own = place()[1] * pair
    row = lax.broadcasted_iota(jnp.int32, (heads, 1), 0)
    for part in range(pair):
        here = slice(part * width, (part + 1) * width)

        def pick(array):
            return jnp.sum(jnp.where(row == own + part, array, 0.0), axis=0, keepdims=True)

        joined = sum(o[here, :].astype(jnp.float32) * pick(f) for o, f in zip(outs, shares))
        attn_ref[:, here] = (joined / pick(total)).T.astype(jnp.bfloat16)


def finish_query_kernel(own_ref, got_ref, gq_ref, token_ref):
    total = own_ref[...].astype(jnp.float32) + got_ref[...].astype(jnp.float32)
    gq_ref[...] = total.T.astype(jnp.bfloat16)
    token_ref[...] = jnp.zeros_like(token_ref)


def finish_kernel(token_ref, *refs):
    *terms, gk_ref, gv_ref = refs
    width = gk_ref.shape[1]
    both = sum(r[...].astype(jnp.float32) for r in terms)
    gk_ref[...] = both[:, :width].astype(jnp.bfloat16)
    gv_ref[...] = both[:, width:].astype(jnp.bfloat16)


def on_device(queries, keys, values, out_grad, segment_ids):
    rows = queries.shape[0]
    width = keys.shape[1]
    seq = segment_ids.shape[0]
    dp_count, ctx_count = lax.axis_size("dp"), lax.axis_size("ctx")
    head_groups = dp_count // KEY_GROUPS
    heads = queries.shape[1] // width // head_groups
    pair = heads // KEY_GROUPS
    chips = ctx_count // 2
    held = rows * ctx_count // KEY_GROUPS
    piece = rows // dp_count
    dims = (heads, rows, width, held, ctx_count)
    seg = segment_ids.reshape(seq // 128, 128)
    params = pltpu.CompilerParams(
        vmem_limit_bytes=min(56 * MIB, 12 * MIB + 12 * 4 * held * rows)
    )
    vmem = pl.BlockSpec(memory_space=pltpu.VMEM)
    bf16, f32 = jnp.bfloat16, jnp.float32

    def call(kernel, outs, ins, name, scratch=(), work=0, **static):
        specs = [a[1] if isinstance(a, tuple) else vmem for a in ins]
        arrays = [a[0] if isinstance(a, tuple) else a for a in ins]
        return pl.pallas_call(
            functools.partial(kernel, **static),
            out_shape=[jax.ShapeDtypeStruct(*o) for o in outs],
            in_specs=specs,
            out_specs=[vmem] * len(outs),
            scratch_shapes=list(scratch),
            compiler_params=params,
            cost_estimate=pl.CostEstimate(
                flops=work * 2 * heads * rows * held * width,
                bytes_accessed=sum(math.prod(o[0]) * 2 for o in outs),
                transcendentals=0,
            ),
            name=name,
        )(*arrays)

    def in_hbm(array):
        return pltpu.with_memory_space_constraint(array, pltpu.HBM), pl.BlockSpec(
            memory_space=pltpu.HBM
        )

    def over_dp(array, flip):
        return lax.ppermute(array, "dp", [(d, d ^ flip) for d in range(dp_count)])

    def over_cores(array):
        return lax.ppermute(array, "ctx", [(c, c ^ 1) for c in range(ctx_count)])

    def gathered(array, moves):
        pairs = []
        for d in range(0, dp_count, KEY_GROUPS):
            for (group, chip, core), (source, home) in moves.items():
                start = (d + source) * ctx_count + home * 2 + core
                pairs.append((start, (d + group) * ctx_count + chip * 2 + core))
        return lax.ppermute(array, ("dp", "ctx"), pairs)

    def spread(array, moves):
        pairs = [(a * 2 + core, b * 2 + core) for a, b in moves.items() for core in range(2)]
        return lax.ppermute(array, "ctx", pairs)

    (own_kv,) = call(
        load_kernel,
        [((rows, 2 * width), bf16)],
        [in_hbm(keys), in_hbm(values)],
        "load",
        scratch=[pltpu.SemaphoreType.DMA((2, dp_count))],
        pieces=dp_count,
    )
    query_v, grad_v, grad_t, bias, token = call(
        prep_kernel,
        [
            ((rows, heads * width), bf16),
            ((rows, heads * width), bf16),
            ((heads * width, rows), bf16),
            ((held, rows), f32),
            ((8, 128), f32),
        ],
        [in_hbm(seg), in_hbm(queries), in_hbm(out_grad)],
        "prepare",
        scratch=[pltpu.VMEM(seg.shape, seg.dtype), pltpu.SemaphoreType.DMA((3, heads))],
        work=1,
        dims=dims,
    )
    rounds = gather_rounds(chips)
    sent = [own_kv] + [gathered(own_kv, moves) for moves in rounds]
    blocks = []
    for spot in range(chips // 2):
        choices = []
        for group in range(KEY_GROUPS):
            for chip in range(chips):
                home = home_chip(spot, group, chip, chips)
                spot_key = (group, chip, 0)
                ways = [k for k, m in enumerate(rounds, 1) if m.get(spot_key, (0, -1))[1] == home]
                choices.append(0 if home == chip else ways[0] if home < chip else -1)
        used = sorted(set(choices) - {-1})
        (picked,) = call(
            pick_kernel,
            [((rows, 2 * width), bf16)],
            [sent[k] for k in used] + [token],
            "pick",
            choices=[used.index(c) if c >= 0 else -1 for c in choices],
        )
        blocks += [picked, over_cores(picked)]
    early = held - rows
    scores, part_stats, part_sums = call(
        part_kernel,
        [((heads, early, rows), f32), ((2 * heads, rows), f32), ((heads, width, rows), f32)],
        [query_v, bias] + blocks[:-1],
        "attend_most",
        scratch=[pltpu.VMEM((width, early), bf16)],
        work=2,
        dims=dims,
    )
    stats, last_scores, *outs = call(
        forward_kernel,
        [((3 * heads, rows), f32), ((heads, rows, rows), f32)]
        + [((pair * width, rows), bf16)] * KEY_GROUPS,
        [query_v, grad_t, bias, blocks[-1], part_stats, part_sums],
        "attend",
        scratch=[
            pltpu.VMEM((heads, rows), f32),
            pltpu.VMEM((width, rows), bf16),
            pltpu.VMEM((heads * width, rows), bf16),
        ],
        work=1,
        dims=dims,
    )
    all_stats = [stats, over_dp(stats, 1)]
    all_outs = [outs[0], over_dp(outs[1], 1)]
    ahead = 4 * heads * held * rows <= 8 * MIB
    dprobs = []
    if ahead:
        dprobs = call(
            dprobs_kernel,
            [((heads, held, rows), f32)],
            [grad_v] + blocks,
            "dprobs",
            work=1,
            dims=dims,
        )

    inputs = [query_v, grad_v] + blocks + [scores, last_scores] + list(dprobs) + all_stats

    def differentiate(own, dtype, after):
        return call(
            backward_kernel,
            [((heads, held // 2, rows), bf16), ((held // 2, 2 * width), dtype)],
            inputs + after,
            "differentiate_own" if own else "differentiate_other",
            scratch=[pltpu.VMEM((held // 2, 2 * width), f32)],
            work=2,
            dims=dims,
            ahead=ahead,
            own=own,
        )

    other_scores, send = differentiate(False, bf16, [])
    got = over_cores(send)
    own_scores, keep = differentiate(True, f32, [other_scores])
    attn_out, token = call(
        finish_out_kernel,
        [((rows, pair * width), bf16), ((8, 128), f32)],
        all_stats + all_outs,
        "finish_out",
        dims=dims,
    )
    quarter = held // 4
    keep, send = call(
        join_kernel,
        [((quarter, 2 * width), f32), ((quarter, 2 * width), bf16)],
        [keep, got],
        "join_cores",
    )
    dqs = call(
        query_kernel,
        [((pair * width, rows), bf16)] * KEY_GROUPS,
        blocks + [own_scores, other_scores, keep],
        "query_terms",
        scratch=[pltpu.VMEM((width, held // 2), bf16)] * 2,
        work=1,
        dims=dims,
    )
    all_dqs = [dqs[0], over_dp(dqs[1], 1)]
    rounds = spread_rounds(chips)
    terms, *pieces = call(
        spread_kernel,
        [((piece, 2 * width), f32)] + [((piece, 2 * width), bf16)] * len(rounds),
        [keep, over_dp(send, 2), token],
        "join_heads",
        rounds=rounds,
    )
    grad_q, token = call(
        finish_query_kernel,
        [((rows, pair * width), bf16), ((8, 128), f32)],
        all_dqs,
        "finish_query",
    )
    got = [spread(p, moves) for p, moves in zip(pieces, rounds)]
    for array in got[:-1]:
        (terms,) = call(add_kernel, [((piece, 2 * width), f32)], [terms, array], "add_terms")
    grad_k, grad_values = call(
        finish_kernel, [((piece, width), bf16)] * 2, [token, terms, got[-1]], "finish"
    )
    return attn_out, grad_q, grad_k, grad_values


def solution(mesh):
    return jax.shard_map(
        on_device,
        mesh=mesh,
        in_specs=(P("ctx", None), P("ctx", None), P("ctx", None), P("ctx", None), P()),
        out_specs=(P("ctx", "dp"), P("ctx", "dp"), P(("dp", "ctx"), None), P(("dp", "ctx"), None)),
        check_vma=False,
    )
```

```python
import functools
import math

import jax
import jax.numpy as jnp
from jax import lax
from jax.experimental import pallas as pl
from jax.experimental.pallas import tpu as pltpu
from jax.sharding import PartitionSpec as P

NEG = -1e30
LOG2E = 1.4426950408889634
DOC_NUMBERS = 4
KEY_GROUPS = 2
MIB = 1024 * 1024


def place():
    dp_index, ctx_index = lax.axis_index("dp"), lax.axis_index("ctx")
    return dp_index // KEY_GROUPS, dp_index % KEY_GROUPS, ctx_index // 2, ctx_index % 2

NT = (((1,), (1,)), ((), ()))


def home_chip(spot, key_group, chip, chips):
    level = chips // 4
    flip = spot // level * (2 * level) + spot % level
    home = chip ^ flip
    return home ^ ((home // level % 2) ^ key_group) * level


def gather_rounds(chips):
    rounds = [{} for _ in range(1, chips)]
    for core in range(2):
        if chips == 4:
            rounds[0][0, 1, core] = (1, 0)
            rounds[0][0, 2, core] = (0, 0)
            rounds[0][1, 2, core] = (1, 1)
            rounds[2][0, 3, core] = (core, 2)
            rounds[1][0, 3, core] = (0, 0)
            rounds[1][1, 3, core] = (1, 1)
            continue
        for flip, moves in enumerate(rounds, 1):
            for home in range(chips):
                group = home // (chips // 4) % 2
                if home ^ flip > home:
                    moves[group, home ^ flip, core] = (group, home)
    return rounds


def spread_rounds(chips):
    flips = list(range(2, chips)) + [1]
    return [{chip: chip ^ flip for chip in range(chips)} for flip in flips]


def mask_bias(seg_ref, rows, held):
    _, key_group, chip, core = place()
    seg = seg_ref[...]
    lines = rows // 128
    seg_own = seg_ref[pl.ds((chip * 2 + core) * lines, lines), :]
    start = jnp.zeros((lines, 128), jnp.int32)
    for number in range(1, DOC_NUMBERS):
        before = jnp.sum((seg < number).astype(jnp.float32), axis=(0, 1), keepdims=True)
        start = jnp.where(seg_own == number, before.astype(jnp.int32), start)
    start = jnp.concatenate([start[k : k + 1] for k in range(lines)], axis=1)
    query_pos = (chip * 2 + core) * rows + lax.broadcasted_iota(jnp.int32, (1, rows), 1)
    blocks = held // rows
    size = rows // 4
    line = lax.broadcasted_iota(jnp.int32, (rows, rows), 0)
    place_of = line // size
    row = (place_of % 2 * 2 + place_of // 2) * size + line % size
    bias = []
    for block in range(blocks):
        home = home_chip(block // 2, key_group, chip, blocks) * 2 + (core ^ block % 2)
        key_pos = home * rows + row
        allowed = (key_pos >= start) & (key_pos <= query_pos)
        bias.append(jnp.where(allowed, 0.0, NEG))
    return bias


def row_order(pieces):
    return list(range(0, pieces, 2)) + list(range(1, pieces, 2))


def load_kernel(k_hbm, v_hbm, *refs, pieces, chips):
    kv_ref, sems = refs[-2:]
    rows, width = k_hbm.shape
    size = rows // pieces
    copies = []
    for spot, piece in enumerate(row_order(pieces)):
        source, target = (slice(k * size, (k + 1) * size) for k in (piece, spot))
        for k, array in enumerate((k_hbm, v_hbm)):
            columns = slice(k * width, (k + 1) * width)
            copies.append(
                pltpu.make_async_copy(
                    array.at[source, :], kv_ref.at[target, columns], sems.at[k, spot]
                )
            )

    def load():
        for copy in copies:
            copy.start()
        for copy in copies:
            copy.wait()

    if chips:
        chip = place()[2]
        pl.when(functools.reduce(jnp.logical_or, [chip == c for c in chips]))(load)
    else:
        load()


def pick_kernel(*refs, choices):
    out_ref = refs[-1]
    _, key_group, chip, _ = place()
    spot = key_group * (len(choices) // 2) + chip
    for choice in sorted(set(choices)):
        wanted = functools.reduce(
            jnp.logical_or, [spot == k for k, c in enumerate(choices) if c == choice]
        )

        @pl.when(wanted)
        def _():
            out_ref[...] = jnp.zeros_like(out_ref) if choice < 0 else refs[choice][...]


def pass_kernel(array_ref, token_ref):
    token_ref[...] = array_ref[:8, :128]


def prep_kernel(
    seg_hbm, q_hbm, g_hbm, q_ref, g_ref, gt_ref, bias_ref, token_ref, seg_ref, sems, *, dims
):
    heads, rows, width, held, ctx_count = dims
    head_group = place()[0]
    seg_copy = pltpu.make_async_copy(seg_hbm, seg_ref, sems.at[2, 0])
    seg_copy.start()
    copies = []
    for head in range(heads):
        source = head_columns(head_group * heads + head, width)
        target = slice(head * width, (head + 1) * width)
        for k, (full, part) in enumerate(((g_hbm, g_ref), (q_hbm, q_ref))):
            copies.append(
                pltpu.make_async_copy(full.at[:, source], part.at[:, target], sems.at[k, head])
            )
            copies[-1].start()
    token_ref[...] = jnp.zeros_like(token_ref)
    seg_copy.wait()
    for k, block in enumerate(mask_bias(seg_ref, rows, held)):
        bias_ref[k * rows : (k + 1) * rows, :] = block
    for head in range(heads):
        cols = slice(head * width, (head + 1) * width)
        copies[2 * head].wait()
        gt_ref[cols, :] = g_ref[:, cols].astype(jnp.float32).T.astype(jnp.bfloat16)
    for head in range(heads):
        copies[2 * head + 1].wait()


def head_columns(head, width):
    return pl.ds(pl.multiple_of(head * width, width), width)


def scores_pass(q_ref, bias_ref, blocks, scores_ref, top_ref, *, dims, first):
    heads, rows, width, held, ctx_count = dims
    for head in range(heads):
        query = q_ref[:, head * width : (head + 1) * width]
        top = None
        for k, kv_ref in enumerate(blocks):
            bias = bias_ref[(first + k) * rows : (first + k + 1) * rows, :]
            raw = lax.dot_general(kv_ref[:, :width], query, NT, preferred_element_type=jnp.float32)
            scores = raw * (width**-0.5 * LOG2E) + bias
            scores_ref[head, k * rows : (k + 1) * rows, :] = scores
            here = jnp.max(scores, axis=0, keepdims=True)
            top = here if top is None else jnp.maximum(top, here)
        top_ref[head : head + 1, :] = top


def transpose_values(blocks, vt_ref, width):
    size = blocks[0].shape[0]
    for k, kv_ref in enumerate(blocks):
        vt = kv_ref[:, width:].astype(jnp.float32).T.astype(jnp.bfloat16)
        vt_ref[:, k * size : (k + 1) * size] = vt


def sums_pass(vt_ref, scores_ref, top, head):
    expd = jnp.exp2(scores_ref[head] - top)
    total = jnp.sum(expd, axis=0, keepdims=True)
    sums = jnp.dot(vt_ref[...], expd.astype(jnp.bfloat16), preferred_element_type=jnp.float32)
    return total, sums


def part_kernel(q_ref, bias_ref, *refs, dims):
    heads, rows, width, held, ctx_count = dims
    *blocks, scores_ref, stats_ref, sums_ref, vt_ref = refs
    transpose_values(blocks, vt_ref, width)
    scores_pass(q_ref, bias_ref, blocks, scores_ref, stats_ref, dims=dims, first=0)
    for head in range(heads):
        total, sums_ref[head] = sums_pass(
            vt_ref, scores_ref, stats_ref[head : head + 1, :], head
        )
        stats_ref[heads + head : heads + head + 1, :] = total


def forward_kernel(
    q_ref, gt_ref, bias_ref, kv_ref, part_ref, part_sums_ref, stats_ref, scores_ref, *refs, dims
):
    heads, rows, width, held, ctx_count = dims
    *outs, top_ref, vt_ref, sums_ref = refs
    pair = heads // KEY_GROUPS
    key_group = place()[1]
    transpose_values([kv_ref], vt_ref, width)
    scores_pass(q_ref, bias_ref, [kv_ref], scores_ref, top_ref, dims=dims, first=held // rows - 1)
    for head in range(heads):
        cols = slice(head * width, (head + 1) * width)
        before = part_ref[head : head + 1, :]
        top = jnp.maximum(top_ref[head : head + 1, :], before)
        share = jnp.exp2(before - top)
        total, accum = sums_pass(vt_ref, scores_ref, top, head)
        total = total + share * part_ref[heads + head : heads + head + 1, :]
        accum = accum + share * part_sums_ref[head]
        delta = jnp.sum(accum * gt_ref[cols, :].astype(jnp.float32), axis=0, keepdims=True)
        for row, value in enumerate((top, total, delta)):
            stats_ref[row * heads + head : row * heads + head + 1, :] = value
        sums_ref[cols, :] = accum.astype(jnp.bfloat16)
    for slot, out_ref in enumerate(outs):
        out_ref[...] = sums_ref[head_columns(key_group ^ slot, pair * width), :]


def dprobs_kernel(g_ref, *refs, dims):
    heads, rows, width, held, ctx_count = dims
    *blocks, dprobs_ref = refs
    for head in range(heads):
        grad = g_ref[:, head * width : (head + 1) * width]
        for part, ref in enumerate(blocks):
            dprobs_ref[head, part * rows : (part + 1) * rows, :] = lax.dot_general(
                ref[:, width:], grad, NT, preferred_element_type=jnp.float32
            )


def merged_stats(stats, heads):
    top = functools.reduce(jnp.maximum, [s[:heads] for s in stats])
    shares = [jnp.exp2(s[:heads] - top) for s in stats]
    total = sum(f * s[heads : 2 * heads] for f, s in zip(shares, stats))
    delta = sum(f * s[2 * heads :] for f, s in zip(shares, stats)) / total
    return top, shares, total, delta


def core_rows(base, side, half):
    return pl.ds(pl.multiple_of(base + side * half, half), half)


def backward_kernel(q_ref, g_ref, *refs, dims, ahead, own):
    heads, rows, width, held, ctx_count = dims
    parts, half = held // rows, rows // 2
    blocks, scores, last_scores, refs = refs[:parts], refs[parts], refs[parts + 1], refs[parts + 2 :]
    dprobs_ref, refs = (refs[0], refs[1:]) if ahead else (None, refs)
    stats = refs[:KEY_GROUPS]
    ds_ref, terms_ref, acc_ref = refs[-3:]
    head_group, key_group, chip, core = place()
    side = core if own else 1 - core
    scale = width**-0.5
    top, _, total, delta = merged_stats([s[...] for s in stats], heads)
    lse = top + jnp.log2(total)
    for head in range(heads):
        cols = slice(head * width, (head + 1) * width)
        query, grad = q_ref[:, cols], g_ref[:, cols]
        for part, ref in enumerate(blocks):
            held_rows, block_rows = core_rows(part * rows, side, half), core_rows(0, side, half)
            if part == parts - 1:
                row = last_scores[head, block_rows, :]
            else:
                row = scores[head, held_rows, :]
            probs = jnp.exp2(row - lse[head : head + 1])
            if ahead:
                dprobs = dprobs_ref[head, held_rows, :]
            else:
                dprobs = lax.dot_general(
                    ref[block_rows, width:], grad, NT, preferred_element_type=jnp.float32
                )
            dscores = (probs * (dprobs - delta[head : head + 1])).astype(jnp.bfloat16)
            here = slice(part * half, (part + 1) * half)
            ds_ref[head, here, :] = dscores
            dv = jnp.dot(probs.astype(jnp.bfloat16), grad, preferred_element_type=jnp.float32)
            dk = jnp.dot(dscores, query, preferred_element_type=jnp.float32)
            if head == 0:
                acc_ref[here, :width] = dk
                acc_ref[here, width:] = dv
            else:
                acc_ref[here, :width] += dk
                acc_ref[here, width:] += dv
    chips, piece = ctx_count // 2, rows // 4
    level = chips // 4
    for spot in range(2 * chips):
        here = slice(spot * piece, (spot + 1) * piece)
        target = chip ^ (spot % chips)
        group = head_group ^ (spot // chips)
        block = group * (ctx_count // 2) + key_group * (ctx_count // 4) + target // 2
        flip = block // 2 ^ chip
        slot = flip // (2 * level) * level + flip % level
        line = (slot * 2 + (block % 2 ^ core)) * half + target % 2 * piece
        mine = pl.ds(pl.multiple_of(line, piece), piece)
        terms_ref[here, :width] = (acc_ref[mine, :width] * scale).astype(terms_ref.dtype)
        terms_ref[here, width:] = acc_ref[mine, width:].astype(terms_ref.dtype)


def query_kernel(*refs, dims):
    heads, rows, width, held, ctx_count = dims
    parts, half = held // rows, rows // 2
    blocks, dscores, refs = refs[:parts], refs[parts : parts + 2], refs[parts + 3 :]
    outs, kts = refs[:KEY_GROUPS], refs[KEY_GROUPS:]
    pair = heads // KEY_GROUPS
    _, key_group, _, core = place()
    scale = width**-0.5
    for kt_ref, side in zip(kts, (core, 1 - core)):
        for part, ref in enumerate(blocks):
            keys = ref[core_rows(0, side, half), :width].astype(jnp.float32)
            kt_ref[:, part * half : (part + 1) * half] = keys.T.astype(jnp.bfloat16)
    for slot in range(KEY_GROUPS):
        for part in range(pair):
            head = (key_group ^ slot) * pair + part
            dq = sum(
                jnp.dot(kt_ref[...], ds_ref[head], preferred_element_type=jnp.float32)
                for kt_ref, ds_ref in zip(kts, dscores)
            )
            outs[slot][part * width : (part + 1) * width, :] = (dq * scale).astype(jnp.bfloat16)


def join_kernel(keep_ref, got_ref, kept_ref, send_ref):
    half = kept_ref.shape[0]
    kept_ref[...] = keep_ref[:half, :] + got_ref[:half, :].astype(jnp.float32)
    send = keep_ref[half:, :] + got_ref[half:, :].astype(jnp.float32)
    send_ref[...] = send.astype(jnp.bfloat16)


def spread_kernel(keep_ref, got_ref, token_ref, own_ref, *outs, rounds):
    piece = own_ref.shape[0]
    chip = place()[2]
    own_ref[...] = keep_ref[:piece, :] + got_ref[:piece, :].astype(jnp.float32)
    for out_ref, moves in zip(outs, rounds):
        flip = 0
        for source, target in moves.items():
            flip = jnp.where(chip == source, source ^ target, flip)
        mine = pl.ds(pl.multiple_of(flip * piece, piece), piece)
        out_ref[...] = (keep_ref[mine, :] + got_ref[mine, :].astype(jnp.float32)).astype(
            jnp.bfloat16
        )


def add_kernel(first_ref, second_ref, out_ref):
    out_ref[...] = first_ref[...] + second_ref[...].astype(jnp.float32)


def finish_out_kernel(*refs, dims):
    heads, rows, width, held, ctx_count = dims
    stats, outs = refs[:KEY_GROUPS], refs[KEY_GROUPS : 2 * KEY_GROUPS]
    attn_ref, token_ref = refs[2 * KEY_GROUPS :]
    token_ref[...] = jnp.zeros_like(token_ref)
    pair = heads // KEY_GROUPS
    top, shares, total, _ = merged_stats([s[...] for s in stats], heads)
    own = place()[1] * pair
    row = lax.broadcasted_iota(jnp.int32, (heads, 1), 0)
    for part in range(pair):
        here = slice(part * width, (part + 1) * width)

        def pick(array):
            return jnp.sum(jnp.where(row == own + part, array, 0.0), axis=0, keepdims=True)

        joined = sum(o[here, :].astype(jnp.float32) * pick(f) for o, f in zip(outs, shares))
        attn_ref[:, here] = (joined / pick(total)).T.astype(jnp.bfloat16)


def finish_query_kernel(own_ref, got_ref, gq_ref, token_ref):
    total = own_ref[...].astype(jnp.float32) + got_ref[...].astype(jnp.float32)
    gq_ref[...] = total.T.astype(jnp.bfloat16)
    token_ref[...] = jnp.zeros_like(token_ref)


def finish_kernel(token_ref, *refs):
    *terms, gk_ref, gv_ref = refs
    width = gk_ref.shape[1]
    both = sum(r[...].astype(jnp.float32) for r in terms)
    gk_ref[...] = both[:, :width].astype(jnp.bfloat16)
    gv_ref[...] = both[:, width:].astype(jnp.bfloat16)


def on_device(queries, keys, values, out_grad, segment_ids):
    rows = queries.shape[0]
    width = keys.shape[1]
    seq = segment_ids.shape[0]
    dp_count, ctx_count = lax.axis_size("dp"), lax.axis_size("ctx")
    head_groups = dp_count // KEY_GROUPS
    heads = queries.shape[1] // width // head_groups
    pair = heads // KEY_GROUPS
    chips = ctx_count // 2
    held = rows * ctx_count // KEY_GROUPS
    piece = rows // dp_count
    dims = (heads, rows, width, held, ctx_count)
    seg = segment_ids.reshape(seq // 128, 128)
    params = pltpu.CompilerParams(
        vmem_limit_bytes=min(56 * MIB, 12 * MIB + 12 * 4 * held * rows)
    )
    vmem = pl.BlockSpec(memory_space=pltpu.VMEM)
    bf16, f32 = jnp.bfloat16, jnp.float32

    def call(kernel, outs, ins, name, scratch=(), work=0, **static):
        specs = [a[1] if isinstance(a, tuple) else vmem for a in ins]
        arrays = [a[0] if isinstance(a, tuple) else a for a in ins]
        return pl.pallas_call(
            functools.partial(kernel, **static),
            out_shape=[jax.ShapeDtypeStruct(*o) for o in outs],
            in_specs=specs,
            out_specs=[vmem] * len(outs),
            scratch_shapes=list(scratch),
            compiler_params=params,
            cost_estimate=pl.CostEstimate(
                flops=work * 2 * heads * rows * held * width,
                bytes_accessed=sum(math.prod(o[0]) * 2 for o in outs),
                transcendentals=0,
            ),
            name=name,
        )(*arrays)

    def in_hbm(array):
        return pltpu.with_memory_space_constraint(array, pltpu.HBM), pl.BlockSpec(
            memory_space=pltpu.HBM
        )

    def over_dp(array, flip):
        return lax.ppermute(array, "dp", [(d, d ^ flip) for d in range(dp_count)])

    def over_cores(array):
        return lax.ppermute(array, "ctx", [(c, c ^ 1) for c in range(ctx_count)])

    def gathered(array, moves):
        pairs = []
        for d in range(0, dp_count, KEY_GROUPS):
            for (group, chip, core), (source, home) in moves.items():
                start = (d + source) * ctx_count + home * 2 + core
                pairs.append((start, (d + group) * ctx_count + chip * 2 + core))
        return lax.ppermute(array, ("dp", "ctx"), pairs)

    def spread(array, moves):
        pairs = [(a * 2 + core, b * 2 + core) for a, b in moves.items() for core in range(2)]
        return lax.ppermute(array, "ctx", pairs)

    rounds = gather_rounds(chips)

    def loaded(only, after):
        (array,) = call(
            load_kernel,
            [((rows, 2 * width), bf16)],
            [in_hbm(keys), in_hbm(values)] + after,
            "load_first" if only else "load",
            scratch=[pltpu.SemaphoreType.DMA((2, dp_count))],
            pieces=dp_count,
            chips=only,
        )
        return array

    first_kv = loaded(sorted({home for _, home in rounds[0].values()}), [])
    own_kv = loaded([], [first_kv])
    query_v, grad_v, grad_t, bias, token = call(
        prep_kernel,
        [
            ((rows, heads * width), bf16),
            ((rows, heads * width), bf16),
            ((heads * width, rows), bf16),
            ((held, rows), f32),
            ((8, 128), f32),
        ],
        [in_hbm(seg), in_hbm(queries), in_hbm(out_grad)],
        "prepare",
        scratch=[pltpu.VMEM(seg.shape, seg.dtype), pltpu.SemaphoreType.DMA((3, heads))],
        work=1,
        dims=dims,
    )
    sent = [own_kv, gathered(first_kv, rounds[0])]
    sent += [gathered(own_kv, moves) for moves in rounds[1:]]
    first = call(pass_kernel, [((8, 128), bf16)], sent[1:2], "pass")
    blocks = []
    for spot in range(chips // 2):
        choices = []
        for group in range(KEY_GROUPS):
            for chip in range(chips):
                home = home_chip(spot, group, chip, chips)
                spot_key = (group, chip, 0)
                ways = [k for k, m in enumerate(rounds, 1) if m.get(spot_key, (0, -1))[1] == home]
                choices.append(0 if home == chip else ways[0] if home < chip else -1)
        used = sorted(set(choices) - {-1})
        (picked,) = call(
            pick_kernel,
            [((rows, 2 * width), bf16)],
            [sent[k] for k in used] + [token] + (list(first) if spot == 0 else []),
            "pick",
            choices=[used.index(c) if c >= 0 else -1 for c in choices],
        )
        blocks += [picked, over_cores(picked)]
    early = held - rows
    scores, part_stats, part_sums = call(
        part_kernel,
        [((heads, early, rows), f32), ((2 * heads, rows), f32), ((heads, width, rows), f32)],
        [query_v, bias] + blocks[:-1],
        "attend_most",
        scratch=[pltpu.VMEM((width, early), bf16)],
        work=2,
        dims=dims,
    )
    stats, last_scores, *outs = call(
        forward_kernel,
        [((3 * heads, rows), f32), ((heads, rows, rows), f32)]
        + [((pair * width, rows), bf16)] * KEY_GROUPS,
        [query_v, grad_t, bias, blocks[-1], part_stats, part_sums],
        "attend",
        scratch=[
            pltpu.VMEM((heads, rows), f32),
            pltpu.VMEM((width, rows), bf16),
            pltpu.VMEM((heads * width, rows), bf16),
        ],
        work=1,
        dims=dims,
    )
    all_stats = [stats, over_dp(stats, 1)]
    all_outs = [outs[0], over_dp(outs[1], 1)]
    ahead = 4 * heads * held * rows <= 8 * MIB
    dprobs = []
    if ahead:
        dprobs = call(
            dprobs_kernel,
            [((heads, held, rows), f32)],
            [grad_v] + blocks,
            "dprobs",
            work=1,
            dims=dims,
        )

    inputs = [query_v, grad_v] + blocks + [scores, last_scores] + list(dprobs) + all_stats

    def differentiate(own, dtype, after):
        return call(
            backward_kernel,
            [((heads, held // 2, rows), bf16), ((held // 2, 2 * width), dtype)],
            inputs + after,
            "differentiate_own" if own else "differentiate_other",
            scratch=[pltpu.VMEM((held // 2, 2 * width), f32)],
            work=2,
            dims=dims,
            ahead=ahead,
            own=own,
        )

    other_scores, send = differentiate(False, bf16, [])
    got = over_cores(send)
    own_scores, keep = differentiate(True, f32, [other_scores])
    attn_out, token = call(
        finish_out_kernel,
        [((rows, pair * width), bf16), ((8, 128), f32)],
        all_stats + all_outs,
        "finish_out",
        dims=dims,
    )
    quarter = held // 4
    keep, send = call(
        join_kernel,
        [((quarter, 2 * width), f32), ((quarter, 2 * width), bf16)],
        [keep, got],
        "join_cores",
    )
    dqs = call(
        query_kernel,
        [((pair * width, rows), bf16)] * KEY_GROUPS,
        blocks + [own_scores, other_scores, keep],
        "query_terms",
        scratch=[pltpu.VMEM((width, held // 2), bf16)] * 2,
        work=1,
        dims=dims,
    )
    all_dqs = [dqs[0], over_dp(dqs[1], 1)]
    rounds = spread_rounds(chips)
    terms, *pieces = call(
        spread_kernel,
        [((piece, 2 * width), f32)] + [((piece, 2 * width), bf16)] * len(rounds),
        [keep, over_dp(send, 2), token],
        "join_heads",
        rounds=rounds,
    )
    grad_q, token = call(
        finish_query_kernel,
        [((rows, pair * width), bf16), ((8, 128), f32)],
        all_dqs,
        "finish_query",
    )
    got = [spread(p, moves) for p, moves in zip(pieces, rounds)]
    for array in got[:-1]:
        (terms,) = call(add_kernel, [((piece, 2 * width), f32)], [terms, array], "add_terms")
    grad_k, grad_values = call(
        finish_kernel, [((piece, width), bf16)] * 2, [token, terms, got[-1]], "finish"
    )
    return attn_out, grad_q, grad_k, grad_values


def solution(mesh):
    return jax.shard_map(
        on_device,
        mesh=mesh,
        in_specs=(P("ctx", None), P("ctx", None), P("ctx", None), P("ctx", None), P()),
        out_specs=(P("ctx", "dp"), P("ctx", "dp"), P(("dp", "ctx"), None), P(("dp", "ctx"), None)),
        check_vma=False,
    )
```

```python
import functools
import math

import jax
import jax.numpy as jnp
from jax import lax
from jax.experimental import pallas as pl
from jax.experimental.pallas import tpu as pltpu
from jax.sharding import PartitionSpec as P

NEG = -1e30
LOG2E = 1.4426950408889634
DOC_NUMBERS = 4
KEY_GROUPS = 2
MIB = 1024 * 1024


def place():
    dp_index, ctx_index = lax.axis_index("dp"), lax.axis_index("ctx")
    return dp_index // KEY_GROUPS, dp_index % KEY_GROUPS, ctx_index // 2, ctx_index % 2

NT = (((1,), (1,)), ((), ()))


def home_chip(spot, key_group, chip, chips):
    level = chips // 4
    flip = spot // level * (2 * level) + spot % level
    home = chip ^ flip
    return home ^ ((home // level % 2) ^ key_group) * level


def gather_rounds(chips):
    rounds = [{} for _ in range(1, chips)]
    for core in range(2):
        if chips == 4:
            rounds[0][0, 1, core] = (1, 0)
            rounds[0][0, 2, core] = (0, 0)
            rounds[0][1, 2, core] = (1, 1)
            rounds[2][0, 3, core] = (core, 2)
            rounds[1][0, 3, core] = (0, 0)
            rounds[1][1, 3, core] = (1, 1)
            continue
        for flip, moves in enumerate(rounds, 1):
            for home in range(chips):
                group = home // (chips // 4) % 2
                if home ^ flip > home:
                    moves[group, home ^ flip, core] = (group, home)
    return rounds


def spread_rounds(chips):
    flips = list(range(2, chips)) + [1]
    return [{chip: chip ^ flip for chip in range(chips)} for flip in flips]


def mask_bias(seg_ref, rows, held):
    _, key_group, chip, core = place()
    seg = seg_ref[...]
    lines = rows // 128
    seg_own = seg_ref[pl.ds((chip * 2 + core) * lines, lines), :]
    start = jnp.zeros((lines, 128), jnp.int32)
    for number in range(1, DOC_NUMBERS):
        before = jnp.sum((seg < number).astype(jnp.float32), axis=(0, 1), keepdims=True)
        start = jnp.where(seg_own == number, before.astype(jnp.int32), start)
    start = jnp.concatenate([start[k : k + 1] for k in range(lines)], axis=1)
    query_pos = (chip * 2 + core) * rows + lax.broadcasted_iota(jnp.int32, (1, rows), 1)
    blocks = held // rows
    size = rows // 4
    line = lax.broadcasted_iota(jnp.int32, (rows, rows), 0)
    place_of = line // size
    row = (place_of % 2 * 2 + place_of // 2) * size + line % size
    bias = []
    for block in range(blocks):
        home = home_chip(block // 2, key_group, chip, blocks) * 2 + (core ^ block % 2)
        key_pos = home * rows + row
        allowed = (key_pos >= start) & (key_pos <= query_pos)
        bias.append(jnp.where(allowed, 0.0, NEG))
    return bias


def row_order(pieces):
    return list(range(0, pieces, 2)) + list(range(1, pieces, 2))


def load_kernel(k_hbm, v_hbm, *refs, pieces, chips):
    kv_ref, sems = refs[-2:]
    rows, width = k_hbm.shape
    size = rows // pieces
    copies = []
    for spot, piece in enumerate(row_order(pieces)):
        source, target = (slice(k * size, (k + 1) * size) for k in (piece, spot))
        for k, array in enumerate((k_hbm, v_hbm)):
            columns = slice(k * width, (k + 1) * width)
            copies.append(
                pltpu.make_async_copy(
                    array.at[source, :], kv_ref.at[target, columns], sems.at[k, spot]
                )
            )

    def load():
        for copy in copies:
            copy.start()
        for copy in copies:
            copy.wait()

    if chips:
        chip = place()[2]
        pl.when(functools.reduce(jnp.logical_or, [chip == c for c in chips]))(load)
    else:
        load()


def pick_kernel(*refs, choices):
    out_ref = refs[-1]
    _, key_group, chip, _ = place()
    spot = key_group * (len(choices) // 2) + chip
    for choice in sorted(set(choices)):
        wanted = functools.reduce(
            jnp.logical_or, [spot == k for k, c in enumerate(choices) if c == choice]
        )

        @pl.when(wanted)
        def _():
            out_ref[...] = jnp.zeros_like(out_ref) if choice < 0 else refs[choice][...]


def pass_kernel(first_ref, second_ref, token_ref):
    token_ref[...] = first_ref[:8, :128]


def prep_kernel(
    seg_hbm, q_hbm, g_hbm, q_ref, g_ref, gt_ref, bias_ref, token_ref, seg_ref, sems, *, dims
):
    heads, rows, width, held, ctx_count = dims
    head_group = place()[0]
    seg_copy = pltpu.make_async_copy(seg_hbm, seg_ref, sems.at[2, 0])
    seg_copy.start()
    copies = []
    for head in range(heads):
        source = head_columns(head_group * heads + head, width)
        target = slice(head * width, (head + 1) * width)
        for k, (full, part) in enumerate(((g_hbm, g_ref), (q_hbm, q_ref))):
            copies.append(
                pltpu.make_async_copy(full.at[:, source], part.at[:, target], sems.at[k, head])
            )
            copies[-1].start()
    token_ref[...] = jnp.zeros_like(token_ref)
    seg_copy.wait()
    for k, block in enumerate(mask_bias(seg_ref, rows, held)):
        bias_ref[k * rows : (k + 1) * rows, :] = block
    for head in range(heads):
        cols = slice(head * width, (head + 1) * width)
        copies[2 * head].wait()
        gt_ref[cols, :] = g_ref[:, cols].astype(jnp.float32).T.astype(jnp.bfloat16)
    for head in range(heads):
        copies[2 * head + 1].wait()


def head_columns(head, width):
    return pl.ds(pl.multiple_of(head * width, width), width)


def scores_pass(q_ref, bias_ref, blocks, scores_ref, top_ref, *, dims, first):
    heads, rows, width, held, ctx_count = dims
    for head in range(heads):
        query = q_ref[:, head * width : (head + 1) * width]
        top = None
        for k, kv_ref in enumerate(blocks):
            bias = bias_ref[(first + k) * rows : (first + k + 1) * rows, :]
            raw = lax.dot_general(kv_ref[:, :width], query, NT, preferred_element_type=jnp.float32)
            scores = raw * (width**-0.5 * LOG2E) + bias
            scores_ref[head, k * rows : (k + 1) * rows, :] = scores
            here = jnp.max(scores, axis=0, keepdims=True)
            top = here if top is None else jnp.maximum(top, here)
        top_ref[head : head + 1, :] = top


def transpose_values(blocks, vt_ref, width):
    size = blocks[0].shape[0]
    for k, kv_ref in enumerate(blocks):
        vt = kv_ref[:, width:].astype(jnp.float32).T.astype(jnp.bfloat16)
        vt_ref[:, k * size : (k + 1) * size] = vt


def sums_pass(vt_ref, scores_ref, top, head):
    expd = jnp.exp2(scores_ref[head] - top)
    total = jnp.sum(expd, axis=0, keepdims=True)
    sums = jnp.dot(vt_ref[...], expd.astype(jnp.bfloat16), preferred_element_type=jnp.float32)
    return total, sums


def part_kernel(q_ref, bias_ref, *refs, dims):
    heads, rows, width, held, ctx_count = dims
    *blocks, scores_ref, stats_ref, sums_ref, vt_ref = refs
    transpose_values(blocks, vt_ref, width)
    scores_pass(q_ref, bias_ref, blocks, scores_ref, stats_ref, dims=dims, first=0)
    for head in range(heads):
        total, sums_ref[head] = sums_pass(
            vt_ref, scores_ref, stats_ref[head : head + 1, :], head
        )
        stats_ref[heads + head : heads + head + 1, :] = total


def forward_kernel(
    q_ref, gt_ref, bias_ref, kv_ref, part_ref, part_sums_ref, stats_ref, scores_ref, *refs, dims
):
    heads, rows, width, held, ctx_count = dims
    *outs, top_ref, vt_ref, sums_ref = refs
    pair = heads // KEY_GROUPS
    key_group = place()[1]
    transpose_values([kv_ref], vt_ref, width)
    scores_pass(q_ref, bias_ref, [kv_ref], scores_ref, top_ref, dims=dims, first=held // rows - 1)
    for head in range(heads):
        cols = slice(head * width, (head + 1) * width)
        before = part_ref[head : head + 1, :]
        top = jnp.maximum(top_ref[head : head + 1, :], before)
        share = jnp.exp2(before - top)
        total, accum = sums_pass(vt_ref, scores_ref, top, head)
        total = total + share * part_ref[heads + head : heads + head + 1, :]
        accum = accum + share * part_sums_ref[head]
        delta = jnp.sum(accum * gt_ref[cols, :].astype(jnp.float32), axis=0, keepdims=True)
        for row, value in enumerate((top, total, delta)):
            stats_ref[row * heads + head : row * heads + head + 1, :] = value
        sums_ref[cols, :] = accum.astype(jnp.bfloat16)
    for slot, out_ref in enumerate(outs):
        out_ref[...] = sums_ref[head_columns(key_group ^ slot, pair * width), :]


def dprobs_kernel(g_ref, *refs, dims):
    heads, rows, width, held, ctx_count = dims
    *blocks, dprobs_ref = refs
    for head in range(heads):
        grad = g_ref[:, head * width : (head + 1) * width]
        for part, ref in enumerate(blocks):
            dprobs_ref[head, part * rows : (part + 1) * rows, :] = lax.dot_general(
                ref[:, width:], grad, NT, preferred_element_type=jnp.float32
            )


def merged_stats(stats, heads):
    top = functools.reduce(jnp.maximum, [s[:heads] for s in stats])
    shares = [jnp.exp2(s[:heads] - top) for s in stats]
    total = sum(f * s[heads : 2 * heads] for f, s in zip(shares, stats))
    delta = sum(f * s[2 * heads :] for f, s in zip(shares, stats)) / total
    return top, shares, total, delta


def core_rows(base, side, half):
    return pl.ds(pl.multiple_of(base + side * half, half), half)


def backward_kernel(q_ref, g_ref, *refs, dims, ahead, own):
    heads, rows, width, held, ctx_count = dims
    parts, half = held // rows, rows // 2
    blocks, scores, last_scores, refs = refs[:parts], refs[parts], refs[parts + 1], refs[parts + 2 :]
    dprobs_ref, refs = (refs[0], refs[1:]) if ahead else (None, refs)
    stats = refs[:KEY_GROUPS]
    ds_ref, terms_ref, acc_ref = refs[-3:]
    head_group, key_group, chip, core = place()
    side = core if own else 1 - core
    scale = width**-0.5
    top, _, total, delta = merged_stats([s[...] for s in stats], heads)
    lse = top + jnp.log2(total)
    for head in range(heads):
        cols = slice(head * width, (head + 1) * width)
        query, grad = q_ref[:, cols], g_ref[:, cols]
        for part, ref in enumerate(blocks):
            held_rows, block_rows = core_rows(part * rows, side, half), core_rows(0, side, half)
            if part == parts - 1:
                row = last_scores[head, block_rows, :]
            else:
                row = scores[head, held_rows, :]
            probs = jnp.exp2(row - lse[head : head + 1])
            if ahead:
                dprobs = dprobs_ref[head, held_rows, :]
            else:
                dprobs = lax.dot_general(
                    ref[block_rows, width:], grad, NT, preferred_element_type=jnp.float32
                )
            dscores = (probs * (dprobs - delta[head : head + 1])).astype(jnp.bfloat16)
            here = slice(part * half, (part + 1) * half)
            ds_ref[head, here, :] = dscores
            dv = jnp.dot(probs.astype(jnp.bfloat16), grad, preferred_element_type=jnp.float32)
            dk = jnp.dot(dscores, query, preferred_element_type=jnp.float32)
            if head == 0:
                acc_ref[here, :width] = dk
                acc_ref[here, width:] = dv
            else:
                acc_ref[here, :width] += dk
                acc_ref[here, width:] += dv
    chips, piece = ctx_count // 2, rows // 4
    level = chips // 4
    for spot in range(2 * chips):
        here = slice(spot * piece, (spot + 1) * piece)
        target = chip ^ (spot % chips)
        group = head_group ^ (spot // chips)
        block = group * (ctx_count // 2) + key_group * (ctx_count // 4) + target // 2
        flip = block // 2 ^ chip
        slot = flip // (2 * level) * level + flip % level
        line = (slot * 2 + (block % 2 ^ core)) * half + target % 2 * piece
        mine = pl.ds(pl.multiple_of(line, piece), piece)
        terms_ref[here, :width] = (acc_ref[mine, :width] * scale).astype(terms_ref.dtype)
        terms_ref[here, width:] = acc_ref[mine, width:].astype(terms_ref.dtype)


def query_kernel(*refs, dims):
    heads, rows, width, held, ctx_count = dims
    parts, half = held // rows, rows // 2
    blocks, dscores, refs = refs[:parts], refs[parts : parts + 2], refs[parts + 3 :]
    outs, kts = refs[:KEY_GROUPS], refs[KEY_GROUPS:]
    pair = heads // KEY_GROUPS
    _, key_group, _, core = place()
    scale = width**-0.5
    for kt_ref, side in zip(kts, (core, 1 - core)):
        for part, ref in enumerate(blocks):
            keys = ref[core_rows(0, side, half), :width].astype(jnp.float32)
            kt_ref[:, part * half : (part + 1) * half] = keys.T.astype(jnp.bfloat16)
    for slot in range(KEY_GROUPS):
        for part in range(pair):
            head = (key_group ^ slot) * pair + part
            dq = sum(
                jnp.dot(kt_ref[...], ds_ref[head], preferred_element_type=jnp.float32)
                for kt_ref, ds_ref in zip(kts, dscores)
            )
            outs[slot][part * width : (part + 1) * width, :] = (dq * scale).astype(jnp.bfloat16)


def join_kernel(keep_ref, got_ref, kept_ref, send_ref):
    half = kept_ref.shape[0]
    kept_ref[...] = keep_ref[:half, :] + got_ref[:half, :].astype(jnp.float32)
    send = keep_ref[half:, :] + got_ref[half:, :].astype(jnp.float32)
    send_ref[...] = send.astype(jnp.bfloat16)


def spread_kernel(keep_ref, got_ref, token_ref, own_ref, *outs, rounds):
    piece = own_ref.shape[0]
    chip = place()[2]
    own_ref[...] = keep_ref[:piece, :] + got_ref[:piece, :].astype(jnp.float32)
    for out_ref, moves in zip(outs, rounds):
        flip = 0
        for source, target in moves.items():
            flip = jnp.where(chip == source, source ^ target, flip)
        mine = pl.ds(pl.multiple_of(flip * piece, piece), piece)
        out_ref[...] = (keep_ref[mine, :] + got_ref[mine, :].astype(jnp.float32)).astype(
            jnp.bfloat16
        )


def add_kernel(first_ref, second_ref, out_ref):
    out_ref[...] = first_ref[...] + second_ref[...].astype(jnp.float32)


def finish_out_kernel(*refs, dims):
    heads, rows, width, held, ctx_count = dims
    stats, outs = refs[:KEY_GROUPS], refs[KEY_GROUPS : 2 * KEY_GROUPS]
    attn_ref, token_ref = refs[2 * KEY_GROUPS :]
    token_ref[...] = jnp.zeros_like(token_ref)
    pair = heads // KEY_GROUPS
    top, shares, total, _ = merged_stats([s[...] for s in stats], heads)
    own = place()[1] * pair
    row = lax.broadcasted_iota(jnp.int32, (heads, 1), 0)
    for part in range(pair):
        here = slice(part * width, (part + 1) * width)

        def pick(array):
            return jnp.sum(jnp.where(row == own + part, array, 0.0), axis=0, keepdims=True)

        joined = sum(o[here, :].astype(jnp.float32) * pick(f) for o, f in zip(outs, shares))
        attn_ref[:, here] = (joined / pick(total)).T.astype(jnp.bfloat16)


def finish_query_kernel(own_ref, got_ref, gq_ref, token_ref):
    total = own_ref[...].astype(jnp.float32) + got_ref[...].astype(jnp.float32)
    gq_ref[...] = total.T.astype(jnp.bfloat16)
    token_ref[...] = jnp.zeros_like(token_ref)


def finish_kernel(token_ref, *refs):
    *terms, gk_ref, gv_ref = refs
    width = gk_ref.shape[1]
    both = sum(r[...].astype(jnp.float32) for r in terms)
    gk_ref[...] = both[:, :width].astype(jnp.bfloat16)
    gv_ref[...] = both[:, width:].astype(jnp.bfloat16)


def on_device(queries, keys, values, out_grad, segment_ids):
    rows = queries.shape[0]
    width = keys.shape[1]
    seq = segment_ids.shape[0]
    dp_count, ctx_count = lax.axis_size("dp"), lax.axis_size("ctx")
    head_groups = dp_count // KEY_GROUPS
    heads = queries.shape[1] // width // head_groups
    pair = heads // KEY_GROUPS
    chips = ctx_count // 2
    held = rows * ctx_count // KEY_GROUPS
    piece = rows // dp_count
    dims = (heads, rows, width, held, ctx_count)
    seg = segment_ids.reshape(seq // 128, 128)
    params = pltpu.CompilerParams(
        vmem_limit_bytes=min(56 * MIB, 12 * MIB + 12 * 4 * held * rows)
    )
    vmem = pl.BlockSpec(memory_space=pltpu.VMEM)
    bf16, f32 = jnp.bfloat16, jnp.float32

    def call(kernel, outs, ins, name, scratch=(), work=0, **static):
        specs = [a[1] if isinstance(a, tuple) else vmem for a in ins]
        arrays = [a[0] if isinstance(a, tuple) else a for a in ins]
        return pl.pallas_call(
            functools.partial(kernel, **static),
            out_shape=[jax.ShapeDtypeStruct(*o) for o in outs],
            in_specs=specs,
            out_specs=[vmem] * len(outs),
            scratch_shapes=list(scratch),
            compiler_params=params,
            cost_estimate=pl.CostEstimate(
                flops=work * 2 * heads * rows * held * width,
                bytes_accessed=sum(math.prod(o[0]) * 2 for o in outs),
                transcendentals=0,
            ),
            name=name,
        )(*arrays)

    def in_hbm(array):
        return pltpu.with_memory_space_constraint(array, pltpu.HBM), pl.BlockSpec(
            memory_space=pltpu.HBM
        )

    def over_dp(array, flip):
        return lax.ppermute(array, "dp", [(d, d ^ flip) for d in range(dp_count)])

    def over_cores(array):
        return lax.ppermute(array, "ctx", [(c, c ^ 1) for c in range(ctx_count)])

    def gathered(array, moves):
        pairs = []
        for d in range(0, dp_count, KEY_GROUPS):
            for (group, chip, core), (source, home) in moves.items():
                start = (d + source) * ctx_count + home * 2 + core
                pairs.append((start, (d + group) * ctx_count + chip * 2 + core))
        return lax.ppermute(array, ("dp", "ctx"), pairs)

    def spread(array, moves):
        pairs = [(a * 2 + core, b * 2 + core) for a, b in moves.items() for core in range(2)]
        return lax.ppermute(array, "ctx", pairs)

    rounds = gather_rounds(chips)

    def loaded(only, after):
        (array,) = call(
            load_kernel,
            [((rows, 2 * width), bf16)],
            [in_hbm(keys), in_hbm(values)] + after,
            "load_first" if only else "load",
            scratch=[pltpu.SemaphoreType.DMA((2, dp_count))],
            pieces=dp_count,
            chips=only,
        )
        return array

    first_kv = loaded(sorted({home for _, home in rounds[0].values()}), [])
    own_kv = loaded([], [first_kv])
    query_v, grad_v, grad_t, bias, token = call(
        prep_kernel,
        [
            ((rows, heads * width), bf16),
            ((rows, heads * width), bf16),
            ((heads * width, rows), bf16),
            ((held, rows), f32),
            ((8, 128), f32),
        ],
        [in_hbm(seg), in_hbm(queries), in_hbm(out_grad)],
        "prepare",
        scratch=[pltpu.VMEM(seg.shape, seg.dtype), pltpu.SemaphoreType.DMA((3, heads))],
        work=1,
        dims=dims,
    )
    sent = [own_kv, gathered(first_kv, rounds[0])]
    sent += [gathered(own_kv, moves) for moves in rounds[1:]]
    first = call(pass_kernel, [((8, 128), bf16)], sent[1:3], "pass")
    blocks = []
    for spot in range(chips // 2):
        choices = []
        for group in range(KEY_GROUPS):
            for chip in range(chips):
                home = home_chip(spot, group, chip, chips)
                spot_key = (group, chip, 0)
                ways = [k for k, m in enumerate(rounds, 1) if m.get(spot_key, (0, -1))[1] == home]
                choices.append(0 if home == chip else ways[0] if home < chip else -1)
        used = sorted(set(choices) - {-1})
        (picked,) = call(
            pick_kernel,
            [((rows, 2 * width), bf16)],
            [sent[k] for k in used] + [token] + (list(first) if spot == 0 else []),
            "pick",
            choices=[used.index(c) if c >= 0 else -1 for c in choices],
        )
        blocks += [picked, over_cores(picked)]
    early = held - rows
    scores, part_stats, part_sums = call(
        part_kernel,
        [((heads, early, rows), f32), ((2 * heads, rows), f32), ((heads, width, rows), f32)],
        [query_v, bias] + blocks[:-1],
        "attend_most",
        scratch=[pltpu.VMEM((width, early), bf16)],
        work=2,
        dims=dims,
    )
    stats, last_scores, *outs = call(
        forward_kernel,
        [((3 * heads, rows), f32), ((heads, rows, rows), f32)]
        + [((pair * width, rows), bf16)] * KEY_GROUPS,
        [query_v, grad_t, bias, blocks[-1], part_stats, part_sums],
        "attend",
        scratch=[
            pltpu.VMEM((heads, rows), f32),
            pltpu.VMEM((width, rows), bf16),
            pltpu.VMEM((heads * width, rows), bf16),
        ],
        work=1,
        dims=dims,
    )
    all_stats = [stats, over_dp(stats, 1)]
    all_outs = [outs[0], over_dp(outs[1], 1)]
    ahead = 4 * heads * held * rows <= 8 * MIB
    dprobs = []
    if ahead:
        dprobs = call(
            dprobs_kernel,
            [((heads, held, rows), f32)],
            [grad_v] + blocks,
            "dprobs",
            work=1,
            dims=dims,
        )

    inputs = [query_v, grad_v] + blocks + [scores, last_scores] + list(dprobs) + all_stats

    def differentiate(own, dtype, after):
        return call(
            backward_kernel,
            [((heads, held // 2, rows), bf16), ((held // 2, 2 * width), dtype)],
            inputs + after,
            "differentiate_own" if own else "differentiate_other",
            scratch=[pltpu.VMEM((held // 2, 2 * width), f32)],
            work=2,
            dims=dims,
            ahead=ahead,
            own=own,
        )

    other_scores, send = differentiate(False, bf16, [])
    got = over_cores(send)
    own_scores, keep = differentiate(True, f32, [other_scores])
    attn_out, token = call(
        finish_out_kernel,
        [((rows, pair * width), bf16), ((8, 128), f32)],
        all_stats + all_outs,
        "finish_out",
        dims=dims,
    )
    quarter = held // 4
    keep, send = call(
        join_kernel,
        [((quarter, 2 * width), f32), ((quarter, 2 * width), bf16)],
        [keep, got],
        "join_cores",
    )
    dqs = call(
        query_kernel,
        [((pair * width, rows), bf16)] * KEY_GROUPS,
        blocks + [own_scores, other_scores, keep],
        "query_terms",
        scratch=[pltpu.VMEM((width, held // 2), bf16)] * 2,
        work=1,
        dims=dims,
    )
    all_dqs = [dqs[0], over_dp(dqs[1], 1)]
    rounds = spread_rounds(chips)
    terms, *pieces = call(
        spread_kernel,
        [((piece, 2 * width), f32)] + [((piece, 2 * width), bf16)] * len(rounds),
        [keep, over_dp(send, 2), token],
        "join_heads",
        rounds=rounds,
    )
    grad_q, token = call(
        finish_query_kernel,
        [((rows, pair * width), bf16), ((8, 128), f32)],
        all_dqs,
        "finish_query",
    )
    got = [spread(p, moves) for p, moves in zip(pieces, rounds)]
    for array in got[:-1]:
        (terms,) = call(add_kernel, [((piece, 2 * width), f32)], [terms, array], "add_terms")
    grad_k, grad_values = call(
        finish_kernel, [((piece, width), bf16)] * 2, [token, terms, got[-1]], "finish"
    )
    return attn_out, grad_q, grad_k, grad_values


def solution(mesh):
    return jax.shard_map(
        on_device,
        mesh=mesh,
        in_specs=(P("ctx", None), P("ctx", None), P("ctx", None), P("ctx", None), P()),
        out_specs=(P("ctx", "dp"), P("ctx", "dp"), P(("dp", "ctx"), None), P(("dp", "ctx"), None)),
        check_vma=False,
    )
```

```python
import functools
import math

import jax
import jax.numpy as jnp
from jax import lax
from jax.experimental import pallas as pl
from jax.experimental.pallas import tpu as pltpu
from jax.sharding import PartitionSpec as P

NEG = -1e30
LOG2E = 1.4426950408889634
DOC_NUMBERS = 4
KEY_GROUPS = 2
MIB = 1024 * 1024


def place():
    dp_index, ctx_index = lax.axis_index("dp"), lax.axis_index("ctx")
    return dp_index // KEY_GROUPS, dp_index % KEY_GROUPS, ctx_index // 2, ctx_index % 2

NT = (((1,), (1,)), ((), ()))


def home_chip(spot, key_group, chip, chips):
    level = chips // 4
    flip = spot // level * (2 * level) + spot % level
    home = chip ^ flip
    return home ^ ((home // level % 2) ^ key_group) * level


def gather_rounds(chips):
    rounds = [{} for _ in range(1, chips)]
    for core in range(2):
        if chips == 4:
            rounds[0][0, 1, core] = (1, 0)
            rounds[0][0, 2, core] = (0, 0)
            rounds[0][1, 2, core] = (1, 1)
            rounds[2][0, 3, core] = (core, 2)
            rounds[1][0, 3, core] = (0, 0)
            rounds[1][1, 3, core] = (1, 1)
            continue
        for flip, moves in enumerate(rounds, 1):
            for home in range(chips):
                group = home // (chips // 4) % 2
                if home ^ flip > home:
                    moves[group, home ^ flip, core] = (group, home)
    return rounds


def spread_rounds(chips):
    flips = list(range(2, chips)) + [1]
    return [{chip: chip ^ flip for chip in range(chips)} for flip in flips]


def mask_bias(seg_ref, rows, held):
    _, key_group, chip, core = place()
    seg = seg_ref[...]
    lines = rows // 128
    seg_own = seg_ref[pl.ds((chip * 2 + core) * lines, lines), :]
    start = jnp.zeros((lines, 128), jnp.int32)
    for number in range(1, DOC_NUMBERS):
        before = jnp.sum((seg < number).astype(jnp.float32), axis=(0, 1), keepdims=True)
        start = jnp.where(seg_own == number, before.astype(jnp.int32), start)
    start = jnp.concatenate([start[k : k + 1] for k in range(lines)], axis=1)
    query_pos = (chip * 2 + core) * rows + lax.broadcasted_iota(jnp.int32, (1, rows), 1)
    blocks = held // rows
    size = rows // 4
    line = lax.broadcasted_iota(jnp.int32, (rows, rows), 0)
    place_of = line // size
    row = (place_of % 2 * 2 + place_of // 2) * size + line % size
    bias = []
    for block in range(blocks):
        home = home_chip(block // 2, key_group, chip, blocks) * 2 + (core ^ block % 2)
        key_pos = home * rows + row
        allowed = (key_pos >= start) & (key_pos <= query_pos)
        bias.append(jnp.where(allowed, 0.0, NEG))
    return bias


def row_order(pieces):
    return list(range(0, pieces, 2)) + list(range(1, pieces, 2))


def load_kernel(k_hbm, v_hbm, *refs, pieces, chips):
    kv_ref, sems = refs[-2:]
    rows, width = k_hbm.shape
    size = rows // pieces
    copies = []
    for spot, piece in enumerate(row_order(pieces)):
        source, target = (slice(k * size, (k + 1) * size) for k in (piece, spot))
        for k, array in enumerate((k_hbm, v_hbm)):
            columns = slice(k * width, (k + 1) * width)
            copies.append(
                pltpu.make_async_copy(
                    array.at[source, :], kv_ref.at[target, columns], sems.at[k, spot]
                )
            )

    def load():
        for copy in copies:
            copy.start()
        for copy in copies:
            copy.wait()

    if chips:
        chip = place()[2]
        pl.when(functools.reduce(jnp.logical_or, [chip == c for c in chips]))(load)
    else:
        load()


def pick_kernel(*refs, choices):
    out_ref = refs[-1]
    _, key_group, chip, _ = place()
    spot = key_group * (len(choices) // 2) + chip
    for choice in sorted(set(choices)):
        wanted = functools.reduce(
            jnp.logical_or, [spot == k for k, c in enumerate(choices) if c == choice]
        )

        @pl.when(wanted)
        def _():
            out_ref[...] = jnp.zeros_like(out_ref) if choice < 0 else refs[choice][...]


def pass_kernel(array_ref, after_ref, token_ref):
    token_ref[...] = array_ref[:8, :128]


def prep_kernel(
    seg_hbm, q_hbm, g_hbm, q_ref, g_ref, gt_ref, bias_ref, token_ref, seg_ref, sems, *, dims
):
    heads, rows, width, held, ctx_count = dims
    head_group = place()[0]
    seg_copy = pltpu.make_async_copy(seg_hbm, seg_ref, sems.at[2, 0])
    seg_copy.start()
    copies = []
    for head in range(heads):
        source = head_columns(head_group * heads + head, width)
        target = slice(head * width, (head + 1) * width)
        for k, (full, part) in enumerate(((g_hbm, g_ref), (q_hbm, q_ref))):
            copies.append(
                pltpu.make_async_copy(full.at[:, source], part.at[:, target], sems.at[k, head])
            )
            copies[-1].start()
    token_ref[...] = jnp.zeros_like(token_ref)
    seg_copy.wait()
    for k, block in enumerate(mask_bias(seg_ref, rows, held)):
        bias_ref[k * rows : (k + 1) * rows, :] = block
    for head in range(heads):
        cols = slice(head * width, (head + 1) * width)
        copies[2 * head].wait()
        gt_ref[cols, :] = g_ref[:, cols].astype(jnp.float32).T.astype(jnp.bfloat16)
    for head in range(heads):
        copies[2 * head + 1].wait()


def head_columns(head, width):
    return pl.ds(pl.multiple_of(head * width, width), width)


def scores_pass(q_ref, bias_ref, blocks, scores_ref, top_ref, *, dims, first):
    heads, rows, width, held, ctx_count = dims
    for head in range(heads):
        query = q_ref[:, head * width : (head + 1) * width]
        top = None
        for k, kv_ref in enumerate(blocks):
            bias = bias_ref[(first + k) * rows : (first + k + 1) * rows, :]
            raw = lax.dot_general(kv_ref[:, :width], query, NT, preferred_element_type=jnp.float32)
            scores = raw * (width**-0.5 * LOG2E) + bias
            scores_ref[head, k * rows : (k + 1) * rows, :] = scores
            here = jnp.max(scores, axis=0, keepdims=True)
            top = here if top is None else jnp.maximum(top, here)
        top_ref[head : head + 1, :] = top


def transpose_values(blocks, vt_ref, width):
    size = blocks[0].shape[0]
    for k, kv_ref in enumerate(blocks):
        vt = kv_ref[:, width:].astype(jnp.float32).T.astype(jnp.bfloat16)
        vt_ref[:, k * size : (k + 1) * size] = vt


def sums_pass(vt_ref, scores_ref, top, head):
    expd = jnp.exp2(scores_ref[head] - top)
    total = jnp.sum(expd, axis=0, keepdims=True)
    sums = jnp.dot(vt_ref[...], expd.astype(jnp.bfloat16), preferred_element_type=jnp.float32)
    return total, sums


def part_kernel(q_ref, bias_ref, *refs, dims):
    heads, rows, width, held, ctx_count = dims
    *blocks, scores_ref, stats_ref, sums_ref, vt_ref = refs
    transpose_values(blocks, vt_ref, width)
    scores_pass(q_ref, bias_ref, blocks, scores_ref, stats_ref, dims=dims, first=0)
    for head in range(heads):
        total, sums_ref[head] = sums_pass(
            vt_ref, scores_ref, stats_ref[head : head + 1, :], head
        )
        stats_ref[heads + head : heads + head + 1, :] = total


def forward_kernel(
    q_ref, gt_ref, bias_ref, kv_ref, part_ref, part_sums_ref, stats_ref, scores_ref, *refs, dims
):
    heads, rows, width, held, ctx_count = dims
    *outs, top_ref, vt_ref, sums_ref = refs
    pair = heads // KEY_GROUPS
    key_group = place()[1]
    transpose_values([kv_ref], vt_ref, width)
    scores_pass(q_ref, bias_ref, [kv_ref], scores_ref, top_ref, dims=dims, first=held // rows - 1)
    for head in range(heads):
        cols = slice(head * width, (head + 1) * width)
        before = part_ref[head : head + 1, :]
        top = jnp.maximum(top_ref[head : head + 1, :], before)
        share = jnp.exp2(before - top)
        total, accum = sums_pass(vt_ref, scores_ref, top, head)
        total = total + share * part_ref[heads + head : heads + head + 1, :]
        accum = accum + share * part_sums_ref[head]
        delta = jnp.sum(accum * gt_ref[cols, :].astype(jnp.float32), axis=0, keepdims=True)
        for row, value in enumerate((top, total, delta)):
            stats_ref[row * heads + head : row * heads + head + 1, :] = value
        sums_ref[cols, :] = accum.astype(jnp.bfloat16)
    for slot, out_ref in enumerate(outs):
        out_ref[...] = sums_ref[head_columns(key_group ^ slot, pair * width), :]


def dprobs_kernel(g_ref, *refs, dims):
    heads, rows, width, held, ctx_count = dims
    *blocks, dprobs_ref = refs
    for head in range(heads):
        grad = g_ref[:, head * width : (head + 1) * width]
        for part, ref in enumerate(blocks):
            dprobs_ref[head, part * rows : (part + 1) * rows, :] = lax.dot_general(
                ref[:, width:], grad, NT, preferred_element_type=jnp.float32
            )


def merged_stats(stats, heads):
    top = functools.reduce(jnp.maximum, [s[:heads] for s in stats])
    shares = [jnp.exp2(s[:heads] - top) for s in stats]
    total = sum(f * s[heads : 2 * heads] for f, s in zip(shares, stats))
    delta = sum(f * s[2 * heads :] for f, s in zip(shares, stats)) / total
    return top, shares, total, delta


def core_rows(base, side, half):
    return pl.ds(pl.multiple_of(base + side * half, half), half)


def backward_kernel(q_ref, g_ref, *refs, dims, ahead, own):
    heads, rows, width, held, ctx_count = dims
    parts, half = held // rows, rows // 2
    blocks, scores, last_scores, refs = refs[:parts], refs[parts], refs[parts + 1], refs[parts + 2 :]
    dprobs_ref, refs = (refs[0], refs[1:]) if ahead else (None, refs)
    stats = refs[:KEY_GROUPS]
    ds_ref, terms_ref, acc_ref = refs[-3:]
    head_group, key_group, chip, core = place()
    side = core if own else 1 - core
    scale = width**-0.5
    top, _, total, delta = merged_stats([s[...] for s in stats], heads)
    lse = top + jnp.log2(total)
    for head in range(heads):
        cols = slice(head * width, (head + 1) * width)
        query, grad = q_ref[:, cols], g_ref[:, cols]
        for part, ref in enumerate(blocks):
            held_rows, block_rows = core_rows(part * rows, side, half), core_rows(0, side, half)
            if part == parts - 1:
                row = last_scores[head, block_rows, :]
            else:
                row = scores[head, held_rows, :]
            probs = jnp.exp2(row - lse[head : head + 1])
            if ahead:
                dprobs = dprobs_ref[head, held_rows, :]
            else:
                dprobs = lax.dot_general(
                    ref[block_rows, width:], grad, NT, preferred_element_type=jnp.float32
                )
            dscores = (probs * (dprobs - delta[head : head + 1])).astype(jnp.bfloat16)
            here = slice(part * half, (part + 1) * half)
            ds_ref[head, here, :] = dscores
            dv = jnp.dot(probs.astype(jnp.bfloat16), grad, preferred_element_type=jnp.float32)
            dk = jnp.dot(dscores, query, preferred_element_type=jnp.float32)
            if head == 0:
                acc_ref[here, :width] = dk
                acc_ref[here, width:] = dv
            else:
                acc_ref[here, :width] += dk
                acc_ref[here, width:] += dv
    chips, piece = ctx_count // 2, rows // 4
    level = chips // 4
    for spot in range(2 * chips):
        here = slice(spot * piece, (spot + 1) * piece)
        target = chip ^ (spot % chips)
        group = head_group ^ (spot // chips)
        block = group * (ctx_count // 2) + key_group * (ctx_count // 4) + target // 2
        flip = block // 2 ^ chip
        slot = flip // (2 * level) * level + flip % level
        line = (slot * 2 + (block % 2 ^ core)) * half + target % 2 * piece
        mine = pl.ds(pl.multiple_of(line, piece), piece)
        terms_ref[here, :width] = (acc_ref[mine, :width] * scale).astype(terms_ref.dtype)
        terms_ref[here, width:] = acc_ref[mine, width:].astype(terms_ref.dtype)


def query_kernel(*refs, dims):
    heads, rows, width, held, ctx_count = dims
    parts, half = held // rows, rows // 2
    blocks, dscores, refs = refs[:parts], refs[parts : parts + 2], refs[parts + 3 :]
    outs, kts = refs[:KEY_GROUPS], refs[KEY_GROUPS:]
    pair = heads // KEY_GROUPS
    _, key_group, _, core = place()
    scale = width**-0.5
    for kt_ref, side in zip(kts, (core, 1 - core)):
        for part, ref in enumerate(blocks):
            keys = ref[core_rows(0, side, half), :width].astype(jnp.float32)
            kt_ref[:, part * half : (part + 1) * half] = keys.T.astype(jnp.bfloat16)
    for slot in range(KEY_GROUPS):
        for part in range(pair):
            head = (key_group ^ slot) * pair + part
            dq = sum(
                jnp.dot(kt_ref[...], ds_ref[head], preferred_element_type=jnp.float32)
                for kt_ref, ds_ref in zip(kts, dscores)
            )
            outs[slot][part * width : (part + 1) * width, :] = (dq * scale).astype(jnp.bfloat16)


def join_kernel(keep_ref, got_ref, kept_ref, send_ref):
    half = kept_ref.shape[0]
    kept_ref[...] = keep_ref[:half, :] + got_ref[:half, :].astype(jnp.float32)
    send = keep_ref[half:, :] + got_ref[half:, :].astype(jnp.float32)
    send_ref[...] = send.astype(jnp.bfloat16)


def spread_kernel(keep_ref, got_ref, token_ref, own_ref, *outs, rounds):
    piece = own_ref.shape[0]
    chip = place()[2]
    own_ref[...] = keep_ref[:piece, :] + got_ref[:piece, :].astype(jnp.float32)
    for out_ref, moves in zip(outs, rounds):
        flip = 0
        for source, target in moves.items():
            flip = jnp.where(chip == source, source ^ target, flip)
        mine = pl.ds(pl.multiple_of(flip * piece, piece), piece)
        out_ref[...] = (keep_ref[mine, :] + got_ref[mine, :].astype(jnp.float32)).astype(
            jnp.bfloat16
        )


def add_kernel(first_ref, second_ref, out_ref):
    out_ref[...] = first_ref[...] + second_ref[...].astype(jnp.float32)


def finish_out_kernel(*refs, dims):
    heads, rows, width, held, ctx_count = dims
    stats, outs = refs[:KEY_GROUPS], refs[KEY_GROUPS : 2 * KEY_GROUPS]
    attn_ref, token_ref = refs[2 * KEY_GROUPS :]
    token_ref[...] = jnp.zeros_like(token_ref)
    pair = heads // KEY_GROUPS
    top, shares, total, _ = merged_stats([s[...] for s in stats], heads)
    own = place()[1] * pair
    row = lax.broadcasted_iota(jnp.int32, (heads, 1), 0)
    for part in range(pair):
        here = slice(part * width, (part + 1) * width)

        def pick(array):
            return jnp.sum(jnp.where(row == own + part, array, 0.0), axis=0, keepdims=True)

        joined = sum(o[here, :].astype(jnp.float32) * pick(f) for o, f in zip(outs, shares))
        attn_ref[:, here] = (joined / pick(total)).T.astype(jnp.bfloat16)


def finish_query_kernel(own_ref, got_ref, gq_ref, token_ref):
    total = own_ref[...].astype(jnp.float32) + got_ref[...].astype(jnp.float32)
    gq_ref[...] = total.T.astype(jnp.bfloat16)
    token_ref[...] = jnp.zeros_like(token_ref)


def finish_kernel(token_ref, *refs):
    *terms, gk_ref, gv_ref = refs
    width = gk_ref.shape[1]
    both = sum(r[...].astype(jnp.float32) for r in terms)
    gk_ref[...] = both[:, :width].astype(jnp.bfloat16)
    gv_ref[...] = both[:, width:].astype(jnp.bfloat16)


def on_device(queries, keys, values, out_grad, segment_ids):
    rows = queries.shape[0]
    width = keys.shape[1]
    seq = segment_ids.shape[0]
    dp_count, ctx_count = lax.axis_size("dp"), lax.axis_size("ctx")
    head_groups = dp_count // KEY_GROUPS
    heads = queries.shape[1] // width // head_groups
    pair = heads // KEY_GROUPS
    chips = ctx_count // 2
    held = rows * ctx_count // KEY_GROUPS
    piece = rows // dp_count
    dims = (heads, rows, width, held, ctx_count)
    seg = segment_ids.reshape(seq // 128, 128)
    params = pltpu.CompilerParams(
        vmem_limit_bytes=min(56 * MIB, 12 * MIB + 12 * 4 * held * rows)
    )
    vmem = pl.BlockSpec(memory_space=pltpu.VMEM)
    bf16, f32 = jnp.bfloat16, jnp.float32

    def call(kernel, outs, ins, name, scratch=(), work=0, **static):
        specs = [a[1] if isinstance(a, tuple) else vmem for a in ins]
        arrays = [a[0] if isinstance(a, tuple) else a for a in ins]
        return pl.pallas_call(
            functools.partial(kernel, **static),
            out_shape=[jax.ShapeDtypeStruct(*o) for o in outs],
            in_specs=specs,
            out_specs=[vmem] * len(outs),
            scratch_shapes=list(scratch),
            compiler_params=params,
            cost_estimate=pl.CostEstimate(
                flops=work * 2 * heads * rows * held * width,
                bytes_accessed=sum(math.prod(o[0]) * 2 for o in outs),
                transcendentals=0,
            ),
            name=name,
        )(*arrays)

    def in_hbm(array):
        return pltpu.with_memory_space_constraint(array, pltpu.HBM), pl.BlockSpec(
            memory_space=pltpu.HBM
        )

    def over_dp(array, flip):
        return lax.ppermute(array, "dp", [(d, d ^ flip) for d in range(dp_count)])

    def over_cores(array):
        return lax.ppermute(array, "ctx", [(c, c ^ 1) for c in range(ctx_count)])

    def gathered(array, moves):
        pairs = []
        for d in range(0, dp_count, KEY_GROUPS):
            for (group, chip, core), (source, home) in moves.items():
                start = (d + source) * ctx_count + home * 2 + core
                pairs.append((start, (d + group) * ctx_count + chip * 2 + core))
        return lax.ppermute(array, ("dp", "ctx"), pairs)

    def spread(array, moves):
        pairs = [(a * 2 + core, b * 2 + core) for a, b in moves.items() for core in range(2)]
        return lax.ppermute(array, "ctx", pairs)

    rounds = gather_rounds(chips)

    def loaded(only, after):
        (array,) = call(
            load_kernel,
            [((rows, 2 * width), bf16)],
            [in_hbm(keys), in_hbm(values)] + after,
            "load_first" if only else "load",
            scratch=[pltpu.SemaphoreType.DMA((2, dp_count))],
            pieces=dp_count,
            chips=only,
        )
        return array

    first_kv = loaded(sorted({home for _, home in rounds[0].values()}), [])
    own_kv = loaded([], [first_kv])
    query_v, grad_v, grad_t, bias, token = call(
        prep_kernel,
        [
            ((rows, heads * width), bf16),
            ((rows, heads * width), bf16),
            ((heads * width, rows), bf16),
            ((held, rows), f32),
            ((8, 128), f32),
        ],
        [in_hbm(seg), in_hbm(queries), in_hbm(out_grad)],
        "prepare",
        scratch=[pltpu.VMEM(seg.shape, seg.dtype), pltpu.SemaphoreType.DMA((3, heads))],
        work=1,
        dims=dims,
    )
    early = 2 if chips == 4 else 1
    sent = [own_kv] + [gathered(first_kv, moves) for moves in rounds[:early]]
    sent += [gathered(own_kv, moves) for moves in rounds[early:]]
    first = [token]
    for array in sent[1 : early + 1]:
        first = call(pass_kernel, [((8, 128), bf16)], [array] + list(first), "pass")
    blocks = []
    for spot in range(chips // 2):
        choices = []
        for group in range(KEY_GROUPS):
            for chip in range(chips):
                home = home_chip(spot, group, chip, chips)
                spot_key = (group, chip, 0)
                ways = [k for k, m in enumerate(rounds, 1) if m.get(spot_key, (0, -1))[1] == home]
                choices.append(0 if home == chip else ways[0] if home < chip else -1)
        used = sorted(set(choices) - {-1})
        (picked,) = call(
            pick_kernel,
            [((rows, 2 * width), bf16)],
            [sent[k] for k in used] + [token] + (list(first) if spot == 0 else []),
            "pick",
            choices=[used.index(c) if c >= 0 else -1 for c in choices],
        )
        blocks += [picked, over_cores(picked)]
    early = held - rows
    scores, part_stats, part_sums = call(
        part_kernel,
        [((heads, early, rows), f32), ((2 * heads, rows), f32), ((heads, width, rows), f32)],
        [query_v, bias] + blocks[:-1],
        "attend_most",
        scratch=[pltpu.VMEM((width, early), bf16)],
        work=2,
        dims=dims,
    )
    stats, last_scores, *outs = call(
        forward_kernel,
        [((3 * heads, rows), f32), ((heads, rows, rows), f32)]
        + [((pair * width, rows), bf16)] * KEY_GROUPS,
        [query_v, grad_t, bias, blocks[-1], part_stats, part_sums],
        "attend",
        scratch=[
            pltpu.VMEM((heads, rows), f32),
            pltpu.VMEM((width, rows), bf16),
            pltpu.VMEM((heads * width, rows), bf16),
        ],
        work=1,
        dims=dims,
    )
    all_stats = [stats, over_dp(stats, 1)]
    all_outs = [outs[0], over_dp(outs[1], 1)]
    ahead = 4 * heads * held * rows <= 8 * MIB
    dprobs = []
    if ahead:
        dprobs = call(
            dprobs_kernel,
            [((heads, held, rows), f32)],
            [grad_v] + blocks,
            "dprobs",
            work=1,
            dims=dims,
        )

    inputs = [query_v, grad_v] + blocks + [scores, last_scores] + list(dprobs) + all_stats

    def differentiate(own, dtype, after):
        return call(
            backward_kernel,
            [((heads, held // 2, rows), bf16), ((held // 2, 2 * width), dtype)],
            inputs + after,
            "differentiate_own" if own else "differentiate_other",
            scratch=[pltpu.VMEM((held // 2, 2 * width), f32)],
            work=2,
            dims=dims,
            ahead=ahead,
            own=own,
        )

    other_scores, send = differentiate(False, bf16, [])
    got = over_cores(send)
    own_scores, keep = differentiate(True, f32, [other_scores])
    attn_out, token = call(
        finish_out_kernel,
        [((rows, pair * width), bf16), ((8, 128), f32)],
        all_stats + all_outs,
        "finish_out",
        dims=dims,
    )
    quarter = held // 4
    keep, send = call(
        join_kernel,
        [((quarter, 2 * width), f32), ((quarter, 2 * width), bf16)],
        [keep, got],
        "join_cores",
    )
    dqs = call(
        query_kernel,
        [((pair * width, rows), bf16)] * KEY_GROUPS,
        blocks + [own_scores, other_scores, keep],
        "query_terms",
        scratch=[pltpu.VMEM((width, held // 2), bf16)] * 2,
        work=1,
        dims=dims,
    )
    all_dqs = [dqs[0], over_dp(dqs[1], 1)]
    rounds = spread_rounds(chips)
    terms, *pieces = call(
        spread_kernel,
        [((piece, 2 * width), f32)] + [((piece, 2 * width), bf16)] * len(rounds),
        [keep, over_dp(send, 2), token],
        "join_heads",
        rounds=rounds,
    )
    grad_q, token = call(
        finish_query_kernel,
        [((rows, pair * width), bf16), ((8, 128), f32)],
        all_dqs,
        "finish_query",
    )
    got = [spread(p, moves) for p, moves in zip(pieces, rounds)]
    for array in got[:-1]:
        (terms,) = call(add_kernel, [((piece, 2 * width), f32)], [terms, array], "add_terms")
    grad_k, grad_values = call(
        finish_kernel, [((piece, width), bf16)] * 2, [token, terms, got[-1]], "finish"
    )
    return attn_out, grad_q, grad_k, grad_values


def solution(mesh):
    return jax.shard_map(
        on_device,
        mesh=mesh,
        in_specs=(P("ctx", None), P("ctx", None), P("ctx", None), P("ctx", None), P()),
        out_specs=(P("ctx", "dp"), P("ctx", "dp"), P(("dp", "ctx"), None), P(("dp", "ctx"), None)),
        check_vma=False,
    )
```
